32 devices in a mesh: dp: 8 (over z, x), tensor: 4 (over y, core).
Axes of the slice: x: 2, y: 2, z: 4, core: 2. Of those that a mesh axis runs over, the one named last changes fastest.
Arguments:
- context: bfloat16 [4096, 4096], P('dp', 'tensor'), may hold values from -134 to 134, as said below
- latents: bfloat16 [4096, 4096], P('dp', 'tensor'), may hold values from -12 to 12, as said below
- gain_ctx: float32 [4096], replicated, may hold values from 0.1 to 1.9
- gain_lat: float32 [4096], replicated, may hold values from 0.1 to 1.9
- w_query: bfloat16 [4096, 1536], P(None, 'tensor'), may hold values from -0.09375 to 0.09375
- key_matrix: bfloat16 [4096, 384], P(None, 'tensor'), may hold values from -0.09375 to 0.09375
- value_matrix: bfloat16 [4096, 384], P(None, 'tensor'), may hold values from -0.09375 to 0.09375
- w_out: bfloat16 [4096, 1536], P(None, 'tensor'), may hold values from -1 to 1
- lengths: int32 [8, 8], P('dp'), may hold values from 1 to 128, 512 in all within a row
- patch_flags: int32 [4096], P('dp'), may hold values 0 or 1
- cotangent: bfloat16 [4096, 4096], P('dp', 'tensor'), may hold values from -6 to 6
Outputs:
- latents_out: bfloat16 [4096, 4096], P('dp', 'tensor')
- grad_context: bfloat16 [4096, 4096], P('dp', 'tensor')
- grad_latents: bfloat16 [4096, 4096], P('dp', 'tensor')
- grad_w_query: float32 [4096, 1536], P('dp', 'tensor')
- grad_w_key: float32 [4096, 384], P('dp', 'tensor')
- grad_w_value: float32 [4096, 384], P('dp', 'tensor')
- grad_w_out: float32 [4096, 1536], P('dp', 'tensor')
- grad_gain_ctx: float32 [4, 1024], P('tensor', 'dp')
- grad_gain_lat: float32 [4, 1024], P('tensor', 'dp')
The draws below stay inside these ranges and needn't reach their ends.
Inputs may be any that keep to these rules, and one draw needn't show every extreme that they name: `lengths`: row b lists, in order, the patch counts of the 8 images whose patches fill rows b * 512 to (b + 1) * 512 - 1 of context; every row sums to 512. `context`: real values. `latents`: real values.
All inputs are finite; a program needn't handle non-finite values. No bound on the sum of `patch_flags` on one device may be relied on, other than what follows from the above.
Results may differ from the reference program's by a relative error of at most 0.013.
Values may be sent and summed in bfloat16 or wider, within the bound.
A program may use at most 192 MiB of HBM per device.

```python
import math
import jax
import jax.numpy as jnp
import numpy as np
from jax import lax

MODEL_DIM = 4096
QUERY_HEADS = 16
KEY_VALUE_HEADS = 4
HEAD_DIM = 96
LAT = 64
IMG_DEV = 8
IMG_PATCH = 64
PATCH_DEV = 512
PATCH_MOST = 128
PATCHES = 4096
LATS = 4096
N_DP = 8
N_TENSOR = 4


def draw_context(key, part):
    key = jax.random.fold_in(key, 11)
    key_base, projected_key_rows = jax.random.split(key, 2)
    total_rows = IMG_PATCH * IMG_DEV * N_DP
    base = jax.random.normal(key_base, (total_rows, MODEL_DIM), jnp.float32)
    base = jnp.clip(base, -4.0, 4.0)
    row_part = 10.0 ** jax.random.uniform(projected_key_rows, (total_rows, 1), jnp.float32)
    col_part = 10.0 ** (jnp.arange(MODEL_DIM, dtype=jnp.float32) / MODEL_DIM)
    return (base * row_part * col_part[None, :] / 3.0).astype(jnp.bfloat16)


def draw_latents(key, part):
    key = jax.random.fold_in(key, 23)
    key_base, projected_key_rows = jax.random.split(key, 2)
    total_rows = LAT * IMG_DEV * N_DP
    base = jax.random.normal(key_base, (total_rows, MODEL_DIM), jnp.float32)
    base = jnp.clip(base, -4.0, 4.0)
    row_part = 2.0 ** (2.0 * jax.random.uniform(projected_key_rows, (total_rows, 1), jnp.float32) - 1.0)
    col_part = 0.5 + jnp.arange(MODEL_DIM, dtype=jnp.float32) / MODEL_DIM
    return (base * row_part * col_part[None, :]).astype(jnp.bfloat16)


def place_ends(entries, rng, low, top_value):
    place = [jax.random.randint(jax.random.fold_in(rng, axis), (), 0, length) for axis, length in enumerate(entries.shape)]
    widest = entries.shape.index(max(entries.shape))
    neighbour = place[:widest] + [(place[widest] + 1) % entries.shape[widest]] + place[widest + 1:]
    return entries.at[tuple(place)].set(low).at[tuple(neighbour)].set(top_value)


def with_spikes(entries, own_key, source, target, blocks, factor):
    owner, partner = [(jnp.arange(entries.shape[dim]) // (entries.shape[dim] // blocks)).reshape([-1 if axis == dim else 1 for axis in range(entries.ndim)]) for dim in (source, target)]
    chosen = jax.random.permutation(own_key, blocks)[partner]
    strong = (owner == chosen) | (owner == (partner + blocks // 2) % blocks)
    return jnp.where(strong, factor * entries, entries)


def block_scale(stream_key, dims, shards, low, top_value):
    factor_of, own = 1.0, jax.random.fold_in(stream_key, 6)
    for position, shards_of in shards:
        steps = jnp.exp(jax.random.uniform(jax.random.fold_in(own, position), (shards_of,), jnp.float32, low / len(shards), top_value / len(shards)))
        factor_of = factor_of * jnp.repeat(steps, dims[position] // shards_of).reshape([-1 if axis == position else 1 for axis in range(len(dims))])
    return factor_of


def split_up(number_of, total, reach, lean):
    weights = [(1 << 20) // math.isqrt(rank ** lean) + 1 for rank in range(2, number_of + 1)]
    surplus, holding = total - reach - (number_of - 1), [1] * (number_of - 1)
    while surplus > 0:
        candidates = [i for i in range(number_of - 1) if holding[i] < reach]
        whole, budget = sum([weights[i] for i in candidates]), surplus
        for i in candidates:
            more = min(reach - holding[i], max(1, budget * weights[i] // whole), surplus)
            holding[i] = holding[i] + more
            surplus = surplus - more
    return np.array([reach] + holding)


def ragged_sizes(rng, number_of, total, reach, lean):
    if number_of == 2:
        one = jax.random.randint(rng, (), max(1, total - reach), min(reach, total - 1) + 1)
        return jnp.stack([one, total - one])
    tallies = jnp.asarray(split_up(number_of, total, reach, lean), jnp.int32)
    twos = (number_of - 1) // 2
    donor, taker = tallies[1:1 + 2 * twos:2], tallies[2:2 + 2 * twos:2]
    slack = jnp.minimum(donor - 1, reach - taker)
    passed = jax.random.randint(jax.random.fold_in(rng, 1), (twos,), 0, 1 << 20) % (slack + 1)
    tallies = tallies.at[1:1 + 2 * twos:2].set(donor - passed).at[2:2 + 2 * twos:2].set(taker + passed)
    return tallies[jax.random.permutation(jax.random.fold_in(rng, 2), number_of)]


def noise(own_key, shape, deviation, bound, pieces=(), kind=jnp.bfloat16):
    factor_of = block_scale(own_key, shape, pieces, -0.22, 0.18) if pieces else 1.0
    result = jax.random.normal(own_key, shape, jnp.float32) * deviation * factor_of
    return jnp.minimum(jnp.maximum(result, -bound), bound).astype(kind)


def heavy_noise(stream_key, dims, scale, limit, pieces, heavy, kind=jnp.bfloat16):
    drawn = scale * jax.random.normal(stream_key, dims, jnp.float32)
    if pieces:
        drawn = drawn * block_scale(stream_key, dims, pieces, -0.22, 0.18)
    return jnp.clip(with_spikes(drawn, jax.random.fold_in(stream_key, 3), *heavy), -limit, limit).astype(kind)


def setup_inputs(seed: int = 0) -> dict:
    key_of = jax.random.split(jax.random.key(seed), 12)
    return {
        "context": draw_context(jax.random.fold_in(key_of[11], 71), 0),
        "latents": draw_latents(jax.random.fold_in(key_of[11], 71), 0),
        "gain_ctx": jnp.clip(1.0 + 0.18 * jax.random.normal(key_of[2], (MODEL_DIM,), jnp.float32), 0.1, 1.9),
        "gain_lat": jnp.clip(1.0 + 0.18 * jax.random.normal(key_of[3], (MODEL_DIM,), jnp.float32), 0.1, 1.9),
        "w_query": noise(key_of[4], (MODEL_DIM, QUERY_HEADS * HEAD_DIM), MODEL_DIM ** -0.5, 0.09375, ((1, 4),)),
        "key_matrix": noise(key_of[5], (MODEL_DIM, KEY_VALUE_HEADS * HEAD_DIM), MODEL_DIM ** -0.5, 0.09375, ((1, 4),)),
        "value_matrix": noise(key_of[6], (MODEL_DIM, KEY_VALUE_HEADS * HEAD_DIM), MODEL_DIM ** -0.5, 0.09375, ((1, 4),)),
        "w_out": noise(key_of[7], (MODEL_DIM, QUERY_HEADS * HEAD_DIM), (max(QUERY_HEADS * HEAD_DIM // 48, 4)) ** -0.5, 1.0, ((1, 4),)),
        "lengths": jax.vmap(lambda own: ragged_sizes(own, IMG_DEV, PATCH_DEV, PATCH_MOST, 2))(jax.random.split(key_of[8], N_DP)).reshape((N_DP, IMG_DEV)).astype(jnp.int32),
        "patch_flags": place_ends((jax.random.randint(key_of[9], (PATCHES,), 0, 8) < 7).astype(jnp.int32), jax.random.fold_in(key_of[9], 1), 0, 1),
        "cotangent": heavy_noise(key_of[10], (LATS, MODEL_DIM), 1.0, 6.0, ((0, 8), (1, 4)), (0, 1, 8, 2.0)),
    }


epsilon = 1e-06
masked_value = -1e+30
precise = lax.Precision.HIGHEST

@jax.custom_vjp
def low(v):
    return lax.optimization_barrier(v.astype(jnp.bfloat16)).astype(jnp.float32)

@jax.custom_vjp
def low_back(v):
    return v

def low_keep(v):
    return (low(v), None)

def low_pass(kept, grad):
    return (grad,)

def back_keep(v):
    return (v, None)

def back_low(kept, grad):
    return (low(grad),)
low.defvjp(low_keep, low_pass)
low_back.defvjp(back_keep, back_low)

def norm_rows(values_in, gain):
    return values_in * lax.rsqrt(lax.optimization_barrier(jnp.mean(values_in * values_in, axis=1, keepdims=True)) + epsilon) * gain

def block_forward(allowed, context_in, latent_in, gain_ctx, gain_lat, w_query, key_matrix, value_matrix, w_out):
    ctx_norm = low(norm_rows(context_in, gain_ctx))
    lat_norm = low(norm_rows(latent_in, gain_lat))
    latent_rows = latent_in.shape[0]
    all_rows = jnp.concatenate([ctx_norm, lat_norm], axis=0)
    count_of_rows = all_rows.shape[0]
    queries = low_back(low(jnp.dot(lat_norm, w_query, precision=precise)))
    projected_key_rows = low_back(low(jnp.dot(all_rows, key_matrix, precision=precise)))
    projected_value_rows = low_back(low(jnp.dot(all_rows, value_matrix, precision=precise)))
    key_value_group = jnp.arange(QUERY_HEADS, dtype=jnp.int32) // (QUERY_HEADS // KEY_VALUE_HEADS)
    query_heads = queries.reshape(latent_rows, QUERY_HEADS, HEAD_DIM).transpose(1, 0, 2)
    key_head_split = projected_key_rows.reshape(count_of_rows, KEY_VALUE_HEADS, HEAD_DIM).transpose(1, 0, 2)[key_value_group]
    value_head_split = projected_value_rows.reshape(count_of_rows, KEY_VALUE_HEADS, HEAD_DIM).transpose(1, 0, 2)[key_value_group]

    def head_attend(member):
        query_head, key_head, value_head = member
        raw_scores = low_back(jnp.dot(query_head, key_head.T, precision=precise) * HEAD_DIM ** (-0.5))
        raw_scores = jnp.where(allowed, raw_scores, masked_value)
        attention = low(jax.nn.softmax(raw_scores, axis=1))
        return jnp.dot(attention, value_head, precision=precise)
    blended = lax.map(jax.checkpoint(head_attend), (query_heads, key_head_split, value_head_split))
    attended = low_back(low(blended.transpose(1, 0, 2).reshape(latent_rows, QUERY_HEADS * HEAD_DIM)))
    return latent_in + jnp.dot(attended, w_out.T, precision=precise)

def reference(context, latents, gain_ctx, gain_lat, w_query, key_matrix, value_matrix, w_out, lengths, patch_flags, cotangent):
    patch_rows = IMG_PATCH * IMG_DEV
    latent_rows = LAT * IMG_DEV
    weights = tuple((arr.astype(jnp.float32) for arr in (gain_ctx, gain_lat, w_query, key_matrix, value_matrix, w_out)))
    ctx_blocks = context.astype(jnp.float32).reshape(N_DP, patch_rows, MODEL_DIM)
    lat_blocks = latents.astype(jnp.float32).reshape(N_DP, latent_rows, MODEL_DIM)
    cot_blocks = cotangent.astype(jnp.float32).reshape(N_DP, latent_rows, MODEL_DIM)
    flag_blocks = patch_flags.reshape(N_DP, patch_rows)

    def scan_step(totals, dev_block):
        context_in, latent_in, counts, keep_flags, grad_out = dev_block
        image_ends = jnp.cumsum(counts).astype(jnp.int32)
        patch_index = jnp.arange(patch_rows, dtype=jnp.int32)
        patch_image = lax.optimization_barrier(jnp.sum((patch_index[:, None] >= image_ends[None, :]).astype(jnp.int32), axis=1))
        latent_image = jnp.arange(latent_rows, dtype=jnp.int32) // LAT
        allowed = jnp.concatenate([(latent_image[:, None] == patch_image[None, :]) & (keep_flags[None, :] == 1), latent_image[:, None] == latent_image[None, :]], axis=1)

        def forward_fn(*operands):
            return block_forward(allowed, *operands)
        out_rows, pull_back = jax.vjp(forward_fn, context_in, latent_in, *weights)
        gradients = pull_back(grad_out)
        totals = tuple((total_sum + grad_part for total_sum, grad_part in zip(totals, gradients[2:])))
        return (totals, (out_rows.astype(jnp.bfloat16), gradients[0].astype(jnp.bfloat16), gradients[1].astype(jnp.bfloat16)))
    start_sums = tuple((jnp.zeros_like(arr) for arr in weights))
    totals, (out_rows, grad_ctx, grad_lat) = lax.scan(scan_step, start_sums, (ctx_blocks, lat_blocks, lengths, flag_blocks, cot_blocks))
    grad_gain_c, grad_gain_l, grad_wq, grad_wk, grad_wv, grad_wo = totals
    return (out_rows.reshape(LAT * IMG_DEV * N_DP, MODEL_DIM), grad_ctx.reshape(IMG_PATCH * IMG_DEV * N_DP, MODEL_DIM), grad_lat.reshape(LAT * IMG_DEV * N_DP, MODEL_DIM), grad_wq, grad_wk, grad_wv, grad_wo, grad_gain_c.reshape(N_TENSOR, MODEL_DIM // N_TENSOR), grad_gain_l.reshape(N_TENSOR, MODEL_DIM // N_TENSOR))
```

```python
import functools

import jax
import jax.numpy as jnp
from jax import lax
from jax.experimental import pallas as pl
from jax.experimental.pallas import tpu as pltpu
from jax.sharding import PartitionSpec as P

HEAD_DIM = 96
LAT = 64


epsilon = 1e-06
masked_value = -1e30
contract_rows = (((0,), (0,)), ((), ()))
contract_cols = (((1,), (1,)), ((), ()))


def row_scales(rows_in):
    values_f = rows_in.astype(jnp.float32)
    return (values_f, lax.rsqrt(jnp.mean(values_f * values_f, axis=1) + epsilon))


def norm_back(grad_norm, local_vals, row_scale, gain_local, row_inner_all, model_width):
    weighted = grad_norm * gain_local
    grad_input = (
        row_scale[:, None] * weighted
        - local_vals * (row_scale**3 * row_inner_all / model_width)[:, None]
    )
    grad_gain = jnp.sum(grad_norm * local_vals * row_scale[:, None], axis=0)
    return (grad_input, grad_gain)


def plain_local(
    context,
    latents,
    gain_ctx,
    gain_lat,
    w_query,
    key_matrix,
    value_matrix,
    w_out,
    lengths,
    patch_flags,
    cotangent,
):
    patch_rows = context.shape[0]
    latent_rows = latents.shape[0]
    local_width = context.shape[1]
    model_width = gain_ctx.shape[0]
    head_size = HEAD_DIM
    kv_local = key_matrix.shape[1] // head_size
    query_local = w_query.shape[1] // head_size
    repeat = query_local // kv_local
    all_count = patch_rows + latent_rows
    score_scale = head_size ** (-0.5)
    column = lax.axis_index("tensor") * local_width
    whole_ctx, whole_lat = (
        lax.all_gather(context, "tensor", axis=1, tiled=True),
        lax.all_gather(latents, "tensor", axis=1, tiled=True),
    )
    ctx_values, ctx_scale = row_scales(whole_ctx)
    lat_values, lat_scale = row_scales(whole_lat)
    ctx_norm = (ctx_values * ctx_scale[:, None] * gain_ctx).astype(jnp.bfloat16)
    lat_norm = (lat_values * lat_scale[:, None] * gain_lat).astype(jnp.bfloat16)
    queries = jnp.dot(lat_norm, w_query, preferred_element_type=jnp.float32).astype(jnp.bfloat16)
    all_rows = jnp.concatenate([ctx_norm, lat_norm], axis=0)
    w_pair = jnp.concatenate([key_matrix, value_matrix], axis=1)
    pair_rows = jnp.dot(all_rows, w_pair, preferred_element_type=jnp.float32).astype(jnp.bfloat16)
    key_head_split = (
        pair_rows[:, : kv_local * head_size]
        .reshape(all_count, kv_local, head_size)
        .transpose(1, 0, 2)
    )
    value_head_split = (
        pair_rows[:, kv_local * head_size :]
        .reshape(all_count, kv_local, head_size)
        .transpose(1, 0, 2)
    )
    query_heads = queries.reshape(latent_rows, query_local, head_size).transpose(1, 0, 2)
    image_ends = jnp.cumsum(lengths[0])
    patch_image = jnp.sum(
        (jnp.arange(patch_rows)[:, None] >= image_ends[None, :]).astype(jnp.int32), axis=1
    )
    latent_image = jnp.arange(latent_rows) // LAT
    allowed = jnp.concatenate(
        [
            (latent_image[:, None] == patch_image[None, :]) & (patch_flags[None, :] == 1),
            latent_image[:, None] == latent_image[None, :],
        ],
        axis=1,
    )
    head_index = jnp.arange(query_local)

    def head_scores(query_head, head_number):
        key_head = key_head_split[head_number // repeat]
        value_head = value_head_split[head_number // repeat]
        raw_scores = (
            lax.dot_general(query_head, key_head, contract_cols, preferred_element_type=jnp.float32)
            * score_scale
        )
        return (jnp.where(allowed, raw_scores, masked_value), key_head, value_head)

    def head_forward(member):
        query_head, head_number = member
        scores, key_head, value_head = head_scores(query_head, head_number)
        row_top = jnp.max(scores, axis=1, keepdims=True)
        exp_scores = jnp.exp(scores - row_top)
        row_total = jnp.sum(exp_scores, axis=1, keepdims=True)
        attention = (exp_scores / row_total).astype(jnp.bfloat16)
        blended = jnp.dot(attention, value_head, preferred_element_type=jnp.float32).astype(
            jnp.bfloat16
        )
        return (blended, row_top[:, 0] + jnp.log(row_total[:, 0]))

    heads_out, log_totals = lax.map(head_forward, (query_heads, head_index))
    attended = heads_out.transpose(1, 0, 2).reshape(latent_rows, query_local * head_size)
    partial_out = lax.dot_general(
        attended, w_out, contract_cols, preferred_element_type=jnp.float32
    )
    branch = lax.psum_scatter(
        partial_out.astype(jnp.bfloat16), "tensor", scatter_dimension=1, tiled=True
    ).astype(jnp.float32)
    latents_out = (latents.astype(jnp.float32) + branch).astype(jnp.bfloat16)
    full_grad = lax.all_gather(cotangent, "tensor", axis=1, tiled=True)
    grad_attended = jnp.dot(full_grad, w_out, preferred_element_type=jnp.float32).astype(
        jnp.bfloat16
    )
    grad_w_out = lax.dot_general(
        full_grad, attended, contract_rows, preferred_element_type=jnp.float32
    )
    grad_heads = grad_attended.reshape(latent_rows, query_local, head_size).transpose(1, 0, 2)

    def head_backward(member):
        query_head, grad_blended, log_total, head_number = member
        scores, key_head, value_head = head_scores(query_head, head_number)
        attention = jnp.exp(scores - log_total[:, None])
        grad_probs = lax.dot_general(
            grad_blended, value_head, contract_cols, preferred_element_type=jnp.float32
        )
        row_inner = jnp.sum(attention * grad_probs, axis=1, keepdims=True)
        grad_scores = (attention * (grad_probs - row_inner)).astype(jnp.bfloat16)
        grad_query = (
            jnp.dot(grad_scores, key_head, preferred_element_type=jnp.float32) * score_scale
        ).astype(jnp.bfloat16)
        grad_key = (
            lax.dot_general(
                grad_scores, query_head, contract_rows, preferred_element_type=jnp.float32
            )
            * score_scale
        )
        grad_value = lax.dot_general(
            attention.astype(jnp.bfloat16),
            grad_blended,
            contract_rows,
            preferred_element_type=jnp.float32,
        )
        return (grad_query, grad_key, grad_value)

    grad_query_heads, grad_key_heads, grad_value_heads = lax.map(
        head_backward, (query_heads, grad_heads, log_totals, head_index)
    )
    grad_keys = grad_key_heads.reshape(kv_local, repeat, all_count, head_size).sum(axis=1)
    grad_values = grad_value_heads.reshape(kv_local, repeat, all_count, head_size).sum(axis=1)
    grad_pair = jnp.concatenate(
        [
            grad_keys.transpose(1, 0, 2).reshape(all_count, kv_local * head_size),
            grad_values.transpose(1, 0, 2).reshape(all_count, kv_local * head_size),
        ],
        axis=1,
    ).astype(jnp.bfloat16)
    grad_q_rows = grad_query_heads.transpose(1, 0, 2).reshape(latent_rows, query_local * head_size)
    grad_w_query = lax.dot_general(
        lat_norm, grad_q_rows, contract_rows, preferred_element_type=jnp.float32
    )
    grad_w_pair = lax.dot_general(
        all_rows, grad_pair, contract_rows, preferred_element_type=jnp.float32
    )
    grad_rows = lax.dot_general(
        grad_pair, w_pair, contract_cols, preferred_element_type=jnp.float32
    )
    lat_terms = grad_rows[patch_rows:] + lax.dot_general(
        grad_q_rows, w_query, contract_cols, preferred_element_type=jnp.float32
    )
    grad_ctx_norm, grad_lat_norm = (
        lax.psum_scatter(
            grad_rows[:patch_rows].astype(jnp.bfloat16), "tensor", scatter_dimension=1, tiled=True
        ).astype(jnp.float32),
        lax.psum_scatter(
            lat_terms.astype(jnp.bfloat16), "tensor", scatter_dimension=1, tiled=True
        ).astype(jnp.float32),
    )
    ctx_local = context.astype(jnp.float32)
    lat_local = latents.astype(jnp.float32)
    gain_ctx_local = lax.dynamic_slice_in_dim(gain_ctx, column, local_width, 0)
    gain_lat_local = lax.dynamic_slice_in_dim(gain_lat, column, local_width, 0)
    ctx_inner = jnp.sum(grad_ctx_norm * gain_ctx_local * ctx_local, axis=1)
    lat_inner = jnp.sum(grad_lat_norm * gain_lat_local * lat_local, axis=1)
    ctx_inner_all, lat_inner_all = lax.psum((ctx_inner, lat_inner), "tensor")
    grad_ctx_in, grad_gain_c = norm_back(
        grad_ctx_norm, ctx_local, ctx_scale, gain_ctx_local, ctx_inner_all, model_width
    )
    grad_lat_in, grad_gain_l = norm_back(
        grad_lat_norm, lat_local, lat_scale, gain_lat_local, lat_inner_all, model_width
    )
    grad_context = grad_ctx_in.astype(jnp.bfloat16)
    grad_latents = (cotangent.astype(jnp.float32) + grad_lat_in).astype(jnp.bfloat16)
    grad_w_key = grad_w_pair[:, : kv_local * head_size]
    grad_w_value = grad_w_pair[:, kv_local * head_size :]
    sum_query, sum_key, sum_value, sum_out, sum_gain_c, sum_gain_l = (
        lax.psum_scatter(grad_w_query, "dp", scatter_dimension=0, tiled=True),
        lax.psum_scatter(grad_w_key, "dp", scatter_dimension=0, tiled=True),
        lax.psum_scatter(grad_w_value, "dp", scatter_dimension=0, tiled=True),
        lax.psum_scatter(grad_w_out, "dp", scatter_dimension=0, tiled=True),
        lax.psum_scatter(grad_gain_c, "dp", scatter_dimension=0, tiled=True),
        lax.psum_scatter(grad_gain_l, "dp", scatter_dimension=0, tiled=True),
    )
    return (
        latents_out,
        grad_context,
        grad_latents,
        sum_query,
        sum_key,
        sum_value,
        sum_out,
        sum_gain_c.reshape(1, -1),
        sum_gain_l.reshape(1, -1),
    )


MESH = pl.DeviceIdType.MESH
f32 = jnp.float32
bf16 = jnp.bfloat16
ROWS = 128


def nn(a, b):
    return jnp.dot(a, b, preferred_element_type=f32)


def nt(a, b):
    return lax.dot_general(a, b, contract_cols, preferred_element_type=f32)


def flip(a):
    return a.astype(f32).T.astype(bf16)


def block_kernel(
    n_dp,
    context,
    latents,
    cotangent,
    gain_ctx,
    gain_lat,
    w_query,
    w_pair,
    w_out,
    lengths,
    flags,
    out_latents,
    out_context,
    out_grad_lat,
    out_query,
    out_key,
    out_value,
    out_out,
    out_gain,
    lat_all,
    ctx_all,
    cot_all,
    raw_lat,
    raw_ctx,
    wq,
    wkv,
    wo,
    acc_q,
    acc_c,
    acc_l,
    q_t,
    ga_t,
    att_t,
    sgq_t,
    q_heads,
    ga_heads,
    att,
    sgq,
    kv_ct,
    kv_lt,
    sgc_t,
    sgl_t,
    sgc,
    sgl,
    probs_c,
    probs_l,
    gkv_c,
    gkv_l,
    sums,
    inners,
    scale_row,
    coef_row,
    gain_part,
    gain_sum,
    gain_recv,
    core_send,
    core_recv,
    y_recv,
    x_send,
    x_send_kv,
    x_recv_o,
    x_recv_q,
    x_recv_kv,
    z_recv_o,
    z_recv_q,
    z_recv_kv,
    dp_acc,
    dp_acc_kv,
    stage,
    stage_kv,
    send_sem,
    recv_sem,
    local_sem,
):
    rows, width = raw_lat.shape
    n_rows = rows // ROWS
    n_hi = n_dp // 2
    feat = 4 * width // n_dp
    heads = q_heads.shape[0]
    head = HEAD_DIM
    model_width = 4 * width
    score_scale = head ** (-0.5)

    dp = lax.axis_index("dp")
    f = lax.axis_index("tensor")
    z, x = dp // 2, lax.rem(dp, 2)
    y, c = f // 2, lax.rem(f, 2)
    f_c = y * 2 + (1 - c)
    f_y = (1 - y) * 2 + c
    f_yc = (1 - y) * 2 + (1 - c)
    core_dev, y_dev, yc_dev = (dp, f_c), (dp, f_y), (dp, f_yc)
    x_dev = (z * 2 + 1 - x, f)
    up_dev, down_dev = ((z + 1) * 2 + x, f), ((z - 1) * 2 + x, f)

    def bit_dev(bit):
        partner = z + bit - 2 * bit * lax.rem(z // bit, 2)
        return (partner * 2 + x, f)

    bits = []
    while 2 ** len(bits) < n_hi:
        bits.append(2 ** len(bits))

    count = [0]

    def take(n):
        count[0] += n
        return count[0] - n

    def remote(src, dst, sem, dev, sem_to=None):
        return pltpu.make_async_remote_copy(
            src_ref=src,
            dst_ref=dst,
            send_sem=send_sem.at[sem],
            recv_sem=recv_sem.at[sem if sem_to is None else sem_to],
            device_id=dev,
            device_id_type=MESH,
        )

    def local_copy(src, dst, i):
        return pltpu.make_async_copy(src, dst, local_sem.at[i])

    def part_rows(k):
        if isinstance(k, int):
            return pl.ds(k * ROWS, ROWS)
        return pl.ds(pl.multiple_of(k * ROWS, ROWS), ROWS)

    loads = [
        local_copy(latents, raw_lat, 0),
        local_copy(context, raw_ctx, 1),
        local_copy(cotangent, cot_all.at[f], 2),
        local_copy(w_query, wq, 3),
        local_copy(w_pair, wkv, 4),
        local_copy(w_out, wo, 5),
    ]
    for load in loads:
        load.start()

    barrier = pltpu.get_barrier_semaphore()

    def greet(dev):
        pl.semaphore_signal(barrier, inc=1, device_id=dev, device_id_type=MESH)

    always = [core_dev, y_dev, yc_dev, x_dev] + [bit_dev(b) for b in bits[1:]]
    for dev in always:
        greet(dev)
    pl.when(z > 0)(lambda: greet(down_dev))
    pl.when(z < n_hi - 1)(lambda: greet(up_dev))
    middle = (z > 0) & (z < n_hi - 1)
    pl.semaphore_wait(barrier, len(always) + 1 + middle.astype(jnp.int32))

    sem_lat, sem_ctx, sem_cot = (take(2 * n_rows + 1) for _ in range(3))

    def gather_y(buf, base, k):
        return remote(buf.at[f, part_rows(k)], buf.at[f, part_rows(k)], base + k, y_dev)

    def gather_core(buf, base):
        return remote(buf.at[f], buf.at[f], base + n_rows, core_dev)

    def gather_on(buf, base, k):
        return remote(
            buf.at[f_y, part_rows(k)], buf.at[f_y, part_rows(k)], base + n_rows + 1 + k, core_dev
        )

    def pass_on(buf, base):
        def step(k, carry):
            gather_y(buf, base, k).wait_recv()
            gather_on(buf, base, k).start()
            return carry

        lax.fori_loop(0, n_rows, step, 0)

    def wait_on(buf, base):
        for k in range(n_rows):
            gather_on(buf, base, k).wait_recv()

    def gather_done(buf, base):
        for k in range(n_rows):
            gather_y(buf, base, k).wait_send()
            gather_on(buf, base, k).wait_send()
        gather_core(buf, base).wait_send()

    def weigh(raw, gain, buf, base, index):
        gain_row = gain[pl.ds(f, 1), :]
        for k in range(n_rows):
            values = raw[part_rows(k), :].astype(f32)
            buf[f, part_rows(k), :] = (values * gain_row).astype(bf16)
            gather_y(buf, base, k).start()
        gather_core(buf, base).start()
        for k in range(n_rows):
            values = raw[part_rows(k), :].astype(f32)
            total = jnp.sum(values * values, axis=1, keepdims=True)
            across = jnp.broadcast_to(total, (ROWS, 128)).T
            sums[f, pl.ds(index, 1), part_rows(k)] = across[0:1, :]

    sums[f] = jnp.zeros(sums.shape[1:], f32)
    inners[f] = jnp.zeros(inners.shape[1:], f32)
    loads[0].wait()
    weigh(raw_lat, gain_lat, lat_all, sem_lat, 1)
    loads[1].wait()
    weigh(raw_ctx, gain_ctx, ctx_all, sem_ctx, 0)
    loads[2].wait()
    for k in range(n_rows):
        gather_y(cot_all, sem_cot, k).start()
    gather_core(cot_all, sem_cot).start()

    peers = [core_dev, y_dev, yc_dev]
    sem_sums, sem_inner = take(3), take(3)

    def exchange(buf, base):
        return [remote(buf.at[f], buf.at[f], base + i, dev) for i, dev in enumerate(peers)]

    sums_out = exchange(sums, sem_sums)
    for copy in sums_out:
        copy.start()

    def project(acc, values, weight, blocks, first):
        def step(i, carry):
            fb = blocks[0] + i * (blocks[1] - blocks[0])
            for m in range(2):
                half = pl.ds(m * (rows // 2), rows // 2)
                product = nn(
                    values[fb, half, :], weight[pl.ds(pl.multiple_of(fb * width, width), width), :]
                )
                if first:
                    @pl.when(i == 0)
                    def _():
                        acc[half, :] = product

                    @pl.when(i > 0)
                    def _():
                        acc[half, :] += product
                else:
                    acc[half, :] += product
            return carry

        lax.fori_loop(0, 2, step, 0)

    mine, theirs = (f, f_c), (f_y, f_yc)
    loads[3].wait()
    loads[4].wait()
    loads[5].wait()
    gather_core(lat_all, sem_lat).wait_recv()
    gather_core(ctx_all, sem_ctx).wait_recv()
    project(acc_q, lat_all, wq, mine, True)
    project(acc_l, lat_all, wkv, mine, True)
    project(acc_c, ctx_all, wkv, mine, True)
    pass_on(lat_all, sem_lat)
    wait_on(lat_all, sem_lat)
    project(acc_q, lat_all, wq, theirs, False)
    project(acc_l, lat_all, wkv, theirs, False)

    for copy in sums_out:
        copy.wait()
    total = sums[0] + sums[1] + sums[2] + sums[3]
    scale_row[...] = lax.rsqrt(total / model_width + epsilon)

    def split_heads(acc, out_t, out_heads, scaled):
        for k in range(n_rows):
            across = acc[part_rows(k), :].T
            if scaled:
                across = across * scale_row[1:2, part_rows(k)]
            across = across.astype(bf16)
            out_t[:, part_rows(k)] = across
            for h in range(heads):
                out_heads[h, part_rows(k), :] = flip(across[h * head : (h + 1) * head, :])

    split_heads(acc_q, q_t, q_heads, True)
    for k in range(n_rows):
        kv_lt[:, part_rows(k)] = (acc_l[part_rows(k), :].T * scale_row[1:2, part_rows(k)]).astype(
            bf16
        )

    pass_on(ctx_all, sem_ctx)
    wait_on(ctx_all, sem_ctx)
    project(acc_c, ctx_all, wkv, theirs, False)
    for k in range(n_rows):
        kv_ct[:, part_rows(k)] = (acc_c[part_rows(k), :].T * scale_row[0:1, part_rows(k)]).astype(
            bf16
        )

    patch = lax.broadcasted_iota(jnp.int32, (1, rows), 1)
    image = jnp.zeros((1, rows), jnp.int32)
    end = jnp.int32(0)
    for i in range(lengths.shape[1]):
        end = end + lengths[0, i]
        image = image + (patch >= end).astype(jnp.int32)
    image = jnp.where(flags[...] == 1, image, -1)
    per_part = ROWS // LAT
    row_image = lax.broadcasted_iota(jnp.int32, (ROWS, 1), 0) // LAT
    col_image = lax.broadcasted_iota(jnp.int32, (1, ROWS), 1) // LAT
    same = row_image == col_image
    keys, vals = pl.ds(0, head), pl.ds(head, head)

    def forward_step(n, carry):
        h, p = n // n_rows, lax.rem(n, n_rows)
        head_rows = pl.ds(pl.multiple_of(h * head, 32), head)
        q = q_heads[h, part_rows(p), :]
        allowed = (row_image + p * per_part) == image
        far = jnp.where(allowed, nn(q, kv_ct[keys, :]) * score_scale, masked_value)
        near = jnp.where(same, nn(q, kv_lt[keys, part_rows(p)]) * score_scale, masked_value)
        top = jnp.maximum(
            jnp.max(far, axis=1, keepdims=True), jnp.max(near, axis=1, keepdims=True)
        )
        far, near = jnp.exp(far - top), jnp.exp(near - top)
        total = jnp.sum(far, axis=1, keepdims=True) + jnp.sum(near, axis=1, keepdims=True)
        far, near = (far / total).astype(bf16), (near / total).astype(bf16)
        probs_c[h, part_rows(p), :] = far
        probs_l[h, part_rows(p), :] = near
        blended = nt(kv_ct[vals, :], far) + nt(kv_lt[vals, part_rows(p)], near)
        att_t[head_rows, part_rows(p)] = blended.astype(bf16)
        return carry

    lax.fori_loop(0, heads * n_rows, forward_step, 0)
    for k in range(n_rows):
        att[part_rows(k), :] = flip(att_t[:, part_rows(k)])

    def features(zt, xt):
        at = (zt * 2 + xt) * feat
        return at // width, pl.ds(pl.multiple_of(lax.rem(at, width), 128), feat)

    def chunk_out(zt, xt):
        fb, cols = features(zt, xt)
        return nn(att_t[...], cot_all[fb, :, cols])

    def chunk_query(zt, xt):
        fb, cols = features(zt, xt)
        return nn(sgq_t[...], lat_all[fb, :, cols])

    def chunk_pair(zt, xt):
        fb, cols = features(zt, xt)
        return nn(sgc_t[...], ctx_all[fb, :, cols]) + nn(sgl_t[...], lat_all[fb, :, cols])

    far_z = jnp.where(z < n_hi // 2, z, n_hi - 1 - z)

    def order(i):
        down = n_hi - 1 - i
        value = jnp.where(i == n_hi - 1, far_z, jnp.where(down <= far_z, down - 1, down))
        return jnp.where(z < n_hi // 2, value, n_hi - 1 - value)

    class Spread:
        def __init__(self, chunk, send, x_recv, z_recv, acc, out):
            self.chunk, self.send, self.x_recv = chunk, send, x_recv
            self.z_recv, self.acc, self.out = z_recv, acc, out
            self.x_sem, self.z_sem = take(n_hi), take(n_hi + 1)

        def x_copy(self, zt):
            return remote(self.send.at[zt], self.x_recv.at[zt], self.x_sem + zt, x_dev)

        def z_copy(self, zt, slot, dev):
            return remote(
                self.x_recv.at[zt], self.z_recv.at[slot], self.z_sem + zt, dev, self.z_sem + slot
            )

        def first(self, zt):
            self.send[zt] = self.chunk(zt, 1 - x).astype(bf16)
            self.x_copy(zt).start()

        def second(self, zt):
            self.x_copy(zt).wait_recv()
            self.acc[...] = self.chunk(zt, x) + self.x_recv[zt].astype(f32)

            def add(slot):
                self.z_copy(zt, slot, up_dev).wait_recv()
                self.acc[...] += self.z_recv[slot].astype(f32)

            from_down = (zt >= z) & (z > 0)
            from_up = (zt < z) & (z < n_hi - 1)
            pl.when(from_down | from_up)(lambda: add(zt))
            pl.when((zt == z) & (z < n_hi - 1))(lambda: add(n_hi))

            @pl.when(zt != z)
            def _():
                self.x_recv[zt] = self.acc[...].astype(bf16)

            @pl.when(zt > z)
            def _():
                self.z_copy(zt, zt, up_dev).start()

            @pl.when((zt < z) & (zt < z - 1))
            def _():
                self.z_copy(zt, zt, down_dev).start()

            @pl.when((zt < z) & (zt == z - 1))
            def _():
                self.z_copy(zt, n_hi, down_dev).start()

        def chain(self):
            def step(i, carry):
                self.second(order(i))
                return carry

            lax.fori_loop(0, n_hi, step, 0)

        def wait_x_sends(self):
            for zt in range(n_hi):
                self.x_copy(zt).wait_send()

        def wait_z_sends(self):
            for zt in range(n_hi):
                pl.when(zt != z)(lambda zt=zt: self.z_copy(zt, zt, up_dev).wait_send())

    grad_o = Spread(chunk_out, x_send, x_recv_o, z_recv_o, dp_acc, out_out)
    grad_q = Spread(chunk_query, x_send, x_recv_q, z_recv_q, dp_acc, out_query)
    grad_kv = Spread(chunk_pair, x_send_kv, x_recv_kv, z_recv_kv, dp_acc_kv, None)

    class Collect:
        def __init__(self, part, index):
            self.part, self.index, self.sem = part, index, take(3 * n_rows)

        def core_copy(self, j, k):
            return remote(
                core_send.at[j, part_rows(k)],
                core_recv.at[self.index, j, part_rows(k)],
                self.sem + j * n_rows + k,
                core_dev,
            )

        def y_copy(self, k):
            return remote(
                core_recv.at[self.index, 0, part_rows(k)],
                y_recv.at[self.index, part_rows(k)],
                self.sem + 2 * n_rows + k,
                y_dev,
            )

        def send(self):
            def core_step(n, carry):
                j, k = n // n_rows, lax.rem(n, n_rows)
                fb = jnp.where(j == 0, f_yc, f_c)
                core_send[j, part_rows(k), :] = self.part(fb, k).astype(bf16)
                self.core_copy(j, k).start()
                return carry

            lax.fori_loop(0, 2 * n_rows, core_step, 0)

            def y_step(k, carry):
                value = self.part(f_y, k)
                self.core_copy(0, k).wait_recv()
                value = value + core_recv[self.index, 0, part_rows(k), :].astype(f32)
                core_recv[self.index, 0, part_rows(k), :] = value.astype(bf16)
                self.y_copy(k).start()
                return carry

            lax.fori_loop(0, n_rows, y_step, 0)
            for j in range(2):
                for k in range(n_rows):
                    self.core_copy(j, k).wait_send()

        def total(self, k):
            value = self.part(f, k)
            self.core_copy(1, k).wait_recv()
            self.y_copy(k).wait_recv()
            return (
                value
                + core_recv[self.index, 1, part_rows(k), :].astype(f32)
                + y_recv[self.index, part_rows(k), :].astype(f32)
            )

        def wait_y_sends(self):
            for k in range(n_rows):
                self.y_copy(k).wait_send()

    def block_of(weight, fb):
        return weight[pl.ds(pl.multiple_of(fb * width, width), width), :]

    def gain_add(index, value, weighed):
        products = (value * weighed.astype(f32)).reshape(ROWS // 8, 8, width)
        gain_part[index] += jnp.sum(products, axis=0)

    def part_branch(fb, k):
        return nt(att[part_rows(k), :], block_of(wo, fb))

    def part_ctx(fb, k):
        value = nt(sgc[part_rows(k), :], block_of(wkv, fb))
        gain_add(fb, value, ctx_all[fb, part_rows(k), :])
        return value

    def part_lat(fb, k):
        value = nt(sgq[part_rows(k), :], block_of(wq, fb))
        value = value + nt(sgl[part_rows(k), :], block_of(wkv, fb))
        gain_add(4 + fb, value, lat_all[fb, part_rows(k), :])
        return value

    branch = Collect(part_branch, 0)
    back_ctx = Collect(part_ctx, 1)
    back_lat = Collect(part_lat, 2)
    gain_part[...] = jnp.zeros(gain_part.shape, f32)

    gather_core(cot_all, sem_cot).wait_recv()
    project(acc_q, cot_all, wo, mine, True)
    for i in range(2):
        grad_o.first(2 * y + i)
    branch.send()
    pass_on(cot_all, sem_cot)
    wait_on(cot_all, sem_cot)
    project(acc_q, cot_all, wo, theirs, False)
    for i in range(2):
        grad_o.first(2 * (1 - y) + i)
    split_heads(acc_q, ga_t, ga_heads, False)

    gkv_c[...] = jnp.zeros(gkv_c.shape, f32)
    gkv_l[...] = jnp.zeros(gkv_l.shape, f32)

    def backward_step(n, carry):
        h, p = n // n_rows, lax.rem(n, n_rows)
        head_rows = pl.ds(pl.multiple_of(h * head, 32), head)
        ga = ga_heads[h, part_rows(p), :]
        far_p, near_p = probs_c[h, part_rows(p), :], probs_l[h, part_rows(p), :]
        far_d = nn(ga, kv_ct[vals, :])
        near_d = nn(ga, kv_lt[vals, part_rows(p)])
        far_f, near_f = far_p.astype(f32), near_p.astype(f32)
        inner = jnp.sum(far_f * far_d, axis=1, keepdims=True) + jnp.sum(
            near_f * near_d, axis=1, keepdims=True
        )
        far_g = (far_f * (far_d - inner)).astype(bf16)
        near_g = (near_f * (near_d - inner)).astype(bf16)
        grad_query = nt(kv_ct[keys, :], far_g) + nt(kv_lt[keys, part_rows(p)], near_g)
        grad_query = grad_query * score_scale
        query = q_t[head_rows, part_rows(p)]
        ga_across = ga_t[head_rows, part_rows(p)]
        inners[f, 1:2, part_rows(p)] += jnp.sum(
            grad_query * query.astype(f32), axis=0, keepdims=True
        )
        sgq_t[head_rows, part_rows(p)] = (grad_query * scale_row[1:2, part_rows(p)]).astype(bf16)
        gkv_c[keys, :] += nn(query, far_g)
        gkv_l[keys, part_rows(p)] += nn(query, near_g)
        gkv_c[vals, :] += nn(ga_across, far_p)
        gkv_l[vals, part_rows(p)] += nn(ga_across, near_p)
        return carry

    lax.fori_loop(0, heads * n_rows, backward_step, 0)
    gkv_c[keys, :] = gkv_c[keys, :] * score_scale
    gkv_l[keys, :] = gkv_l[keys, :] * score_scale
    inners[f, 0:1, :] = jnp.sum(gkv_c[...] * kv_ct[...].astype(f32), axis=0, keepdims=True)
    inners[f, 1:2, :] += jnp.sum(gkv_l[...] * kv_lt[...].astype(f32), axis=0, keepdims=True)
    inner_out = exchange(inners, sem_inner)
    for copy in inner_out:
        copy.start()
    sgc_t[...] = (gkv_c[...] * scale_row[0:1, :]).astype(bf16)
    sgl_t[...] = (gkv_l[...] * scale_row[1:2, :]).astype(bf16)
    for k in range(n_rows):
        sgq[part_rows(k), :] = flip(sgq_t[:, part_rows(k)])
        sgc[part_rows(k), :] = flip(sgc_t[:, part_rows(k)])
        sgl[part_rows(k), :] = flip(sgl_t[:, part_rows(k)])

    back_ctx.send()
    back_lat.send()
    grad_o.wait_x_sends()
    for i in range(n_hi):
        grad_q.first(order(jnp.int32(i)))
    for i in range(n_hi):
        grad_kv.first(order(jnp.int32(i)))
    grad_o.chain()

    outs = []

    def put(src, dst, i):
        copy = local_copy(src, dst, i)
        copy.start()
        outs.append(copy)

    def put_weight(spread, at, i):
        stage[at] = spread.acc[...].T
        put(stage.at[at], spread.out, i)

    put_weight(grad_o, 0, 6)
    grad_q.chain()
    put_weight(grad_q, 1, 7)

    def finish(k, carry):
        value = raw_lat[part_rows(k), :].astype(f32) + branch.total(k)
        y_recv[0, part_rows(k), :] = value.astype(bf16)
        return carry

    lax.fori_loop(0, n_rows, finish, 0)
    put(y_recv.at[0], out_latents, 9)
    for copy in inner_out:
        copy.wait()
    coef_row[...] = (
        scale_row[...]
        * scale_row[...]
        * (inners[0] + inners[1] + inners[2] + inners[3])
        / model_width
    )

    def finish_ctx(k, carry):
        coef = coef_row[:, part_rows(k)].T
        value = back_ctx.total(k) * gain_ctx[pl.ds(f, 1), :]
        value = value - raw_ctx[part_rows(k), :].astype(f32) * coef[:, 0:1]
        y_recv[1, part_rows(k), :] = value.astype(bf16)
        return carry

    lax.fori_loop(0, n_rows, finish_ctx, 0)
    put(y_recv.at[1], out_context, 10)

    def finish_lat(k, carry):
        coef = coef_row[:, part_rows(k)].T
        value = back_lat.total(k) * gain_lat[pl.ds(f, 1), :]
        value = value - raw_lat[part_rows(k), :].astype(f32) * coef[:, 1:2]
        value = value + cot_all[f, part_rows(k), :].astype(f32)
        y_recv[2, part_rows(k), :] = value.astype(bf16)
        return carry

    lax.fori_loop(0, n_rows, finish_lat, 0)
    put(y_recv.at[2], out_grad_lat, 11)
    grad_kv.chain()
    for i, out in enumerate((out_key, out_value)):
        stage_kv[i] = dp_acc_kv[i * head : (i + 1) * head, :].T
        put(stage_kv.at[i], out, 8 + 5 * i)

    for i in range(4):
        gain_sum[i : i + 1, :] = (
            jnp.sum(gain_part[i], axis=0, keepdims=True) / gain_ctx[i : i + 1, :]
        )
        gain_sum[4 + i : 5 + i, :] = (
            jnp.sum(gain_part[4 + i], axis=0, keepdims=True) / gain_lat[i : i + 1, :]
        )
    for i, dev in enumerate([core_dev, y_dev, x_dev] + [bit_dev(b) for b in bits]):
        copy = remote(gain_sum, gain_recv.at[i], take(1), dev)
        copy.start()
        copy.wait()
        gain_sum[...] += gain_recv[i]
    put(gain_sum, out_gain, 12)

    for copy in outs:
        copy.wait()
    for buf, base in ((lat_all, sem_lat), (ctx_all, sem_ctx), (cot_all, sem_cot)):
        gather_done(buf, base)
    for collect in (branch, back_ctx, back_lat):
        collect.wait_y_sends()
    grad_q.wait_x_sends()
    grad_kv.wait_x_sends()
    for spread in (grad_o, grad_q, grad_kv):
        spread.wait_z_sends()


def kernel_local(
    n_dp,
    context,
    latents,
    gain_ctx,
    gain_lat,
    w_query,
    key_matrix,
    value_matrix,
    w_out,
    lengths,
    patch_flags,
    cotangent,
):
    rows, width = context.shape
    model_width = gain_ctx.shape[0]
    units = w_query.shape[1]
    kv = 2 * key_matrix.shape[1]
    heads = units // HEAD_DIM
    n_hi = n_dp // 2
    feat = model_width // n_dp
    w_pair = jnp.concatenate([key_matrix, value_matrix], axis=1)
    steps = 3 + max(1, (n_hi - 1).bit_length())
    any_space = pl.BlockSpec(memory_space=pl.ANY)
    vmem = pl.BlockSpec(memory_space=pltpu.VMEM)
    block = jax.ShapeDtypeStruct((rows, width), bf16)
    shaped = jax.ShapeDtypeStruct
    out = pl.pallas_call(
        functools.partial(block_kernel, n_dp),
        out_shape=(
            block,
            block,
            block,
            shaped((feat, units), f32),
            shaped((feat, kv // 2), f32),
            shaped((feat, kv // 2), f32),
            shaped((feat, units), f32),
            shaped((8, width), f32),
        ),
        in_specs=[
            any_space,
            any_space,
            any_space,
            vmem,
            vmem,
            any_space,
            any_space,
            any_space,
            pl.BlockSpec(memory_space=pltpu.SMEM),
            vmem,
        ],
        out_specs=(any_space,) * 8,
        scratch_shapes=[
            pltpu.VMEM((4, rows, width), bf16),
            pltpu.VMEM((4, rows, width), bf16),
            pltpu.VMEM((4, rows, width), bf16),
            pltpu.VMEM((rows, width), bf16),
            pltpu.VMEM((rows, width), bf16),
            pltpu.VMEM((model_width, units), bf16),
            pltpu.VMEM((model_width, kv), bf16),
            pltpu.VMEM((model_width, units), bf16),
            pltpu.VMEM((rows, units), f32),
            pltpu.VMEM((rows, kv), f32),
            pltpu.VMEM((rows, kv), f32),
            pltpu.VMEM((units, rows), bf16),
            pltpu.VMEM((units, rows), bf16),
            pltpu.VMEM((units, rows), bf16),
            pltpu.VMEM((units, rows), bf16),
            pltpu.VMEM((heads, rows, HEAD_DIM), bf16),
            pltpu.VMEM((heads, rows, HEAD_DIM), bf16),
            pltpu.VMEM((rows, units), bf16),
            pltpu.VMEM((rows, units), bf16),
            pltpu.VMEM((kv, rows), bf16),
            pltpu.VMEM((kv, rows), bf16),
            pltpu.VMEM((kv, rows), bf16),
            pltpu.VMEM((kv, rows), bf16),
            pltpu.VMEM((rows, kv), bf16),
            pltpu.VMEM((rows, kv), bf16),
            pltpu.VMEM((heads, rows, rows), bf16),
            pltpu.VMEM((heads, rows, ROWS), bf16),
            pltpu.VMEM((kv, rows), f32),
            pltpu.VMEM((kv, rows), f32),
            pltpu.VMEM((4, 8, rows), f32),
            pltpu.VMEM((4, 8, rows), f32),
            pltpu.VMEM((8, rows), f32),
            pltpu.VMEM((8, rows), f32),
            pltpu.VMEM((8, 8, width), f32),
            pltpu.VMEM((8, width), f32),
            pltpu.VMEM((steps, 8, width), f32),
            pltpu.VMEM((2, rows, width), bf16),
            pltpu.VMEM((3, 2, rows, width), bf16),
            pltpu.VMEM((3, rows, width), bf16),
            pltpu.VMEM((n_hi, units, feat), bf16),
            pltpu.VMEM((n_hi, kv, feat), bf16),
            pltpu.VMEM((n_hi, units, feat), bf16),
            pltpu.VMEM((n_hi, units, feat), bf16),
            pltpu.VMEM((n_hi, kv, feat), bf16),
            pltpu.VMEM((n_hi + 1, units, feat), bf16),
            pltpu.VMEM((n_hi + 1, units, feat), bf16),
            pltpu.VMEM((n_hi + 1, kv, feat), bf16),
            pltpu.VMEM((units, feat), f32),
            pltpu.VMEM((kv, feat), f32),
            pltpu.VMEM((2, feat, units), f32),
            pltpu.VMEM((2, feat, HEAD_DIM), f32),
            pltpu.SemaphoreType.DMA((128,)),
            pltpu.SemaphoreType.DMA((128,)),
            pltpu.SemaphoreType.DMA((16,)),
        ],
        compiler_params=pltpu.CompilerParams(
            collective_id=0, has_side_effects=True, vmem_limit_bytes=64 << 20
        ),
        name="block",
    )(
        context,
        latents,
        cotangent,
        gain_ctx.reshape(4, width),
        gain_lat.reshape(4, width),
        w_query,
        w_pair,
        w_out,
        lengths,
        patch_flags.reshape(1, rows),
    )
    latents_out, grad_context, grad_latents, g_query, g_key, g_value, g_out, gains = out
    dp, t = lax.axis_index("dp"), lax.axis_index("tensor")
    part = width // n_dp
    gain_c = lax.dynamic_slice(gains, (t, dp * part), (1, part))
    gain_l = lax.dynamic_slice(gains, (4 + t, dp * part), (1, part))
    return (
        latents_out,
        grad_context,
        grad_latents,
        g_query,
        g_key,
        g_value,
        g_out,
        gain_c,
        gain_l,
    )


def solution(mesh):
    n_dp = mesh.shape["dp"]
    body = functools.partial(kernel_local, n_dp) if n_dp <= 8 else plain_local
    return jax.shard_map(
        body,
        mesh=mesh,
        in_specs=(
            P("dp", "tensor"),
            P("dp", "tensor"),
            P(),
            P(),
            P(None, "tensor"),
            P(None, "tensor"),
            P(None, "tensor"),
            P(None, "tensor"),
            P("dp", None),
            P("dp"),
            P("dp", "tensor"),
        ),
        out_specs=(
            P("dp", "tensor"),
            P("dp", "tensor"),
            P("dp", "tensor"),
            P("dp", "tensor"),
            P("dp", "tensor"),
            P("dp", "tensor"),
            P("dp", "tensor"),
            P("tensor", "dp"),
            P("tensor", "dp"),
        ),
        check_vma=False,
    )
```

```python
import functools

import jax
import jax.numpy as jnp
from jax import lax
from jax.experimental import pallas as pl
from jax.experimental.pallas import tpu as pltpu
from jax.sharding import PartitionSpec as P

HEAD_DIM = 96
LAT = 64


epsilon = 1e-06
masked_value = -1e30
contract_rows = (((0,), (0,)), ((), ()))
contract_cols = (((1,), (1,)), ((), ()))


def row_scales(rows_in):
    values_f = rows_in.astype(jnp.float32)
    return (values_f, lax.rsqrt(jnp.mean(values_f * values_f, axis=1) + epsilon))


def norm_back(grad_norm, local_vals, row_scale, gain_local, row_inner_all, model_width):
    weighted = grad_norm * gain_local
    grad_input = (
        row_scale[:, None] * weighted
        - local_vals * (row_scale**3 * row_inner_all / model_width)[:, None]
    )
    grad_gain = jnp.sum(grad_norm * local_vals * row_scale[:, None], axis=0)
    return (grad_input, grad_gain)


def plain_local(
    context,
    latents,
    gain_ctx,
    gain_lat,
    w_query,
    key_matrix,
    value_matrix,
    w_out,
    lengths,
    patch_flags,
    cotangent,
):
    patch_rows = context.shape[0]
    latent_rows = latents.shape[0]
    local_width = context.shape[1]
    model_width = gain_ctx.shape[0]
    head_size = HEAD_DIM
    kv_local = key_matrix.shape[1] // head_size
    query_local = w_query.shape[1] // head_size
    repeat = query_local // kv_local
    all_count = patch_rows + latent_rows
    score_scale = head_size ** (-0.5)
    column = lax.axis_index("tensor") * local_width
    whole_ctx, whole_lat = (
        lax.all_gather(context, "tensor", axis=1, tiled=True),
        lax.all_gather(latents, "tensor", axis=1, tiled=True),
    )
    ctx_values, ctx_scale = row_scales(whole_ctx)
    lat_values, lat_scale = row_scales(whole_lat)
    ctx_norm = (ctx_values * ctx_scale[:, None] * gain_ctx).astype(jnp.bfloat16)
    lat_norm = (lat_values * lat_scale[:, None] * gain_lat).astype(jnp.bfloat16)
    queries = jnp.dot(lat_norm, w_query, preferred_element_type=jnp.float32).astype(jnp.bfloat16)
    all_rows = jnp.concatenate([ctx_norm, lat_norm], axis=0)
    w_pair = jnp.concatenate([key_matrix, value_matrix], axis=1)
    pair_rows = jnp.dot(all_rows, w_pair, preferred_element_type=jnp.float32).astype(jnp.bfloat16)
    key_head_split = (
        pair_rows[:, : kv_local * head_size]
        .reshape(all_count, kv_local, head_size)
        .transpose(1, 0, 2)
    )
    value_head_split = (
        pair_rows[:, kv_local * head_size :]
        .reshape(all_count, kv_local, head_size)
        .transpose(1, 0, 2)
    )
    query_heads = queries.reshape(latent_rows, query_local, head_size).transpose(1, 0, 2)
    image_ends = jnp.cumsum(lengths[0])
    patch_image = jnp.sum(
        (jnp.arange(patch_rows)[:, None] >= image_ends[None, :]).astype(jnp.int32), axis=1
    )
    latent_image = jnp.arange(latent_rows) // LAT
    allowed = jnp.concatenate(
        [
            (latent_image[:, None] == patch_image[None, :]) & (patch_flags[None, :] == 1),
            latent_image[:, None] == latent_image[None, :],
        ],
        axis=1,
    )
    head_index = jnp.arange(query_local)

    def head_scores(query_head, head_number):
        key_head = key_head_split[head_number // repeat]
        value_head = value_head_split[head_number // repeat]
        raw_scores = (
            lax.dot_general(query_head, key_head, contract_cols, preferred_element_type=jnp.float32)
            * score_scale
        )
        return (jnp.where(allowed, raw_scores, masked_value), key_head, value_head)

    def head_forward(member):
        query_head, head_number = member
        scores, key_head, value_head = head_scores(query_head, head_number)
        row_top = jnp.max(scores, axis=1, keepdims=True)
        exp_scores = jnp.exp(scores - row_top)
        row_total = jnp.sum(exp_scores, axis=1, keepdims=True)
        attention = (exp_scores / row_total).astype(jnp.bfloat16)
        blended = jnp.dot(attention, value_head, preferred_element_type=jnp.float32).astype(
            jnp.bfloat16
        )
        return (blended, row_top[:, 0] + jnp.log(row_total[:, 0]))

    heads_out, log_totals = lax.map(head_forward, (query_heads, head_index))
    attended = heads_out.transpose(1, 0, 2).reshape(latent_rows, query_local * head_size)
    partial_out = lax.dot_general(
        attended, w_out, contract_cols, preferred_element_type=jnp.float32
    )
    branch = lax.psum_scatter(
        partial_out.astype(jnp.bfloat16), "tensor", scatter_dimension=1, tiled=True
    ).astype(jnp.float32)
    latents_out = (latents.astype(jnp.float32) + branch).astype(jnp.bfloat16)
    full_grad = lax.all_gather(cotangent, "tensor", axis=1, tiled=True)
    grad_attended = jnp.dot(full_grad, w_out, preferred_element_type=jnp.float32).astype(
        jnp.bfloat16
    )
    grad_w_out = lax.dot_general(
        full_grad, attended, contract_rows, preferred_element_type=jnp.float32
    )
    grad_heads = grad_attended.reshape(latent_rows, query_local, head_size).transpose(1, 0, 2)

    def head_backward(member):
        query_head, grad_blended, log_total, head_number = member
        scores, key_head, value_head = head_scores(query_head, head_number)
        attention = jnp.exp(scores - log_total[:, None])
        grad_probs = lax.dot_general(
            grad_blended, value_head, contract_cols, preferred_element_type=jnp.float32
        )
        row_inner = jnp.sum(attention * grad_probs, axis=1, keepdims=True)
        grad_scores = (attention * (grad_probs - row_inner)).astype(jnp.bfloat16)
        grad_query = (
            jnp.dot(grad_scores, key_head, preferred_element_type=jnp.float32) * score_scale
        ).astype(jnp.bfloat16)
        grad_key = (
            lax.dot_general(
                grad_scores, query_head, contract_rows, preferred_element_type=jnp.float32
            )
            * score_scale
        )
        grad_value = lax.dot_general(
            attention.astype(jnp.bfloat16),
            grad_blended,
            contract_rows,
            preferred_element_type=jnp.float32,
        )
        return (grad_query, grad_key, grad_value)

    grad_query_heads, grad_key_heads, grad_value_heads = lax.map(
        head_backward, (query_heads, grad_heads, log_totals, head_index)
    )
    grad_keys = grad_key_heads.reshape(kv_local, repeat, all_count, head_size).sum(axis=1)
    grad_values = grad_value_heads.reshape(kv_local, repeat, all_count, head_size).sum(axis=1)
    grad_pair = jnp.concatenate(
        [
            grad_keys.transpose(1, 0, 2).reshape(all_count, kv_local * head_size),
            grad_values.transpose(1, 0, 2).reshape(all_count, kv_local * head_size),
        ],
        axis=1,
    ).astype(jnp.bfloat16)
    grad_q_rows = grad_query_heads.transpose(1, 0, 2).reshape(latent_rows, query_local * head_size)
    grad_w_query = lax.dot_general(
        lat_norm, grad_q_rows, contract_rows, preferred_element_type=jnp.float32
    )
    grad_w_pair = lax.dot_general(
        all_rows, grad_pair, contract_rows, preferred_element_type=jnp.float32
    )
    grad_rows = lax.dot_general(
        grad_pair, w_pair, contract_cols, preferred_element_type=jnp.float32
    )
    lat_terms = grad_rows[patch_rows:] + lax.dot_general(
        grad_q_rows, w_query, contract_cols, preferred_element_type=jnp.float32
    )
    grad_ctx_norm, grad_lat_norm = (
        lax.psum_scatter(
            grad_rows[:patch_rows].astype(jnp.bfloat16), "tensor", scatter_dimension=1, tiled=True
        ).astype(jnp.float32),
        lax.psum_scatter(
            lat_terms.astype(jnp.bfloat16), "tensor", scatter_dimension=1, tiled=True
        ).astype(jnp.float32),
    )
    ctx_local = context.astype(jnp.float32)
    lat_local = latents.astype(jnp.float32)
    gain_ctx_local = lax.dynamic_slice_in_dim(gain_ctx, column, local_width, 0)
    gain_lat_local = lax.dynamic_slice_in_dim(gain_lat, column, local_width, 0)
    ctx_inner = jnp.sum(grad_ctx_norm * gain_ctx_local * ctx_local, axis=1)
    lat_inner = jnp.sum(grad_lat_norm * gain_lat_local * lat_local, axis=1)
    ctx_inner_all, lat_inner_all = lax.psum((ctx_inner, lat_inner), "tensor")
    grad_ctx_in, grad_gain_c = norm_back(
        grad_ctx_norm, ctx_local, ctx_scale, gain_ctx_local, ctx_inner_all, model_width
    )
    grad_lat_in, grad_gain_l = norm_back(
        grad_lat_norm, lat_local, lat_scale, gain_lat_local, lat_inner_all, model_width
    )
    grad_context = grad_ctx_in.astype(jnp.bfloat16)
    grad_latents = (cotangent.astype(jnp.float32) + grad_lat_in).astype(jnp.bfloat16)
    grad_w_key = grad_w_pair[:, : kv_local * head_size]
    grad_w_value = grad_w_pair[:, kv_local * head_size :]
    sum_query, sum_key, sum_value, sum_out, sum_gain_c, sum_gain_l = (
        lax.psum_scatter(grad_w_query, "dp", scatter_dimension=0, tiled=True),
        lax.psum_scatter(grad_w_key, "dp", scatter_dimension=0, tiled=True),
        lax.psum_scatter(grad_w_value, "dp", scatter_dimension=0, tiled=True),
        lax.psum_scatter(grad_w_out, "dp", scatter_dimension=0, tiled=True),
        lax.psum_scatter(grad_gain_c, "dp", scatter_dimension=0, tiled=True),
        lax.psum_scatter(grad_gain_l, "dp", scatter_dimension=0, tiled=True),
    )
    return (
        latents_out,
        grad_context,
        grad_latents,
        sum_query,
        sum_key,
        sum_value,
        sum_out,
        sum_gain_c.reshape(1, -1),
        sum_gain_l.reshape(1, -1),
    )


MESH = pl.DeviceIdType.MESH
f32 = jnp.float32
bf16 = jnp.bfloat16
ROWS = 128


def nn(a, b):
    return jnp.dot(a, b, preferred_element_type=f32)


def nt(a, b):
    return lax.dot_general(a, b, contract_cols, preferred_element_type=f32)


def flip(a):
    return a.astype(f32).T.astype(bf16)


def block_kernel(
    n_dp,
    context,
    latents,
    cotangent,
    gain_ctx,
    gain_lat,
    w_query,
    key_across,
    value_across,
    w_out,
    lengths,
    flags,
    out_latents,
    out_context,
    out_grad_lat,
    out_query,
    out_key,
    out_value,
    out_out,
    out_gain_c,
    out_gain_l,
    lat_all,
    cot_all,
    ctx_own,
    raw_lat,
    raw_ctx,
    wq,
    wkv,
    w_own,
    wo,
    acc_q,
    kv_acc,
    q_t,
    ga_t,
    att_t,
    sgq_t,
    q_heads,
    ga_heads,
    att,
    sgq,
    kv_t,
    kv_send,
    kv_core,
    kv_y,
    probs_c,
    probs_l,
    gkv,
    sgkv_all,
    stage_ctx,
    sums,
    inners,
    scale_row,
    coef_row,
    gain_part,
    gain_sum,
    gain_recv,
    core_send,
    core_recv,
    y_recv,
    lat_x,
    cot_x,
    att_xt,
    sgq_xt,
    z_send_o,
    z_send_q,
    z_recv_o,
    z_recv_q,
    x_send_kv,
    x_recv_kv,
    z_recv_kv,
    own_send,
    own_recv,
    dp_acc,
    stage,
    send_sem,
    recv_sem,
    local_sem,
):
    rows, width = raw_lat.shape
    n_rows = rows // ROWS
    n_hi = n_dp // 2
    feat = 4 * width // n_dp
    heads = q_heads.shape[0]
    head = HEAD_DIM
    model_width = 4 * width
    score_scale = head ** (-0.5)

    dp = lax.axis_index("dp")
    f = lax.axis_index("tensor")
    z, x = dp // 2, lax.rem(dp, 2)
    y, c = f // 2, lax.rem(f, 2)
    f_c = y * 2 + (1 - c)
    f_y = (1 - y) * 2 + c
    f_yc = (1 - y) * 2 + (1 - c)
    core_dev, y_dev, yc_dev = (dp, f_c), (dp, f_y), (dp, f_yc)
    x_dev = (z * 2 + 1 - x, f)
    z_1 = z + 1 - 2 * lax.rem(z, 2)
    z_2 = z + 2 - 4 * (z // 2)
    z1_dev, z2_dev = (z_1 * 2 + x, f), (z_2 * 2 + x, f)
    x_mine = pl.ds(pl.multiple_of(x * feat, 128), feat)
    x_other = pl.ds(pl.multiple_of((1 - x) * feat, 128), feat)

    count = [0]

    def take(n):
        count[0] += n
        return count[0] - n

    def remote(src, dst, sem, dev, sem_to=None):
        return pltpu.make_async_remote_copy(
            src_ref=src,
            dst_ref=dst,
            send_sem=send_sem.at[sem],
            recv_sem=recv_sem.at[sem if sem_to is None else sem_to],
            device_id=dev,
            device_id_type=MESH,
        )

    def local_copy(src, dst, i):
        return pltpu.make_async_copy(src, dst, local_sem.at[i])

    def part_rows(k):
        if isinstance(k, int):
            return pl.ds(k * ROWS, ROWS)
        return pl.ds(pl.multiple_of(k * ROWS, ROWS), ROWS)

    def block_cols(fb):
        if isinstance(fb, int):
            return pl.ds(fb * width, width)
        return pl.ds(pl.multiple_of(fb * width, width), width)

    loads = [
        local_copy(latents, raw_lat, 0),
        local_copy(key_across, wkv.at[pl.ds(0, head)], 4),
        local_copy(value_across, wkv.at[pl.ds(head, head)], 14),
        local_copy(context, raw_ctx, 1),
        local_copy(cotangent, cot_all.at[f], 2),
        local_copy(w_query, wq, 3),
        local_copy(w_out, wo, 5),
    ]
    for load in loads:
        load.start()

    barrier = pltpu.get_barrier_semaphore()

    def greet(dev):
        pl.semaphore_signal(barrier, inc=1, device_id=dev, device_id_type=MESH)

    others = [i for i in range(1, n_hi)]

    def far_dev(i):
        return (lax.rem(z + i, n_hi) * 2 + x, f)

    always = [core_dev, y_dev, yc_dev, x_dev] + [far_dev(i) for i in others]
    for dev in always:
        greet(dev)
    pl.semaphore_wait(barrier, len(always))

    sem_lat, sem_cot = (take(2 * n_rows + 1) for _ in range(2))

    def gather_y(buf, base, k):
        return remote(buf.at[f, part_rows(k)], buf.at[f, part_rows(k)], base + k, y_dev)

    def gather_core(buf, base):
        return remote(buf.at[f], buf.at[f], base + n_rows, core_dev)

    def gather_on(buf, base, k):
        return remote(
            buf.at[f_y, part_rows(k)], buf.at[f_y, part_rows(k)], base + n_rows + 1 + k, core_dev
        )

    def pass_on(buf, base):
        def step(k, carry):
            gather_y(buf, base, k).wait_recv()
            gather_on(buf, base, k).start()
            return carry

        lax.fori_loop(0, n_rows, step, 0)

    def wait_on(buf, base):
        for k in range(n_rows):
            gather_on(buf, base, k).wait_recv()

    def gather_done(buf, base):
        for k in range(n_rows):
            gather_y(buf, base, k).wait_send()
            gather_on(buf, base, k).wait_send()
        gather_core(buf, base).wait_send()

    def weigh(raw, gain, buf, base, index):
        gain_row = gain[:, block_cols(f)]
        for k in range(n_rows):
            values = raw[part_rows(k), :].astype(f32)
            buf[part_rows(k), :] = (values * gain_row).astype(bf16)
            if base is not None:
                gather_y(lat_all, base, k).start()
        if base is not None:
            gather_core(lat_all, base).start()
        for k in range(n_rows):
            values = raw[part_rows(k), :].astype(f32)
            total = jnp.sum(values * values, axis=1, keepdims=True)
            across = jnp.broadcast_to(total, (ROWS, 128)).T
            sums[f, pl.ds(index, 1), part_rows(k)] = across[0:1, :]

    sem_lat_x, sem_cot_x, sem_att_x, sem_sgq_x = take(4), take(4), take(1), take(1)

    def across_x(buf, held, base, i):
        fb = (f, f_y)[i]
        return remote(buf.at[fb, :, x_other], held.at[fb], base + i, x_dev)

    def across_core(held, base, i):
        fb = (f, f_y)[i]
        return remote(held.at[fb], held.at[fb], base + 2 + i, core_dev)

    def hold_across(buf, held, base, i):
        across_x(buf, held, base, i).wait_recv()
        across_core(held, base, i).start()

    kv = 2 * head
    slice_width = width // n_dp
    pair_rows = pl.ds(pl.multiple_of((1 - y) * 2 * kv, 64), 2 * kv)
    sem_w_core, sem_w_y, sem_w_z, sem_w_x = take(1), take(2), take(n_hi), take(n_hi)

    def head_rows_of(t):
        return pl.ds(pl.multiple_of(t * kv, 64), kv)

    def slice_cols(d, at=0):
        return pl.ds(pl.multiple_of(at + d * slice_width, 128), slice_width)

    def w_y(dev, f_to, i, sender=c):
        return remote(
            wkv.at[:, slice_cols(dp, f_to * width)],
            w_own.at[head_rows_of(f), slice_cols(dp)],
            sem_w_y + i,
            dev,
            sem_w_y + sender,
        )

    def w_core():
        return remote(
            wkv.at[:, block_cols(f_c)], w_own.at[head_rows_of(f)], sem_w_core, core_dev
        )

    def w_z(i):
        piece = w_own.at[pair_rows, slice_cols(dp)]
        return remote(piece, piece, sem_w_z + i, far_dev(i))

    def w_x(i):
        piece = w_own.at[pair_rows, slice_cols(lax.rem(z + i, n_hi) * 2 + x)]
        return remote(piece, piece, sem_w_x + lax.rem(z + i, n_hi), x_dev)

    sums[f] = jnp.zeros(sums.shape[1:], f32)
    inners[f] = jnp.zeros(inners.shape[1:], f32)
    loads[1].wait()
    loads[2].wait()
    w_y(y_dev, f_y, 0).start()
    w_y(yc_dev, f_yc, 1).start()
    w_core().start()
    loads[0].wait()
    weigh(raw_lat, gain_lat, lat_all.at[f], sem_lat, 1)
    loads[3].wait()
    weigh(raw_ctx, gain_ctx, ctx_own, None, 0)
    loads[4].wait()
    gather_core(cot_all, sem_cot).start()
    across_x(lat_all, lat_x, sem_lat_x, 0).start()
    for i in range(2):
        w_y(y_dev, f_y, i, i).wait_recv()
    for i in others:
        w_z(i).start()
    w_x(0).start()
    w_own[head_rows_of(f), :] = wkv[:, block_cols(f)]

    peers = [core_dev, y_dev, yc_dev]
    sem_sums, sem_inner = take(3), take(3)

    def exchange(buf, base):
        return [remote(buf.at[f], buf.at[f], base + i, dev) for i, dev in enumerate(peers)]

    sums_out = exchange(sums, sem_sums)
    for copy in sums_out:
        copy.start()

    def project(acc, values, weight, blocks, first):
        def step(i, carry):
            fb = blocks[0] + i * (blocks[1] - blocks[0])
            for m in range(2):
                half = pl.ds(m * (rows // 2), rows // 2)
                product = nn(values[fb, half, :], weight[block_cols(fb), :])
                if first:
                    @pl.when(i == 0)
                    def _():
                        acc[half, :] = product

                    @pl.when(i > 0)
                    def _():
                        acc[half, :] += product
                else:
                    acc[half, :] += product
            return carry

        lax.fori_loop(0, 2, step, 0)

    mine, theirs = (f, f_c), (f_y, f_yc)
    loads[5].wait()
    loads[6].wait()
    gather_core(lat_all, sem_lat).wait_recv()
    project(acc_q, lat_all, wq, mine, True)
    for i in others:
        w_z(n_hi - i).wait_recv()
        w_x(i).start()
    w_core().wait_recv()
    across_x(cot_all, cot_x, sem_cot_x, 0).start()
    for i in range(n_hi):
        w_x(i).wait_recv()

    sem_kv_core, sem_kv_y = take(2), take(1)

    def kv_core_copy(j):
        return remote(kv_send.at[j], kv_core.at[j], sem_kv_core + j, core_dev)

    def kv_y_copy():
        return remote(kv_core.at[0], kv_y, sem_kv_y, y_dev)

    for n in range(2 * rows // 256):
        at = n * 256
        source = ctx_own[at : at + 256, :] if at < rows else lat_all[f, at - rows : at - rows + 256, :]
        kv_acc[:, at : at + 256] = nt(w_own[...], source)
    for j, t in enumerate((f_yc, f_c)):
        kv_send[j] = kv_acc[head_rows_of(t), :].astype(bf16)
        kv_core_copy(j).start()
    kv_core_copy(0).wait_recv()
    kv_core[0] = (kv_acc[head_rows_of(f_y), :] + kv_core[0].astype(f32)).astype(bf16)
    kv_y_copy().start()
    for k in range(n_rows):
        gather_y(cot_all, sem_cot, k).start()

    pass_on(lat_all, sem_lat)
    across_x(lat_all, lat_x, sem_lat_x, 1).start()
    wait_on(lat_all, sem_lat)
    project(acc_q, lat_all, wq, theirs, False)

    for copy in sums_out:
        copy.wait()
    total = sums[0] + sums[1] + sums[2] + sums[3]
    scale_row[...] = lax.rsqrt(total / model_width + epsilon)

    def split_heads(acc, out_t, out_heads, scaled):
        for k in range(n_rows):
            across = acc[part_rows(k), :].T
            if scaled:
                across = across * scale_row[1:2, part_rows(k)]
            across = across.astype(bf16)
            out_t[:, part_rows(k)] = across
            for h in range(heads):
                out_heads[h, part_rows(k), :] = flip(across[h * head : (h + 1) * head, :])

    split_heads(acc_q, q_t, q_heads, True)
    kv_core_copy(1).wait_recv()
    kv_y_copy().wait_recv()
    summed = kv_acc[head_rows_of(f), :] + kv_core[1].astype(f32) + kv_y[...].astype(f32)
    kv_t[:, 0:rows] = (summed[:, 0:rows] * scale_row[0:1, :]).astype(bf16)
    kv_t[:, rows:] = (summed[:, rows:] * scale_row[1:2, :]).astype(bf16)

    hold_across(lat_all, lat_x, sem_lat_x, 0)
    hold_across(cot_all, cot_x, sem_cot_x, 0)
    patch = lax.broadcasted_iota(jnp.int32, (1, rows), 1)
    image = jnp.zeros((1, rows), jnp.int32)
    end = jnp.int32(0)
    for i in range(lengths.shape[1]):
        end = end + lengths[0, i]
        image = image + (patch >= end).astype(jnp.int32)
    image = jnp.where(flags[...] == 1, image, -1)
    per_part = ROWS // LAT
    row_image = lax.broadcasted_iota(jnp.int32, (ROWS, 1), 0) // LAT
    col_image = lax.broadcasted_iota(jnp.int32, (1, ROWS), 1) // LAT
    same = row_image == col_image
    keys, vals = pl.ds(0, head), pl.ds(head, head)
    patches = pl.ds(0, rows)

    def own_latents(p):
        return pl.ds(pl.multiple_of(rows + p * ROWS, ROWS), ROWS)


    def forward_step(n, carry):
        h, p = n // n_rows, lax.rem(n, n_rows)
        head_rows = pl.ds(pl.multiple_of(h * head, 32), head)
        q = q_heads[h, part_rows(p), :]
        allowed = (row_image + p * per_part) == image
        far = jnp.where(allowed, nn(q, kv_t[keys, patches]) * score_scale, masked_value)
        near = jnp.where(same, nn(q, kv_t[keys, own_latents(p)]) * score_scale, masked_value)
        top = jnp.maximum(
            jnp.max(far, axis=1, keepdims=True), jnp.max(near, axis=1, keepdims=True)
        )
        far, near = jnp.exp(far - top), jnp.exp(near - top)
        total = jnp.sum(far, axis=1, keepdims=True) + jnp.sum(near, axis=1, keepdims=True)
        far, near = (far / total).astype(bf16), (near / total).astype(bf16)
        probs_c[h, part_rows(p), :] = far
        probs_l[h, part_rows(p), :] = near
        blended = nt(kv_t[vals, patches], far) + nt(kv_t[vals, own_latents(p)], near)
        att_t[head_rows, part_rows(p)] = blended.astype(bf16)
        return carry

    lax.fori_loop(0, heads * n_rows, forward_step, 0)
    def att_x_copy():
        return remote(att_t, att_xt, sem_att_x, x_dev)

    def sgq_x_copy():
        return remote(sgq_t, sgq_xt, sem_sgq_x, x_dev)

    att_x_copy().start()
    def chunk_out(zt):
        return nn(att_t[...], cot_all[zt, :, x_mine]) + nn(att_xt[...], cot_x[zt])

    def chunk_query(zt):
        return nn(sgq_t[...], lat_all[zt, :, x_mine]) + nn(sgq_xt[...], lat_x[zt])

    def chunk_pair(xt):
        cols = pl.ds(pl.multiple_of(xt * feat, 128), feat)
        return nn(sgkv_all[:, patches], ctx_own[:, cols]) + nn(
            sgkv_all[:, pl.ds(rows, rows)], lat_all[f, :, cols]
        )

    class Spread:
        def __init__(self, chunk, send, recv):
            self.chunk, self.send, self.recv, self.sem = chunk, send, recv, take(3)

        def copy(self, j, dev):
            return remote(self.send.at[j], self.recv.at[j], self.sem + j, dev)

        def first(self, j):
            zt = z_1 + j * (z_2 - z)
            self.send[j] = self.chunk(zt).astype(bf16)
            self.copy(j, z1_dev).start()

        def second(self):
            value = self.chunk(z_2)
            self.copy(1, z1_dev).wait_recv()
            self.send[2] = (value + self.recv[1].astype(f32)).astype(bf16)
            self.copy(2, z2_dev).start()

        def final(self):
            dp_acc[...] = self.chunk(z)
            self.copy(0, z1_dev).wait_recv()
            self.copy(2, z2_dev).wait_recv()
            dp_acc[...] += self.recv[0].astype(f32) + self.recv[2].astype(f32)

        def wait_sends(self):
            for j in range(3):
                self.copy(j, z1_dev).wait_send()

    grad_o = Spread(chunk_out, z_send_o, z_recv_o)
    grad_q = Spread(chunk_query, z_send_q, z_recv_q)

    sem_kv_x, sem_kv_z1, sem_kv_z2, sem_kv_own = take(4), take(4), take(4), take(4)
    pair_acc = kv_acc.at[:, pl.ds(0, feat)]
    passes = lax.rem(z + f, 2) == 1
    middle = z_2 == f

    def head_rows_at(t):
        return pl.ds(t * kv, kv)

    def pair_x_copy(t):
        at = head_rows_at(t)
        return remote(x_send_kv.at[at], x_recv_kv.at[at], sem_kv_x + t, x_dev)

    def pair_z_copy(t, i):
        at = head_rows_at(t)
        base, dev = ((sem_kv_z1, z1_dev), (sem_kv_z2, z2_dev))[i]
        return remote(x_recv_kv.at[at], z_recv_kv.at[i, at], base + t, dev)

    def pair_own_copy(i):
        t = (f_c, f_y, f_yc)[i]
        return remote(own_send.at[i], own_recv, sem_kv_own + i, (dp, t), sem_kv_own + 3)

    def pair_first():
        x_send_kv[...] = chunk_pair(1 - x).astype(bf16)
        for t in range(4):
            pair_x_copy(t).start()
        pair_acc[...] = chunk_pair(x)

    def pair_step(t, i):
        at = head_rows_at(t)
        if i == 0:
            pair_x_copy(t).wait_recv()
            pair_acc[at, :] += x_recv_kv[at, :].astype(f32)
            sends = passes
        else:
            @pl.when(jnp.logical_not(passes))
            def _():
                pair_z_copy(t, 0).wait_recv()
                pair_acc[at, :] += z_recv_kv[0, at, :].astype(f32)

            sends = middle

        @pl.when(sends)
        def _():
            x_recv_kv[at, :] = pair_acc[at, :].astype(bf16)
            pair_z_copy(t, i).start()

    def pair_last():
        @pl.when(z == f)
        def _():
            for t in range(4):
                at = head_rows_at(t)
                pair_z_copy(t, 1).wait_recv()
                pair_acc[at, :] += z_recv_kv[1, at, :].astype(f32)
            for i, t in enumerate((f_c, f_y, f_yc)):
                own_send[i] = kv_acc[head_rows_of(t), pl.ds(0, feat)].astype(bf16)
                pair_own_copy(i).start()

    def pair_result():
        @pl.when(z == f)
        def _():
            kv_acc[0:kv, pl.ds(feat, feat)] = kv_acc[head_rows_of(f), pl.ds(0, feat)]

        @pl.when(z != f)
        def _():
            pair_own_copy(0).wait_recv()
            kv_acc[0:kv, pl.ds(feat, feat)] = own_recv[...].astype(f32)

    def pair_sends_done():
        for t in range(4):
            pair_x_copy(t).wait_send()
            pl.when(passes)(lambda t=t: pair_z_copy(t, 0).wait_send())
            pl.when(middle)(lambda t=t: pair_z_copy(t, 1).wait_send())

        @pl.when(z == f)
        def _():
            for i in range(3):
                pair_own_copy(i).wait_send()

    class Collect:
        def __init__(self, part, index):
            self.part, self.index, self.sem = part, index, take(3 * n_rows)

        def core_copy(self, j, k):
            return remote(
                core_send.at[j, part_rows(k)],
                core_recv.at[self.index, j, part_rows(k)],
                self.sem + j * n_rows + k,
                core_dev,
            )

        def y_copy(self, k):
            return remote(
                core_recv.at[self.index, 0, part_rows(k)],
                y_recv.at[self.index, part_rows(k)],
                self.sem + 2 * n_rows + k,
                y_dev,
            )

        def send_core(self):
            def core_step(n, carry):
                j, k = n // n_rows, lax.rem(n, n_rows)
                fb = jnp.where(j == 0, f_yc, f_c)
                core_send[j, part_rows(k), :] = self.part(fb, k).astype(bf16)
                self.core_copy(j, k).start()
                return carry

            lax.fori_loop(0, 2 * n_rows, core_step, 0)

        def send_y(self, first, last):
            def y_step(k, carry):
                value = self.part(f_y, k)
                self.core_copy(0, k).wait_recv()
                value = value + core_recv[self.index, 0, part_rows(k), :].astype(f32)
                core_recv[self.index, 0, part_rows(k), :] = value.astype(bf16)
                self.y_copy(k).start()
                return carry

            lax.fori_loop(first, last, y_step, 0)

        def core_sends_done(self):
            for j in range(2):
                for k in range(n_rows):
                    self.core_copy(j, k).wait_send()

        def total(self, k):
            value = self.part(f, k)
            self.core_copy(1, k).wait_recv()
            self.y_copy(k).wait_recv()
            return (
                value
                + core_recv[self.index, 1, part_rows(k), :].astype(f32)
                + y_recv[self.index, part_rows(k), :].astype(f32)
            )

        def wait_y_sends(self):
            for k in range(n_rows):
                self.y_copy(k).wait_send()

    def block_of(weight, fb):
        return weight[block_cols(fb), :]

    def gain_add(index, value, weighed):
        products = (value * weighed.astype(f32)).reshape(ROWS // 8, 8, width)
        gain_part[index] += jnp.sum(products, axis=0)

    def part_branch(fb, k):
        return nt(att[part_rows(k), :], block_of(wo, fb))

    def part_lat(fb, k):
        return nt(sgq[part_rows(k), :], block_of(wq, fb))

    branch = Collect(part_branch, 0)
    back_lat = Collect(part_lat, 1)
    gain_part[...] = jnp.zeros(gain_part.shape, f32)

    gather_core(cot_all, sem_cot).wait_recv()
    project(acc_q, cot_all, wo, mine, True)
    hold_across(lat_all, lat_x, sem_lat_x, 1)
    for k in range(n_rows):
        att[part_rows(k), :] = flip(att_t[:, part_rows(k)])
    branch.send_core()
    branch.send_y(0, n_rows // 2)
    for i in range(2):
        across_core(lat_x, sem_lat_x, i).wait_recv()
    across_core(cot_x, sem_cot_x, 0).wait_recv()
    att_x_copy().wait_recv()
    near_j = jnp.where(z // 2 == y, 0, 1)
    grad_o.first(near_j)
    pass_on(cot_all, sem_cot)
    across_x(cot_all, cot_x, sem_cot_x, 1).start()
    wait_on(cot_all, sem_cot)
    project(acc_q, cot_all, wo, theirs, False)
    split_heads(acc_q, ga_t, ga_heads, False)

    gkv[...] = jnp.zeros(gkv.shape, f32)

    def backward_step(n, carry):
        h, p = n // n_rows, lax.rem(n, n_rows)
        head_rows = pl.ds(pl.multiple_of(h * head, 32), head)
        ga = ga_heads[h, part_rows(p), :]
        far_p, near_p = probs_c[h, part_rows(p), :], probs_l[h, part_rows(p), :]
        far_d = nn(ga, kv_t[vals, patches])
        near_d = nn(ga, kv_t[vals, own_latents(p)])
        far_f, near_f = far_p.astype(f32), near_p.astype(f32)
        inner = jnp.sum(far_f * far_d, axis=1, keepdims=True) + jnp.sum(
            near_f * near_d, axis=1, keepdims=True
        )
        far_g = (far_f * (far_d - inner)).astype(bf16)
        near_g = (near_f * (near_d - inner)).astype(bf16)
        grad_query = nt(kv_t[keys, patches], far_g) + nt(kv_t[keys, own_latents(p)], near_g)
        grad_query = grad_query * score_scale
        query = q_t[head_rows, part_rows(p)]
        ga_across = ga_t[head_rows, part_rows(p)]
        inners[f, 1:2, part_rows(p)] += jnp.sum(
            grad_query * query.astype(f32), axis=0, keepdims=True
        )
        sgq_t[head_rows, part_rows(p)] = (grad_query * scale_row[1:2, part_rows(p)]).astype(bf16)
        gkv[keys, patches] += nn(query, far_g)
        gkv[keys, own_latents(p)] += nn(query, near_g)
        gkv[vals, patches] += nn(ga_across, far_p)
        gkv[vals, own_latents(p)] += nn(ga_across, near_p)
        return carry

    lax.fori_loop(0, heads * n_rows, backward_step, 0)
    gkv[keys, :] = gkv[keys, :] * score_scale
    products = jnp.sum(gkv[...] * kv_t[...].astype(f32), axis=0, keepdims=True)
    inners[f, 0:1, :] = products[:, 0:rows]
    inners[f, 1:2, :] += products[:, rows:]
    inner_out = exchange(inners, sem_inner)
    for copy in inner_out:
        copy.start()
    sgkv_all[head_rows_of(f), 0:rows] = (gkv[:, 0:rows] * scale_row[0:1, :]).astype(bf16)
    sgkv_all[head_rows_of(f), rows:] = (gkv[:, rows:] * scale_row[1:2, :]).astype(bf16)
    sem_gkv = take(3)

    def gkv_copy(t, i, dev):
        piece = sgkv_all.at[head_rows_of(t)]
        return remote(piece, piece, sem_gkv + i, dev)

    gkv_copy(f, 0, y_dev).start()
    gkv_copy(f, 1, core_dev).start()
    for k in range(n_rows):
        sgq[part_rows(k), :] = flip(sgq_t[:, part_rows(k)])

    sgq_x_copy().start()
    branch.send_y(n_rows // 2, n_rows)
    hold_across(cot_all, cot_x, sem_cot_x, 1)
    branch.core_sends_done()
    back_lat.send_core()
    back_lat.send_y(0, n_rows)
    across_core(cot_x, sem_cot_x, 1).wait_recv()
    grad_o.first(1 - near_j)
    gkv_copy(f, 0, y_dev).wait_recv()
    gkv_copy(f_y, 2, core_dev).start()
    gkv_copy(f, 1, core_dev).wait_recv()
    gkv_copy(f_y, 2, core_dev).wait_recv()
    pair_first()
    sgq_x_copy().wait_recv()
    grad_q.first(0)
    grad_q.first(1)
    grad_o.second()

    outs = []

    def put(src, dst, i):
        copy = local_copy(src, dst, i)
        copy.start()
        outs.append(copy)

    for copy in inner_out:
        copy.wait()
    coef_row[...] = (
        scale_row[...]
        * scale_row[...]
        * (inners[0] + inners[1] + inners[2] + inners[3])
        / model_width
    )

    def finish_ctx(k, carry):
        coef = coef_row[:, part_rows(k)].T
        value = nn(flip(sgkv_all[:, part_rows(k)]), w_own[...])
        gain_add(f, value, ctx_own[part_rows(k), :])
        value = value * gain_ctx[:, block_cols(f)]
        value = value - raw_ctx[part_rows(k), :].astype(f32) * coef[:, 0:1]
        stage_ctx[part_rows(k), :] = value.astype(bf16)
        return carry

    lax.fori_loop(0, n_rows, finish_ctx, 0)
    put(stage_ctx, out_context, 10)
    for t in range(4):
        pair_step(t, 0)

    def gain_step(n, carry):
        fb, k = n // n_rows, lax.rem(n, n_rows)
        gain_add(4 + fb, part_lat(fb, k), lat_all[fb, part_rows(k), :])
        return carry

    lax.fori_loop(0, 4 * n_rows, gain_step, 0)

    def finish_kv(k, carry):
        own = nn(flip(sgkv_all[:, own_latents(k)]), w_own[...])
        gain_add(4 + f, own, lat_all[f, part_rows(k), :])
        return carry

    lax.fori_loop(0, n_rows, finish_kv, 0)
    for i in range(4):
        gain_sum[i : i + 1, :] = (
            jnp.sum(gain_part[i], axis=0, keepdims=True) / gain_ctx[:, block_cols(i)]
        )
        gain_sum[4 + i : 5 + i, :] = (
            jnp.sum(gain_part[4 + i], axis=0, keepdims=True) / gain_lat[:, block_cols(i)]
        )
    gain_copies = [
        remote(gain_sum, gain_recv.at[i], take(1), dev)
        for i, dev in enumerate([x_dev, z1_dev, z2_dev, core_dev, y_dev])
    ]

    def gain_next(i):
        if i > 0:
            gain_copies[i - 1].wait()
            gain_sum[...] += gain_recv[i - 1]
        if i < len(gain_copies):
            gain_copies[i].start()

    gain_next(0)
    grad_q.second()
    gain_next(1)
    for t in range(4):
        pair_step(t, 1)
    gain_next(2)

    def finish(k, carry):
        value = raw_lat[part_rows(k), :].astype(f32) + branch.total(k)
        y_recv[0, part_rows(k), :] = value.astype(bf16)
        return carry

    lax.fori_loop(0, n_rows, finish, 0)
    put(y_recv.at[0], out_latents, 9)
    gain_next(3)

    def put_weight(spread, at, out, i):
        spread.final()
        stage[at] = dp_acc[...].T
        put(stage.at[at], out, i)

    put_weight(grad_o, 0, out_out, 6)
    gain_next(4)
    put_weight(grad_q, 1, out_query, 7)
    pair_last()

    def finish_lat(k, carry):
        coef = coef_row[:, part_rows(k)].T
        own = nn(flip(sgkv_all[:, own_latents(k)]), w_own[...])
        value = (back_lat.total(k) + own) * gain_lat[:, block_cols(f)]
        value = value - raw_lat[part_rows(k), :].astype(f32) * coef[:, 1:2]
        value = value + cot_all[f, part_rows(k), :].astype(f32)
        y_recv[1, part_rows(k), :] = value.astype(bf16)
        return carry

    lax.fori_loop(0, n_rows, finish_lat, 0)
    put(y_recv.at[1], out_grad_lat, 11)
    pair_result()
    for i, out in enumerate((out_key, out_value)):
        put(kv_acc.at[pl.ds(i * head, head), pl.ds(feat, feat)], out, 8 + 5 * i)
    gain_next(5)
    own = pl.ds(pl.multiple_of(dp * (width // n_dp), 128), width // n_dp)
    mine_all = gain_sum[:, own]
    index = lax.broadcasted_iota(jnp.int32, mine_all.shape, 0)
    out_gain_c[...] = jnp.sum(jnp.where(index == f, mine_all, 0.0), axis=0, keepdims=True)
    out_gain_l[...] = jnp.sum(jnp.where(index == 4 + f, mine_all, 0.0), axis=0, keepdims=True)

    for copy in outs:
        copy.wait()
    for buf, base in ((lat_all, sem_lat), (cot_all, sem_cot)):
        gather_done(buf, base)
    for collect in (branch, back_lat):
        collect.wait_y_sends()
    back_lat.core_sends_done()
    for spread in (grad_o, grad_q):
        spread.wait_sends()
    for buf, held, base in ((lat_all, lat_x, sem_lat_x), (cot_all, cot_x, sem_cot_x)):
        for i in range(2):
            across_x(buf, held, base, i).wait_send()
            across_core(held, base, i).wait_send()
    att_x_copy().wait_send()
    sgq_x_copy().wait_send()
    pair_sends_done()
    w_core().wait_send()
    for i in range(2):
        w_y(y_dev, f_y, i).wait_send()
    for i in others:
        w_z(i).wait_send()
    for i in range(n_hi):
        w_x(i).wait_send()
    for j in range(2):
        kv_core_copy(j).wait_send()
    kv_y_copy().wait_send()
    for i in range(3):
        gkv_copy(f, i, core_dev).wait_send()


def hand_on(*refs):
    n = (len(refs) - 2) // 3
    ins, outs, held, sem_in, sem_out = refs[:n], refs[n : 2 * n], refs[2 * n : 3 * n], *refs[3 * n :]
    take_in = [pltpu.make_async_copy(ins[i], held[i], sem_in.at[i]) for i in range(n)]
    give_out = [pltpu.make_async_copy(held[i], outs[i], sem_out.at[i]) for i in range(n)]
    for copy in take_in:
        copy.start()
    for i in range(n):
        take_in[i].wait()
        give_out[i].start()
    for copy in give_out:
        copy.wait()


def kernel_local(
    n_dp,
    context,
    latents,
    gain_ctx,
    gain_lat,
    w_query,
    key_matrix,
    value_matrix,
    w_out,
    lengths,
    patch_flags,
    cotangent,
):
    rows, width = context.shape
    model_width = gain_ctx.shape[0]
    units = w_query.shape[1]
    kv = 2 * key_matrix.shape[1]
    heads = units // HEAD_DIM
    n_hi = n_dp // 2
    feat = model_width // n_dp
    steps = 5
    any_space = pl.BlockSpec(memory_space=pl.ANY)
    vmem = pl.BlockSpec(memory_space=pltpu.VMEM)
    block = jax.ShapeDtypeStruct((rows, width), bf16)
    shaped = jax.ShapeDtypeStruct
    out = pl.pallas_call(
        functools.partial(block_kernel, n_dp),
        out_shape=(
            block,
            block,
            block,
            shaped((feat, units), f32),
            shaped((kv // 2, feat), f32),
            shaped((kv // 2, feat), f32),
            shaped((feat, units), f32),
            shaped((1, width // n_dp), f32),
            shaped((1, width // n_dp), f32),
        ),
        in_specs=[
            any_space,
            any_space,
            any_space,
            vmem,
            vmem,
            any_space,
            any_space,
            any_space,
            any_space,
            pl.BlockSpec(memory_space=pltpu.SMEM),
            vmem,
        ],
        out_specs=(any_space,) * 7 + (vmem,) * 2,
        scratch_shapes=[
            pltpu.VMEM((4, rows, width), bf16),
            pltpu.VMEM((4, rows, width), bf16),
            pltpu.VMEM((rows, width), bf16),
            pltpu.VMEM((rows, width), bf16),
            pltpu.VMEM((rows, width), bf16),
            pltpu.VMEM((model_width, units), bf16),
            pltpu.VMEM((kv, model_width), bf16),
            pltpu.VMEM((4 * kv, width), bf16),
            pltpu.VMEM((model_width, units), bf16),
            pltpu.VMEM((rows, units), f32),
            pltpu.VMEM((4 * kv, 2 * rows), f32),
            pltpu.VMEM((units, rows), bf16),
            pltpu.VMEM((units, rows), bf16),
            pltpu.VMEM((units, rows), bf16),
            pltpu.VMEM((units, rows), bf16),
            pltpu.VMEM((heads, rows, HEAD_DIM), bf16),
            pltpu.VMEM((heads, rows, HEAD_DIM), bf16),
            pltpu.VMEM((rows, units), bf16),
            pltpu.VMEM((rows, units), bf16),
            pltpu.VMEM((kv, 2 * rows), bf16),
            pltpu.VMEM((2, kv, 2 * rows), bf16),
            pltpu.VMEM((2, kv, 2 * rows), bf16),
            pltpu.VMEM((kv, 2 * rows), bf16),
            pltpu.VMEM((heads, rows, rows), bf16),
            pltpu.VMEM((heads, rows, ROWS), bf16),
            pltpu.VMEM((kv, 2 * rows), f32),
            pltpu.VMEM((4 * kv, 2 * rows), bf16),
            pltpu.VMEM((rows, width), bf16),
            pltpu.VMEM((4, 8, rows), f32),
            pltpu.VMEM((4, 8, rows), f32),
            pltpu.VMEM((8, rows), f32),
            pltpu.VMEM((8, rows), f32),
            pltpu.VMEM((8, 8, width), f32),
            pltpu.VMEM((8, width), f32),
            pltpu.VMEM((steps, 8, width), f32),
            pltpu.VMEM((2, rows, width), bf16),
            pltpu.VMEM((2, 2, rows, width), bf16),
            pltpu.VMEM((2, rows, width), bf16),
            pltpu.VMEM((4, rows, feat), bf16),
            pltpu.VMEM((4, rows, feat), bf16),
            pltpu.VMEM((units, rows), bf16),
            pltpu.VMEM((units, rows), bf16),
            pltpu.VMEM((3, units, feat), bf16),
            pltpu.VMEM((3, units, feat), bf16),
            pltpu.VMEM((3, units, feat), bf16),
            pltpu.VMEM((3, units, feat), bf16),
            pltpu.VMEM((4 * kv, feat), bf16),
            pltpu.VMEM((4 * kv, feat), bf16),
            pltpu.VMEM((2, 4 * kv, feat), bf16),
            pltpu.VMEM((3, kv, feat), bf16),
            pltpu.VMEM((kv, feat), bf16),
            pltpu.VMEM((units, feat), f32),
            pltpu.VMEM((2, feat, units), f32),
            pltpu.SemaphoreType.DMA((128,)),
            pltpu.SemaphoreType.DMA((128,)),
            pltpu.SemaphoreType.DMA((16,)),
        ],
        compiler_params=pltpu.CompilerParams(
            collective_id=0, has_side_effects=True, vmem_limit_bytes=64 << 20
        ),
        name="block",
    )(
        context,
        latents,
        cotangent,
        gain_ctx.reshape(1, model_width),
        gain_lat.reshape(1, model_width),
        w_query,
        key_matrix.T,
        value_matrix.T,
        w_out,
        lengths,
        patch_flags.reshape(1, rows),
    )
    out = pl.pallas_call(
        hand_on,
        out_shape=tuple(shaped(a.shape, a.dtype) for a in out),
        in_specs=[any_space] * 9,
        out_specs=(any_space,) * 9,
        scratch_shapes=[pltpu.VMEM(a.shape, a.dtype) for a in out]
        + [pltpu.SemaphoreType.DMA((9,)), pltpu.SemaphoreType.DMA((9,))],
        compiler_params=pltpu.CompilerParams(vmem_limit_bytes=64 << 20),
        name="hand_on",
    )(*out)
    latents_out, grad_context, grad_latents, g_query, g_key, g_value, g_out, gain_c, gain_l = out
    return (
        latents_out,
        grad_context,
        grad_latents,
        g_query,
        g_key.T,
        g_value.T,
        g_out,
        gain_c,
        gain_l,
    )


def solution(mesh):
    n_dp = mesh.shape["dp"]
    body = functools.partial(kernel_local, n_dp) if n_dp == 8 else plain_local
    return jax.shard_map(
        body,
        mesh=mesh,
        in_specs=(
            P("dp", "tensor"),
            P("dp", "tensor"),
            P(),
            P(),
            P(None, "tensor"),
            P(None, "tensor"),
            P(None, "tensor"),
            P(None, "tensor"),
            P("dp", None),
            P("dp"),
            P("dp", "tensor"),
        ),
        out_specs=(
            P("dp", "tensor"),
            P("dp", "tensor"),
            P("dp", "tensor"),
            P("dp", "tensor"),
            P("dp", "tensor"),
            P("dp", "tensor"),
            P("dp", "tensor"),
            P("tensor", "dp"),
            P("tensor", "dp"),
        ),
        check_vma=False,
    )
```

```python
import functools

import jax
import jax.numpy as jnp
from jax import lax
from jax.experimental import pallas as pl
from jax.experimental.pallas import tpu as pltpu
from jax.sharding import PartitionSpec as P

HEAD_DIM = 96
LAT = 64


epsilon = 1e-06
masked_value = -1e30
contract_rows = (((0,), (0,)), ((), ()))
contract_cols = (((1,), (1,)), ((), ()))


def row_scales(rows_in):
    values_f = rows_in.astype(jnp.float32)
    return (values_f, lax.rsqrt(jnp.mean(values_f * values_f, axis=1) + epsilon))


def norm_back(grad_norm, local_vals, row_scale, gain_local, row_inner_all, model_width):
    weighted = grad_norm * gain_local
    grad_input = (
        row_scale[:, None] * weighted
        - local_vals * (row_scale**3 * row_inner_all / model_width)[:, None]
    )
    grad_gain = jnp.sum(grad_norm * local_vals * row_scale[:, None], axis=0)
    return (grad_input, grad_gain)


def plain_local(
    context,
    latents,
    gain_ctx,
    gain_lat,
    w_query,
    key_matrix,
    value_matrix,
    w_out,
    lengths,
    patch_flags,
    cotangent,
):
    patch_rows = context.shape[0]
    latent_rows = latents.shape[0]
    local_width = context.shape[1]
    model_width = gain_ctx.shape[0]
    head_size = HEAD_DIM
    kv_local = key_matrix.shape[1] // head_size
    query_local = w_query.shape[1] // head_size
    repeat = query_local // kv_local
    all_count = patch_rows + latent_rows
    score_scale = head_size ** (-0.5)
    column = lax.axis_index("tensor") * local_width
    whole_ctx, whole_lat = (
        lax.all_gather(context, "tensor", axis=1, tiled=True),
        lax.all_gather(latents, "tensor", axis=1, tiled=True),
    )
    ctx_values, ctx_scale = row_scales(whole_ctx)
    lat_values, lat_scale = row_scales(whole_lat)
    ctx_norm = (ctx_values * ctx_scale[:, None] * gain_ctx).astype(jnp.bfloat16)
    lat_norm = (lat_values * lat_scale[:, None] * gain_lat).astype(jnp.bfloat16)
    queries = jnp.dot(lat_norm, w_query, preferred_element_type=jnp.float32).astype(jnp.bfloat16)
    all_rows = jnp.concatenate([ctx_norm, lat_norm], axis=0)
    w_pair = jnp.concatenate([key_matrix, value_matrix], axis=1)
    pair_rows = jnp.dot(all_rows, w_pair, preferred_element_type=jnp.float32).astype(jnp.bfloat16)
    key_head_split = (
        pair_rows[:, : kv_local * head_size]
        .reshape(all_count, kv_local, head_size)
        .transpose(1, 0, 2)
    )
    value_head_split = (
        pair_rows[:, kv_local * head_size :]
        .reshape(all_count, kv_local, head_size)
        .transpose(1, 0, 2)
    )
    query_heads = queries.reshape(latent_rows, query_local, head_size).transpose(1, 0, 2)
    image_ends = jnp.cumsum(lengths[0])
    patch_image = jnp.sum(
        (jnp.arange(patch_rows)[:, None] >= image_ends[None, :]).astype(jnp.int32), axis=1
    )
    latent_image = jnp.arange(latent_rows) // LAT
    allowed = jnp.concatenate(
        [
            (latent_image[:, None] == patch_image[None, :]) & (patch_flags[None, :] == 1),
            latent_image[:, None] == latent_image[None, :],
        ],
        axis=1,
    )
    head_index = jnp.arange(query_local)

    def head_scores(query_head, head_number):
        key_head = key_head_split[head_number // repeat]
        value_head = value_head_split[head_number // repeat]
        raw_scores = (
            lax.dot_general(query_head, key_head, contract_cols, preferred_element_type=jnp.float32)
            * score_scale
        )
        return (jnp.where(allowed, raw_scores, masked_value), key_head, value_head)

    def head_forward(member):
        query_head, head_number = member
        scores, key_head, value_head = head_scores(query_head, head_number)
        row_top = jnp.max(scores, axis=1, keepdims=True)
        exp_scores = jnp.exp(scores - row_top)
        row_total = jnp.sum(exp_scores, axis=1, keepdims=True)
        attention = (exp_scores / row_total).astype(jnp.bfloat16)
        blended = jnp.dot(attention, value_head, preferred_element_type=jnp.float32).astype(
            jnp.bfloat16
        )
        return (blended, row_top[:, 0] + jnp.log(row_total[:, 0]))

    heads_out, log_totals = lax.map(head_forward, (query_heads, head_index))
    attended = heads_out.transpose(1, 0, 2).reshape(latent_rows, query_local * head_size)
    partial_out = lax.dot_general(
        attended, w_out, contract_cols, preferred_element_type=jnp.float32
    )
    branch = lax.psum_scatter(
        partial_out.astype(jnp.bfloat16), "tensor", scatter_dimension=1, tiled=True
    ).astype(jnp.float32)
    latents_out = (latents.astype(jnp.float32) + branch).astype(jnp.bfloat16)
    full_grad = lax.all_gather(cotangent, "tensor", axis=1, tiled=True)
    grad_attended = jnp.dot(full_grad, w_out, preferred_element_type=jnp.float32).astype(
        jnp.bfloat16
    )
    grad_w_out = lax.dot_general(
        full_grad, attended, contract_rows, preferred_element_type=jnp.float32
    )
    grad_heads = grad_attended.reshape(latent_rows, query_local, head_size).transpose(1, 0, 2)

    def head_backward(member):
        query_head, grad_blended, log_total, head_number = member
        scores, key_head, value_head = head_scores(query_head, head_number)
        attention = jnp.exp(scores - log_total[:, None])
        grad_probs = lax.dot_general(
            grad_blended, value_head, contract_cols, preferred_element_type=jnp.float32
        )
        row_inner = jnp.sum(attention * grad_probs, axis=1, keepdims=True)
        grad_scores = (attention * (grad_probs - row_inner)).astype(jnp.bfloat16)
        grad_query = (
            jnp.dot(grad_scores, key_head, preferred_element_type=jnp.float32) * score_scale
        ).astype(jnp.bfloat16)
        grad_key = (
            lax.dot_general(
                grad_scores, query_head, contract_rows, preferred_element_type=jnp.float32
            )
            * score_scale
        )
        grad_value = lax.dot_general(
            attention.astype(jnp.bfloat16),
            grad_blended,
            contract_rows,
            preferred_element_type=jnp.float32,
        )
        return (grad_query, grad_key, grad_value)

    grad_query_heads, grad_key_heads, grad_value_heads = lax.map(
        head_backward, (query_heads, grad_heads, log_totals, head_index)
    )
    grad_keys = grad_key_heads.reshape(kv_local, repeat, all_count, head_size).sum(axis=1)
    grad_values = grad_value_heads.reshape(kv_local, repeat, all_count, head_size).sum(axis=1)
    grad_pair = jnp.concatenate(
        [
            grad_keys.transpose(1, 0, 2).reshape(all_count, kv_local * head_size),
            grad_values.transpose(1, 0, 2).reshape(all_count, kv_local * head_size),
        ],
        axis=1,
    ).astype(jnp.bfloat16)
    grad_q_rows = grad_query_heads.transpose(1, 0, 2).reshape(latent_rows, query_local * head_size)
    grad_w_query = lax.dot_general(
        lat_norm, grad_q_rows, contract_rows, preferred_element_type=jnp.float32
    )
    grad_w_pair = lax.dot_general(
        all_rows, grad_pair, contract_rows, preferred_element_type=jnp.float32
    )
    grad_rows = lax.dot_general(
        grad_pair, w_pair, contract_cols, preferred_element_type=jnp.float32
    )
    lat_terms = grad_rows[patch_rows:] + lax.dot_general(
        grad_q_rows, w_query, contract_cols, preferred_element_type=jnp.float32
    )
    grad_ctx_norm, grad_lat_norm = (
        lax.psum_scatter(
            grad_rows[:patch_rows].astype(jnp.bfloat16), "tensor", scatter_dimension=1, tiled=True
        ).astype(jnp.float32),
        lax.psum_scatter(
            lat_terms.astype(jnp.bfloat16), "tensor", scatter_dimension=1, tiled=True
        ).astype(jnp.float32),
    )
    ctx_local = context.astype(jnp.float32)
    lat_local = latents.astype(jnp.float32)
    gain_ctx_local = lax.dynamic_slice_in_dim(gain_ctx, column, local_width, 0)
    gain_lat_local = lax.dynamic_slice_in_dim(gain_lat, column, local_width, 0)
    ctx_inner = jnp.sum(grad_ctx_norm * gain_ctx_local * ctx_local, axis=1)
    lat_inner = jnp.sum(grad_lat_norm * gain_lat_local * lat_local, axis=1)
    ctx_inner_all, lat_inner_all = lax.psum((ctx_inner, lat_inner), "tensor")
    grad_ctx_in, grad_gain_c = norm_back(
        grad_ctx_norm, ctx_local, ctx_scale, gain_ctx_local, ctx_inner_all, model_width
    )
    grad_lat_in, grad_gain_l = norm_back(
        grad_lat_norm, lat_local, lat_scale, gain_lat_local, lat_inner_all, model_width
    )
    grad_context = grad_ctx_in.astype(jnp.bfloat16)
    grad_latents = (cotangent.astype(jnp.float32) + grad_lat_in).astype(jnp.bfloat16)
    grad_w_key = grad_w_pair[:, : kv_local * head_size]
    grad_w_value = grad_w_pair[:, kv_local * head_size :]
    sum_query, sum_key, sum_value, sum_out, sum_gain_c, sum_gain_l = (
        lax.psum_scatter(grad_w_query, "dp", scatter_dimension=0, tiled=True),
        lax.psum_scatter(grad_w_key, "dp", scatter_dimension=0, tiled=True),
        lax.psum_scatter(grad_w_value, "dp", scatter_dimension=0, tiled=True),
        lax.psum_scatter(grad_w_out, "dp", scatter_dimension=0, tiled=True),
        lax.psum_scatter(grad_gain_c, "dp", scatter_dimension=0, tiled=True),
        lax.psum_scatter(grad_gain_l, "dp", scatter_dimension=0, tiled=True),
    )
    return (
        latents_out,
        grad_context,
        grad_latents,
        sum_query,
        sum_key,
        sum_value,
        sum_out,
        sum_gain_c.reshape(1, -1),
        sum_gain_l.reshape(1, -1),
    )


MESH = pl.DeviceIdType.MESH
f32 = jnp.float32
bf16 = jnp.bfloat16
ROWS = 128
LOG2_E = 1.4426950408889634


def nn(a, b):
    return jnp.dot(a, b, preferred_element_type=f32)


def nt(a, b):
    return lax.dot_general(a, b, contract_cols, preferred_element_type=f32)


def flip(a):
    return a.astype(f32).T.astype(bf16)


def block_kernel(
    n_dp,
    context,
    latents,
    cotangent,
    gain_ctx,
    gain_lat,
    w_query,
    key_across,
    value_across,
    w_out,
    lengths,
    flags,
    out_latents,
    out_context,
    out_grad_lat,
    out_query,
    out_key,
    out_value,
    out_out,
    out_gain_c,
    out_gain_l,
    lat_all,
    cot_all,
    ctx_own,
    raw_lat,
    raw_ctx,
    wq,
    wkv,
    w_own,
    wo,
    acc_q,
    kv_acc,
    att_t,
    sgq_t,
    q_rows,
    q_cols,
    ga_rows,
    ga_cols,
    k_rows,
    v_rows,
    far_s,
    near_s,
    far_g,
    near_g,
    att,
    sgq,
    kv_t,
    kv_send,
    kv_core,
    kv_y,
    probs_c,
    probs_l,
    gkv,
    sgkv_all,
    sgc,
    sgl,
    sums,
    inners,
    scale_row,
    coef_row,
    gain_part,
    gain_sum,
    gain_recv,
    gain_pair,
    gain_one,
    core_send,
    core_recv,
    y_recv,
    lat_x,
    cot_x,
    att_xt,
    sgq_xt,
    z_send_o,
    z_send_q,
    z_recv_o,
    z_recv_q,
    x_send_kv,
    x_recv_kv,
    z_recv_kv,
    own_send,
    own_recv,
    dp_acc,
    send_sem,
    recv_sem,
    local_sem,
):
    rows, width = raw_lat.shape
    n_rows = rows // ROWS
    n_hi = n_dp // 2
    feat = 4 * width // n_dp
    head = HEAD_DIM
    heads = acc_q.shape[1] // head
    model_width = 4 * width
    score_scale = head ** (-0.5)

    dp = lax.axis_index("dp")
    f = lax.axis_index("tensor")
    z, x = dp // 2, lax.rem(dp, 2)
    y, c = f // 2, lax.rem(f, 2)
    f_c = y * 2 + (1 - c)
    f_y = (1 - y) * 2 + c
    f_yc = (1 - y) * 2 + (1 - c)
    core_dev, y_dev, yc_dev = (dp, f_c), (dp, f_y), (dp, f_yc)
    x_dev = (z * 2 + 1 - x, f)
    z_1 = z + 1 - 2 * lax.rem(z, 2)
    z_2 = z + 2 - 4 * (z // 2)
    z1_dev, z2_dev = (z_1 * 2 + x, f), (z_2 * 2 + x, f)
    x_mine = pl.ds(pl.multiple_of(x * feat, 128), feat)
    x_other = pl.ds(pl.multiple_of((1 - x) * feat, 128), feat)

    urgent = lax.rem(c + z, 2) == 1
    patient = jnp.logical_not(urgent)

    count = [0]

    def take(n):
        count[0] += n
        return count[0] - n

    def remote(src, dst, sem, dev, sem_to=None):
        return pltpu.make_async_remote_copy(
            src_ref=src,
            dst_ref=dst,
            send_sem=send_sem.at[sem],
            recv_sem=recv_sem.at[sem if sem_to is None else sem_to],
            device_id=dev,
            device_id_type=MESH,
        )

    def local_copy(src, dst, i):
        return pltpu.make_async_copy(src, dst, local_sem.at[i])

    def part_rows(k):
        if isinstance(k, int):
            return pl.ds(k * ROWS, ROWS)
        return pl.ds(pl.multiple_of(k * ROWS, ROWS), ROWS)

    n_cols = 4
    piece = width // n_cols

    def part_cols(k):
        if isinstance(k, int):
            return pl.ds(k * piece, piece)
        return pl.ds(pl.multiple_of(k * piece, 128), piece)

    def cols_at(fb, k):
        return pl.ds(pl.multiple_of(fb * width + k * piece, 128), piece)

    def block_cols(fb):
        if isinstance(fb, int):
            return pl.ds(fb * width, width)
        return pl.ds(pl.multiple_of(fb * width, width), width)

    loads = [
        local_copy(latents, raw_lat, 0),
        local_copy(key_across, wkv.at[pl.ds(0, head)], 4),
        local_copy(value_across, wkv.at[pl.ds(head, head)], 14),
        local_copy(context, raw_ctx, 1),
        local_copy(cotangent, cot_all.at[f], 2),
        local_copy(w_query, wq, 3),
        local_copy(w_out, wo, 5),
    ]
    for load in loads:
        load.start()

    barrier = pltpu.get_barrier_semaphore()

    def greet(dev):
        pl.semaphore_signal(barrier, inc=1, device_id=dev, device_id_type=MESH)

    others = [i for i in range(1, n_hi)]

    def far_dev(i):
        return (lax.rem(z + i, n_hi) * 2 + x, f)

    always = [core_dev, y_dev, yc_dev, x_dev] + [far_dev(i) for i in others]
    for dev in always:
        greet(dev)
    pl.semaphore_wait(barrier, len(always))

    sem_lat, sem_cot = (take(2 * n_rows + 1) for _ in range(2))

    def gather_y(buf, base, k):
        return remote(buf.at[f, part_rows(k)], buf.at[f, part_rows(k)], base + k, y_dev)

    def gather_core(buf, base):
        return remote(buf.at[f], buf.at[f], base + n_rows, core_dev)

    def gather_on(buf, base, k):
        return remote(
            buf.at[f_y, part_rows(k)], buf.at[f_y, part_rows(k)], base + n_rows + 1 + k, core_dev
        )

    def pass_on(buf, base, held=None, base_x=None):
        def step(k, carry):
            gather_y(buf, base, k).wait_recv()
            gather_on(buf, base, k).start()
            if held is not None:
                rows_x(buf, held, base_x, k).start()
            return carry

        lax.fori_loop(0, n_rows, step, 0)

    def wait_on(buf, base):
        for k in range(n_rows):
            gather_on(buf, base, k).wait_recv()

    def gather_done(buf, base):
        for k in range(n_rows):
            gather_y(buf, base, k).wait_send()
            gather_on(buf, base, k).wait_send()
        gather_core(buf, base).wait_send()

    def weigh(raw, gain, buf, base, index):
        gain_row = gain[:, block_cols(f)]
        for k in range(n_rows):
            values = raw[part_rows(k), :].astype(f32)
            buf[part_rows(k), :] = (values * gain_row).astype(bf16)
            if base is not None:
                gather_y(lat_all, base, k).start()
        if base is not None:
            gather_core(lat_all, base).start()
        for k in range(n_rows):
            values = raw[part_rows(k), :].astype(f32)
            total = jnp.sum(values * values, axis=1, keepdims=True)
            across = jnp.broadcast_to(total, (ROWS, 128)).T
            sums[f, pl.ds(index, 1), part_rows(k)] = across[0:1, :]

    sem_lat_x, sem_cot_x = take(2 * n_rows + 2), take(2 * n_rows + 2)
    sem_att_x, sem_sgq_x = take(n_rows), take(n_rows)

    def across_x(buf, held, base):
        return remote(buf.at[f, :, x_other], held.at[f], base, x_dev)

    def across_core(held, base):
        return remote(held.at[f], held.at[f], base + 1, core_dev)

    def rows_x(buf, held, base, k):
        return remote(
            buf.at[f_y, part_rows(k), x_other], held.at[f_y, part_rows(k)], base + 2 + k, x_dev
        )

    def rows_core(held, base, k):
        piece = held.at[f_y, part_rows(k)]
        return remote(piece, piece, base + 2 + n_rows + k, core_dev)

    def hold_own(buf, held, base):
        across_x(buf, held, base).wait_recv()
        across_core(held, base).start()

    def hold_rows(buf, held, base):
        def step(k, carry):
            rows_x(buf, held, base, k).wait_recv()
            rows_core(held, base, k).start()
            return carry

        lax.fori_loop(0, n_rows, step, 0)

    def rows_core_done(held, base):
        for k in range(n_rows):
            rows_core(held, base, k).wait_recv()

    kv = 2 * head
    slice_width = width // n_dp
    pair_rows = pl.ds(pl.multiple_of((1 - y) * 2 * kv, 64), 2 * kv)
    sem_w_core, sem_w_y, sem_w_z, sem_w_x = take(1), take(2), take(n_hi), take(n_hi)

    def head_rows_of(t):
        return pl.ds(pl.multiple_of(t * kv, 64), kv)

    def slice_cols(d, at=0):
        return pl.ds(pl.multiple_of(at + d * slice_width, 128), slice_width)

    def w_y(dev, f_to, i, sender=c):
        return remote(
            wkv.at[:, slice_cols(dp, f_to * width)],
            w_own.at[head_rows_of(f), slice_cols(dp)],
            sem_w_y + i,
            dev,
            sem_w_y + sender,
        )

    def w_core():
        return remote(
            wkv.at[:, block_cols(f_c)], w_own.at[head_rows_of(f)], sem_w_core, core_dev
        )

    def w_z(i):
        piece = w_own.at[pair_rows, slice_cols(dp)]
        return remote(piece, piece, sem_w_z + i, far_dev(i))

    def w_x(i):
        piece = w_own.at[pair_rows, slice_cols(lax.rem(z + i, n_hi) * 2 + x)]
        return remote(piece, piece, sem_w_x + lax.rem(z + i, n_hi), x_dev)

    sums[f] = jnp.zeros(sums.shape[1:], f32)
    inners[f] = jnp.zeros(inners.shape[1:], f32)
    loads[1].wait()
    loads[2].wait()
    w_y(y_dev, f_y, 0).start()
    w_y(yc_dev, f_yc, 1).start()
    w_core().start()
    loads[0].wait()
    weigh(raw_lat, gain_lat, lat_all.at[f], sem_lat, 1)
    pl.when(urgent)(lambda: across_x(lat_all, lat_x, sem_lat_x).start())
    loads[3].wait()
    weigh(raw_ctx, gain_ctx, ctx_own, None, 0)
    loads[4].wait()
    gather_core(cot_all, sem_cot).start()
    for i in range(2):
        w_y(y_dev, f_y, i, i).wait_recv()
    for i in others:
        w_z(i).start()
    w_x(0).start()
    w_own[head_rows_of(f), :] = wkv[:, block_cols(f)]

    peers = [core_dev, y_dev, yc_dev]
    sem_sums, sem_inner = take(3), take(3)

    def exchange(buf, base):
        return [remote(buf.at[f], buf.at[f], base + i, dev) for i, dev in enumerate(peers)]

    sums_out = exchange(sums, sem_sums)
    for copy in sums_out:
        copy.start()

    def project(acc, values, weight, blocks, first):
        def step(i, carry):
            fb = blocks[0] + i * (blocks[1] - blocks[0])
            for m in range(2):
                half = pl.ds(m * (rows // 2), rows // 2)
                product = nn(values[fb, half, :], weight[block_cols(fb), :])
                if first:
                    @pl.when(i == 0)
                    def _():
                        acc[half, :] = product

                    @pl.when(i > 0)
                    def _():
                        acc[half, :] += product
                else:
                    acc[half, :] += product
            return carry

        lax.fori_loop(0, 2, step, 0)

    def project_pair(blocks, first):
        latent_cols = pl.ds(rows, rows)
        for i, fb in enumerate(blocks):
            product = nt(wkv[:, block_cols(fb)], lat_all[fb])
            if first and i == 0:
                kv_acc[0:kv, latent_cols] = product
            else:
                kv_acc[0:kv, latent_cols] += product

    mine, theirs = (f, f_c), (f_y, f_yc)
    loads[5].wait()
    loads[6].wait()
    gather_core(lat_all, sem_lat).wait_recv()
    project(acc_q, lat_all, wq, mine, True)
    project_pair(mine, True)
    for i in others:
        w_z(n_hi - i).wait_recv()
        w_x(i).start()
    w_core().wait_recv()
    across_x(cot_all, cot_x, sem_cot_x).start()
    for i in range(n_hi):
        w_x(i).wait_recv()

    sem_kv_core, sem_kv_y = take(2), take(1)

    def kv_core_copy(j):
        return remote(kv_send.at[j], kv_core.at[j], sem_kv_core + j, core_dev)

    def kv_y_copy():
        return remote(kv_core.at[0], kv_y, sem_kv_y, y_dev)

    patches = pl.ds(0, rows)
    for n in range(2):
        half = slice(n * (rows // 2), (n + 1) * (rows // 2))
        kv_acc[:, half] = nt(w_own[...], ctx_own[half, :])
    for j, t in enumerate((f_yc, f_c)):
        kv_send[j] = kv_acc[head_rows_of(t), patches].astype(bf16)
        kv_core_copy(j).start()
    kv_core_copy(0).wait_recv()
    kv_core[0] = (kv_acc[head_rows_of(f_y), patches] + kv_core[0].astype(f32)).astype(bf16)
    kv_y_copy().start()

    def cot_across_y():
        for k in range(n_rows):
            gather_y(cot_all, sem_cot, k).start()

    pl.when(urgent)(cot_across_y)

    pass_on(lat_all, sem_lat)
    wait_on(lat_all, sem_lat)
    project(acc_q, lat_all, wq, theirs, False)
    project_pair(theirs, False)

    for copy in sums_out:
        copy.wait()
    total = sums[0] + sums[1] + sums[2] + sums[3]
    scale_row[...] = lax.rsqrt(total / model_width + epsilon)

    def split_heads(acc, by_rows, by_cols, row_scale, factor):
        for k in range(n_rows):
            across = acc[part_rows(k), :].T
            if row_scale is not None:
                across = across * row_scale[:, part_rows(k)]
            for h in range(heads):
                one = across[h * head : (h + 1) * head, :]
                at = pl.ds(h * ROWS, ROWS)
                by_cols[k, :, at] = one.astype(bf16)
                by_rows[k, at, :] = (one * factor).T.astype(bf16)

    def kv_by_rows(first):
        for n in range(first, first + n_rows):
            k_rows[part_rows(n), :] = flip(kv_t[0:head, part_rows(n)])
            v_rows[part_rows(n), :] = flip(kv_t[head:, part_rows(n)])

    split_heads(acc_q, q_rows, q_cols, scale_row[1:2, :], score_scale * LOG2_E)
    kv_t[:, rows:] = (kv_acc[0:kv, rows:] * scale_row[1:2, :]).astype(bf16)
    kv_by_rows(n_rows)
    kv_core_copy(1).wait_recv()
    kv_y_copy().wait_recv()
    summed = kv_acc[head_rows_of(f), patches] + kv_core[1].astype(f32) + kv_y[...].astype(f32)
    kv_t[:, 0:rows] = (summed * scale_row[0:1, :]).astype(bf16)
    kv_by_rows(0)

    patch = lax.broadcasted_iota(jnp.int32, (1, rows), 1)
    image = jnp.zeros((1, rows), jnp.int32)
    end = jnp.int32(0)
    for i in range(lengths.shape[1]):
        end = end + lengths[0, i]
        image = image + (patch >= end).astype(jnp.int32)
    image = jnp.where(flags[...] == 1, image, -1)
    per_part = ROWS // LAT
    row_image = lax.broadcasted_iota(jnp.int32, (ROWS, 1), 0) // LAT
    col_image = lax.broadcasted_iota(jnp.int32, (1, ROWS), 1) // LAT
    same = row_image == col_image
    keys, vals = pl.ds(0, head), pl.ds(head, head)
    def own_latents(p):
        return pl.ds(pl.multiple_of(rows + p * ROWS, ROWS), ROWS)


    def head_part(h):
        return slice(h * ROWS, (h + 1) * ROWS)

    def att_x_copy(p):
        cols = part_rows(p)
        return remote(att_t.at[:, cols], att_xt.at[:, cols], sem_att_x + p, x_dev)

    def sgq_x_copy(p):
        cols = part_rows(p)
        return remote(sgq_t.at[:, cols], sgq_xt.at[:, cols], sem_sgq_x + p, x_dev)

    def forward_step(p, carry):
        far_s[...] = nn(q_rows[p], kv_t[keys, patches])
        near_s[...] = nn(q_rows[p], kv_t[keys, own_latents(p)])
        allowed = (row_image + p * per_part) == image
        for h in range(heads):
            far = jnp.where(allowed, far_s[head_part(h), :], masked_value)
            near = jnp.where(same, near_s[head_part(h), :], masked_value)
            top = jnp.maximum(
                jnp.max(far, axis=1, keepdims=True), jnp.max(near, axis=1, keepdims=True)
            )
            far, near = jnp.exp2(far - top), jnp.exp2(near - top)
            total = jnp.sum(far, axis=1, keepdims=True) + jnp.sum(near, axis=1, keepdims=True)
            inverse = 1.0 / total
            probs_c[p, head_part(h), :] = (far * inverse).astype(bf16)
            probs_l[p, head_part(h), :] = (near * inverse).astype(bf16)
        blended = nn(probs_c[p], v_rows[patches, :]) + nn(probs_l[p], v_rows[own_latents(p), :])
        for h in range(heads):
            one = blended[head_part(h), :]
            att_t[h * head : (h + 1) * head, part_rows(p)] = one.T.astype(bf16)
        att_x_copy(p).start()
        return carry

    lax.fori_loop(0, n_rows, forward_step, 0)
    def chunk_out(zt):
        return nn(att_t[...], cot_all[zt, :, x_mine]) + nn(att_xt[...], cot_x[zt])

    def chunk_query(zt):
        return nn(sgq_t[...], lat_all[zt, :, x_mine]) + nn(sgq_xt[...], lat_x[zt])

    def chunk_pair(xt):
        cols = pl.ds(pl.multiple_of(xt * feat, 128), feat)
        return nn(sgkv_all[:, patches], ctx_own[:, cols]) + nn(
            sgkv_all[:, pl.ds(rows, rows)], lat_all[f, :, cols]
        )

    class Spread:
        def __init__(self, chunk, send, recv):
            self.chunk, self.send, self.recv, self.sem = chunk, send, recv, take(3)

        def copy(self, j, dev):
            return remote(self.send.at[j], self.recv.at[j], self.sem + j, dev)

        def first(self, j):
            zt = z_1 + j * (z_2 - z)
            self.send[j] = self.chunk(zt).astype(bf16)
            self.copy(j, z1_dev).start()

        def second(self):
            value = self.chunk(z_2)
            self.copy(1, z1_dev).wait_recv()
            self.send[2] = (value + self.recv[1].astype(f32)).astype(bf16)
            self.copy(2, z2_dev).start()

        def final(self):
            dp_acc[...] = self.chunk(z)
            self.copy(0, z1_dev).wait_recv()
            self.copy(2, z2_dev).wait_recv()
            dp_acc[...] += self.recv[0].astype(f32) + self.recv[2].astype(f32)

        def wait_sends(self):
            for j in range(3):
                self.copy(j, z1_dev).wait_send()

    grad_o = Spread(chunk_out, z_send_o, z_recv_o)
    grad_q = Spread(chunk_query, z_send_q, z_recv_q)

    sem_kv_x, sem_kv_z1, sem_kv_z2, sem_kv_own = take(4), take(4), take(4), take(5)
    pair_acc = kv_acc.at[:, pl.ds(0, feat)]
    passes = lax.rem(z + f, 2) == 1
    middle = z_2 == f

    def head_rows_at(t):
        return pl.ds(t * kv, kv)

    def pair_x_copy(t):
        at = head_rows_at(t)
        return remote(x_send_kv.at[at], x_recv_kv.at[at], sem_kv_x + t, x_dev)

    def pair_z_copy(t, i):
        at = head_rows_at(t)
        base, dev = ((sem_kv_z1, z1_dev), (sem_kv_z2, z2_dev))[i]
        return remote(x_recv_kv.at[at], z_recv_kv.at[i, at], base + t, dev)

    def pair_own_copy(t):
        return remote(own_send.at[t], own_recv, sem_kv_own + t, (dp, t), sem_kv_own + 4)

    def pair_first():
        x_send_kv[...] = chunk_pair(1 - x).astype(bf16)
        for t in range(4):
            pair_x_copy(t).start()
        pair_acc[...] = chunk_pair(x)

    def pair_step(t, i):
        at = head_rows_at(t)
        if i == 0:
            pair_x_copy(t).wait_recv()
            pair_acc[at, :] += x_recv_kv[at, :].astype(f32)
            sends = passes
        else:
            @pl.when(jnp.logical_not(passes))
            def _():
                pair_z_copy(t, 0).wait_recv()
                pair_acc[at, :] += z_recv_kv[0, at, :].astype(f32)

            sends = middle

        @pl.when(sends)
        def _():
            x_recv_kv[at, :] = pair_acc[at, :].astype(bf16)
            pair_z_copy(t, i).start()

    def pair_last():
        @pl.when(z == f)
        def _():
            for t in range(4):
                at = head_rows_at(t)
                pair_z_copy(t, 1).wait_recv()
                pair_acc[at, :] += z_recv_kv[1, at, :].astype(f32)

                @pl.when(f != t)
                def _():
                    own_send[t] = pair_acc[at, :].astype(bf16)
                    pair_own_copy(t).start()

    def pair_result():
        @pl.when(z == f)
        def _():
            kv_acc[0:kv, pl.ds(feat, feat)] = kv_acc[head_rows_of(f), pl.ds(0, feat)]

        @pl.when(z != f)
        def _():
            pair_own_copy(0).wait_recv()
            kv_acc[0:kv, pl.ds(feat, feat)] = own_recv[...].astype(f32)

    def pair_sends_done():
        for t in range(4):
            pair_x_copy(t).wait_send()
            pl.when(passes)(lambda t=t: pair_z_copy(t, 0).wait_send())
            pl.when(middle)(lambda t=t: pair_z_copy(t, 1).wait_send())

        @pl.when(z == f)
        def _():
            for t in range(4):
                pl.when(f != t)(lambda t=t: pair_own_copy(t).wait_send())

    class Collect:
        def __init__(self, part, index, seen=None):
            self.part, self.index, self.sem = part, index, take(3 * n_cols)
            self.seen = seen

        def core_copy(self, j, k):
            return remote(
                core_send.at[j, :, part_cols(k)],
                core_recv.at[self.index, j, :, part_cols(k)],
                self.sem + j * n_cols + k,
                core_dev,
            )

        def y_copy(self, k):
            return remote(
                core_recv.at[self.index, 0, :, part_cols(k)],
                y_recv.at[self.index, :, part_cols(k)],
                self.sem + 2 * n_cols + k,
                y_dev,
            )

        def product(self, fb, k):
            value = self.part(fb, k)
            if self.seen is not None:
                self.seen(fb, k, value)
            return value

        def send_core(self):
            def core_step(n, carry):
                j, k = n // n_cols, lax.rem(n, n_cols)
                fb = jnp.where(j == 0, f_yc, f_c)
                core_send[j, :, part_cols(k)] = self.product(fb, k).astype(bf16)
                self.core_copy(j, k).start()
                return carry

            lax.fori_loop(0, 2 * n_cols, core_step, 0)

        def send_y(self, first, last):
            def y_step(k, carry):
                value = self.product(f_y, k)
                self.core_copy(0, k).wait_recv()
                value = value + core_recv[self.index, 0, :, part_cols(k)].astype(f32)
                core_recv[self.index, 0, :, part_cols(k)] = value.astype(bf16)
                self.y_copy(k).start()
                return carry

            lax.fori_loop(first, last, y_step, 0)

        def core_sends_done(self):
            for j in range(2):
                for k in range(n_cols):
                    self.core_copy(j, k).wait_send()

        def total(self, k):
            value = self.part(f, k)
            self.core_copy(1, k).wait_recv()
            self.y_copy(k).wait_recv()
            return (
                value
                + core_recv[self.index, 1, :, part_cols(k)].astype(f32)
                + y_recv[self.index, :, part_cols(k)].astype(f32)
            )

        def wait_y_sends(self):
            for k in range(n_cols):
                self.y_copy(k).wait_send()

    def gain_add(index, k, value, weighed):
        products = (value * weighed.astype(f32)).reshape(rows // 8, 8, piece)
        gain_part[index, :, part_cols(k)] += jnp.sum(products, axis=0)

    def part_branch(fb, k):
        return nt(att[...], wo[cols_at(fb, k), :])

    def part_lat(fb, k):
        return nt(sgq[...], wq[cols_at(fb, k), :])

    def seen_lat(fb, k, value):
        gain_add(4 + fb, k, value, lat_all[fb, :, part_cols(k)])

    branch = Collect(part_branch, 0)
    back_lat = Collect(part_lat, 1, seen_lat)
    gain_part[...] = jnp.zeros(gain_part.shape, f32)

    gather_core(cot_all, sem_cot).wait_recv()
    project(acc_q, cot_all, wo, mine, True)
    for k in range(n_rows):
        att[part_rows(k), :] = flip(att_t[:, part_rows(k)])
    pl.when(patient)(cot_across_y)
    branch.send_core()
    hold_own(cot_all, cot_x, sem_cot_x)
    pl.when(urgent)(lambda: hold_own(lat_all, lat_x, sem_lat_x))
    across_core(cot_x, sem_cot_x).wait_recv()
    for p in range(n_rows):
        att_x_copy(p).wait_recv()
    near_j = jnp.where(z // 2 == y, 0, 1)
    grad_o.first(near_j)

    @pl.when(urgent)
    def _():
        pass_on(cot_all, sem_cot, cot_x, sem_cot_x)
        for k in range(n_rows):
            rows_x(lat_all, lat_x, sem_lat_x, k).start()
        hold_rows(cot_all, cot_x, sem_cot_x)

    @pl.when(patient)
    def _():
        wait_on(cot_all, sem_cot)
        rows_core_done(cot_x, sem_cot_x)

    grad_o.first(1 - near_j)

    @pl.when(patient)
    def _():
        pass_on(cot_all, sem_cot, cot_x, sem_cot_x)

    pl.when(urgent)(lambda: wait_on(cot_all, sem_cot))
    project(acc_q, cot_all, wo, theirs, False)
    split_heads(acc_q, ga_rows, ga_cols, None, 1.0)
    branch.send_y(0, 1)

    gkv[:, patches] = jnp.zeros((kv, rows), f32)

    def backward_step(p, carry):
        far_s[...] = nn(ga_rows[p], kv_t[vals, patches])
        near_s[...] = nn(ga_rows[p], kv_t[vals, own_latents(p)])
        for h in range(heads):
            far_p = probs_c[p, head_part(h), :].astype(f32)
            near_p = probs_l[p, head_part(h), :].astype(f32)
            far_d, near_d = far_s[head_part(h), :], near_s[head_part(h), :]
            inner = jnp.sum(far_p * far_d, axis=1, keepdims=True) + jnp.sum(
                near_p * near_d, axis=1, keepdims=True
            )
            far_g[head_part(h), :] = (far_p * (far_d - inner)).astype(bf16)
            near_g[head_part(h), :] = (near_p * (near_d - inner)).astype(bf16)
        grad_query = nn(far_g[...], k_rows[patches, :]) + nn(near_g[...], k_rows[own_latents(p), :])
        total = jnp.zeros((1, ROWS), f32)
        for h in range(heads):
            one = grad_query[head_part(h), :].T * score_scale
            query = q_cols[p, :, head_part(h)].astype(f32)
            total = total + jnp.sum(one * query, axis=0, keepdims=True)
            sgq_t[h * head : (h + 1) * head, part_rows(p)] = (
                one * scale_row[1:2, part_rows(p)]
            ).astype(bf16)
        inners[f, 1:2, part_rows(p)] = total
        sgq_x_copy(p).start()
        gkv[keys, patches] += nn(q_cols[p], far_g[...])
        gkv[keys, own_latents(p)] = nn(q_cols[p], near_g[...])
        gkv[vals, patches] += nn(ga_cols[p], probs_c[p])
        gkv[vals, own_latents(p)] = nn(ga_cols[p], probs_l[p])
        return carry

    lax.fori_loop(0, n_rows, backward_step, 0)
    gkv[keys, :] = gkv[keys, :] * score_scale
    products = jnp.sum(gkv[...] * kv_t[...].astype(f32), axis=0, keepdims=True)
    inners[f, 0:1, :] = products[:, 0:rows]
    inners[f, 1:2, :] += products[:, rows:]
    inner_out = exchange(inners, sem_inner)
    for copy in inner_out:
        copy.start()
    sgkv_all[head_rows_of(f), 0:rows] = (gkv[:, 0:rows] * scale_row[0:1, :]).astype(bf16)
    sgkv_all[head_rows_of(f), rows:] = (gkv[:, rows:] * scale_row[1:2, :]).astype(bf16)
    sem_gkv = take(3)

    def gkv_copy(t, i, dev):
        piece = sgkv_all.at[head_rows_of(t)]
        return remote(piece, piece, sem_gkv + i, dev)

    gkv_copy(f, 0, y_dev).start()
    gkv_copy(f, 1, core_dev).start()
    for k in range(n_rows):
        sgq[part_rows(k), :] = flip(sgq_t[:, part_rows(k)])

    pl.when(patient)(lambda: hold_rows(cot_all, cot_x, sem_cot_x))
    pl.when(urgent)(lambda: rows_core_done(cot_x, sem_cot_x))
    grad_o.second()

    @pl.when(patient)
    def _():
        across_x(lat_all, lat_x, sem_lat_x).start()
        for k in range(n_rows):
            rows_x(lat_all, lat_x, sem_lat_x, k).start()
        across_core(lat_x, sem_lat_x).wait_recv()
        rows_core_done(lat_x, sem_lat_x)

    pl.when(urgent)(lambda: hold_rows(lat_all, lat_x, sem_lat_x))
    for p in range(n_rows):
        sgq_x_copy(p).wait_recv()
    grad_q.first(1)
    grad_q.first(0)
    branch.send_y(1, n_cols)
    branch.core_sends_done()
    gkv_copy(f, 0, y_dev).wait_recv()
    gkv_copy(f_y, 2, core_dev).start()
    gkv_copy(f, 1, core_dev).wait_recv()
    gkv_copy(f_y, 2, core_dev).wait_recv()
    pair_first()
    back_lat.send_core()
    back_lat.send_y(0, n_cols)

    @pl.when(patient)
    def _():
        hold_own(lat_all, lat_x, sem_lat_x)
        hold_rows(lat_all, lat_x, sem_lat_x)

    @pl.when(urgent)
    def _():
        across_core(lat_x, sem_lat_x).wait_recv()
        rows_core_done(lat_x, sem_lat_x)

    grad_q.second()
    outs = []

    def put(src, dst, i):
        copy = local_copy(src, dst, i)
        copy.start()
        outs.append(copy)

    for copy in inner_out:
        copy.wait()
    coef_row[...] = (
        scale_row[...]
        * scale_row[...]
        * (inners[0] + inners[1] + inners[2] + inners[3])
        / model_width
    )

    coef_cols = coef_row[...].T
    back_lat.core_sends_done()
    for k in range(n_rows):
        sgc[part_rows(k), :] = flip(sgkv_all[:, part_rows(k)])
        sgl[part_rows(k), :] = flip(sgkv_all[:, part_rows(n_rows + k)])

    def finish_ctx(k, carry):
        value = nn(sgc[...], w_own[:, part_cols(k)])
        gain_add(f, k, value, ctx_own[:, part_cols(k)])
        value = value * gain_ctx[:, cols_at(f, k)]
        value = value - raw_ctx[:, part_cols(k)].astype(f32) * coef_cols[:, 0:1]
        core_send[0, :, part_cols(k)] = value.astype(bf16)
        return carry

    lax.fori_loop(0, n_cols, finish_ctx, 0)
    put(core_send.at[0], out_context, 10)

    def gain_own(k, carry):
        value = part_lat(f, k) + nn(sgl[...], w_own[:, part_cols(k)])
        gain_add(4 + f, k, value, lat_all[f, :, part_cols(k)])
        return carry

    lax.fori_loop(0, n_cols, gain_own, 0)
    for i in range(4):
        gain_sum[i : i + 1, :] = (
            jnp.sum(gain_part[i], axis=0, keepdims=True) / gain_ctx[:, block_cols(i)]
        )
        gain_sum[4 + i : 5 + i, :] = (
            jnp.sum(gain_part[4 + i], axis=0, keepdims=True) / gain_lat[:, block_cols(i)]
        )
    part = width // n_dp

    def dp_cols(d, n):
        return pl.ds(pl.multiple_of(d * part, 128), n * part)

    sem_gain = take(n_hi + 2)

    def gain_z(i):
        return remote(
            gain_sum.at[:, dp_cols(lax.rem(z + i, n_hi) * 2, 2)],
            gain_recv.at[i],
            sem_gain + i,
            far_dev(i),
        )

    def gain_x():
        return remote(
            gain_pair.at[:, dp_cols(1 - x, 1)], gain_one.at[0], sem_gain, x_dev
        )

    def gain_core():
        return remote(gain_one.at[1], gain_one.at[2], sem_gain + n_hi, core_dev)

    def gain_y():
        return remote(gain_one.at[3], gain_one.at[4], sem_gain + n_hi + 1, y_dev)

    for i in others:
        gain_z(i).start()
    pair_step(0, 0)
    pair_step(1, 0)
    pair_step(0, 1)
    pair_step(2, 0)
    pair_step(1, 1)
    pair_step(3, 0)
    pair_step(2, 1)
    pair_step(3, 1)
    summed = gain_sum[:, dp_cols(z * 2, 2)]
    for i in others:
        gain_z(i).wait()
        summed = summed + gain_recv[i]
    gain_pair[...] = summed
    gain_x().start()

    def finish(k, carry):
        value = raw_lat[:, part_cols(k)].astype(f32) + branch.total(k)
        y_recv[0, :, part_cols(k)] = value.astype(bf16)
        return carry

    lax.fori_loop(0, n_cols, finish, 0)
    put(y_recv.at[0], out_latents, 9)
    gain_x().wait()
    gain_one[1] = gain_pair[:, dp_cols(x, 1)] + gain_one[0]
    gain_core().start()

    def put_weight(spread, at, out, i):
        spread.final()
        at[...] = dp_acc[...].T
        put(at, out, i)

    put_weight(grad_o, acc_q, out_out, 6)
    gain_core().wait()
    gain_one[3] = gain_one[1] + gain_one[2]
    gain_y().start()

    def finish_lat(k, carry):
        value = back_lat.total(k) + nn(sgl[...], w_own[:, part_cols(k)])
        value = value * gain_lat[:, cols_at(f, k)]
        value = value - raw_lat[:, part_cols(k)].astype(f32) * coef_cols[:, 1:2]
        value = value + cot_all[f, :, part_cols(k)].astype(f32)
        y_recv[1, :, part_cols(k)] = value.astype(bf16)
        return carry

    lax.fori_loop(0, n_cols, finish_lat, 0)
    put(y_recv.at[1], out_grad_lat, 11)
    pair_last()
    gain_y().wait()
    mine_all = gain_one[3] + gain_one[4]
    index = lax.broadcasted_iota(jnp.int32, mine_all.shape, 0)
    out_gain_c[...] = jnp.sum(jnp.where(index == f, mine_all, 0.0), axis=0, keepdims=True)
    out_gain_l[...] = jnp.sum(jnp.where(index == 4 + f, mine_all, 0.0), axis=0, keepdims=True)
    put_weight(grad_q, far_s.at[:, pl.ds(0, heads * head)], out_query, 7)
    pair_result()
    for i, out in enumerate((out_key, out_value)):
        put(kv_acc.at[pl.ds(i * head, head), pl.ds(feat, feat)], out, 8 + 5 * i)

    for copy in outs:
        copy.wait()
    for buf, base in ((lat_all, sem_lat), (cot_all, sem_cot)):
        gather_done(buf, base)
    for collect in (branch, back_lat):
        collect.wait_y_sends()
    for spread in (grad_o, grad_q):
        spread.wait_sends()
    for buf, held, base in ((lat_all, lat_x, sem_lat_x), (cot_all, cot_x, sem_cot_x)):
        across_x(buf, held, base).wait_send()
        across_core(held, base).wait_send()
        for k in range(n_rows):
            rows_x(buf, held, base, k).wait_send()
            rows_core(held, base, k).wait_send()
    for p in range(n_rows):
        att_x_copy(p).wait_send()
        sgq_x_copy(p).wait_send()
    pair_sends_done()
    w_core().wait_send()
    for i in range(2):
        w_y(y_dev, f_y, i).wait_send()
    for i in others:
        w_z(i).wait_send()
    for i in range(n_hi):
        w_x(i).wait_send()
    for j in range(2):
        kv_core_copy(j).wait_send()
    kv_y_copy().wait_send()
    for i in range(3):
        gkv_copy(f, i, core_dev).wait_send()


def hand_on(*refs):
    n = (len(refs) - 2) // 3
    ins, outs, held, sem_in, sem_out = refs[:n], refs[n : 2 * n], refs[2 * n : 3 * n], *refs[3 * n :]
    take_in = [pltpu.make_async_copy(ins[i], held[i], sem_in.at[i]) for i in range(n)]
    give_out = [pltpu.make_async_copy(held[i], outs[i], sem_out.at[i]) for i in range(n)]
    for copy in take_in:
        copy.start()
    for i in range(n):
        take_in[i].wait()
        give_out[i].start()
    for copy in give_out:
        copy.wait()


def kernel_local(
    n_dp,
    context,
    latents,
    gain_ctx,
    gain_lat,
    w_query,
    key_matrix,
    value_matrix,
    w_out,
    lengths,
    patch_flags,
    cotangent,
):
    rows, width = context.shape
    model_width = gain_ctx.shape[0]
    units = w_query.shape[1]
    kv = 2 * key_matrix.shape[1]
    heads = units // HEAD_DIM
    n_hi = n_dp // 2
    feat = model_width // n_dp
    any_space = pl.BlockSpec(memory_space=pl.ANY)
    vmem = pl.BlockSpec(memory_space=pltpu.VMEM)
    block = jax.ShapeDtypeStruct((rows, width), bf16)
    shaped = jax.ShapeDtypeStruct
    out = pl.pallas_call(
        functools.partial(block_kernel, n_dp),
        out_shape=(
            block,
            block,
            block,
            shaped((feat, units), f32),
            shaped((kv // 2, feat), f32),
            shaped((kv // 2, feat), f32),
            shaped((feat, units), f32),
            shaped((1, width // n_dp), f32),
            shaped((1, width // n_dp), f32),
        ),
        in_specs=[
            any_space,
            any_space,
            any_space,
            vmem,
            vmem,
            any_space,
            any_space,
            any_space,
            any_space,
            pl.BlockSpec(memory_space=pltpu.SMEM),
            vmem,
        ],
        out_specs=(any_space,) * 7 + (vmem,) * 2,
        scratch_shapes=[
            pltpu.VMEM((4, rows, width), bf16),
            pltpu.VMEM((4, rows, width), bf16),
            pltpu.VMEM((rows, width), bf16),
            pltpu.VMEM((rows, width), bf16),
            pltpu.VMEM((rows, width), bf16),
            pltpu.VMEM((model_width, units), bf16),
            pltpu.VMEM((kv, model_width), bf16),
            pltpu.VMEM((4 * kv, width), bf16),
            pltpu.VMEM((model_width, units), bf16),
            pltpu.VMEM((rows, units), f32),
            pltpu.VMEM((4 * kv, 2 * rows), f32),
            pltpu.VMEM((units, rows), bf16),
            pltpu.VMEM((units, rows), bf16),
            pltpu.VMEM((rows // ROWS, heads * ROWS, HEAD_DIM), bf16),
            pltpu.VMEM((rows // ROWS, HEAD_DIM, heads * ROWS), bf16),
            pltpu.VMEM((rows // ROWS, heads * ROWS, HEAD_DIM), bf16),
            pltpu.VMEM((rows // ROWS, HEAD_DIM, heads * ROWS), bf16),
            pltpu.VMEM((2 * rows, HEAD_DIM), bf16),
            pltpu.VMEM((2 * rows, HEAD_DIM), bf16),
            pltpu.VMEM((heads * ROWS, rows), f32),
            pltpu.VMEM((heads * ROWS, ROWS), f32),
            pltpu.VMEM((heads * ROWS, rows), bf16),
            pltpu.VMEM((heads * ROWS, ROWS), bf16),
            pltpu.VMEM((rows, units), bf16),
            pltpu.VMEM((rows, units), bf16),
            pltpu.VMEM((kv, 2 * rows), bf16),
            pltpu.VMEM((2, kv, rows), bf16),
            pltpu.VMEM((2, kv, rows), bf16),
            pltpu.VMEM((kv, rows), bf16),
            pltpu.VMEM((rows // ROWS, heads * ROWS, rows), bf16),
            pltpu.VMEM((rows // ROWS, heads * ROWS, ROWS), bf16),
            pltpu.VMEM((kv, 2 * rows), f32),
            pltpu.VMEM((4 * kv, 2 * rows), bf16),
            pltpu.VMEM((rows, 4 * kv), bf16),
            pltpu.VMEM((rows, 4 * kv), bf16),
            pltpu.VMEM((4, 8, rows), f32),
            pltpu.VMEM((4, 8, rows), f32),
            pltpu.VMEM((8, rows), f32),
            pltpu.VMEM((8, rows), f32),
            pltpu.VMEM((8, 8, width), f32),
            pltpu.VMEM((8, width), f32),
            pltpu.VMEM((n_hi, 8, 2 * width // n_dp), f32),
            pltpu.VMEM((8, 2 * width // n_dp), f32),
            pltpu.VMEM((5, 8, width // n_dp), f32),
            pltpu.VMEM((2, rows, width), bf16),
            pltpu.VMEM((2, 2, rows, width), bf16),
            pltpu.VMEM((2, rows, width), bf16),
            pltpu.VMEM((4, rows, feat), bf16),
            pltpu.VMEM((4, rows, feat), bf16),
            pltpu.VMEM((units, rows), bf16),
            pltpu.VMEM((units, rows), bf16),
            pltpu.VMEM((3, units, feat), bf16),
            pltpu.VMEM((3, units, feat), bf16),
            pltpu.VMEM((3, units, feat), bf16),
            pltpu.VMEM((3, units, feat), bf16),
            pltpu.VMEM((4 * kv, feat), bf16),
            pltpu.VMEM((4 * kv, feat), bf16),
            pltpu.VMEM((2, 4 * kv, feat), bf16),
            pltpu.VMEM((4, kv, feat), bf16),
            pltpu.VMEM((kv, feat), bf16),
            pltpu.VMEM((units, feat), f32),
            pltpu.SemaphoreType.DMA((160,)),
            pltpu.SemaphoreType.DMA((160,)),
            pltpu.SemaphoreType.DMA((16,)),
        ],
        compiler_params=pltpu.CompilerParams(
            collective_id=0, has_side_effects=True, vmem_limit_bytes=64 << 20
        ),
        name="block",
    )(
        context,
        latents,
        cotangent,
        gain_ctx.reshape(1, model_width),
        gain_lat.reshape(1, model_width),
        w_query,
        key_matrix.T,
        value_matrix.T,
        w_out,
        lengths,
        patch_flags.reshape(1, rows),
    )
    out = pl.pallas_call(
        hand_on,
        out_shape=tuple(shaped(a.shape, a.dtype) for a in out),
        in_specs=[any_space] * 9,
        out_specs=(any_space,) * 9,
        scratch_shapes=[pltpu.VMEM(a.shape, a.dtype) for a in out]
        + [pltpu.SemaphoreType.DMA((9,)), pltpu.SemaphoreType.DMA((9,))],
        compiler_params=pltpu.CompilerParams(vmem_limit_bytes=64 << 20),
        name="hand_on",
    )(*out)
    latents_out, grad_context, grad_latents, g_query, g_key, g_value, g_out, gain_c, gain_l = out
    return (
        latents_out,
        grad_context,
        grad_latents,
        g_query,
        g_key.T,
        g_value.T,
        g_out,
        gain_c,
        gain_l,
    )


def solution(mesh):
    n_dp = mesh.shape["dp"]
    body = functools.partial(kernel_local, n_dp) if n_dp == 8 else plain_local
    return jax.shard_map(
        body,
        mesh=mesh,
        in_specs=(
            P("dp", "tensor"),
            P("dp", "tensor"),
            P(),
            P(),
            P(None, "tensor"),
            P(None, "tensor"),
            P(None, "tensor"),
            P(None, "tensor"),
            P("dp", None),
            P("dp"),
            P("dp", "tensor"),
        ),
        out_specs=(
            P("dp", "tensor"),
            P("dp", "tensor"),
            P("dp", "tensor"),
            P("dp", "tensor"),
            P("dp", "tensor"),
            P("dp", "tensor"),
            P("dp", "tensor"),
            P("tensor", "dp"),
            P("tensor", "dp"),
        ),
        check_vma=False,
    )
```

```python
import functools

import jax
import jax.numpy as jnp
from jax import lax
from jax.experimental import pallas as pl
from jax.experimental.pallas import tpu as pltpu
from jax.sharding import PartitionSpec as P

HEAD_DIM = 96
LAT = 64


epsilon = 1e-06
masked_value = -1e30
contract_rows = (((0,), (0,)), ((), ()))
contract_cols = (((1,), (1,)), ((), ()))


def row_scales(rows_in):
    values_f = rows_in.astype(jnp.float32)
    return (values_f, lax.rsqrt(jnp.mean(values_f * values_f, axis=1) + epsilon))


def norm_back(grad_norm, local_vals, row_scale, gain_local, row_inner_all, model_width):
    weighted = grad_norm * gain_local
    grad_input = (
        row_scale[:, None] * weighted
        - local_vals * (row_scale**3 * row_inner_all / model_width)[:, None]
    )
    grad_gain = jnp.sum(grad_norm * local_vals * row_scale[:, None], axis=0)
    return (grad_input, grad_gain)


def plain_local(
    context,
    latents,
    gain_ctx,
    gain_lat,
    w_query,
    key_matrix,
    value_matrix,
    w_out,
    lengths,
    patch_flags,
    cotangent,
):
    patch_rows = context.shape[0]
    latent_rows = latents.shape[0]
    local_width = context.shape[1]
    model_width = gain_ctx.shape[0]
    head_size = HEAD_DIM
    kv_local = key_matrix.shape[1] // head_size
    query_local = w_query.shape[1] // head_size
    repeat = query_local // kv_local
    all_count = patch_rows + latent_rows
    score_scale = head_size ** (-0.5)
    column = lax.axis_index("tensor") * local_width
    whole_ctx, whole_lat = (
        lax.all_gather(context, "tensor", axis=1, tiled=True),
        lax.all_gather(latents, "tensor", axis=1, tiled=True),
    )
    ctx_values, ctx_scale = row_scales(whole_ctx)
    lat_values, lat_scale = row_scales(whole_lat)
    ctx_norm = (ctx_values * ctx_scale[:, None] * gain_ctx).astype(jnp.bfloat16)
    lat_norm = (lat_values * lat_scale[:, None] * gain_lat).astype(jnp.bfloat16)
    queries = jnp.dot(lat_norm, w_query, preferred_element_type=jnp.float32).astype(jnp.bfloat16)
    all_rows = jnp.concatenate([ctx_norm, lat_norm], axis=0)
    w_pair = jnp.concatenate([key_matrix, value_matrix], axis=1)
    pair_rows = jnp.dot(all_rows, w_pair, preferred_element_type=jnp.float32).astype(jnp.bfloat16)
    key_head_split = (
        pair_rows[:, : kv_local * head_size]
        .reshape(all_count, kv_local, head_size)
        .transpose(1, 0, 2)
    )
    value_head_split = (
        pair_rows[:, kv_local * head_size :]
        .reshape(all_count, kv_local, head_size)
        .transpose(1, 0, 2)
    )
    query_heads = queries.reshape(latent_rows, query_local, head_size).transpose(1, 0, 2)
    image_ends = jnp.cumsum(lengths[0])
    patch_image = jnp.sum(
        (jnp.arange(patch_rows)[:, None] >= image_ends[None, :]).astype(jnp.int32), axis=1
    )
    latent_image = jnp.arange(latent_rows) // LAT
    allowed = jnp.concatenate(
        [
            (latent_image[:, None] == patch_image[None, :]) & (patch_flags[None, :] == 1),
            latent_image[:, None] == latent_image[None, :],
        ],
        axis=1,
    )
    head_index = jnp.arange(query_local)

    def head_scores(query_head, head_number):
        key_head = key_head_split[head_number // repeat]
        value_head = value_head_split[head_number // repeat]
        raw_scores = (
            lax.dot_general(query_head, key_head, contract_cols, preferred_element_type=jnp.float32)
            * score_scale
        )
        return (jnp.where(allowed, raw_scores, masked_value), key_head, value_head)

    def head_forward(member):
        query_head, head_number = member
        scores, key_head, value_head = head_scores(query_head, head_number)
        row_top = jnp.max(scores, axis=1, keepdims=True)
        exp_scores = jnp.exp(scores - row_top)
        row_total = jnp.sum(exp_scores, axis=1, keepdims=True)
        attention = (exp_scores / row_total).astype(jnp.bfloat16)
        blended = jnp.dot(attention, value_head, preferred_element_type=jnp.float32).astype(
            jnp.bfloat16
        )
        return (blended, row_top[:, 0] + jnp.log(row_total[:, 0]))

    heads_out, log_totals = lax.map(head_forward, (query_heads, head_index))
    attended = heads_out.transpose(1, 0, 2).reshape(latent_rows, query_local * head_size)
    partial_out = lax.dot_general(
        attended, w_out, contract_cols, preferred_element_type=jnp.float32
    )
    branch = lax.psum_scatter(
        partial_out.astype(jnp.bfloat16), "tensor", scatter_dimension=1, tiled=True
    ).astype(jnp.float32)
    latents_out = (latents.astype(jnp.float32) + branch).astype(jnp.bfloat16)
    full_grad = lax.all_gather(cotangent, "tensor", axis=1, tiled=True)
    grad_attended = jnp.dot(full_grad, w_out, preferred_element_type=jnp.float32).astype(
        jnp.bfloat16
    )
    grad_w_out = lax.dot_general(
        full_grad, attended, contract_rows, preferred_element_type=jnp.float32
    )
    grad_heads = grad_attended.reshape(latent_rows, query_local, head_size).transpose(1, 0, 2)

    def head_backward(member):
        query_head, grad_blended, log_total, head_number = member
        scores, key_head, value_head = head_scores(query_head, head_number)
        attention = jnp.exp(scores - log_total[:, None])
        grad_probs = lax.dot_general(
            grad_blended, value_head, contract_cols, preferred_element_type=jnp.float32
        )
        row_inner = jnp.sum(attention * grad_probs, axis=1, keepdims=True)
        grad_scores = (attention * (grad_probs - row_inner)).astype(jnp.bfloat16)
        grad_query = (
            jnp.dot(grad_scores, key_head, preferred_element_type=jnp.float32) * score_scale
        ).astype(jnp.bfloat16)
        grad_key = (
            lax.dot_general(
                grad_scores, query_head, contract_rows, preferred_element_type=jnp.float32
            )
            * score_scale
        )
        grad_value = lax.dot_general(
            attention.astype(jnp.bfloat16),
            grad_blended,
            contract_rows,
            preferred_element_type=jnp.float32,
        )
        return (grad_query, grad_key, grad_value)

    grad_query_heads, grad_key_heads, grad_value_heads = lax.map(
        head_backward, (query_heads, grad_heads, log_totals, head_index)
    )
    grad_keys = grad_key_heads.reshape(kv_local, repeat, all_count, head_size).sum(axis=1)
    grad_values = grad_value_heads.reshape(kv_local, repeat, all_count, head_size).sum(axis=1)
    grad_pair = jnp.concatenate(
        [
            grad_keys.transpose(1, 0, 2).reshape(all_count, kv_local * head_size),
            grad_values.transpose(1, 0, 2).reshape(all_count, kv_local * head_size),
        ],
        axis=1,
    ).astype(jnp.bfloat16)
    grad_q_rows = grad_query_heads.transpose(1, 0, 2).reshape(latent_rows, query_local * head_size)
    grad_w_query = lax.dot_general(
        lat_norm, grad_q_rows, contract_rows, preferred_element_type=jnp.float32
    )
    grad_w_pair = lax.dot_general(
        all_rows, grad_pair, contract_rows, preferred_element_type=jnp.float32
    )
    grad_rows = lax.dot_general(
        grad_pair, w_pair, contract_cols, preferred_element_type=jnp.float32
    )
    lat_terms = grad_rows[patch_rows:] + lax.dot_general(
        grad_q_rows, w_query, contract_cols, preferred_element_type=jnp.float32
    )
    grad_ctx_norm, grad_lat_norm = (
        lax.psum_scatter(
            grad_rows[:patch_rows].astype(jnp.bfloat16), "tensor", scatter_dimension=1, tiled=True
        ).astype(jnp.float32),
        lax.psum_scatter(
            lat_terms.astype(jnp.bfloat16), "tensor", scatter_dimension=1, tiled=True
        ).astype(jnp.float32),
    )
    ctx_local = context.astype(jnp.float32)
    lat_local = latents.astype(jnp.float32)
    gain_ctx_local = lax.dynamic_slice_in_dim(gain_ctx, column, local_width, 0)
    gain_lat_local = lax.dynamic_slice_in_dim(gain_lat, column, local_width, 0)
    ctx_inner = jnp.sum(grad_ctx_norm * gain_ctx_local * ctx_local, axis=1)
    lat_inner = jnp.sum(grad_lat_norm * gain_lat_local * lat_local, axis=1)
    ctx_inner_all, lat_inner_all = lax.psum((ctx_inner, lat_inner), "tensor")
    grad_ctx_in, grad_gain_c = norm_back(
        grad_ctx_norm, ctx_local, ctx_scale, gain_ctx_local, ctx_inner_all, model_width
    )
    grad_lat_in, grad_gain_l = norm_back(
        grad_lat_norm, lat_local, lat_scale, gain_lat_local, lat_inner_all, model_width
    )
    grad_context = grad_ctx_in.astype(jnp.bfloat16)
    grad_latents = (cotangent.astype(jnp.float32) + grad_lat_in).astype(jnp.bfloat16)
    grad_w_key = grad_w_pair[:, : kv_local * head_size]
    grad_w_value = grad_w_pair[:, kv_local * head_size :]
    sum_query, sum_key, sum_value, sum_out, sum_gain_c, sum_gain_l = (
        lax.psum_scatter(grad_w_query, "dp", scatter_dimension=0, tiled=True),
        lax.psum_scatter(grad_w_key, "dp", scatter_dimension=0, tiled=True),
        lax.psum_scatter(grad_w_value, "dp", scatter_dimension=0, tiled=True),
        lax.psum_scatter(grad_w_out, "dp", scatter_dimension=0, tiled=True),
        lax.psum_scatter(grad_gain_c, "dp", scatter_dimension=0, tiled=True),
        lax.psum_scatter(grad_gain_l, "dp", scatter_dimension=0, tiled=True),
    )
    return (
        latents_out,
        grad_context,
        grad_latents,
        sum_query,
        sum_key,
        sum_value,
        sum_out,
        sum_gain_c.reshape(1, -1),
        sum_gain_l.reshape(1, -1),
    )


MESH = pl.DeviceIdType.MESH
f32 = jnp.float32
bf16 = jnp.bfloat16
ROWS = 128
LOG2_E = 1.4426950408889634


def nn(a, b):
    return jnp.dot(a, b, preferred_element_type=f32)


def nt(a, b):
    return lax.dot_general(a, b, contract_cols, preferred_element_type=f32)


def flip(a):
    return a.astype(f32).T.astype(bf16)


def block_kernel(
    n_dp,
    context,
    latents,
    cotangent,
    gain_ctx_in,
    gain_lat_in,
    w_query,
    key_across,
    value_across,
    w_out,
    lengths_in,
    flags_in,
    out_latents,
    out_context,
    out_grad_lat,
    out_query,
    out_key,
    out_value,
    out_out,
    out_gain_c,
    out_gain_l,
    gain_ctx,
    gain_lat,
    lengths,
    flags,
    gain_out,
    lat_all,
    cot_all,
    ctx_own,
    raw_lat,
    raw_ctx,
    wq,
    wkv,
    w_own,
    wo,
    acc_q,
    kv_acc,
    att_t,
    sgq_t,
    q_rows,
    q_cols,
    ga_rows,
    ga_cols,
    k_rows,
    v_rows,
    far_s,
    near_s,
    far_g,
    near_g,
    att,
    sgq,
    kv_t,
    kv_send,
    kv_core,
    kv_y,
    probs_c,
    probs_l,
    gkv,
    sgkv_all,
    sgc,
    sgl,
    sums,
    inners,
    scale_row,
    coef_row,
    gain_part,
    gain_sum,
    gain_recv,
    gain_pair,
    gain_one,
    core_send,
    core_recv,
    y_recv,
    lat_x,
    cot_x,
    att_xt,
    sgq_xt,
    z_send_o,
    z_send_q,
    z_recv_o,
    z_recv_q,
    x_send_kv,
    x_recv_kv,
    z_recv_kv,
    own_send,
    own_recv,
    dp_acc,
    send_sem,
    recv_sem,
    local_sem,
):
    rows, width = raw_lat.shape
    n_rows = rows // ROWS
    n_hi = n_dp // 2
    feat = 4 * width // n_dp
    head = HEAD_DIM
    heads = acc_q.shape[1] // head
    model_width = 4 * width
    score_scale = head ** (-0.5)

    dp = lax.axis_index("dp")
    f = lax.axis_index("tensor")
    z, x = dp // 2, lax.rem(dp, 2)
    y, c = f // 2, lax.rem(f, 2)
    f_c = y * 2 + (1 - c)
    f_y = (1 - y) * 2 + c
    f_yc = (1 - y) * 2 + (1 - c)
    core_dev, y_dev, yc_dev = (dp, f_c), (dp, f_y), (dp, f_yc)
    x_dev = (z * 2 + 1 - x, f)
    z_1 = z + 1 - 2 * lax.rem(z, 2)
    z_2 = z + 2 - 4 * (z // 2)
    z1_dev, z2_dev = (z_1 * 2 + x, f), (z_2 * 2 + x, f)
    x_mine = pl.ds(pl.multiple_of(x * feat, 128), feat)
    x_other = pl.ds(pl.multiple_of((1 - x) * feat, 128), feat)

    urgent = lax.rem(c + z, 2) == 1
    patient = jnp.logical_not(urgent)

    count = [0]

    def take(n):
        count[0] += n
        return count[0] - n

    def remote(src, dst, sem, dev, sem_to=None):
        return pltpu.make_async_remote_copy(
            src_ref=src,
            dst_ref=dst,
            send_sem=send_sem.at[sem],
            recv_sem=recv_sem.at[sem if sem_to is None else sem_to],
            device_id=dev,
            device_id_type=MESH,
        )

    def local_copy(src, dst, i):
        return pltpu.make_async_copy(src, dst, local_sem.at[i])

    def part_rows(k):
        if isinstance(k, int):
            return pl.ds(k * ROWS, ROWS)
        return pl.ds(pl.multiple_of(k * ROWS, ROWS), ROWS)

    n_cols = 4
    piece = width // n_cols

    def part_cols(k):
        if isinstance(k, int):
            return pl.ds(k * piece, piece)
        return pl.ds(pl.multiple_of(k * piece, 128), piece)

    def cols_at(fb, k):
        return pl.ds(pl.multiple_of(fb * width + k * piece, 128), piece)

    def block_cols(fb):
        if isinstance(fb, int):
            return pl.ds(fb * width, width)
        return pl.ds(pl.multiple_of(fb * width, width), width)

    loads = [
        local_copy(latents, raw_lat, 0),
        local_copy(key_across, wkv.at[pl.ds(0, head)], 4),
        local_copy(value_across, wkv.at[pl.ds(head, head)], 14),
        local_copy(context, raw_ctx, 1),
        local_copy(cotangent, cot_all.at[f], 13),
        local_copy(w_query, wq, 3),
        local_copy(w_out, wo, 5),
    ]
    small = [
        local_copy(gain_lat_in, gain_lat, 2),
        local_copy(gain_ctx_in, gain_ctx, 6),
        local_copy(lengths_in, lengths, 7),
        local_copy(flags_in, flags, 8),
    ]
    for load in small[:1] + loads + small[1:]:
        load.start()

    barrier = pltpu.get_barrier_semaphore()

    def greet(dev):
        pl.semaphore_signal(barrier, inc=1, device_id=dev, device_id_type=MESH)

    others = [i for i in range(1, n_hi)]

    def far_dev(i):
        return (lax.rem(z + i, n_hi) * 2 + x, f)

    always = [core_dev, y_dev, yc_dev, x_dev] + [far_dev(i) for i in others]
    for dev in always:
        greet(dev)
    pl.when(z != f)(lambda: greet((z_2 * 2 + x, z)))

    def weigh(raw, gain, buf):
        gain_row = gain[:, block_cols(f)]
        for k in range(n_rows):
            values = raw[part_rows(k), :].astype(f32)
            buf[part_rows(k), :] = (values * gain_row).astype(bf16)

    small[0].wait()
    loads[0].wait()
    weigh(raw_lat, gain_lat, lat_all.at[f])
    middle = z_2 == f
    pl.semaphore_wait(barrier, len(always) + 3 * middle.astype(jnp.int32))

    sem_lat, sem_cot = (take(2 * n_rows + 1) for _ in range(2))

    def gather_y(buf, base, k):
        return remote(buf.at[f, part_rows(k)], buf.at[f, part_rows(k)], base + k, y_dev)

    def gather_core(buf, base):
        return remote(buf.at[f], buf.at[f], base + n_rows, core_dev)

    def gather_on(buf, base, k):
        return remote(
            buf.at[f_y, part_rows(k)], buf.at[f_y, part_rows(k)], base + n_rows + 1 + k, core_dev
        )

    def pass_on(buf, base, held=None, base_x=None):
        def step(k, carry):
            gather_y(buf, base, k).wait_recv()
            gather_on(buf, base, k).start()
            if held is not None:
                rows_x(buf, held, base_x, k).start()
            return carry

        lax.fori_loop(0, n_rows, step, 0)

    def wait_on(buf, base):
        for k in range(n_rows):
            gather_on(buf, base, k).wait_recv()

    def gather_done(buf, base):
        for k in range(n_rows):
            gather_y(buf, base, k).wait_send()
            gather_on(buf, base, k).wait_send()
        gather_core(buf, base).wait_send()

    def square_sums(raw, index):
        for k in range(n_rows):
            values = raw[part_rows(k), :].astype(f32)
            total = jnp.sum(values * values, axis=1, keepdims=True)
            across = jnp.broadcast_to(total, (ROWS, 128)).T
            sums[f, pl.ds(index, 1), part_rows(k)] = across[0:1, :]

    sem_lat_x, sem_cot_x = take(2 * n_rows + 2), take(2 * n_rows + 2)
    sem_att_x, sem_sgq_x = take(n_rows), take(n_rows)

    def across_x(buf, held, base):
        return remote(buf.at[f, :, x_other], held.at[f], base, x_dev)

    def across_core(held, base):
        return remote(held.at[f], held.at[f], base + 1, core_dev)

    def rows_x(buf, held, base, k):
        return remote(
            buf.at[f_y, part_rows(k), x_other], held.at[f_y, part_rows(k)], base + 2 + k, x_dev
        )

    def rows_core(held, base, k):
        piece = held.at[f_y, part_rows(k)]
        return remote(piece, piece, base + 2 + n_rows + k, core_dev)

    def hold_own(buf, held, base):
        across_x(buf, held, base).wait_recv()
        across_core(held, base).start()

    def hold_rows(buf, held, base):
        def step(k, carry):
            rows_x(buf, held, base, k).wait_recv()
            rows_core(held, base, k).start()
            return carry

        lax.fori_loop(0, n_rows, step, 0)

    def rows_core_done(held, base):
        for k in range(n_rows):
            rows_core(held, base, k).wait_recv()

    kv = 2 * head
    slice_width = width // n_dp
    pair_rows = pl.ds(pl.multiple_of((1 - y) * 2 * kv, 64), 2 * kv)
    sem_w_core, sem_w_y, sem_w_z, sem_w_x = take(1), take(2), take(n_hi), take(n_hi)

    def head_rows_of(t):
        return pl.ds(pl.multiple_of(t * kv, 64), kv)

    def slice_cols(d, at=0):
        return pl.ds(pl.multiple_of(at + d * slice_width, 128), slice_width)

    def w_y(dev, f_to, i, sender=c):
        return remote(
            wkv.at[:, slice_cols(dp, f_to * width)],
            w_own.at[head_rows_of(f), slice_cols(dp)],
            sem_w_y + i,
            dev,
            sem_w_y + sender,
        )

    def w_core():
        return remote(
            wkv.at[:, block_cols(f_c)], w_own.at[head_rows_of(f)], sem_w_core, core_dev
        )

    def w_z(i):
        piece = w_own.at[pair_rows, slice_cols(dp)]
        return remote(piece, piece, sem_w_z + i, far_dev(i))

    def w_x(i):
        piece = w_own.at[pair_rows, slice_cols(lax.rem(z + i, n_hi) * 2 + x)]
        return remote(piece, piece, sem_w_x + lax.rem(z + i, n_hi), x_dev)

    loads[1].wait()
    loads[2].wait()
    w_y(y_dev, f_y, 0).start()
    w_y(yc_dev, f_yc, 1).start()
    w_core().start()
    for k in range(n_rows):
        gather_y(lat_all, sem_lat, k).start()
    gather_core(lat_all, sem_lat).start()
    across_x(lat_all, lat_x, sem_lat_x).start()
    sums[f] = jnp.zeros(sums.shape[1:], f32)
    inners[f] = jnp.zeros(inners.shape[1:], f32)
    loads[3].wait()
    for load in small[1:]:
        load.wait()
    weigh(raw_ctx, gain_ctx, ctx_own)
    loads[4].wait()
    gather_core(cot_all, sem_cot).start()
    for i in range(2):
        w_y(y_dev, f_y, i, i).wait_recv()
    for i in others:
        w_z(i).start()
    w_x(0).start()
    w_own[head_rows_of(f), :] = wkv[:, block_cols(f)]
    square_sums(raw_lat, 1)
    square_sums(raw_ctx, 0)

    peers = [core_dev, y_dev, yc_dev]
    sem_sums, sem_inner = take(3), take(3)

    def exchange(buf, base):
        return [remote(buf.at[f], buf.at[f], base + i, dev) for i, dev in enumerate(peers)]

    sums_out = exchange(sums, sem_sums)
    for copy in sums_out:
        copy.start()

    def project(acc, values, weight, blocks, first):
        def step(i, carry):
            fb = blocks[0] + i * (blocks[1] - blocks[0])
            for m in range(2):
                half = pl.ds(m * (rows // 2), rows // 2)
                product = nn(values[fb, half, :], weight[block_cols(fb), :])
                if first:
                    @pl.when(i == 0)
                    def _():
                        acc[half, :] = product

                    @pl.when(i > 0)
                    def _():
                        acc[half, :] += product
                else:
                    acc[half, :] += product
            return carry

        lax.fori_loop(0, 2, step, 0)

    def project_pair(blocks, first):
        latent_cols = pl.ds(rows, rows)
        for i, fb in enumerate(blocks):
            product = nt(wkv[:, block_cols(fb)], lat_all[fb])
            if first and i == 0:
                kv_acc[0:kv, latent_cols] = product
            else:
                kv_acc[0:kv, latent_cols] += product

    mine, theirs = (f, f_c), (f_y, f_yc)
    loads[5].wait()
    loads[6].wait()
    gather_core(lat_all, sem_lat).wait_recv()
    project(acc_q, lat_all, wq, mine, True)
    project_pair(mine, True)
    for i in others:
        w_z(n_hi - i).wait_recv()
        w_x(i).start()
    w_core().wait_recv()
    across_x(cot_all, cot_x, sem_cot_x).start()
    for i in range(n_hi):
        w_x(i).wait_recv()

    sem_kv_core, sem_kv_y = take(2), take(1)

    def kv_core_copy(j):
        return remote(kv_send.at[j], kv_core.at[j], sem_kv_core + j, core_dev)

    def kv_y_copy():
        return remote(kv_core.at[0], kv_y, sem_kv_y, y_dev)

    patches = pl.ds(0, rows)
    for n in range(2):
        half = slice(n * (rows // 2), (n + 1) * (rows // 2))
        kv_acc[:, half] = nt(w_own[...], ctx_own[half, :])
    for j, t in enumerate((f_yc, f_c)):
        kv_send[j] = kv_acc[head_rows_of(t), patches].astype(bf16)
        kv_core_copy(j).start()
    kv_core_copy(0).wait_recv()
    kv_core[0] = (kv_acc[head_rows_of(f_y), patches] + kv_core[0].astype(f32)).astype(bf16)
    kv_y_copy().start()

    def cot_across_y():
        for k in range(n_rows):
            gather_y(cot_all, sem_cot, k).start()

    pl.when(urgent)(cot_across_y)

    pass_on(lat_all, sem_lat)
    wait_on(lat_all, sem_lat)
    project(acc_q, lat_all, wq, theirs, False)
    project_pair(theirs, False)

    for copy in sums_out:
        copy.wait()
    total = sums[0] + sums[1] + sums[2] + sums[3]
    scale_row[...] = lax.rsqrt(total / model_width + epsilon)

    def split_heads(acc, by_rows, by_cols, row_scale, factor):
        for k in range(n_rows):
            across = acc[part_rows(k), :].T
            if row_scale is not None:
                across = across * row_scale[:, part_rows(k)]
            for h in range(heads):
                one = across[h * head : (h + 1) * head, :]
                at = pl.ds(h * ROWS, ROWS)
                by_cols[k, :, at] = one.astype(bf16)
                by_rows[k, at, :] = (one * factor).T.astype(bf16)

    def kv_by_rows(first):
        for n in range(first, first + n_rows):
            k_rows[part_rows(n), :] = flip(kv_t[0:head, part_rows(n)])
            v_rows[part_rows(n), :] = flip(kv_t[head:, part_rows(n)])

    split_heads(acc_q, q_rows, q_cols, scale_row[1:2, :], score_scale * LOG2_E)
    kv_t[:, rows:] = (kv_acc[0:kv, rows:] * scale_row[1:2, :]).astype(bf16)
    kv_by_rows(n_rows)
    kv_core_copy(1).wait_recv()
    kv_y_copy().wait_recv()
    summed = kv_acc[head_rows_of(f), patches] + kv_core[1].astype(f32) + kv_y[...].astype(f32)
    kv_t[:, 0:rows] = (summed * scale_row[0:1, :]).astype(bf16)
    kv_by_rows(0)

    patch = lax.broadcasted_iota(jnp.int32, (1, rows), 1)
    image = jnp.zeros((1, rows), jnp.int32)
    end = jnp.int32(0)
    for i in range(lengths.shape[1]):
        end = end + lengths[0, i]
        image = image + (patch >= end).astype(jnp.int32)
    image = jnp.where(flags[...] == 1, image, -1)
    per_part = ROWS // LAT
    row_image = lax.broadcasted_iota(jnp.int32, (ROWS, 1), 0) // LAT
    col_image = lax.broadcasted_iota(jnp.int32, (1, ROWS), 1) // LAT
    same = row_image == col_image
    keys, vals = pl.ds(0, head), pl.ds(head, head)
    def own_latents(p):
        return pl.ds(pl.multiple_of(rows + p * ROWS, ROWS), ROWS)


    def head_part(h):
        return slice(h * ROWS, (h + 1) * ROWS)

    def att_x_copy(p):
        cols = part_rows(p)
        return remote(att_t.at[:, cols], att_xt.at[:, cols], sem_att_x + p, x_dev)

    def sgq_x_copy(p):
        cols = part_rows(p)
        return remote(sgq_t.at[:, cols], sgq_xt.at[:, cols], sem_sgq_x + p, x_dev)

    def forward_step(p, carry):
        far_s[...] = nn(q_rows[p], kv_t[keys, patches])
        near_s[...] = nn(q_rows[p], kv_t[keys, own_latents(p)])
        allowed = (row_image + p * per_part) == image
        for h in range(heads):
            far = jnp.where(allowed, far_s[head_part(h), :], masked_value)
            near = jnp.where(same, near_s[head_part(h), :], masked_value)
            top = jnp.maximum(
                jnp.max(far, axis=1, keepdims=True), jnp.max(near, axis=1, keepdims=True)
            )
            far, near = jnp.exp2(far - top), jnp.exp2(near - top)
            total = jnp.sum(far, axis=1, keepdims=True) + jnp.sum(near, axis=1, keepdims=True)
            inverse = 1.0 / total
            probs_c[p, head_part(h), :] = (far * inverse).astype(bf16)
            probs_l[p, head_part(h), :] = (near * inverse).astype(bf16)
        blended = nn(probs_c[p], v_rows[patches, :]) + nn(probs_l[p], v_rows[own_latents(p), :])
        for h in range(heads):
            one = blended[head_part(h), :]
            att_t[h * head : (h + 1) * head, part_rows(p)] = one.T.astype(bf16)
        att_x_copy(p).start()
        return carry

    lax.fori_loop(0, n_rows, forward_step, 0)
    def chunk_out(zt):
        return nn(att_t[...], cot_all[zt, :, x_mine]) + nn(att_xt[...], cot_x[zt])

    def chunk_query(zt):
        return nn(sgq_t[...], lat_all[zt, :, x_mine]) + nn(sgq_xt[...], lat_x[zt])

    def chunk_pair(xt):
        cols = pl.ds(pl.multiple_of(xt * feat, 128), feat)
        return nn(sgkv_all[:, patches], ctx_own[:, cols]) + nn(
            sgkv_all[:, pl.ds(rows, rows)], lat_all[f, :, cols]
        )

    class Spread:
        def __init__(self, chunk, send, recv):
            self.chunk, self.send, self.recv, self.sem = chunk, send, recv, take(3)

        def copy(self, j, dev):
            return remote(self.send.at[j], self.recv.at[j], self.sem + j, dev)

        def first(self, j):
            zt = z_1 + j * (z_2 - z)
            self.send[j] = self.chunk(zt).astype(bf16)
            self.copy(j, z1_dev).start()

        def second(self):
            value = self.chunk(z_2)
            self.copy(1, z1_dev).wait_recv()
            self.send[2] = (value + self.recv[1].astype(f32)).astype(bf16)
            self.copy(2, z2_dev).start()

        def final(self):
            dp_acc[...] = self.chunk(z)
            self.copy(0, z1_dev).wait_recv()
            self.copy(2, z2_dev).wait_recv()
            dp_acc[...] += self.recv[0].astype(f32) + self.recv[2].astype(f32)

        def wait_sends(self):
            for j in range(3):
                self.copy(j, z1_dev).wait_send()

    grad_o = Spread(chunk_out, z_send_o, z_recv_o)
    grad_q = Spread(chunk_query, z_send_q, z_recv_q)

    sem_kv_x, sem_kv_z1, sem_kv_z2, sem_kv_own = take(4), take(4), take(4), take(6)
    pair_acc = kv_acc.at[:, pl.ds(0, feat)]
    passes = lax.rem(z + f, 2) == 1

    def head_rows_at(t):
        return pl.ds(t * kv, kv)

    def pair_x_copy(t):
        at = head_rows_at(t)
        return remote(x_send_kv.at[at], x_recv_kv.at[at], sem_kv_x + t, x_dev)

    def pair_z_copy(t):
        at = head_rows_at(t)
        return remote(x_recv_kv.at[at], z_recv_kv.at[at], sem_kv_z1 + t, z1_dev)

    def pair_far_copy(t):
        at = head_rows_at(t)
        dev = (z_2 * 2 + x, t)
        return remote(x_recv_kv.at[at], own_recv.at[1], sem_kv_z2 + t, dev, sem_kv_own + 5)

    def pair_own_copy(t):
        return remote(
            own_send.at[t], own_recv.at[0], sem_kv_own + t, (dp, t), sem_kv_own + 4
        )

    def pair_first():
        x_send_kv[...] = chunk_pair(1 - x).astype(bf16)
        for t in range(4):
            pair_x_copy(t).start()
        pair_acc[...] = chunk_pair(x)

    def pair_step(t, i):
        at = head_rows_at(t)
        if i == 0:
            pair_x_copy(t).wait_recv()
            pair_acc[at, :] += x_recv_kv[at, :].astype(f32)

            @pl.when(passes)
            def _():
                x_recv_kv[at, :] = pair_acc[at, :].astype(bf16)
                pair_z_copy(t).start()

            return

        @pl.when(jnp.logical_not(passes))
        def _():
            pair_z_copy(t).wait_recv()
            pair_acc[at, :] += z_recv_kv[at, :].astype(f32)

        @pl.when(middle)
        def _():
            x_recv_kv[at, :] = pair_acc[at, :].astype(bf16)
            pair_far_copy(t).start()

        @pl.when((z == f) & (f != t))
        def _():
            own_send[t] = pair_acc[at, :].astype(bf16)
            pair_own_copy(t).start()

    def pair_result():
        pair_far_copy(0).wait_recv()
        far = own_recv[1].astype(f32)
        at = pl.ds(feat, feat)

        @pl.when(z == f)
        def _():
            kv_acc[0:kv, at] = kv_acc[head_rows_of(f), pl.ds(0, feat)] + far

        @pl.when(z != f)
        def _():
            pair_own_copy(0).wait_recv()
            kv_acc[0:kv, at] = own_recv[0].astype(f32) + far

    def pair_sends_done():
        for t in range(4):
            pair_x_copy(t).wait_send()
            pl.when(passes)(lambda t=t: pair_z_copy(t).wait_send())
            pl.when(middle)(lambda t=t: pair_far_copy(t).wait_send())

        @pl.when(z == f)
        def _():
            for t in range(4):
                pl.when(f != t)(lambda t=t: pair_own_copy(t).wait_send())

    class Collect:
        def __init__(self, part, index, seen=None):
            self.part, self.index, self.sem = part, index, take(3 * n_cols)
            self.seen = seen

        def core_copy(self, j, k):
            return remote(
                core_send.at[j, :, part_cols(k)],
                core_recv.at[self.index, j, :, part_cols(k)],
                self.sem + j * n_cols + k,
                core_dev,
            )

        def y_copy(self, k):
            return remote(
                core_recv.at[self.index, 0, :, part_cols(k)],
                y_recv.at[self.index, :, part_cols(k)],
                self.sem + 2 * n_cols + k,
                y_dev,
            )

        def product(self, fb, k):
            value = self.part(fb, k)
            if self.seen is not None:
                self.seen(fb, k, value)
            return value

        def send_core(self):
            def core_step(n, carry):
                j, k = n // n_cols, lax.rem(n, n_cols)
                fb = jnp.where(j == 0, f_yc, f_c)
                core_send[j, :, part_cols(k)] = self.product(fb, k).astype(bf16)
                self.core_copy(j, k).start()
                return carry

            lax.fori_loop(0, 2 * n_cols, core_step, 0)

        def send_y(self, first, last):
            def y_step(k, carry):
                value = self.product(f_y, k)
                self.core_copy(0, k).wait_recv()
                value = value + core_recv[self.index, 0, :, part_cols(k)].astype(f32)
                core_recv[self.index, 0, :, part_cols(k)] = value.astype(bf16)
                self.y_copy(k).start()
                return carry

            lax.fori_loop(first, last, y_step, 0)

        def core_sends_done(self):
            for j in range(2):
                for k in range(n_cols):
                    self.core_copy(j, k).wait_send()

        def total(self, k):
            value = self.part(f, k)
            self.core_copy(1, k).wait_recv()
            self.y_copy(k).wait_recv()
            return (
                value
                + core_recv[self.index, 1, :, part_cols(k)].astype(f32)
                + y_recv[self.index, :, part_cols(k)].astype(f32)
            )

        def wait_y_sends(self):
            for k in range(n_cols):
                self.y_copy(k).wait_send()

    def gain_add(index, k, value, weighed):
        products = (value * weighed.astype(f32)).reshape(rows // 8, 8, piece)
        gain_part[index, :, part_cols(k)] += jnp.sum(products, axis=0)

    def part_branch(fb, k):
        return nt(att[...], wo[cols_at(fb, k), :])

    def part_lat(fb, k):
        return nt(sgq[...], wq[cols_at(fb, k), :])

    def seen_lat(fb, k, value):
        gain_add(4 + fb, k, value, lat_all[fb, :, part_cols(k)])

    branch = Collect(part_branch, 0)
    back_lat = Collect(part_lat, 1, seen_lat)
    gain_part[...] = jnp.zeros(gain_part.shape, f32)

    gather_core(cot_all, sem_cot).wait_recv()
    project(acc_q, cot_all, wo, mine, True)
    for k in range(n_rows):
        att[part_rows(k), :] = flip(att_t[:, part_rows(k)])
    pl.when(patient)(cot_across_y)
    branch.send_core()

    hold_own(cot_all, cot_x, sem_cot_x)
    hold_own(lat_all, lat_x, sem_lat_x)
    across_core(cot_x, sem_cot_x).wait_recv()
    for p in range(n_rows):
        att_x_copy(p).wait_recv()
    near_j = jnp.where(z // 2 == y, 0, 1)
    grad_o.first(near_j)

    @pl.when(urgent)
    def _():
        pass_on(cot_all, sem_cot, cot_x, sem_cot_x)
        for k in range(n_rows):
            rows_x(lat_all, lat_x, sem_lat_x, k).start()
        hold_rows(cot_all, cot_x, sem_cot_x)

    @pl.when(patient)
    def _():
        wait_on(cot_all, sem_cot)
        rows_core_done(cot_x, sem_cot_x)

    grad_o.first(1 - near_j)
    early = z // 2 != y
    pl.when(early)(grad_o.second)

    @pl.when(patient)
    def _():
        pass_on(cot_all, sem_cot, cot_x, sem_cot_x)

    pl.when(urgent)(lambda: wait_on(cot_all, sem_cot))
    project(acc_q, cot_all, wo, theirs, False)
    split_heads(acc_q, ga_rows, ga_cols, None, 1.0)
    branch.send_y(0, 1)

    gkv[:, patches] = jnp.zeros((kv, rows), f32)

    def backward_step(p, carry):
        far_s[...] = nn(ga_rows[p], kv_t[vals, patches])
        near_s[...] = nn(ga_rows[p], kv_t[vals, own_latents(p)])
        for h in range(heads):
            far_p = probs_c[p, head_part(h), :].astype(f32)
            near_p = probs_l[p, head_part(h), :].astype(f32)
            far_d, near_d = far_s[head_part(h), :], near_s[head_part(h), :]
            inner = jnp.sum(far_p * far_d, axis=1, keepdims=True) + jnp.sum(
                near_p * near_d, axis=1, keepdims=True
            )
            far_g[head_part(h), :] = (far_p * (far_d - inner)).astype(bf16)
            near_g[head_part(h), :] = (near_p * (near_d - inner)).astype(bf16)
        grad_query = nn(far_g[...], k_rows[patches, :]) + nn(near_g[...], k_rows[own_latents(p), :])
        total = jnp.zeros((1, ROWS), f32)
        for h in range(heads):
            one = grad_query[head_part(h), :].T * score_scale
            query = q_cols[p, :, head_part(h)].astype(f32)
            total = total + jnp.sum(one * query, axis=0, keepdims=True)
            sgq_t[h * head : (h + 1) * head, part_rows(p)] = (
                one * scale_row[1:2, part_rows(p)]
            ).astype(bf16)
        inners[f, 1:2, part_rows(p)] = total
        sgq_x_copy(p).start()
        gkv[keys, patches] += nn(q_cols[p], far_g[...])
        gkv[keys, own_latents(p)] = nn(q_cols[p], near_g[...])
        gkv[vals, patches] += nn(ga_cols[p], probs_c[p])
        gkv[vals, own_latents(p)] = nn(ga_cols[p], probs_l[p])
        return carry

    lax.fori_loop(0, n_rows, backward_step, 0)
    gkv[keys, :] = gkv[keys, :] * score_scale
    products = jnp.sum(gkv[...] * kv_t[...].astype(f32), axis=0, keepdims=True)
    inners[f, 0:1, :] = products[:, 0:rows]
    inners[f, 1:2, :] += products[:, rows:]
    inner_out = exchange(inners, sem_inner)
    for copy in inner_out:
        copy.start()
    sgkv_all[head_rows_of(f), 0:rows] = (gkv[:, 0:rows] * scale_row[0:1, :]).astype(bf16)
    sgkv_all[head_rows_of(f), rows:] = (gkv[:, rows:] * scale_row[1:2, :]).astype(bf16)
    sem_gkv = take(3)

    def gkv_copy(t, i, dev):
        piece = sgkv_all.at[head_rows_of(t)]
        return remote(piece, piece, sem_gkv + i, dev)

    gkv_copy(f, 0, y_dev).start()
    gkv_copy(f, 1, core_dev).start()
    for k in range(n_rows):
        sgq[part_rows(k), :] = flip(sgq_t[:, part_rows(k)])

    pl.when(patient)(lambda: hold_rows(cot_all, cot_x, sem_cot_x))
    pl.when(urgent)(lambda: rows_core_done(cot_x, sem_cot_x))
    pl.when(jnp.logical_not(early))(grad_o.second)

    @pl.when(patient)
    def _():
        for k in range(n_rows):
            rows_x(lat_all, lat_x, sem_lat_x, k).start()
        across_core(lat_x, sem_lat_x).wait_recv()
        rows_core_done(lat_x, sem_lat_x)

    pl.when(urgent)(lambda: hold_rows(lat_all, lat_x, sem_lat_x))
    for p in range(n_rows):
        sgq_x_copy(p).wait_recv()
    grad_q.first(1)
    grad_q.first(0)
    branch.send_y(1, n_cols)
    branch.core_sends_done()
    gkv_copy(f, 0, y_dev).wait_recv()
    gkv_copy(f_y, 2, core_dev).start()
    gkv_copy(f, 1, core_dev).wait_recv()
    gkv_copy(f_y, 2, core_dev).wait_recv()
    pair_first()
    back_lat.send_core()
    back_lat.send_y(0, n_cols)
    outs = []

    def put(src, dst, i):
        copy = local_copy(src, dst, i)
        copy.start()
        outs.append(copy)

    for copy in inner_out:
        copy.wait()
    coef_row[...] = (
        scale_row[...]
        * scale_row[...]
        * (inners[0] + inners[1] + inners[2] + inners[3])
        / model_width
    )

    coef_cols = coef_row[...].T
    back_lat.core_sends_done()
    for k in range(n_rows):
        sgc[part_rows(k), :] = flip(sgkv_all[:, part_rows(k)])
        sgl[part_rows(k), :] = flip(sgkv_all[:, part_rows(n_rows + k)])

    def finish_ctx(k, carry):
        value = nn(sgc[...], w_own[:, part_cols(k)])
        gain_add(f, k, value, ctx_own[:, part_cols(k)])
        value = value * gain_ctx[:, cols_at(f, k)]
        value = value - raw_ctx[:, part_cols(k)].astype(f32) * coef_cols[:, 0:1]
        core_send[0, :, part_cols(k)] = value.astype(bf16)
        return carry

    lax.fori_loop(0, n_cols, finish_ctx, 0)
    put(core_send.at[0], out_context, 10)

    def gain_own(k, carry):
        value = part_lat(f, k) + nn(sgl[...], w_own[:, part_cols(k)])
        gain_add(4 + f, k, value, lat_all[f, :, part_cols(k)])
        return carry

    lax.fori_loop(0, n_cols, gain_own, 0)
    for i in range(4):
        gain_sum[i : i + 1, :] = (
            jnp.sum(gain_part[i], axis=0, keepdims=True) / gain_ctx[:, block_cols(i)]
        )
        gain_sum[4 + i : 5 + i, :] = (
            jnp.sum(gain_part[4 + i], axis=0, keepdims=True) / gain_lat[:, block_cols(i)]
        )
    part = width // n_dp

    def dp_cols(d, n):
        return pl.ds(pl.multiple_of(d * part, 128), n * part)

    sem_gain = take(n_hi + 2)

    def gain_z(i):
        return remote(
            gain_sum.at[:, dp_cols(lax.rem(z + i, n_hi) * 2, 2)],
            gain_recv.at[i],
            sem_gain + i,
            far_dev(i),
        )

    def gain_x():
        return remote(
            gain_pair.at[:, dp_cols(1 - x, 1)], gain_one.at[0], sem_gain, x_dev
        )

    def gain_core():
        return remote(gain_one.at[1], gain_one.at[2], sem_gain + n_hi, core_dev)

    def gain_y():
        return remote(gain_one.at[3], gain_one.at[4], sem_gain + n_hi + 1, y_dev)

    for i in others:
        gain_z(i).start()

    @pl.when(patient)
    def _():
        hold_rows(lat_all, lat_x, sem_lat_x)

    @pl.when(urgent)
    def _():
        across_core(lat_x, sem_lat_x).wait_recv()
        rows_core_done(lat_x, sem_lat_x)

    grad_q.second()
    pair_step(0, 0)
    pair_step(1, 0)
    pair_step(0, 1)
    pair_step(2, 0)
    pair_step(1, 1)
    pair_step(3, 0)
    pair_step(2, 1)
    pair_step(3, 1)
    summed = gain_sum[:, dp_cols(z * 2, 2)]
    for i in others:
        gain_z(i).wait()
        summed = summed + gain_recv[i]
    gain_pair[...] = summed
    gain_x().start()

    def finish(k, carry):
        value = raw_lat[:, part_cols(k)].astype(f32) + branch.total(k)
        y_recv[0, :, part_cols(k)] = value.astype(bf16)
        return carry

    lax.fori_loop(0, n_cols, finish, 0)
    put(y_recv.at[0], out_latents, 9)
    gain_x().wait()
    gain_one[1] = gain_pair[:, dp_cols(x, 1)] + gain_one[0]
    gain_core().start()

    def put_weight(spread, at, out, i):
        spread.final()
        at[...] = dp_acc[...].T
        put(at, out, i)

    put_weight(grad_o, acc_q, out_out, 6)
    gain_core().wait()
    gain_one[3] = gain_one[1] + gain_one[2]
    gain_y().start()

    def finish_lat(k, carry):
        value = back_lat.total(k) + nn(sgl[...], w_own[:, part_cols(k)])
        value = value * gain_lat[:, cols_at(f, k)]
        value = value - raw_lat[:, part_cols(k)].astype(f32) * coef_cols[:, 1:2]
        value = value + cot_all[f, :, part_cols(k)].astype(f32)
        y_recv[1, :, part_cols(k)] = value.astype(bf16)
        return carry

    lax.fori_loop(0, n_cols, finish_lat, 0)
    put(y_recv.at[1], out_grad_lat, 11)
    gain_y().wait()
    mine_all = gain_one[3] + gain_one[4]
    index = lax.broadcasted_iota(jnp.int32, mine_all.shape, 0)
    gain_out[0] = jnp.sum(jnp.where(index == f, mine_all, 0.0), axis=0, keepdims=True)
    gain_out[1] = jnp.sum(jnp.where(index == 4 + f, mine_all, 0.0), axis=0, keepdims=True)
    put(gain_out.at[0], out_gain_c, 2)
    put(gain_out.at[1], out_gain_l, 14)
    put_weight(grad_q, far_s.at[:, pl.ds(0, heads * head)], out_query, 7)
    pair_result()
    for i, out in enumerate((out_key, out_value)):
        put(kv_acc.at[pl.ds(i * head, head), pl.ds(feat, feat)], out, 8 + 5 * i)

    for copy in outs:
        copy.wait()
    for buf, base in ((lat_all, sem_lat), (cot_all, sem_cot)):
        gather_done(buf, base)
    for collect in (branch, back_lat):
        collect.wait_y_sends()
    for spread in (grad_o, grad_q):
        spread.wait_sends()
    for buf, held, base in ((lat_all, lat_x, sem_lat_x), (cot_all, cot_x, sem_cot_x)):
        across_x(buf, held, base).wait_send()
        across_core(held, base).wait_send()
        for k in range(n_rows):
            rows_x(buf, held, base, k).wait_send()
            rows_core(held, base, k).wait_send()
    for p in range(n_rows):
        att_x_copy(p).wait_send()
        sgq_x_copy(p).wait_send()
    pair_sends_done()
    w_core().wait_send()
    for i in range(2):
        w_y(y_dev, f_y, i).wait_send()
    for i in others:
        w_z(i).wait_send()
    for i in range(n_hi):
        w_x(i).wait_send()
    for j in range(2):
        kv_core_copy(j).wait_send()
    kv_y_copy().wait_send()
    for i in range(3):
        gkv_copy(f, i, core_dev).wait_send()


def hand_on(*refs):
    n = (len(refs) - 2) // 3
    ins, outs, held, sem_in, sem_out = refs[:n], refs[n : 2 * n], refs[2 * n : 3 * n], *refs[3 * n :]
    take_in = [pltpu.make_async_copy(ins[i], held[i], sem_in.at[i]) for i in range(n)]
    give_out = [pltpu.make_async_copy(held[i], outs[i], sem_out.at[i]) for i in range(n)]
    for copy in take_in:
        copy.start()
    for i in range(n):
        take_in[i].wait()
        give_out[i].start()
    for copy in give_out:
        copy.wait()


def kernel_local(
    n_dp,
    context,
    latents,
    gain_ctx,
    gain_lat,
    w_query,
    key_matrix,
    value_matrix,
    w_out,
    lengths,
    patch_flags,
    cotangent,
):
    rows, width = context.shape
    model_width = gain_ctx.shape[0]
    units = w_query.shape[1]
    kv = 2 * key_matrix.shape[1]
    heads = units // HEAD_DIM
    n_hi = n_dp // 2
    feat = model_width // n_dp
    any_space = pl.BlockSpec(memory_space=pl.ANY)
    block = jax.ShapeDtypeStruct((rows, width), bf16)
    shaped = jax.ShapeDtypeStruct
    out = pl.pallas_call(
        functools.partial(block_kernel, n_dp),
        out_shape=(
            block,
            block,
            block,
            shaped((feat, units), f32),
            shaped((kv // 2, feat), f32),
            shaped((kv // 2, feat), f32),
            shaped((feat, units), f32),
            shaped((1, width // n_dp), f32),
            shaped((1, width // n_dp), f32),
        ),
        in_specs=[any_space] * 11,
        out_specs=(any_space,) * 9,
        scratch_shapes=[
            pltpu.VMEM((1, model_width), f32),
            pltpu.VMEM((1, model_width), f32),
            pltpu.SMEM(lengths.shape, jnp.int32),
            pltpu.VMEM((1, rows), jnp.int32),
            pltpu.VMEM((2, 1, width // n_dp), f32),
            pltpu.VMEM((4, rows, width), bf16),
            pltpu.VMEM((4, rows, width), bf16),
            pltpu.VMEM((rows, width), bf16),
            pltpu.VMEM((rows, width), bf16),
            pltpu.VMEM((rows, width), bf16),
            pltpu.VMEM((model_width, units), bf16),
            pltpu.VMEM((kv, model_width), bf16),
            pltpu.VMEM((4 * kv, width), bf16),
            pltpu.VMEM((model_width, units), bf16),
            pltpu.VMEM((rows, units), f32),
            pltpu.VMEM((4 * kv, 2 * rows), f32),
            pltpu.VMEM((units, rows), bf16),
            pltpu.VMEM((units, rows), bf16),
            pltpu.VMEM((rows // ROWS, heads * ROWS, HEAD_DIM), bf16),
            pltpu.VMEM((rows // ROWS, HEAD_DIM, heads * ROWS), bf16),
            pltpu.VMEM((rows // ROWS, heads * ROWS, HEAD_DIM), bf16),
            pltpu.VMEM((rows // ROWS, HEAD_DIM, heads * ROWS), bf16),
            pltpu.VMEM((2 * rows, HEAD_DIM), bf16),
            pltpu.VMEM((2 * rows, HEAD_DIM), bf16),
            pltpu.VMEM((heads * ROWS, rows), f32),
            pltpu.VMEM((heads * ROWS, ROWS), f32),
            pltpu.VMEM((heads * ROWS, rows), bf16),
            pltpu.VMEM((heads * ROWS, ROWS), bf16),
            pltpu.VMEM((rows, units), bf16),
            pltpu.VMEM((rows, units), bf16),
            pltpu.VMEM((kv, 2 * rows), bf16),
            pltpu.VMEM((2, kv, rows), bf16),
            pltpu.VMEM((2, kv, rows), bf16),
            pltpu.VMEM((kv, rows), bf16),
            pltpu.VMEM((rows // ROWS, heads * ROWS, rows), bf16),
            pltpu.VMEM((rows // ROWS, heads * ROWS, ROWS), bf16),
            pltpu.VMEM((kv, 2 * rows), f32),
            pltpu.VMEM((4 * kv, 2 * rows), bf16),
            pltpu.VMEM((rows, 4 * kv), bf16),
            pltpu.VMEM((rows, 4 * kv), bf16),
            pltpu.VMEM((4, 8, rows), f32),
            pltpu.VMEM((4, 8, rows), f32),
            pltpu.VMEM((8, rows), f32),
            pltpu.VMEM((8, rows), f32),
            pltpu.VMEM((8, 8, width), f32),
            pltpu.VMEM((8, width), f32),
            pltpu.VMEM((n_hi, 8, 2 * width // n_dp), f32),
            pltpu.VMEM((8, 2 * width // n_dp), f32),
            pltpu.VMEM((5, 8, width // n_dp), f32),
            pltpu.VMEM((2, rows, width), bf16),
            pltpu.VMEM((2, 2, rows, width), bf16),
            pltpu.VMEM((2, rows, width), bf16),
            pltpu.VMEM((4, rows, feat), bf16),
            pltpu.VMEM((4, rows, feat), bf16),
            pltpu.VMEM((units, rows), bf16),
            pltpu.VMEM((units, rows), bf16),
            pltpu.VMEM((3, units, feat), bf16),
            pltpu.VMEM((3, units, feat), bf16),
            pltpu.VMEM((3, units, feat), bf16),
            pltpu.VMEM((3, units, feat), bf16),
            pltpu.VMEM((4 * kv, feat), bf16),
            pltpu.VMEM((4 * kv, feat), bf16),
            pltpu.VMEM((4 * kv, feat), bf16),
            pltpu.VMEM((4, kv, feat), bf16),
            pltpu.VMEM((2, kv, feat), bf16),
            pltpu.VMEM((units, feat), f32),
            pltpu.SemaphoreType.DMA((160,)),
            pltpu.SemaphoreType.DMA((160,)),
            pltpu.SemaphoreType.DMA((16,)),
        ],
        compiler_params=pltpu.CompilerParams(
            collective_id=0, has_side_effects=True, vmem_limit_bytes=64 << 20
        ),
        name="block",
    )(
        context,
        latents,
        cotangent,
        gain_ctx.reshape(1, model_width),
        gain_lat.reshape(1, model_width),
        w_query,
        key_matrix.T,
        value_matrix.T,
        w_out,
        lengths,
        patch_flags.reshape(1, rows),
    )
    out = pl.pallas_call(
        hand_on,
        out_shape=tuple(shaped(a.shape, a.dtype) for a in out),
        in_specs=[any_space] * 9,
        out_specs=(any_space,) * 9,
        scratch_shapes=[pltpu.VMEM(a.shape, a.dtype) for a in out]
        + [pltpu.SemaphoreType.DMA((9,)), pltpu.SemaphoreType.DMA((9,))],
        compiler_params=pltpu.CompilerParams(vmem_limit_bytes=64 << 20),
        name="hand_on",
    )(*out)
    latents_out, grad_context, grad_latents, g_query, g_key, g_value, g_out, gain_c, gain_l = out
    return (
        latents_out,
        grad_context,
        grad_latents,
        g_query,
        g_key.T,
        g_value.T,
        g_out,
        gain_c,
        gain_l,
    )


def solution(mesh):
    n_dp = mesh.shape["dp"]
    body = functools.partial(kernel_local, n_dp) if n_dp == 8 else plain_local
    return jax.shard_map(
        body,
        mesh=mesh,
        in_specs=(
            P("dp", "tensor"),
            P("dp", "tensor"),
            P(),
            P(),
            P(None, "tensor"),
            P(None, "tensor"),
            P(None, "tensor"),
            P(None, "tensor"),
            P("dp", None),
            P("dp"),
            P("dp", "tensor"),
        ),
        out_specs=(
            P("dp", "tensor"),
            P("dp", "tensor"),
            P("dp", "tensor"),
            P("dp", "tensor"),
            P("dp", "tensor"),
            P("dp", "tensor"),
            P("dp", "tensor"),
            P("tensor", "dp"),
            P("tensor", "dp"),
        ),
        check_vma=False,
    )
```

```python
import functools

import jax
import jax.numpy as jnp
from jax import lax
from jax.experimental import pallas as pl
from jax.experimental.pallas import tpu as pltpu
from jax.sharding import PartitionSpec as P

HEAD_DIM = 96
LAT = 64


epsilon = 1e-06
masked_value = -1e30
contract_rows = (((0,), (0,)), ((), ()))
contract_cols = (((1,), (1,)), ((), ()))


def row_scales(rows_in):
    values_f = rows_in.astype(jnp.float32)
    return (values_f, lax.rsqrt(jnp.mean(values_f * values_f, axis=1) + epsilon))


def norm_back(grad_norm, local_vals, row_scale, gain_local, row_inner_all, model_width):
    weighted = grad_norm * gain_local
    grad_input = (
        row_scale[:, None] * weighted
        - local_vals * (row_scale**3 * row_inner_all / model_width)[:, None]
    )
    grad_gain = jnp.sum(grad_norm * local_vals * row_scale[:, None], axis=0)
    return (grad_input, grad_gain)


def plain_local(
    context,
    latents,
    gain_ctx,
    gain_lat,
    w_query,
    key_matrix,
    value_matrix,
    w_out,
    lengths,
    patch_flags,
    cotangent,
):
    patch_rows = context.shape[0]
    latent_rows = latents.shape[0]
    local_width = context.shape[1]
    model_width = gain_ctx.shape[0]
    head_size = HEAD_DIM
    kv_local = key_matrix.shape[1] // head_size
    query_local = w_query.shape[1] // head_size
    repeat = query_local // kv_local
    all_count = patch_rows + latent_rows
    score_scale = head_size ** (-0.5)
    column = lax.axis_index("tensor") * local_width
    whole_ctx, whole_lat = (
        lax.all_gather(context, "tensor", axis=1, tiled=True),
        lax.all_gather(latents, "tensor", axis=1, tiled=True),
    )
    ctx_values, ctx_scale = row_scales(whole_ctx)
    lat_values, lat_scale = row_scales(whole_lat)
    ctx_norm = (ctx_values * ctx_scale[:, None] * gain_ctx).astype(jnp.bfloat16)
    lat_norm = (lat_values * lat_scale[:, None] * gain_lat).astype(jnp.bfloat16)
    queries = jnp.dot(lat_norm, w_query, preferred_element_type=jnp.float32).astype(jnp.bfloat16)
    all_rows = jnp.concatenate([ctx_norm, lat_norm], axis=0)
    w_pair = jnp.concatenate([key_matrix, value_matrix], axis=1)
    pair_rows = jnp.dot(all_rows, w_pair, preferred_element_type=jnp.float32).astype(jnp.bfloat16)
    key_head_split = (
        pair_rows[:, : kv_local * head_size]
        .reshape(all_count, kv_local, head_size)
        .transpose(1, 0, 2)
    )
    value_head_split = (
        pair_rows[:, kv_local * head_size :]
        .reshape(all_count, kv_local, head_size)
        .transpose(1, 0, 2)
    )
    query_heads = queries.reshape(latent_rows, query_local, head_size).transpose(1, 0, 2)
    image_ends = jnp.cumsum(lengths[0])
    patch_image = jnp.sum(
        (jnp.arange(patch_rows)[:, None] >= image_ends[None, :]).astype(jnp.int32), axis=1
    )
    latent_image = jnp.arange(latent_rows) // LAT
    allowed = jnp.concatenate(
        [
            (latent_image[:, None] == patch_image[None, :]) & (patch_flags[None, :] == 1),
            latent_image[:, None] == latent_image[None, :],
        ],
        axis=1,
    )
    head_index = jnp.arange(query_local)

    def head_scores(query_head, head_number):
        key_head = key_head_split[head_number // repeat]
        value_head = value_head_split[head_number // repeat]
        raw_scores = (
            lax.dot_general(query_head, key_head, contract_cols, preferred_element_type=jnp.float32)
            * score_scale
        )
        return (jnp.where(allowed, raw_scores, masked_value), key_head, value_head)

    def head_forward(member):
        query_head, head_number = member
        scores, key_head, value_head = head_scores(query_head, head_number)
        row_top = jnp.max(scores, axis=1, keepdims=True)
        exp_scores = jnp.exp(scores - row_top)
        row_total = jnp.sum(exp_scores, axis=1, keepdims=True)
        attention = (exp_scores / row_total).astype(jnp.bfloat16)
        blended = jnp.dot(attention, value_head, preferred_element_type=jnp.float32).astype(
            jnp.bfloat16
        )
        return (blended, row_top[:, 0] + jnp.log(row_total[:, 0]))

    heads_out, log_totals = lax.map(head_forward, (query_heads, head_index))
    attended = heads_out.transpose(1, 0, 2).reshape(latent_rows, query_local * head_size)
    partial_out = lax.dot_general(
        attended, w_out, contract_cols, preferred_element_type=jnp.float32
    )
    branch = lax.psum_scatter(
        partial_out.astype(jnp.bfloat16), "tensor", scatter_dimension=1, tiled=True
    ).astype(jnp.float32)
    latents_out = (latents.astype(jnp.float32) + branch).astype(jnp.bfloat16)
    full_grad = lax.all_gather(cotangent, "tensor", axis=1, tiled=True)
    grad_attended = jnp.dot(full_grad, w_out, preferred_element_type=jnp.float32).astype(
        jnp.bfloat16
    )
    grad_w_out = lax.dot_general(
        full_grad, attended, contract_rows, preferred_element_type=jnp.float32
    )
    grad_heads = grad_attended.reshape(latent_rows, query_local, head_size).transpose(1, 0, 2)

    def head_backward(member):
        query_head, grad_blended, log_total, head_number = member
        scores, key_head, value_head = head_scores(query_head, head_number)
        attention = jnp.exp(scores - log_total[:, None])
        grad_probs = lax.dot_general(
            grad_blended, value_head, contract_cols, preferred_element_type=jnp.float32
        )
        row_inner = jnp.sum(attention * grad_probs, axis=1, keepdims=True)
        grad_scores = (attention * (grad_probs - row_inner)).astype(jnp.bfloat16)
        grad_query = (
            jnp.dot(grad_scores, key_head, preferred_element_type=jnp.float32) * score_scale
        ).astype(jnp.bfloat16)
        grad_key = (
            lax.dot_general(
                grad_scores, query_head, contract_rows, preferred_element_type=jnp.float32
            )
            * score_scale
        )
        grad_value = lax.dot_general(
            attention.astype(jnp.bfloat16),
            grad_blended,
            contract_rows,
            preferred_element_type=jnp.float32,
        )
        return (grad_query, grad_key, grad_value)

    grad_query_heads, grad_key_heads, grad_value_heads = lax.map(
        head_backward, (query_heads, grad_heads, log_totals, head_index)
    )
    grad_keys = grad_key_heads.reshape(kv_local, repeat, all_count, head_size).sum(axis=1)
    grad_values = grad_value_heads.reshape(kv_local, repeat, all_count, head_size).sum(axis=1)
    grad_pair = jnp.concatenate(
        [
            grad_keys.transpose(1, 0, 2).reshape(all_count, kv_local * head_size),
            grad_values.transpose(1, 0, 2).reshape(all_count, kv_local * head_size),
        ],
        axis=1,
    ).astype(jnp.bfloat16)
    grad_q_rows = grad_query_heads.transpose(1, 0, 2).reshape(latent_rows, query_local * head_size)
    grad_w_query = lax.dot_general(
        lat_norm, grad_q_rows, contract_rows, preferred_element_type=jnp.float32
    )
    grad_w_pair = lax.dot_general(
        all_rows, grad_pair, contract_rows, preferred_element_type=jnp.float32
    )
    grad_rows = lax.dot_general(
        grad_pair, w_pair, contract_cols, preferred_element_type=jnp.float32
    )
    lat_terms = grad_rows[patch_rows:] + lax.dot_general(
        grad_q_rows, w_query, contract_cols, preferred_element_type=jnp.float32
    )
    grad_ctx_norm, grad_lat_norm = (
        lax.psum_scatter(
            grad_rows[:patch_rows].astype(jnp.bfloat16), "tensor", scatter_dimension=1, tiled=True
        ).astype(jnp.float32),
        lax.psum_scatter(
            lat_terms.astype(jnp.bfloat16), "tensor", scatter_dimension=1, tiled=True
        ).astype(jnp.float32),
    )
    ctx_local = context.astype(jnp.float32)
    lat_local = latents.astype(jnp.float32)
    gain_ctx_local = lax.dynamic_slice_in_dim(gain_ctx, column, local_width, 0)
    gain_lat_local = lax.dynamic_slice_in_dim(gain_lat, column, local_width, 0)
    ctx_inner = jnp.sum(grad_ctx_norm * gain_ctx_local * ctx_local, axis=1)
    lat_inner = jnp.sum(grad_lat_norm * gain_lat_local * lat_local, axis=1)
    ctx_inner_all, lat_inner_all = lax.psum((ctx_inner, lat_inner), "tensor")
    grad_ctx_in, grad_gain_c = norm_back(
        grad_ctx_norm, ctx_local, ctx_scale, gain_ctx_local, ctx_inner_all, model_width
    )
    grad_lat_in, grad_gain_l = norm_back(
        grad_lat_norm, lat_local, lat_scale, gain_lat_local, lat_inner_all, model_width
    )
    grad_context = grad_ctx_in.astype(jnp.bfloat16)
    grad_latents = (cotangent.astype(jnp.float32) + grad_lat_in).astype(jnp.bfloat16)
    grad_w_key = grad_w_pair[:, : kv_local * head_size]
    grad_w_value = grad_w_pair[:, kv_local * head_size :]
    sum_query, sum_key, sum_value, sum_out, sum_gain_c, sum_gain_l = (
        lax.psum_scatter(grad_w_query, "dp", scatter_dimension=0, tiled=True),
        lax.psum_scatter(grad_w_key, "dp", scatter_dimension=0, tiled=True),
        lax.psum_scatter(grad_w_value, "dp", scatter_dimension=0, tiled=True),
        lax.psum_scatter(grad_w_out, "dp", scatter_dimension=0, tiled=True),
        lax.psum_scatter(grad_gain_c, "dp", scatter_dimension=0, tiled=True),
        lax.psum_scatter(grad_gain_l, "dp", scatter_dimension=0, tiled=True),
    )
    return (
        latents_out,
        grad_context,
        grad_latents,
        sum_query,
        sum_key,
        sum_value,
        sum_out,
        sum_gain_c.reshape(1, -1),
        sum_gain_l.reshape(1, -1),
    )


MESH = pl.DeviceIdType.MESH
f32 = jnp.float32
bf16 = jnp.bfloat16
ROWS = 128
LOG2_E = 1.4426950408889634


def nn(a, b):
    return jnp.dot(a, b, preferred_element_type=f32)


def nt(a, b):
    return lax.dot_general(a, b, contract_cols, preferred_element_type=f32)


def flip(a):
    return a.astype(f32).T.astype(bf16)


def block_kernel(
    n_dp,
    context,
    latents,
    cotangent,
    gain_ctx_in,
    gain_lat_in,
    w_query,
    key_across,
    value_across,
    w_out,
    lengths_in,
    flags_in,
    out_latents,
    out_context,
    out_grad_lat,
    out_query,
    out_key,
    out_value,
    out_out,
    out_gain_c,
    out_gain_l,
    gain_ctx,
    gain_lat,
    lengths,
    flags,
    gain_out,
    lat_all,
    cot_all,
    ctx_own,
    raw_lat,
    raw_ctx,
    wq,
    wkv,
    w_own,
    wo,
    acc_q,
    kv_acc,
    att_t,
    sgq_t,
    q_rows,
    q_cols,
    ga_rows,
    ga_cols,
    k_rows,
    v_rows,
    far_s,
    near_s,
    far_g,
    near_g,
    att,
    sgq,
    kv_t,
    kv_send,
    kv_core,
    kv_y,
    probs_c,
    probs_l,
    gkv,
    sgkv_all,
    sgc,
    sgl,
    sums,
    inners,
    scale_row,
    coef_row,
    gain_part,
    gain_sum,
    gain_recv,
    gain_one,
    core_send,
    core_recv,
    y_recv,
    lat_x,
    cot_x,
    att_xt,
    sgq_xt,
    z_send_o,
    z_send_q,
    z_recv_o,
    z_recv_q,
    x_send_kv,
    x_recv_kv,
    z_recv_kv,
    own_send,
    own_recv,
    dp_acc,
    send_sem,
    recv_sem,
    local_sem,
):
    rows, width = raw_lat.shape
    n_rows = rows // ROWS
    n_hi = n_dp // 2
    feat = 4 * width // n_dp
    head = HEAD_DIM
    heads = acc_q.shape[1] // head
    model_width = 4 * width
    score_scale = head ** (-0.5)

    dp = lax.axis_index("dp")
    f = lax.axis_index("tensor")
    z, x = dp // 2, lax.rem(dp, 2)
    y, c = f // 2, lax.rem(f, 2)
    f_c = y * 2 + (1 - c)
    f_y = (1 - y) * 2 + c
    f_yc = (1 - y) * 2 + (1 - c)
    core_dev, y_dev, yc_dev = (dp, f_c), (dp, f_y), (dp, f_yc)
    x_dev = (z * 2 + 1 - x, f)
    z_1 = z + 1 - 2 * lax.rem(z, 2)
    z_2 = z + 2 - 4 * (z // 2)
    z1_dev, z2_dev = (z_1 * 2 + x, f), (z_2 * 2 + x, f)
    x_mine = pl.ds(pl.multiple_of(x * feat, 128), feat)
    x_other = pl.ds(pl.multiple_of((1 - x) * feat, 128), feat)

    urgent = lax.rem(c + z, 2) == 1
    patient = jnp.logical_not(urgent)

    count = [0]

    def take(n):
        count[0] += n
        return count[0] - n

    def remote(src, dst, sem, dev, sem_to=None):
        return pltpu.make_async_remote_copy(
            src_ref=src,
            dst_ref=dst,
            send_sem=send_sem.at[sem],
            recv_sem=recv_sem.at[sem if sem_to is None else sem_to],
            device_id=dev,
            device_id_type=MESH,
        )

    def local_copy(src, dst, i):
        return pltpu.make_async_copy(src, dst, local_sem.at[i])

    def part_rows(k):
        if isinstance(k, int):
            return pl.ds(k * ROWS, ROWS)
        return pl.ds(pl.multiple_of(k * ROWS, ROWS), ROWS)

    n_cols = 4
    piece = width // n_cols

    def part_cols(k):
        if isinstance(k, int):
            return pl.ds(k * piece, piece)
        return pl.ds(pl.multiple_of(k * piece, 128), piece)

    def cols_at(fb, k):
        return pl.ds(pl.multiple_of(fb * width + k * piece, 128), piece)

    def block_cols(fb):
        if isinstance(fb, int):
            return pl.ds(fb * width, width)
        return pl.ds(pl.multiple_of(fb * width, width), width)

    loads = [
        local_copy(latents, raw_lat, 0),
        local_copy(key_across, wkv.at[pl.ds(0, head)], 4),
        local_copy(value_across, wkv.at[pl.ds(head, head)], 14),
        local_copy(context, raw_ctx, 1),
        local_copy(cotangent, cot_all.at[f], 13),
        local_copy(w_query, wq, 3),
        local_copy(w_out, wo, 5),
    ]
    small = [
        local_copy(gain_lat_in, gain_lat, 2),
        local_copy(gain_ctx_in, gain_ctx, 6),
        local_copy(lengths_in, lengths, 7),
        local_copy(flags_in, flags, 8),
    ]
    for load in small[:1] + loads + small[1:]:
        load.start()

    barrier = pltpu.get_barrier_semaphore()

    def greet(dev):
        pl.semaphore_signal(barrier, inc=1, device_id=dev, device_id_type=MESH)

    others = [i for i in range(1, n_hi)]

    def far_dev(i):
        return (lax.rem(z + i, n_hi) * 2 + x, f)

    def far_x_dev(i):
        return (lax.rem(z + i, n_hi) * 2 + 1 - x, f)

    always = [core_dev, y_dev, yc_dev, x_dev] + [far_dev(i) for i in others]
    always += [far_x_dev(i) for i in others]
    for dev in always:
        greet(dev)
    pl.when(z != f)(lambda: greet((z_2 * 2 + x, z)))

    def weigh(raw, gain, buf):
        gain_row = gain[:, block_cols(f)]
        for k in range(n_rows):
            values = raw[part_rows(k), :].astype(f32)
            buf[part_rows(k), :] = (values * gain_row).astype(bf16)

    small[0].wait()
    loads[0].wait()
    weigh(raw_lat, gain_lat, lat_all.at[f])
    middle = z_2 == f
    pl.semaphore_wait(barrier, len(always) + 3 * middle.astype(jnp.int32))

    sem_lat, sem_cot = (take(2 * n_rows + 1) for _ in range(2))

    def gather_y(buf, base, k):
        return remote(buf.at[f, part_rows(k)], buf.at[f, part_rows(k)], base + k, y_dev)

    def gather_core(buf, base):
        return remote(buf.at[f], buf.at[f], base + n_rows, core_dev)

    def gather_on(buf, base, k):
        return remote(
            buf.at[f_y, part_rows(k)], buf.at[f_y, part_rows(k)], base + n_rows + 1 + k, core_dev
        )

    def pass_on(buf, base, held=None, base_x=None):
        def step(k, carry):
            gather_y(buf, base, k).wait_recv()
            gather_on(buf, base, k).start()
            if held is not None:
                rows_x(buf, held, base_x, k).start()
            return carry

        lax.fori_loop(0, n_rows, step, 0)

    def wait_on(buf, base):
        for k in range(n_rows):
            gather_on(buf, base, k).wait_recv()

    def gather_done(buf, base):
        for k in range(n_rows):
            gather_y(buf, base, k).wait_send()
            gather_on(buf, base, k).wait_send()
        gather_core(buf, base).wait_send()

    def square_sums(raw, index):
        for k in range(n_rows):
            values = raw[part_rows(k), :].astype(f32)
            total = jnp.sum(values * values, axis=1, keepdims=True)
            across = jnp.broadcast_to(total, (ROWS, 128)).T
            sums[f, pl.ds(index, 1), part_rows(k)] = across[0:1, :]

    sem_lat_x, sem_cot_x = take(2 * n_rows + 2), take(2 * n_rows + 2)
    sem_att_x, sem_sgq_x = take(n_rows), take(n_rows)

    def across_x(buf, held, base):
        return remote(buf.at[f, :, x_other], held.at[f], base, x_dev)

    def across_core(held, base):
        return remote(held.at[f], held.at[f], base + 1, core_dev)

    def rows_x(buf, held, base, k):
        return remote(
            buf.at[f_y, part_rows(k), x_other], held.at[f_y, part_rows(k)], base + 2 + k, x_dev
        )

    def rows_core(held, base, k):
        piece = held.at[f_y, part_rows(k)]
        return remote(piece, piece, base + 2 + n_rows + k, core_dev)

    def hold_own(buf, held, base):
        across_x(buf, held, base).wait_recv()
        across_core(held, base).start()

    def hold_rows(buf, held, base):
        def step(k, carry):
            rows_x(buf, held, base, k).wait_recv()
            rows_core(held, base, k).start()
            return carry

        lax.fori_loop(0, n_rows, step, 0)

    def rows_core_done(held, base):
        for k in range(n_rows):
            rows_core(held, base, k).wait_recv()

    kv = 2 * head
    slice_width = width // n_dp
    pair_rows = pl.ds(pl.multiple_of((1 - y) * 2 * kv, 64), 2 * kv)
    sem_w_core, sem_w_y, sem_w_z, sem_w_x = take(1), take(2), take(n_hi), take(n_hi)

    def head_rows_of(t):
        return pl.ds(pl.multiple_of(t * kv, 64), kv)

    def slice_cols(d, at=0):
        return pl.ds(pl.multiple_of(at + d * slice_width, 128), slice_width)

    def w_y(dev, f_to, i, sender=c):
        return remote(
            wkv.at[:, slice_cols(dp, f_to * width)],
            w_own.at[head_rows_of(f), slice_cols(dp)],
            sem_w_y + i,
            dev,
            sem_w_y + sender,
        )

    def w_core():
        return remote(
            wkv.at[:, block_cols(f_c)], w_own.at[head_rows_of(f)], sem_w_core, core_dev
        )

    def w_z(i):
        piece = w_own.at[pair_rows, slice_cols(dp)]
        return remote(piece, piece, sem_w_z + i, far_dev(i))

    def w_x(i):
        piece = w_own.at[pair_rows, slice_cols(lax.rem(z + i, n_hi) * 2 + x)]
        return remote(piece, piece, sem_w_x + lax.rem(z + i, n_hi), x_dev)

    loads[1].wait()
    loads[2].wait()
    w_y(y_dev, f_y, 0).start()
    w_y(yc_dev, f_yc, 1).start()
    w_core().start()
    for k in range(n_rows):
        gather_y(lat_all, sem_lat, k).start()
    gather_core(lat_all, sem_lat).start()
    loads[4].wait()
    gather_core(cot_all, sem_cot).start()
    across_x(cot_all, cot_x, sem_cot_x).start()
    sums[f] = jnp.zeros(sums.shape[1:], f32)
    inners[f] = jnp.zeros(inners.shape[1:], f32)
    loads[3].wait()
    for load in small[1:]:
        load.wait()
    weigh(raw_ctx, gain_ctx, ctx_own)
    for i in range(2):
        w_y(y_dev, f_y, i, i).wait_recv()
    for i in others:
        w_z(i).start()
    w_x(0).start()
    w_own[head_rows_of(f), :] = wkv[:, block_cols(f)]
    square_sums(raw_lat, 1)
    square_sums(raw_ctx, 0)

    peers = [core_dev, y_dev, yc_dev]
    sem_sums, sem_inner = take(3), take(3)

    def exchange(buf, base):
        return [remote(buf.at[f], buf.at[f], base + i, dev) for i, dev in enumerate(peers)]

    sums_out = exchange(sums, sem_sums)
    for copy in sums_out:
        copy.start()

    def project(acc, values, weight, blocks, first):
        def step(i, carry):
            fb = blocks[0] + i * (blocks[1] - blocks[0])
            for m in range(2):
                half = pl.ds(m * (rows // 2), rows // 2)
                product = nn(values[fb, half, :], weight[block_cols(fb), :])
                if first:
                    @pl.when(i == 0)
                    def _():
                        acc[half, :] = product

                    @pl.when(i > 0)
                    def _():
                        acc[half, :] += product
                else:
                    acc[half, :] += product
            return carry

        lax.fori_loop(0, 2, step, 0)

    def project_pair(blocks, first):
        latent_cols = pl.ds(rows, rows)
        for i, fb in enumerate(blocks):
            product = nt(wkv[:, block_cols(fb)], lat_all[fb])
            if first and i == 0:
                kv_acc[0:kv, latent_cols] = product
            else:
                kv_acc[0:kv, latent_cols] += product

    mine, theirs = (f, f_c), (f_y, f_yc)
    loads[5].wait()
    loads[6].wait()
    gather_core(lat_all, sem_lat).wait_recv()
    project(acc_q, lat_all, wq, mine, True)
    project_pair(mine, True)
    for i in others:
        w_z(n_hi - i).wait_recv()
        w_x(i).start()
    w_core().wait_recv()
    pl.when(urgent)(lambda: across_x(lat_all, lat_x, sem_lat_x).start())
    for i in range(n_hi):
        w_x(i).wait_recv()

    sem_kv_core, sem_kv_y = take(2), take(1)

    def kv_core_copy(j):
        return remote(kv_send.at[j], kv_core.at[j], sem_kv_core + j, core_dev)

    def kv_y_copy():
        return remote(kv_core.at[0], kv_y, sem_kv_y, y_dev)

    patches = pl.ds(0, rows)
    for n in range(2):
        half = slice(n * (rows // 2), (n + 1) * (rows // 2))
        kv_acc[:, half] = nt(w_own[...], ctx_own[half, :])
    for j, t in enumerate((f_yc, f_c)):
        kv_send[j] = kv_acc[head_rows_of(t), patches].astype(bf16)
        kv_core_copy(j).start()
    kv_core_copy(0).wait_recv()
    kv_core[0] = (kv_acc[head_rows_of(f_y), patches] + kv_core[0].astype(f32)).astype(bf16)
    kv_y_copy().start()

    def cot_across_y():
        for k in range(n_rows):
            gather_y(cot_all, sem_cot, k).start()

    pl.when(urgent)(cot_across_y)

    pl.when(urgent)(lambda: pass_on(lat_all, sem_lat, lat_x, sem_lat_x))
    pl.when(patient)(lambda: pass_on(lat_all, sem_lat))
    wait_on(lat_all, sem_lat)
    project(acc_q, lat_all, wq, theirs, False)
    project_pair(theirs, False)

    for copy in sums_out:
        copy.wait()
    total = sums[0] + sums[1] + sums[2] + sums[3]
    scale_row[...] = lax.rsqrt(total / model_width + epsilon)

    def split_heads(acc, by_rows, by_cols, row_scale, factor):
        for k in range(n_rows):
            across = acc[part_rows(k), :].T
            if row_scale is not None:
                across = across * row_scale[:, part_rows(k)]
            for h in range(heads):
                one = across[h * head : (h + 1) * head, :]
                at = pl.ds(h * ROWS, ROWS)
                by_cols[k, :, at] = one.astype(bf16)
                by_rows[k, at, :] = (one * factor).T.astype(bf16)

    def kv_by_rows(first):
        for n in range(first, first + n_rows):
            k_rows[part_rows(n), :] = flip(kv_t[0:head, part_rows(n)])
            v_rows[part_rows(n), :] = flip(kv_t[head:, part_rows(n)])

    split_heads(acc_q, q_rows, q_cols, scale_row[1:2, :], score_scale * LOG2_E)
    kv_t[:, rows:] = (kv_acc[0:kv, rows:] * scale_row[1:2, :]).astype(bf16)
    kv_by_rows(n_rows)
    kv_core_copy(1).wait_recv()
    kv_y_copy().wait_recv()
    summed = kv_acc[head_rows_of(f), patches] + kv_core[1].astype(f32) + kv_y[...].astype(f32)
    kv_t[:, 0:rows] = (summed * scale_row[0:1, :]).astype(bf16)
    kv_by_rows(0)

    patch = lax.broadcasted_iota(jnp.int32, (1, rows), 1)
    image = jnp.zeros((1, rows), jnp.int32)
    end = jnp.int32(0)
    for i in range(lengths.shape[1]):
        end = end + lengths[0, i]
        image = image + (patch >= end).astype(jnp.int32)
    image = jnp.where(flags[...] == 1, image, -1)
    per_part = ROWS // LAT
    row_image = lax.broadcasted_iota(jnp.int32, (ROWS, 1), 0) // LAT
    col_image = lax.broadcasted_iota(jnp.int32, (1, ROWS), 1) // LAT
    same = row_image == col_image
    keys, vals = pl.ds(0, head), pl.ds(head, head)
    def own_latents(p):
        return pl.ds(pl.multiple_of(rows + p * ROWS, ROWS), ROWS)


    def head_part(h):
        return slice(h * ROWS, (h + 1) * ROWS)

    def att_x_copy(p):
        cols = part_rows(p)
        return remote(att_t.at[:, cols], att_xt.at[:, cols], sem_att_x + p, x_dev)

    def sgq_x_copy(p):
        cols = part_rows(p)
        return remote(sgq_t.at[:, cols], sgq_xt.at[:, cols], sem_sgq_x + p, x_dev)

    def forward_step(p, carry):
        far_s[...] = nn(q_rows[p], kv_t[keys, patches])
        near_s[...] = nn(q_rows[p], kv_t[keys, own_latents(p)])
        allowed = (row_image + p * per_part) == image
        for h in range(heads):
            far = jnp.where(allowed, far_s[head_part(h), :], masked_value)
            near = jnp.where(same, near_s[head_part(h), :], masked_value)
            top = jnp.maximum(
                jnp.max(far, axis=1, keepdims=True), jnp.max(near, axis=1, keepdims=True)
            )
            far, near = jnp.exp2(far - top), jnp.exp2(near - top)
            total = jnp.sum(far, axis=1, keepdims=True) + jnp.sum(near, axis=1, keepdims=True)
            inverse = 1.0 / total
            probs_c[p, head_part(h), :] = (far * inverse).astype(bf16)
            probs_l[p, head_part(h), :] = (near * inverse).astype(bf16)
        blended = nn(probs_c[p], v_rows[patches, :]) + nn(probs_l[p], v_rows[own_latents(p), :])
        for h in range(heads):
            one = blended[head_part(h), :]
            att_t[h * head : (h + 1) * head, part_rows(p)] = one.T.astype(bf16)
        att_x_copy(p).start()
        return carry

    lax.fori_loop(0, n_rows, forward_step, 0)
    def chunk_out(zt):
        return nn(att_t[...], cot_all[zt, :, x_mine]) + nn(att_xt[...], cot_x[zt])

    def chunk_query(zt):
        return nn(sgq_t[...], lat_all[zt, :, x_mine]) + nn(sgq_xt[...], lat_x[zt])

    def chunk_pair(xt):
        cols = pl.ds(pl.multiple_of(xt * feat, 128), feat)
        return nn(sgkv_all[:, patches], ctx_own[:, cols]) + nn(
            sgkv_all[:, pl.ds(rows, rows)], lat_all[f, :, cols]
        )

    class Spread:
        def __init__(self, chunk, send, recv):
            self.chunk, self.send, self.recv, self.sem = chunk, send, recv, take(3)

        def copy(self, j, dev):
            return remote(self.send.at[j], self.recv.at[j], self.sem + j, dev)

        def first(self, j):
            zt = z_1 + j * (z_2 - z)
            self.send[j] = self.chunk(zt).astype(bf16)
            self.copy(j, z1_dev).start()

        def second(self):
            value = self.chunk(z_2)
            self.copy(1, z1_dev).wait_recv()
            self.send[2] = (value + self.recv[1].astype(f32)).astype(bf16)
            self.copy(2, z2_dev).start()

        def final(self):
            dp_acc[...] = self.chunk(z)
            self.copy(0, z1_dev).wait_recv()
            self.copy(2, z2_dev).wait_recv()
            dp_acc[...] += self.recv[0].astype(f32) + self.recv[2].astype(f32)

        def wait_sends(self):
            for j in range(3):
                self.copy(j, z1_dev).wait_send()

    grad_o = Spread(chunk_out, z_send_o, z_recv_o)
    grad_q = Spread(chunk_query, z_send_q, z_recv_q)

    sem_kv_x, sem_kv_z1, sem_kv_z2, sem_kv_own = take(4), take(4), take(4), take(6)
    pair_acc = kv_acc.at[:, pl.ds(0, feat)]
    passes = lax.rem(z + f, 2) == 1

    def head_rows_at(t):
        return pl.ds(t * kv, kv)

    def pair_x_copy(t):
        at = head_rows_at(t)
        return remote(x_send_kv.at[at], x_recv_kv.at[at], sem_kv_x + t, x_dev)

    def pair_z_copy(t):
        at = head_rows_at(t)
        return remote(x_recv_kv.at[at], z_recv_kv.at[at], sem_kv_z1 + t, z1_dev)

    def pair_far_copy(t):
        at = head_rows_at(t)
        dev = (z_2 * 2 + x, t)
        return remote(x_recv_kv.at[at], own_recv.at[1], sem_kv_z2 + t, dev, sem_kv_own + 5)

    def pair_own_copy(t):
        return remote(
            own_send.at[t], own_recv.at[0], sem_kv_own + t, (dp, t), sem_kv_own + 4
        )

    def pair_first():
        x_send_kv[...] = chunk_pair(1 - x).astype(bf16)
        for t in range(4):
            pair_x_copy(t).start()
        pair_acc[...] = chunk_pair(x)

    def pair_step(t, i):
        at = head_rows_at(t)
        if i == 0:
            pair_x_copy(t).wait_recv()
            pair_acc[at, :] += x_recv_kv[at, :].astype(f32)

            @pl.when(passes)
            def _():
                x_recv_kv[at, :] = pair_acc[at, :].astype(bf16)
                pair_z_copy(t).start()

            return

        @pl.when(jnp.logical_not(passes))
        def _():
            pair_z_copy(t).wait_recv()
            pair_acc[at, :] += z_recv_kv[at, :].astype(f32)

        @pl.when(middle)
        def _():
            x_recv_kv[at, :] = pair_acc[at, :].astype(bf16)
            pair_far_copy(t).start()

        @pl.when((z == f) & (f != t))
        def _():
            own_send[t] = pair_acc[at, :].astype(bf16)
            pair_own_copy(t).start()

    def pair_result():
        pair_far_copy(0).wait_recv()
        far = own_recv[1].astype(f32)
        at = pl.ds(feat, feat)

        @pl.when(z == f)
        def _():
            kv_acc[0:kv, at] = kv_acc[head_rows_of(f), pl.ds(0, feat)] + far

        @pl.when(z != f)
        def _():
            pair_own_copy(0).wait_recv()
            kv_acc[0:kv, at] = own_recv[0].astype(f32) + far

    def pair_sends_done():
        for t in range(4):
            pair_x_copy(t).wait_send()
            pl.when(passes)(lambda t=t: pair_z_copy(t).wait_send())
            pl.when(middle)(lambda t=t: pair_far_copy(t).wait_send())

        @pl.when(z == f)
        def _():
            for t in range(4):
                pl.when(f != t)(lambda t=t: pair_own_copy(t).wait_send())

    class Collect:
        def __init__(self, part, index, seen=None):
            self.part, self.index, self.sem = part, index, take(3 * n_cols)
            self.seen = seen

        def core_copy(self, j, k):
            return remote(
                core_send.at[j, :, part_cols(k)],
                core_recv.at[self.index, j, :, part_cols(k)],
                self.sem + j * n_cols + k,
                core_dev,
            )

        def y_copy(self, k):
            return remote(
                core_recv.at[self.index, 0, :, part_cols(k)],
                y_recv.at[self.index, :, part_cols(k)],
                self.sem + 2 * n_cols + k,
                y_dev,
            )

        def product(self, fb, k):
            value = self.part(fb, k)
            if self.seen is not None:
                self.seen(fb, k, value)
            return value

        def send_core(self):
            def core_step(n, carry):
                j, k = n // n_cols, lax.rem(n, n_cols)
                fb = jnp.where(j == 0, f_yc, f_c)
                core_send[j, :, part_cols(k)] = self.product(fb, k).astype(bf16)
                self.core_copy(j, k).start()
                return carry

            lax.fori_loop(0, 2 * n_cols, core_step, 0)

        def send_y(self, first, last):
            def y_step(k, carry):
                value = self.product(f_y, k)
                self.core_copy(0, k).wait_recv()
                value = value + core_recv[self.index, 0, :, part_cols(k)].astype(f32)
                core_recv[self.index, 0, :, part_cols(k)] = value.astype(bf16)
                self.y_copy(k).start()
                return carry

            lax.fori_loop(first, last, y_step, 0)

        def core_sends_done(self):
            for j in range(2):
                for k in range(n_cols):
                    self.core_copy(j, k).wait_send()

        def total(self, k):
            value = self.part(f, k)
            self.core_copy(1, k).wait_recv()
            self.y_copy(k).wait_recv()
            return (
                value
                + core_recv[self.index, 1, :, part_cols(k)].astype(f32)
                + y_recv[self.index, :, part_cols(k)].astype(f32)
            )

        def wait_y_sends(self):
            for k in range(n_cols):
                self.y_copy(k).wait_send()

    def gain_add(index, k, value, weighed):
        products = (value * weighed.astype(f32)).reshape(rows // 8, 8, piece)
        gain_part[index, :, part_cols(k)] += jnp.sum(products, axis=0)

    def part_branch(fb, k):
        return nt(att[...], wo[cols_at(fb, k), :])

    def part_lat(fb, k):
        return nt(sgq[...], wq[cols_at(fb, k), :])

    def seen_lat(fb, k, value):
        gain_add(4 + fb, k, value, lat_all[fb, :, part_cols(k)])

    branch = Collect(part_branch, 0)
    back_lat = Collect(part_lat, 1, seen_lat)
    gain_part[...] = jnp.zeros(gain_part.shape, f32)

    gather_core(cot_all, sem_cot).wait_recv()
    project(acc_q, cot_all, wo, mine, True)
    for k in range(n_rows):
        att[part_rows(k), :] = flip(att_t[:, part_rows(k)])
    pl.when(patient)(cot_across_y)
    branch.send_core()

    hold_own(cot_all, cot_x, sem_cot_x)
    pl.when(urgent)(lambda: hold_own(lat_all, lat_x, sem_lat_x))
    across_core(cot_x, sem_cot_x).wait_recv()
    for p in range(n_rows):
        att_x_copy(p).wait_recv()
    near_j = jnp.where(z // 2 == y, 0, 1)
    grad_o.first(near_j)

    @pl.when(urgent)
    def _():
        pass_on(cot_all, sem_cot, cot_x, sem_cot_x)
        hold_rows(lat_all, lat_x, sem_lat_x)
        hold_rows(cot_all, cot_x, sem_cot_x)

    @pl.when(patient)
    def _():
        wait_on(cot_all, sem_cot)
        rows_core_done(cot_x, sem_cot_x)

    grad_o.first(1 - near_j)
    early = z // 2 != y
    pl.when(early)(grad_o.second)

    pl.when(patient)(lambda: pass_on(cot_all, sem_cot))
    pl.when(urgent)(lambda: wait_on(cot_all, sem_cot))
    project(acc_q, cot_all, wo, theirs, False)
    split_heads(acc_q, ga_rows, ga_cols, None, 1.0)
    branch.send_y(0, 1)

    gkv[:, patches] = jnp.zeros((kv, rows), f32)

    def backward_step(p, carry):
        far_s[...] = nn(ga_rows[p], kv_t[vals, patches])
        near_s[...] = nn(ga_rows[p], kv_t[vals, own_latents(p)])
        for h in range(heads):
            far_p = probs_c[p, head_part(h), :].astype(f32)
            near_p = probs_l[p, head_part(h), :].astype(f32)
            far_d, near_d = far_s[head_part(h), :], near_s[head_part(h), :]
            inner = jnp.sum(far_p * far_d, axis=1, keepdims=True) + jnp.sum(
                near_p * near_d, axis=1, keepdims=True
            )
            far_g[head_part(h), :] = (far_p * (far_d - inner)).astype(bf16)
            near_g[head_part(h), :] = (near_p * (near_d - inner)).astype(bf16)
        grad_query = nn(far_g[...], k_rows[patches, :]) + nn(near_g[...], k_rows[own_latents(p), :])
        total = jnp.zeros((1, ROWS), f32)
        for h in range(heads):
            one = grad_query[head_part(h), :].T * score_scale
            query = q_cols[p, :, head_part(h)].astype(f32)
            total = total + jnp.sum(one * query, axis=0, keepdims=True)
            sgq_t[h * head : (h + 1) * head, part_rows(p)] = (
                one * scale_row[1:2, part_rows(p)]
            ).astype(bf16)
        inners[f, 1:2, part_rows(p)] = total
        sgq_x_copy(p).start()
        gkv[keys, patches] += nn(q_cols[p], far_g[...])
        gkv[keys, own_latents(p)] = nn(q_cols[p], near_g[...])
        gkv[vals, patches] += nn(ga_cols[p], probs_c[p])
        gkv[vals, own_latents(p)] = nn(ga_cols[p], probs_l[p])
        return carry

    lax.fori_loop(0, n_rows, backward_step, 0)
    gkv[keys, :] = gkv[keys, :] * score_scale
    products = jnp.sum(gkv[...] * kv_t[...].astype(f32), axis=0, keepdims=True)
    inners[f, 0:1, :] = products[:, 0:rows]
    inners[f, 1:2, :] += products[:, rows:]
    inner_out = exchange(inners, sem_inner)
    for copy in inner_out:
        copy.start()
    sgkv_all[head_rows_of(f), 0:rows] = (gkv[:, 0:rows] * scale_row[0:1, :]).astype(bf16)
    sgkv_all[head_rows_of(f), rows:] = (gkv[:, rows:] * scale_row[1:2, :]).astype(bf16)
    sem_gkv = take(3)

    def gkv_copy(t, i, dev):
        piece = sgkv_all.at[head_rows_of(t)]
        return remote(piece, piece, sem_gkv + i, dev)

    gkv_copy(f, 0, y_dev).start()
    gkv_copy(f, 1, core_dev).start()
    for k in range(n_rows):
        sgq[part_rows(k), :] = flip(sgq_t[:, part_rows(k)])

    late = jnp.logical_not(early)

    def all_rows_x(buf, held, base):
        for k in range(n_rows):
            rows_x(buf, held, base, k).start()

    @pl.when(patient & early)
    def _():
        across_x(lat_all, lat_x, sem_lat_x).start()
        all_rows_x(cot_all, cot_x, sem_cot_x)

    @pl.when(patient & late)
    def _():
        all_rows_x(cot_all, cot_x, sem_cot_x)
        all_rows_x(lat_all, lat_x, sem_lat_x)

    @pl.when(patient)
    def _():
        across_core(lat_x, sem_lat_x).wait_recv()
        rows_core_done(lat_x, sem_lat_x)

    for p in range(n_rows):
        sgq_x_copy(p).wait_recv()
    grad_q.first(1)
    grad_q.first(0)
    branch.send_y(1, n_cols)
    branch.core_sends_done()
    gkv_copy(f, 0, y_dev).wait_recv()
    gkv_copy(f_y, 2, core_dev).start()
    gkv_copy(f, 1, core_dev).wait_recv()
    gkv_copy(f_y, 2, core_dev).wait_recv()
    pair_first()

    pl.when(patient & early)(lambda: all_rows_x(lat_all, lat_x, sem_lat_x))
    pl.when(patient & late)(lambda: across_x(lat_all, lat_x, sem_lat_x).start())
    back_lat.send_core()
    back_lat.send_y(0, n_cols)

    def patient_own_lat():
        pl.when(patient)(lambda: hold_own(lat_all, lat_x, sem_lat_x))
        pl.when(urgent)(lambda: across_core(lat_x, sem_lat_x).wait_recv())

    def patient_rows(buf, held, base):
        pl.when(patient)(lambda: hold_rows(buf, held, base))
        pl.when(urgent)(lambda: rows_core_done(held, base))

    @pl.when(early)
    def _():
        patient_own_lat()
        grad_q.second()

    @pl.when(late)
    def _():
        patient_rows(cot_all, cot_x, sem_cot_x)
        grad_o.second()

    outs = []

    def put(src, dst, i):
        copy = local_copy(src, dst, i)
        copy.start()
        outs.append(copy)

    for copy in inner_out:
        copy.wait()
    coef_row[...] = (
        scale_row[...]
        * scale_row[...]
        * (inners[0] + inners[1] + inners[2] + inners[3])
        / model_width
    )

    coef_cols = coef_row[...].T
    back_lat.core_sends_done()
    for k in range(n_rows):
        sgc[part_rows(k), :] = flip(sgkv_all[:, part_rows(k)])
        sgl[part_rows(k), :] = flip(sgkv_all[:, part_rows(n_rows + k)])

    def finish_ctx(k, carry):
        value = nn(sgc[...], w_own[:, part_cols(k)])
        gain_add(f, k, value, ctx_own[:, part_cols(k)])
        value = value * gain_ctx[:, cols_at(f, k)]
        value = value - raw_ctx[:, part_cols(k)].astype(f32) * coef_cols[:, 0:1]
        core_send[0, :, part_cols(k)] = value.astype(bf16)
        return carry

    lax.fori_loop(0, n_cols, finish_ctx, 0)
    put(core_send.at[0], out_context, 10)

    def gain_own(k, carry):
        value = part_lat(f, k) + nn(sgl[...], w_own[:, part_cols(k)])
        gain_add(4 + f, k, value, lat_all[f, :, part_cols(k)])
        return carry

    lax.fori_loop(0, n_cols, gain_own, 0)
    for i in range(4):
        gain_sum[i : i + 1, :] = (
            jnp.sum(gain_part[i], axis=0, keepdims=True) / gain_ctx[:, block_cols(i)]
        )
        gain_sum[4 + i : 5 + i, :] = (
            jnp.sum(gain_part[4 + i], axis=0, keepdims=True) / gain_lat[:, block_cols(i)]
        )
    part = width // n_dp

    def dp_cols(d, n):
        return pl.ds(pl.multiple_of(d * part, 128), n * part)

    sem_gain, sem_gain_sum = take(2 * n_hi), take(3)
    gain_targets = [(i, lax.rem(z + i, n_hi) * 2 + x, far_dev(i)) for i in others]
    gain_targets += [(n_hi, z * 2 + 1 - x, x_dev)]
    gain_targets += [(n_hi + i, lax.rem(z + i, n_hi) * 2 + 1 - x, far_x_dev(i)) for i in others]
    gain_copies = [
        remote(gain_sum.at[:, dp_cols(d, 1)], gain_recv.at[i], sem_gain + i, dev)
        for i, d, dev in gain_targets
    ]
    for copy in gain_copies:
        copy.start()

    @pl.when(late)
    def _():
        patient_rows(lat_all, lat_x, sem_lat_x)
        grad_q.second()

    def finish(k, carry):
        value = raw_lat[:, part_cols(k)].astype(f32) + branch.total(k)
        y_recv[0, :, part_cols(k)] = value.astype(bf16)
        return carry

    def finish_lat(k):
        value = back_lat.total(k) + nn(sgl[...], w_own[:, part_cols(k)])
        value = value * gain_lat[:, cols_at(f, k)]
        value = value - raw_lat[:, part_cols(k)].astype(f32) * coef_cols[:, 1:2]
        value = value + cot_all[f, :, part_cols(k)].astype(f32)
        y_recv[1, :, part_cols(k)] = value.astype(bf16)
        put(y_recv.at[1, :, part_cols(k)], out_grad_lat.at[:, part_cols(k)], 20 + k)

    def put_weight(spread, at, out, i):
        spread.final()
        at[...] = dp_acc[...].T
        put(at, out, i)

    pair_step(0, 0)
    pair_step(1, 0)
    pair_step(0, 1)
    pair_step(2, 0)
    pair_step(1, 1)
    pair_step(3, 0)
    lax.fori_loop(0, n_cols, finish, 0)
    put(y_recv.at[0], out_latents, 9)
    pair_step(2, 1)
    finish_lat(0)
    pair_step(3, 1)
    finish_lat(1)
    pl.when(early)(lambda: patient_rows(lat_all, lat_x, sem_lat_x))
    pl.when(late)(patient_own_lat)
    pl.when(early)(lambda: patient_rows(cot_all, cot_x, sem_cot_x))
    put_weight(grad_o, acc_q, out_out, 6)
    finish_lat(2)
    summed = gain_sum[:, dp_cols(dp, 1)]
    for copy in gain_copies:
        copy.wait()
    for i, _, _ in gain_targets:
        summed = summed + gain_recv[i]
    gain_one[f] = summed
    gain_out_copies = exchange(gain_one, sem_gain_sum)
    for copy in gain_out_copies:
        copy.start()
    put_weight(grad_q, far_s.at[:, pl.ds(0, heads * head)], out_query, 7)
    finish_lat(3)
    pair_result()
    for i, out in enumerate((out_key, out_value)):
        put(kv_acc.at[pl.ds(i * head, head), pl.ds(feat, feat)], out, 8 + 5 * i)
    for copy in gain_out_copies:
        copy.wait()
    mine_all = gain_one[0] + gain_one[1] + gain_one[2] + gain_one[3]
    index = lax.broadcasted_iota(jnp.int32, mine_all.shape, 0)
    gain_out[0] = jnp.sum(jnp.where(index == f, mine_all, 0.0), axis=0, keepdims=True)
    gain_out[1] = jnp.sum(jnp.where(index == 4 + f, mine_all, 0.0), axis=0, keepdims=True)
    put(gain_out.at[0], out_gain_c, 2)
    put(gain_out.at[1], out_gain_l, 14)

    for copy in outs:
        copy.wait()
    for buf, base in ((lat_all, sem_lat), (cot_all, sem_cot)):
        gather_done(buf, base)
    for collect in (branch, back_lat):
        collect.wait_y_sends()
    for spread in (grad_o, grad_q):
        spread.wait_sends()
    for buf, held, base in ((lat_all, lat_x, sem_lat_x), (cot_all, cot_x, sem_cot_x)):
        across_x(buf, held, base).wait_send()
        across_core(held, base).wait_send()
        for k in range(n_rows):
            rows_x(buf, held, base, k).wait_send()
            rows_core(held, base, k).wait_send()
    for p in range(n_rows):
        att_x_copy(p).wait_send()
        sgq_x_copy(p).wait_send()
    pair_sends_done()
    w_core().wait_send()
    for i in range(2):
        w_y(y_dev, f_y, i).wait_send()
    for i in others:
        w_z(i).wait_send()
    for i in range(n_hi):
        w_x(i).wait_send()
    for j in range(2):
        kv_core_copy(j).wait_send()
    kv_y_copy().wait_send()
    for i in range(3):
        gkv_copy(f, i, core_dev).wait_send()


def hand_on(*refs):
    n = (len(refs) - 2) // 3
    ins, outs, held, sem_in, sem_out = refs[:n], refs[n : 2 * n], refs[2 * n : 3 * n], *refs[3 * n :]
    take_in = [pltpu.make_async_copy(ins[i], held[i], sem_in.at[i]) for i in range(n)]
    give_out = [pltpu.make_async_copy(held[i], outs[i], sem_out.at[i]) for i in range(n)]
    for copy in take_in:
        copy.start()
    for i in range(n):
        take_in[i].wait()
        give_out[i].start()
    for copy in give_out:
        copy.wait()


def kernel_local(
    n_dp,
    context,
    latents,
    gain_ctx,
    gain_lat,
    w_query,
    key_matrix,
    value_matrix,
    w_out,
    lengths,
    patch_flags,
    cotangent,
):
    rows, width = context.shape
    model_width = gain_ctx.shape[0]
    units = w_query.shape[1]
    kv = 2 * key_matrix.shape[1]
    heads = units // HEAD_DIM
    n_hi = n_dp // 2
    feat = model_width // n_dp
    any_space = pl.BlockSpec(memory_space=pl.ANY)
    block = jax.ShapeDtypeStruct((rows, width), bf16)
    shaped = jax.ShapeDtypeStruct
    out = pl.pallas_call(
        functools.partial(block_kernel, n_dp),
        out_shape=(
            block,
            block,
            block,
            shaped((feat, units), f32),
            shaped((kv // 2, feat), f32),
            shaped((kv // 2, feat), f32),
            shaped((feat, units), f32),
            shaped((1, width // n_dp), f32),
            shaped((1, width // n_dp), f32),
        ),
        in_specs=[any_space] * 11,
        out_specs=(any_space,) * 9,
        scratch_shapes=[
            pltpu.VMEM((1, model_width), f32),
            pltpu.VMEM((1, model_width), f32),
            pltpu.SMEM(lengths.shape, jnp.int32),
            pltpu.VMEM((1, rows), jnp.int32),
            pltpu.VMEM((2, 1, width // n_dp), f32),
            pltpu.VMEM((4, rows, width), bf16),
            pltpu.VMEM((4, rows, width), bf16),
            pltpu.VMEM((rows, width), bf16),
            pltpu.VMEM((rows, width), bf16),
            pltpu.VMEM((rows, width), bf16),
            pltpu.VMEM((model_width, units), bf16),
            pltpu.VMEM((kv, model_width), bf16),
            pltpu.VMEM((4 * kv, width), bf16),
            pltpu.VMEM((model_width, units), bf16),
            pltpu.VMEM((rows, units), f32),
            pltpu.VMEM((4 * kv, 2 * rows), f32),
            pltpu.VMEM((units, rows), bf16),
            pltpu.VMEM((units, rows), bf16),
            pltpu.VMEM((rows // ROWS, heads * ROWS, HEAD_DIM), bf16),
            pltpu.VMEM((rows // ROWS, HEAD_DIM, heads * ROWS), bf16),
            pltpu.VMEM((rows // ROWS, heads * ROWS, HEAD_DIM), bf16),
            pltpu.VMEM((rows // ROWS, HEAD_DIM, heads * ROWS), bf16),
            pltpu.VMEM((2 * rows, HEAD_DIM), bf16),
            pltpu.VMEM((2 * rows, HEAD_DIM), bf16),
            pltpu.VMEM((heads * ROWS, rows), f32),
            pltpu.VMEM((heads * ROWS, ROWS), f32),
            pltpu.VMEM((heads * ROWS, rows), bf16),
            pltpu.VMEM((heads * ROWS, ROWS), bf16),
            pltpu.VMEM((rows, units), bf16),
            pltpu.VMEM((rows, units), bf16),
            pltpu.VMEM((kv, 2 * rows), bf16),
            pltpu.VMEM((2, kv, rows), bf16),
            pltpu.VMEM((2, kv, rows), bf16),
            pltpu.VMEM((kv, rows), bf16),
            pltpu.VMEM((rows // ROWS, heads * ROWS, rows), bf16),
            pltpu.VMEM((rows // ROWS, heads * ROWS, ROWS), bf16),
            pltpu.VMEM((kv, 2 * rows), f32),
            pltpu.VMEM((4 * kv, 2 * rows), bf16),
            pltpu.VMEM((rows, 4 * kv), bf16),
            pltpu.VMEM((rows, 4 * kv), bf16),
            pltpu.VMEM((4, 8, rows), f32),
            pltpu.VMEM((4, 8, rows), f32),
            pltpu.VMEM((8, rows), f32),
            pltpu.VMEM((8, rows), f32),
            pltpu.VMEM((8, 8, width), f32),
            pltpu.VMEM((8, width), f32),
            pltpu.VMEM((2 * n_hi, 8, width // n_dp), f32),
            pltpu.VMEM((4, 8, width // n_dp), f32),
            pltpu.VMEM((2, rows, width), bf16),
            pltpu.VMEM((2, 2, rows, width), bf16),
            pltpu.VMEM((2, rows, width), bf16),
            pltpu.VMEM((4, rows, feat), bf16),
            pltpu.VMEM((4, rows, feat), bf16),
            pltpu.VMEM((units, rows), bf16),
            pltpu.VMEM((units, rows), bf16),
            pltpu.VMEM((3, units, feat), bf16),
            pltpu.VMEM((3, units, feat), bf16),
            pltpu.VMEM((3, units, feat), bf16),
            pltpu.VMEM((3, units, feat), bf16),
            pltpu.VMEM((4 * kv, feat), bf16),
            pltpu.VMEM((4 * kv, feat), bf16),
            pltpu.VMEM((4 * kv, feat), bf16),
            pltpu.VMEM((4, kv, feat), bf16),
            pltpu.VMEM((2, kv, feat), bf16),
            pltpu.VMEM((units, feat), f32),
            pltpu.SemaphoreType.DMA((160,)),
            pltpu.SemaphoreType.DMA((160,)),
            pltpu.SemaphoreType.DMA((24,)),
        ],
        compiler_params=pltpu.CompilerParams(
            collective_id=0, has_side_effects=True, vmem_limit_bytes=64 << 20
        ),
        name="block",
    )(
        context,
        latents,
        cotangent,
        gain_ctx.reshape(1, model_width),
        gain_lat.reshape(1, model_width),
        w_query,
        key_matrix.T,
        value_matrix.T,
        w_out,
        lengths,
        patch_flags.reshape(1, rows),
    )
    out = pl.pallas_call(
        hand_on,
        out_shape=tuple(shaped(a.shape, a.dtype) for a in out),
        in_specs=[any_space] * 9,
        out_specs=(any_space,) * 9,
        scratch_shapes=[pltpu.VMEM(a.shape, a.dtype) for a in out]
        + [pltpu.SemaphoreType.DMA((9,)), pltpu.SemaphoreType.DMA((9,))],
        compiler_params=pltpu.CompilerParams(vmem_limit_bytes=64 << 20),
        name="hand_on",
    )(*out)
    latents_out, grad_context, grad_latents, g_query, g_key, g_value, g_out, gain_c, gain_l = out
    return (
        latents_out,
        grad_context,
        grad_latents,
        g_query,
        g_key.T,
        g_value.T,
        g_out,
        gain_c,
        gain_l,
    )


def solution(mesh):
    n_dp = mesh.shape["dp"]
    body = functools.partial(kernel_local, n_dp) if n_dp == 8 else plain_local
    return jax.shard_map(
        body,
        mesh=mesh,
        in_specs=(
            P("dp", "tensor"),
            P("dp", "tensor"),
            P(),
            P(),
            P(None, "tensor"),
            P(None, "tensor"),
            P(None, "tensor"),
            P(None, "tensor"),
            P("dp", None),
            P("dp"),
            P("dp", "tensor"),
        ),
        out_specs=(
            P("dp", "tensor"),
            P("dp", "tensor"),
            P("dp", "tensor"),
            P("dp", "tensor"),
            P("dp", "tensor"),
            P("dp", "tensor"),
            P("dp", "tensor"),
            P("tensor", "dp"),
            P("tensor", "dp"),
        ),
        check_vma=False,
    )
```

```python
import functools

import jax
import jax.numpy as jnp
from jax import lax
from jax.experimental import pallas as pl
from jax.experimental.pallas import tpu as pltpu
from jax.sharding import PartitionSpec as P

HEAD_DIM = 96
LAT = 64


epsilon = 1e-06
masked_value = -1e30
contract_rows = (((0,), (0,)), ((), ()))
contract_cols = (((1,), (1,)), ((), ()))


def row_scales(rows_in):
    values_f = rows_in.astype(jnp.float32)
    return (values_f, lax.rsqrt(jnp.mean(values_f * values_f, axis=1) + epsilon))


def norm_back(grad_norm, local_vals, row_scale, gain_local, row_inner_all, model_width):
    weighted = grad_norm * gain_local
    grad_input = (
        row_scale[:, None] * weighted
        - local_vals * (row_scale**3 * row_inner_all / model_width)[:, None]
    )
    grad_gain = jnp.sum(grad_norm * local_vals * row_scale[:, None], axis=0)
    return (grad_input, grad_gain)


def plain_local(
    context,
    latents,
    gain_ctx,
    gain_lat,
    w_query,
    key_matrix,
    value_matrix,
    w_out,
    lengths,
    patch_flags,
    cotangent,
):
    patch_rows = context.shape[0]
    latent_rows = latents.shape[0]
    local_width = context.shape[1]
    model_width = gain_ctx.shape[0]
    head_size = HEAD_DIM
    kv_local = key_matrix.shape[1] // head_size
    query_local = w_query.shape[1] // head_size
    repeat = query_local // kv_local
    all_count = patch_rows + latent_rows
    score_scale = head_size ** (-0.5)
    column = lax.axis_index("tensor") * local_width
    whole_ctx, whole_lat = (
        lax.all_gather(context, "tensor", axis=1, tiled=True),
        lax.all_gather(latents, "tensor", axis=1, tiled=True),
    )
    ctx_values, ctx_scale = row_scales(whole_ctx)
    lat_values, lat_scale = row_scales(whole_lat)
    ctx_norm = (ctx_values * ctx_scale[:, None] * gain_ctx).astype(jnp.bfloat16)
    lat_norm = (lat_values * lat_scale[:, None] * gain_lat).astype(jnp.bfloat16)
    queries = jnp.dot(lat_norm, w_query, preferred_element_type=jnp.float32).astype(jnp.bfloat16)
    all_rows = jnp.concatenate([ctx_norm, lat_norm], axis=0)
    w_pair = jnp.concatenate([key_matrix, value_matrix], axis=1)
    pair_rows = jnp.dot(all_rows, w_pair, preferred_element_type=jnp.float32).astype(jnp.bfloat16)
    key_head_split = (
        pair_rows[:, : kv_local * head_size]
        .reshape(all_count, kv_local, head_size)
        .transpose(1, 0, 2)
    )
    value_head_split = (
        pair_rows[:, kv_local * head_size :]
        .reshape(all_count, kv_local, head_size)
        .transpose(1, 0, 2)
    )
    query_heads = queries.reshape(latent_rows, query_local, head_size).transpose(1, 0, 2)
    image_ends = jnp.cumsum(lengths[0])
    patch_image = jnp.sum(
        (jnp.arange(patch_rows)[:, None] >= image_ends[None, :]).astype(jnp.int32), axis=1
    )
    latent_image = jnp.arange(latent_rows) // LAT
    allowed = jnp.concatenate(
        [
            (latent_image[:, None] == patch_image[None, :]) & (patch_flags[None, :] == 1),
            latent_image[:, None] == latent_image[None, :],
        ],
        axis=1,
    )
    head_index = jnp.arange(query_local)

    def head_scores(query_head, head_number):
        key_head = key_head_split[head_number // repeat]
        value_head = value_head_split[head_number // repeat]
        raw_scores = (
            lax.dot_general(query_head, key_head, contract_cols, preferred_element_type=jnp.float32)
            * score_scale
        )
        return (jnp.where(allowed, raw_scores, masked_value), key_head, value_head)

    def head_forward(member):
        query_head, head_number = member
        scores, key_head, value_head = head_scores(query_head, head_number)
        row_top = jnp.max(scores, axis=1, keepdims=True)
        exp_scores = jnp.exp(scores - row_top)
        row_total = jnp.sum(exp_scores, axis=1, keepdims=True)
        attention = (exp_scores / row_total).astype(jnp.bfloat16)
        blended = jnp.dot(attention, value_head, preferred_element_type=jnp.float32).astype(
            jnp.bfloat16
        )
        return (blended, row_top[:, 0] + jnp.log(row_total[:, 0]))

    heads_out, log_totals = lax.map(head_forward, (query_heads, head_index))
    attended = heads_out.transpose(1, 0, 2).reshape(latent_rows, query_local * head_size)
    partial_out = lax.dot_general(
        attended, w_out, contract_cols, preferred_element_type=jnp.float32
    )
    branch = lax.psum_scatter(
        partial_out.astype(jnp.bfloat16), "tensor", scatter_dimension=1, tiled=True
    ).astype(jnp.float32)
    latents_out = (latents.astype(jnp.float32) + branch).astype(jnp.bfloat16)
    full_grad = lax.all_gather(cotangent, "tensor", axis=1, tiled=True)
    grad_attended = jnp.dot(full_grad, w_out, preferred_element_type=jnp.float32).astype(
        jnp.bfloat16
    )
    grad_w_out = lax.dot_general(
        full_grad, attended, contract_rows, preferred_element_type=jnp.float32
    )
    grad_heads = grad_attended.reshape(latent_rows, query_local, head_size).transpose(1, 0, 2)

    def head_backward(member):
        query_head, grad_blended, log_total, head_number = member
        scores, key_head, value_head = head_scores(query_head, head_number)
        attention = jnp.exp(scores - log_total[:, None])
        grad_probs = lax.dot_general(
            grad_blended, value_head, contract_cols, preferred_element_type=jnp.float32
        )
        row_inner = jnp.sum(attention * grad_probs, axis=1, keepdims=True)
        grad_scores = (attention * (grad_probs - row_inner)).astype(jnp.bfloat16)
        grad_query = (
            jnp.dot(grad_scores, key_head, preferred_element_type=jnp.float32) * score_scale
        ).astype(jnp.bfloat16)
        grad_key = (
            lax.dot_general(
                grad_scores, query_head, contract_rows, preferred_element_type=jnp.float32
            )
            * score_scale
        )
        grad_value = lax.dot_general(
            attention.astype(jnp.bfloat16),
            grad_blended,
            contract_rows,
            preferred_element_type=jnp.float32,
        )
        return (grad_query, grad_key, grad_value)

    grad_query_heads, grad_key_heads, grad_value_heads = lax.map(
        head_backward, (query_heads, grad_heads, log_totals, head_index)
    )
    grad_keys = grad_key_heads.reshape(kv_local, repeat, all_count, head_size).sum(axis=1)
    grad_values = grad_value_heads.reshape(kv_local, repeat, all_count, head_size).sum(axis=1)
    grad_pair = jnp.concatenate(
        [
            grad_keys.transpose(1, 0, 2).reshape(all_count, kv_local * head_size),
            grad_values.transpose(1, 0, 2).reshape(all_count, kv_local * head_size),
        ],
        axis=1,
    ).astype(jnp.bfloat16)
    grad_q_rows = grad_query_heads.transpose(1, 0, 2).reshape(latent_rows, query_local * head_size)
    grad_w_query = lax.dot_general(
        lat_norm, grad_q_rows, contract_rows, preferred_element_type=jnp.float32
    )
    grad_w_pair = lax.dot_general(
        all_rows, grad_pair, contract_rows, preferred_element_type=jnp.float32
    )
    grad_rows = lax.dot_general(
        grad_pair, w_pair, contract_cols, preferred_element_type=jnp.float32
    )
    lat_terms = grad_rows[patch_rows:] + lax.dot_general(
        grad_q_rows, w_query, contract_cols, preferred_element_type=jnp.float32
    )
    grad_ctx_norm, grad_lat_norm = (
        lax.psum_scatter(
            grad_rows[:patch_rows].astype(jnp.bfloat16), "tensor", scatter_dimension=1, tiled=True
        ).astype(jnp.float32),
        lax.psum_scatter(
            lat_terms.astype(jnp.bfloat16), "tensor", scatter_dimension=1, tiled=True
        ).astype(jnp.float32),
    )
    ctx_local = context.astype(jnp.float32)
    lat_local = latents.astype(jnp.float32)
    gain_ctx_local = lax.dynamic_slice_in_dim(gain_ctx, column, local_width, 0)
    gain_lat_local = lax.dynamic_slice_in_dim(gain_lat, column, local_width, 0)
    ctx_inner = jnp.sum(grad_ctx_norm * gain_ctx_local * ctx_local, axis=1)
    lat_inner = jnp.sum(grad_lat_norm * gain_lat_local * lat_local, axis=1)
    ctx_inner_all, lat_inner_all = lax.psum((ctx_inner, lat_inner), "tensor")
    grad_ctx_in, grad_gain_c = norm_back(
        grad_ctx_norm, ctx_local, ctx_scale, gain_ctx_local, ctx_inner_all, model_width
    )
    grad_lat_in, grad_gain_l = norm_back(
        grad_lat_norm, lat_local, lat_scale, gain_lat_local, lat_inner_all, model_width
    )
    grad_context = grad_ctx_in.astype(jnp.bfloat16)
    grad_latents = (cotangent.astype(jnp.float32) + grad_lat_in).astype(jnp.bfloat16)
    grad_w_key = grad_w_pair[:, : kv_local * head_size]
    grad_w_value = grad_w_pair[:, kv_local * head_size :]
    sum_query, sum_key, sum_value, sum_out, sum_gain_c, sum_gain_l = (
        lax.psum_scatter(grad_w_query, "dp", scatter_dimension=0, tiled=True),
        lax.psum_scatter(grad_w_key, "dp", scatter_dimension=0, tiled=True),
        lax.psum_scatter(grad_w_value, "dp", scatter_dimension=0, tiled=True),
        lax.psum_scatter(grad_w_out, "dp", scatter_dimension=0, tiled=True),
        lax.psum_scatter(grad_gain_c, "dp", scatter_dimension=0, tiled=True),
        lax.psum_scatter(grad_gain_l, "dp", scatter_dimension=0, tiled=True),
    )
    return (
        latents_out,
        grad_context,
        grad_latents,
        sum_query,
        sum_key,
        sum_value,
        sum_out,
        sum_gain_c.reshape(1, -1),
        sum_gain_l.reshape(1, -1),
    )


MESH = pl.DeviceIdType.MESH
f32 = jnp.float32
bf16 = jnp.bfloat16
ROWS = 128
LOG2_E = 1.4426950408889634


def nn(a, b):
    return jnp.dot(a, b, preferred_element_type=f32)


def nt(a, b):
    return lax.dot_general(a, b, contract_cols, preferred_element_type=f32)


def flip(a):
    return a.astype(f32).T.astype(bf16)


def block_kernel(
    n_dp,
    context,
    latents,
    cotangent,
    gain_ctx_in,
    gain_lat_in,
    w_query,
    key_across,
    value_across,
    w_out,
    lengths_in,
    flags_in,
    out_latents,
    out_context,
    out_grad_lat,
    out_query,
    out_key,
    out_value,
    out_out,
    out_gain_c,
    out_gain_l,
    gain_ctx,
    gain_lat,
    lengths,
    flags,
    gain_out,
    lat_all,
    cot_all,
    ctx_own,
    raw_lat,
    raw_ctx,
    wq,
    wkv,
    w_own,
    wo,
    acc_q,
    kv_acc,
    att_t,
    sgq_t,
    q_rows,
    q_cols,
    ga_rows,
    ga_cols,
    k_rows,
    v_rows,
    far_s,
    near_s,
    far_g,
    near_g,
    att,
    sgq,
    kv_t,
    kv_send,
    kv_core,
    kv_y,
    probs_c,
    probs_l,
    gkv,
    sgkv_all,
    sgc,
    sgl,
    sums,
    inners,
    scale_row,
    coef_row,
    gain_part,
    gain_sum,
    gain_recv,
    gain_all,
    core_send,
    core_recv,
    y_recv,
    lat_x,
    cot_x,
    att_xt,
    sgq_xt,
    z_send_o,
    z_send_q,
    z_recv_o,
    z_recv_q,
    x_send_kv,
    x_recv_kv,
    z_recv_kv,
    own_send,
    own_recv,
    dp_acc,
    send_sem,
    recv_sem,
    local_sem,
):
    rows, width = raw_lat.shape
    n_rows = rows // ROWS
    n_hi = n_dp // 2
    feat = 4 * width // n_dp
    head = HEAD_DIM
    heads = acc_q.shape[1] // head
    model_width = 4 * width
    score_scale = head ** (-0.5)

    dp = lax.axis_index("dp")
    f = lax.axis_index("tensor")
    z, x = dp // 2, lax.rem(dp, 2)
    y, c = f // 2, lax.rem(f, 2)
    f_c = y * 2 + (1 - c)
    f_y = (1 - y) * 2 + c
    f_yc = (1 - y) * 2 + (1 - c)
    core_dev, y_dev, yc_dev = (dp, f_c), (dp, f_y), (dp, f_yc)
    x_dev = (z * 2 + 1 - x, f)
    z_1 = z + 1 - 2 * lax.rem(z, 2)
    z_2 = z + 2 - 4 * (z // 2)
    z1_dev, z2_dev = (z_1 * 2 + x, f), (z_2 * 2 + x, f)
    x_mine = pl.ds(pl.multiple_of(x * feat, 128), feat)
    x_other = pl.ds(pl.multiple_of((1 - x) * feat, 128), feat)

    urgent = lax.rem(c + z, 2) == 1
    patient = jnp.logical_not(urgent)

    count = [0]

    def take(n):
        count[0] += n
        return count[0] - n

    def remote(src, dst, sem, dev, sem_to=None):
        return pltpu.make_async_remote_copy(
            src_ref=src,
            dst_ref=dst,
            send_sem=send_sem.at[sem],
            recv_sem=recv_sem.at[sem if sem_to is None else sem_to],
            device_id=dev,
            device_id_type=MESH,
        )

    def local_copy(src, dst, i):
        return pltpu.make_async_copy(src, dst, local_sem.at[i])

    def part_rows(k):
        if isinstance(k, int):
            return pl.ds(k * ROWS, ROWS)
        return pl.ds(pl.multiple_of(k * ROWS, ROWS), ROWS)

    n_cols = 4
    piece = width // n_cols

    def part_cols(k):
        if isinstance(k, int):
            return pl.ds(k * piece, piece)
        return pl.ds(pl.multiple_of(k * piece, 128), piece)

    def cols_at(fb, k):
        return pl.ds(pl.multiple_of(fb * width + k * piece, 128), piece)

    def block_cols(fb):
        if isinstance(fb, int):
            return pl.ds(fb * width, width)
        return pl.ds(pl.multiple_of(fb * width, width), width)

    loads = [
        local_copy(latents, raw_lat, 0),
        local_copy(key_across, wkv.at[pl.ds(0, head)], 4),
        local_copy(value_across, wkv.at[pl.ds(head, head)], 14),
        local_copy(context, raw_ctx, 1),
        local_copy(cotangent, cot_all.at[f], 13),
        local_copy(w_query, wq, 3),
        local_copy(w_out, wo, 5),
    ]
    small = [
        local_copy(gain_lat_in, gain_lat, 2),
        local_copy(gain_ctx_in, gain_ctx, 6),
        local_copy(lengths_in, lengths, 7),
        local_copy(flags_in, flags, 8),
    ]
    for load in small[:1] + loads + small[1:]:
        load.start()

    barrier = pltpu.get_barrier_semaphore()

    def greet(dev):
        pl.semaphore_signal(barrier, inc=1, device_id=dev, device_id_type=MESH)

    others = [i for i in range(1, n_hi)]

    def far_dev(i):
        return (lax.rem(z + i, n_hi) * 2 + x, f)

    def far_x_dev(i):
        return (lax.rem(z + i, n_hi) * 2 + 1 - x, f)

    always = [core_dev, y_dev, yc_dev, x_dev] + [far_dev(i) for i in others]
    always += [far_x_dev(i) for i in others]
    for dev in always:
        greet(dev)
    pl.when(z != f)(lambda: greet((z_2 * 2 + x, z)))

    def weigh(raw, gain, buf):
        gain_row = gain[:, block_cols(f)]
        for k in range(n_rows):
            values = raw[part_rows(k), :].astype(f32)
            buf[part_rows(k), :] = (values * gain_row).astype(bf16)

    small[0].wait()
    loads[0].wait()
    weigh(raw_lat, gain_lat, lat_all.at[f])
    middle = z_2 == f
    pl.semaphore_wait(barrier, len(always) + 3 * middle.astype(jnp.int32))

    sem_lat, sem_cot = (take(2 * n_rows + 1) for _ in range(2))

    def gather_y(buf, base, k):
        return remote(buf.at[f, part_rows(k)], buf.at[f, part_rows(k)], base + k, y_dev)

    def gather_core(buf, base):
        return remote(buf.at[f], buf.at[f], base + n_rows, core_dev)

    def gather_on(buf, base, k):
        return remote(
            buf.at[f_y, part_rows(k)], buf.at[f_y, part_rows(k)], base + n_rows + 1 + k, core_dev
        )

    def pass_on(buf, base, held=None, base_x=None):
        def step(k, carry):
            gather_y(buf, base, k).wait_recv()
            gather_on(buf, base, k).start()
            if held is not None:
                rows_x(buf, held, base_x, k).start()
            return carry

        lax.fori_loop(0, n_rows, step, 0)

    def wait_on(buf, base):
        for k in range(n_rows):
            gather_on(buf, base, k).wait_recv()

    def gather_done(buf, base):
        for k in range(n_rows):
            gather_y(buf, base, k).wait_send()
            gather_on(buf, base, k).wait_send()
        gather_core(buf, base).wait_send()

    def square_sums(raw, index):
        for k in range(n_rows):
            values = raw[part_rows(k), :].astype(f32)
            total = jnp.sum(values * values, axis=1, keepdims=True)
            across = jnp.broadcast_to(total, (ROWS, 128)).T
            sums[f, pl.ds(index, 1), part_rows(k)] = across[0:1, :]

    sem_lat_x, sem_cot_x = take(2 * n_rows + 2), take(2 * n_rows + 2)
    sem_att_x, sem_sgq_x = take(n_rows), take(n_rows)

    def across_x(buf, held, base):
        return remote(buf.at[f, :, x_other], held.at[f], base, x_dev)

    def across_core(held, base):
        return remote(held.at[f], held.at[f], base + 1, core_dev)

    def rows_x(buf, held, base, k):
        return remote(
            buf.at[f_y, part_rows(k), x_other], held.at[f_y, part_rows(k)], base + 2 + k, x_dev
        )

    def rows_core(held, base, k):
        piece = held.at[f_y, part_rows(k)]
        return remote(piece, piece, base + 2 + n_rows + k, core_dev)

    def hold_own(buf, held, base):
        across_x(buf, held, base).wait_recv()
        across_core(held, base).start()

    def hold_rows(buf, held, base):
        def step(k, carry):
            rows_x(buf, held, base, k).wait_recv()
            rows_core(held, base, k).start()
            return carry

        lax.fori_loop(0, n_rows, step, 0)

    def rows_core_done(held, base):
        for k in range(n_rows):
            rows_core(held, base, k).wait_recv()

    kv = 2 * head
    slice_width = width // n_dp
    pair_rows = pl.ds(pl.multiple_of((1 - y) * 2 * kv, 64), 2 * kv)
    sem_w_core, sem_w_y, sem_w_z, sem_w_x = take(1), take(2), take(n_hi), take(n_hi)

    def head_rows_of(t):
        return pl.ds(pl.multiple_of(t * kv, 64), kv)

    def slice_cols(d, at=0):
        return pl.ds(pl.multiple_of(at + d * slice_width, 128), slice_width)

    def w_y(dev, f_to, i, sender=c):
        return remote(
            wkv.at[:, slice_cols(dp, f_to * width)],
            w_own.at[head_rows_of(f), slice_cols(dp)],
            sem_w_y + i,
            dev,
            sem_w_y + sender,
        )

    def w_core():
        return remote(
            wkv.at[:, block_cols(f_c)], w_own.at[head_rows_of(f)], sem_w_core, core_dev
        )

    def w_z(i):
        piece = w_own.at[pair_rows, slice_cols(dp)]
        return remote(piece, piece, sem_w_z + i, far_dev(i))

    def w_x(i):
        piece = w_own.at[pair_rows, slice_cols(lax.rem(z + i, n_hi) * 2 + x)]
        return remote(piece, piece, sem_w_x + lax.rem(z + i, n_hi), x_dev)

    loads[1].wait()
    loads[2].wait()
    w_y(y_dev, f_y, 0).start()
    w_y(yc_dev, f_yc, 1).start()
    w_core().start()
    for k in range(n_rows):
        gather_y(lat_all, sem_lat, k).start()
    gather_core(lat_all, sem_lat).start()
    loads[4].wait()
    gather_core(cot_all, sem_cot).start()
    across_x(cot_all, cot_x, sem_cot_x).start()
    sums[f] = jnp.zeros(sums.shape[1:], f32)
    inners[f] = jnp.zeros(inners.shape[1:], f32)
    loads[3].wait()
    for load in small[1:]:
        load.wait()
    weigh(raw_ctx, gain_ctx, ctx_own)
    for i in range(2):
        w_y(y_dev, f_y, i, i).wait_recv()
    for i in others:
        w_z(i).start()
    w_x(0).start()
    w_own[head_rows_of(f), :] = wkv[:, block_cols(f)]
    square_sums(raw_lat, 1)
    square_sums(raw_ctx, 0)

    peers = [core_dev, y_dev, yc_dev]
    sem_sums, sem_inner = take(3), take(3)

    def exchange(buf, base):
        return [remote(buf.at[f], buf.at[f], base + i, dev) for i, dev in enumerate(peers)]

    sums_out = exchange(sums, sem_sums)
    for copy in sums_out:
        copy.start()

    def project(acc, values, weight, blocks, first):
        def step(i, carry):
            fb = blocks[0] + i * (blocks[1] - blocks[0])
            for m in range(2):
                half = pl.ds(m * (rows // 2), rows // 2)
                product = nn(values[fb, half, :], weight[block_cols(fb), :])
                if first:
                    @pl.when(i == 0)
                    def _():
                        acc[half, :] = product

                    @pl.when(i > 0)
                    def _():
                        acc[half, :] += product
                else:
                    acc[half, :] += product
            return carry

        lax.fori_loop(0, 2, step, 0)

    def project_pair(blocks, first):
        latent_cols = pl.ds(rows, rows)
        for i, fb in enumerate(blocks):
            product = nt(wkv[:, block_cols(fb)], lat_all[fb])
            if first and i == 0:
                kv_acc[0:kv, latent_cols] = product
            else:
                kv_acc[0:kv, latent_cols] += product

    mine, theirs = (f, f_c), (f_y, f_yc)
    loads[5].wait()
    loads[6].wait()
    gather_core(lat_all, sem_lat).wait_recv()
    project(acc_q, lat_all, wq, mine, True)
    project_pair(mine, True)
    for i in others:
        w_z(n_hi - i).wait_recv()
        w_x(i).start()
    w_core().wait_recv()
    pl.when(urgent)(lambda: across_x(lat_all, lat_x, sem_lat_x).start())
    for i in range(n_hi):
        w_x(i).wait_recv()

    sem_kv_core, sem_kv_y = take(2), take(1)

    def kv_core_copy(j):
        return remote(kv_send.at[j], kv_core.at[j], sem_kv_core + j, core_dev)

    def kv_y_copy():
        return remote(kv_core.at[0], kv_y, sem_kv_y, y_dev)

    patches = pl.ds(0, rows)
    for n in range(2):
        half = slice(n * (rows // 2), (n + 1) * (rows // 2))
        kv_acc[:, half] = nt(w_own[...], ctx_own[half, :])
    for j, t in enumerate((f_yc, f_c)):
        kv_send[j] = kv_acc[head_rows_of(t), patches].astype(bf16)
        kv_core_copy(j).start()
    kv_core_copy(0).wait_recv()
    kv_core[0] = (kv_acc[head_rows_of(f_y), patches] + kv_core[0].astype(f32)).astype(bf16)
    kv_y_copy().start()

    def cot_across_y():
        for k in range(n_rows):
            gather_y(cot_all, sem_cot, k).start()

    pl.when(urgent)(cot_across_y)

    pl.when(urgent)(lambda: pass_on(lat_all, sem_lat, lat_x, sem_lat_x))
    pl.when(patient)(lambda: pass_on(lat_all, sem_lat))
    wait_on(lat_all, sem_lat)
    project(acc_q, lat_all, wq, theirs, False)
    project_pair(theirs, False)

    for copy in sums_out:
        copy.wait()
    total = sums[0] + sums[1] + sums[2] + sums[3]
    scale_row[...] = lax.rsqrt(total / model_width + epsilon)

    def split_heads(across, p, by_rows, by_cols, factor):
        for h in range(heads):
            one = across[h * head : (h + 1) * head, :]
            at = pl.ds(h * ROWS, ROWS)
            by_cols[p, :, at] = one.astype(bf16)
            by_rows[p, at, :] = (one * factor).T.astype(bf16)

    def kv_by_rows(first):
        for n in range(first, first + n_rows):
            k_rows[part_rows(n), :] = flip(kv_t[0:head, part_rows(n)])
            v_rows[part_rows(n), :] = flip(kv_t[head:, part_rows(n)])

    for k in range(n_rows):
        across = acc_q[part_rows(k), :].T * scale_row[1:2, part_rows(k)]
        split_heads(across, k, q_rows, q_cols, score_scale * LOG2_E)
    kv_t[:, rows:] = (kv_acc[0:kv, rows:] * scale_row[1:2, :]).astype(bf16)
    kv_by_rows(n_rows)
    kv_core_copy(1).wait_recv()
    kv_y_copy().wait_recv()
    summed = kv_acc[head_rows_of(f), patches] + kv_core[1].astype(f32) + kv_y[...].astype(f32)
    kv_t[:, 0:rows] = (summed * scale_row[0:1, :]).astype(bf16)
    kv_by_rows(0)

    patch = lax.broadcasted_iota(jnp.int32, (1, rows), 1)
    image = jnp.zeros((1, rows), jnp.int32)
    end = jnp.int32(0)
    for i in range(lengths.shape[1]):
        end = end + lengths[0, i]
        image = image + (patch >= end).astype(jnp.int32)
    image = jnp.where(flags[...] == 1, image, -1)
    per_part = ROWS // LAT
    row_image = lax.broadcasted_iota(jnp.int32, (ROWS, 1), 0) // LAT
    col_image = lax.broadcasted_iota(jnp.int32, (1, ROWS), 1) // LAT
    same = row_image == col_image
    keys, vals = pl.ds(0, head), pl.ds(head, head)
    def own_latents(p):
        return pl.ds(pl.multiple_of(rows + p * ROWS, ROWS), ROWS)


    def head_part(h):
        return slice(h * ROWS, (h + 1) * ROWS)

    def att_x_copy(p):
        cols = part_rows(p)
        return remote(att_t.at[:, cols], att_xt.at[:, cols], sem_att_x + p, x_dev)

    def sgq_x_copy(p):
        cols = part_rows(p)
        return remote(sgq_t.at[:, cols], sgq_xt.at[:, cols], sem_sgq_x + p, x_dev)

    def forward_step(p, carry):
        far_s[...] = nn(q_rows[p], kv_t[keys, patches])
        near_s[...] = nn(q_rows[p], kv_t[keys, own_latents(p)])
        allowed = (row_image + p * per_part) == image
        for h in range(heads):
            far = jnp.where(allowed, far_s[head_part(h), :], masked_value)
            near = jnp.where(same, near_s[head_part(h), :], masked_value)
            top = jnp.maximum(
                jnp.max(far, axis=1, keepdims=True), jnp.max(near, axis=1, keepdims=True)
            )
            far, near = jnp.exp2(far - top), jnp.exp2(near - top)
            total = jnp.sum(far, axis=1, keepdims=True) + jnp.sum(near, axis=1, keepdims=True)
            inverse = 1.0 / total
            probs_c[p, head_part(h), :] = (far * inverse).astype(bf16)
            probs_l[p, head_part(h), :] = (near * inverse).astype(bf16)
        blended = nn(probs_c[p], v_rows[patches, :]) + nn(probs_l[p], v_rows[own_latents(p), :])
        for h in range(heads):
            one = blended[head_part(h), :]
            att_t[h * head : (h + 1) * head, part_rows(p)] = one.T.astype(bf16)
        att_x_copy(p).start()
        return carry

    lax.fori_loop(0, n_rows, forward_step, 0)
    def chunk_out(zt):
        return nn(att_t[...], cot_all[zt, :, x_mine]) + nn(att_xt[...], cot_x[zt])

    def chunk_query(zt):
        return nn(sgq_t[...], lat_all[zt, :, x_mine]) + nn(sgq_xt[...], lat_x[zt])

    def chunk_pair(xt):
        cols = pl.ds(pl.multiple_of(xt * feat, 128), feat)
        return nn(sgkv_all[:, patches], ctx_own[:, cols]) + nn(
            sgkv_all[:, pl.ds(rows, rows)], lat_all[f, :, cols]
        )

    class Spread:
        def __init__(self, chunk, send, recv):
            self.chunk, self.send, self.recv, self.sem = chunk, send, recv, take(3)

        def copy(self, j, dev):
            return remote(self.send.at[j], self.recv.at[j], self.sem + j, dev)

        def first(self, j):
            zt = z_1 + j * (z_2 - z)
            self.send[j] = self.chunk(zt).astype(bf16)
            self.copy(j, z1_dev).start()

        def second(self):
            value = self.chunk(z_2)
            self.copy(1, z1_dev).wait_recv()
            self.send[2] = (value + self.recv[1].astype(f32)).astype(bf16)
            self.copy(2, z2_dev).start()

        def final(self):
            dp_acc[...] = self.chunk(z)
            self.copy(0, z1_dev).wait_recv()
            self.copy(2, z2_dev).wait_recv()
            dp_acc[...] += self.recv[0].astype(f32) + self.recv[2].astype(f32)

        def wait_sends(self):
            for j in range(3):
                self.copy(j, z1_dev).wait_send()

    grad_o = Spread(chunk_out, z_send_o, z_recv_o)
    grad_q = Spread(chunk_query, z_send_q, z_recv_q)

    sem_kv_x, sem_kv_z1, sem_kv_z2, sem_kv_own = take(4), take(4), take(4), take(6)
    pair_acc = kv_acc.at[:, pl.ds(0, feat)]
    passes = lax.rem(z + f, 2) == 1

    def head_rows_at(t):
        return pl.ds(t * kv, kv)

    def pair_x_copy(t):
        at = head_rows_at(t)
        return remote(x_send_kv.at[at], x_recv_kv.at[at], sem_kv_x + t, x_dev)

    def pair_z_copy(t):
        at = head_rows_at(t)
        return remote(x_recv_kv.at[at], z_recv_kv.at[at], sem_kv_z1 + t, z1_dev)

    def pair_far_copy(t):
        at = head_rows_at(t)
        dev = (z_2 * 2 + x, t)
        return remote(x_recv_kv.at[at], own_recv.at[1], sem_kv_z2 + t, dev, sem_kv_own + 5)

    def pair_own_copy(t):
        return remote(
            own_send.at[t], own_recv.at[0], sem_kv_own + t, (dp, t), sem_kv_own + 4
        )

    def pair_first():
        x_send_kv[...] = chunk_pair(1 - x).astype(bf16)
        for t in range(4):
            pair_x_copy(t).start()
        pair_acc[...] = chunk_pair(x)

    def pair_step(t, i):
        at = head_rows_at(t)
        if i == 0:
            pair_x_copy(t).wait_recv()
            pair_acc[at, :] += x_recv_kv[at, :].astype(f32)

            @pl.when(passes)
            def _():
                x_recv_kv[at, :] = pair_acc[at, :].astype(bf16)
                pair_z_copy(t).start()

            return

        @pl.when(jnp.logical_not(passes))
        def _():
            pair_z_copy(t).wait_recv()
            pair_acc[at, :] += z_recv_kv[at, :].astype(f32)

        @pl.when(middle)
        def _():
            x_recv_kv[at, :] = pair_acc[at, :].astype(bf16)
            pair_far_copy(t).start()

        @pl.when((z == f) & (f != t))
        def _():
            own_send[t] = pair_acc[at, :].astype(bf16)
            pair_own_copy(t).start()

    def pair_result():
        pair_far_copy(0).wait_recv()
        far = own_recv[1].astype(f32)
        at = pl.ds(feat, feat)

        @pl.when(z == f)
        def _():
            kv_acc[0:kv, at] = kv_acc[head_rows_of(f), pl.ds(0, feat)] + far

        @pl.when(z != f)
        def _():
            pair_own_copy(0).wait_recv()
            kv_acc[0:kv, at] = own_recv[0].astype(f32) + far

    def pair_sends_done():
        for t in range(4):
            pair_x_copy(t).wait_send()
            pl.when(passes)(lambda t=t: pair_z_copy(t).wait_send())
            pl.when(middle)(lambda t=t: pair_far_copy(t).wait_send())

        @pl.when(z == f)
        def _():
            for t in range(4):
                pl.when(f != t)(lambda t=t: pair_own_copy(t).wait_send())

    class Collect:
        def __init__(self, part, index, seen=None):
            self.part, self.index, self.sem = part, index, take(3 * n_cols)
            self.seen = seen

        def core_copy(self, j, k):
            return remote(
                core_send.at[j, :, part_cols(k)],
                core_recv.at[self.index, j, :, part_cols(k)],
                self.sem + j * n_cols + k,
                core_dev,
            )

        def y_copy(self, k):
            return remote(
                core_recv.at[self.index, 0, :, part_cols(k)],
                y_recv.at[self.index, :, part_cols(k)],
                self.sem + 2 * n_cols + k,
                y_dev,
            )

        def product(self, fb, k):
            value = self.part(fb, k)
            if self.seen is not None:
                self.seen(fb, k, value)
            return value

        def send_core(self):
            def core_step(n, carry):
                j, k = n // n_cols, lax.rem(n, n_cols)
                fb = jnp.where(j == 0, f_yc, f_c)
                core_send[j, :, part_cols(k)] = self.product(fb, k).astype(bf16)
                self.core_copy(j, k).start()
                return carry

            lax.fori_loop(0, 2 * n_cols, core_step, 0)

        def send_y(self, first, last, start=True):
            def y_step(k, carry):
                value = self.product(f_y, k)
                self.core_copy(0, k).wait_recv()
                value = value + core_recv[self.index, 0, :, part_cols(k)].astype(f32)
                core_recv[self.index, 0, :, part_cols(k)] = value.astype(bf16)
                if start:
                    self.y_copy(k).start()
                return carry

            lax.fori_loop(first, last, y_step, 0)

        def core_sends_done(self):
            for j in range(2):
                for k in range(n_cols):
                    self.core_copy(j, k).wait_send()

        def total(self, k):
            value = self.part(f, k)
            self.core_copy(1, k).wait_recv()
            self.y_copy(k).wait_recv()
            return (
                value
                + core_recv[self.index, 1, :, part_cols(k)].astype(f32)
                + y_recv[self.index, :, part_cols(k)].astype(f32)
            )

        def wait_y_sends(self):
            for k in range(n_cols):
                self.y_copy(k).wait_send()

    def gain_add(index, k, value, weighed):
        products = (value * weighed.astype(f32)).reshape(rows // 8, 8, piece)
        gain_part[index, :, part_cols(k)] += jnp.sum(products, axis=0)

    def part_branch(fb, k):
        return nt(att[...], wo[cols_at(fb, k), :])

    def part_lat(fb, k):
        return nt(sgq[...], wq[cols_at(fb, k), :])

    def seen_lat(fb, k, value):
        gain_add(4 + fb, k, value, lat_all[fb, :, part_cols(k)])

    branch = Collect(part_branch, 0)
    back_lat = Collect(part_lat, 1, seen_lat)
    gain_part[...] = jnp.zeros(gain_part.shape, f32)

    gather_core(cot_all, sem_cot).wait_recv()
    project(acc_q, cot_all, wo, mine, True)
    for k in range(n_rows):
        att[part_rows(k), :] = flip(att_t[:, part_rows(k)])
    pl.when(patient)(cot_across_y)
    branch.send_core()

    hold_own(cot_all, cot_x, sem_cot_x)
    pl.when(urgent)(lambda: hold_own(lat_all, lat_x, sem_lat_x))
    across_core(cot_x, sem_cot_x).wait_recv()
    for p in range(n_rows):
        att_x_copy(p).wait_recv()
    near_j = jnp.where(z // 2 == y, 0, 1)
    grad_o.first(near_j)

    @pl.when(urgent)
    def _():
        pass_on(cot_all, sem_cot, cot_x, sem_cot_x)
        hold_rows(lat_all, lat_x, sem_lat_x)

    pl.when(patient)(lambda: wait_on(cot_all, sem_cot))

    gkv[:, patches] = jnp.zeros((kv, rows), f32)

    def backward_step(p, carry):
        far_s[...] = nn(ga_rows[p], kv_t[vals, patches])
        near_s[...] = nn(ga_rows[p], kv_t[vals, own_latents(p)])
        for h in range(heads):
            far_p = probs_c[p, head_part(h), :].astype(f32)
            near_p = probs_l[p, head_part(h), :].astype(f32)
            far_d, near_d = far_s[head_part(h), :], near_s[head_part(h), :]
            inner = jnp.sum(far_p * far_d, axis=1, keepdims=True) + jnp.sum(
                near_p * near_d, axis=1, keepdims=True
            )
            far_g[head_part(h), :] = (far_p * (far_d - inner)).astype(bf16)
            near_g[head_part(h), :] = (near_p * (near_d - inner)).astype(bf16)
        grad_query = nn(far_g[...], k_rows[patches, :]) + nn(near_g[...], k_rows[own_latents(p), :])
        total = jnp.zeros((1, ROWS), f32)
        for h in range(heads):
            one = grad_query[head_part(h), :].T * score_scale
            query = q_cols[p, :, head_part(h)].astype(f32)
            total = total + jnp.sum(one * query, axis=0, keepdims=True)
            sgq_t[h * head : (h + 1) * head, part_rows(p)] = (
                one * scale_row[1:2, part_rows(p)]
            ).astype(bf16)
        inners[f, 1:2, part_rows(p)] = total
        sgq_x_copy(p).start()
        gkv[keys, patches] += nn(q_cols[p], far_g[...])
        gkv[keys, own_latents(p)] = nn(q_cols[p], near_g[...])
        gkv[vals, patches] += nn(ga_cols[p], probs_c[p])
        gkv[vals, own_latents(p)] = nn(ga_cols[p], probs_l[p])
        return carry

    def cot_step(p, carry):
        @pl.when(patient)
        def _():
            gather_y(cot_all, sem_cot, p).wait_recv()
            gather_on(cot_all, sem_cot, p).start()

        pl.when(urgent)(lambda: gather_on(cot_all, sem_cot, p).wait_recv())
        value = acc_q[part_rows(p), :]
        for fb in (f_y, f_yc):
            value = value + nn(cot_all[fb, part_rows(p), :], wo[block_cols(fb), :])
        split_heads(value.T, p, ga_rows, ga_cols, 1.0)
        return backward_step(p, carry)

    lax.fori_loop(0, n_rows // 2, cot_step, 0)
    pl.when(urgent)(lambda: hold_rows(cot_all, cot_x, sem_cot_x))
    pl.when(patient)(lambda: rows_core_done(cot_x, sem_cot_x))
    grad_o.first(1 - near_j)
    early = z // 2 != y
    pl.when(early)(grad_o.second)
    branch.send_y(0, 1)
    lax.fori_loop(n_rows // 2, n_rows, cot_step, 0)
    gkv[keys, :] = gkv[keys, :] * score_scale
    products = jnp.sum(gkv[...] * kv_t[...].astype(f32), axis=0, keepdims=True)
    inners[f, 0:1, :] = products[:, 0:rows]
    inners[f, 1:2, :] += products[:, rows:]
    inner_out = exchange(inners, sem_inner)
    for copy in inner_out:
        copy.start()
    sgkv_all[head_rows_of(f), 0:rows] = (gkv[:, 0:rows] * scale_row[0:1, :]).astype(bf16)
    sgkv_all[head_rows_of(f), rows:] = (gkv[:, rows:] * scale_row[1:2, :]).astype(bf16)
    sem_gkv = take(3)

    def gkv_copy(t, i, dev):
        piece = sgkv_all.at[head_rows_of(t)]
        return remote(piece, piece, sem_gkv + i, dev)

    gkv_copy(f, 0, y_dev).start()
    gkv_copy(f, 1, core_dev).start()
    for k in range(n_rows):
        sgq[part_rows(k), :] = flip(sgq_t[:, part_rows(k)])

    late = jnp.logical_not(early)

    def all_rows_x(buf, held, base):
        for k in range(n_rows):
            rows_x(buf, held, base, k).start()

    pl.when(patient & early)(lambda: across_x(lat_all, lat_x, sem_lat_x).start())

    @pl.when(patient & late)
    def _():
        all_rows_x(cot_all, cot_x, sem_cot_x)
        all_rows_x(lat_all, lat_x, sem_lat_x)

    @pl.when(patient)
    def _():
        across_core(lat_x, sem_lat_x).wait_recv()
        rows_core_done(lat_x, sem_lat_x)

    for p in range(n_rows):
        sgq_x_copy(p).wait_recv()
    grad_q.first(1)
    grad_q.first(0)
    branch.send_y(1, n_cols)
    branch.core_sends_done()
    back_lat.send_core()
    gkv_copy(f, 0, y_dev).wait_recv()
    gkv_copy(f_y, 2, core_dev).start()
    gkv_copy(f, 1, core_dev).wait_recv()
    gkv_copy(f_y, 2, core_dev).wait_recv()
    pair_first()

    @pl.when(patient & early)
    def _():
        all_rows_x(cot_all, cot_x, sem_cot_x)
        all_rows_x(lat_all, lat_x, sem_lat_x)

    pl.when(patient & late)(lambda: across_x(lat_all, lat_x, sem_lat_x).start())

    def patient_own_lat():
        pl.when(patient)(lambda: hold_own(lat_all, lat_x, sem_lat_x))
        pl.when(urgent)(lambda: across_core(lat_x, sem_lat_x).wait_recv())

    def patient_rows(buf, held, base):
        pl.when(patient)(lambda: hold_rows(buf, held, base))
        pl.when(urgent)(lambda: rows_core_done(held, base))

    @pl.when(early)
    def _():
        patient_own_lat()
        grad_q.second()

    @pl.when(late)
    def _():
        patient_rows(cot_all, cot_x, sem_cot_x)
        grad_o.second()

    back_lat.send_y(0, n_cols, False)
    outs = []

    def put(src, dst, i):
        copy = local_copy(src, dst, i)
        copy.start()
        outs.append(copy)

    for copy in inner_out:
        copy.wait()
    coef_row[...] = (
        scale_row[...]
        * scale_row[...]
        * (inners[0] + inners[1] + inners[2] + inners[3])
        / model_width
    )

    coef_cols = coef_row[...].T
    back_lat.core_sends_done()
    for k in range(n_rows):
        sgc[part_rows(k), :] = flip(sgkv_all[:, part_rows(k)])
        sgl[part_rows(k), :] = flip(sgkv_all[:, part_rows(n_rows + k)])

    def finish_ctx(k, carry):
        value = nn(sgc[...], w_own[:, part_cols(k)])
        gain_add(f, k, value, ctx_own[:, part_cols(k)])
        value = value * gain_ctx[:, cols_at(f, k)]
        value = value - raw_ctx[:, part_cols(k)].astype(f32) * coef_cols[:, 0:1]
        core_send[0, :, part_cols(k)] = value.astype(bf16)
        return carry

    lax.fori_loop(0, n_cols, finish_ctx, 0)
    put(core_send.at[0], out_context, 10)
    pair_step(0, 0)

    def gain_own(k, carry):
        value = part_lat(f, k) + nn(sgl[...], w_own[:, part_cols(k)])
        gain_add(4 + f, k, value, lat_all[f, :, part_cols(k)])
        return carry

    lax.fori_loop(0, n_cols, gain_own, 0)
    for i in range(4):
        gain_all[f, i : i + 1, :] = (
            jnp.sum(gain_part[i], axis=0, keepdims=True) / gain_ctx[:, block_cols(i)]
        )
        gain_all[f, 4 + i : 5 + i, :] = (
            jnp.sum(gain_part[4 + i], axis=0, keepdims=True) / gain_lat[:, block_cols(i)]
        )
    sem_gain, sem_gain_sum = take(2 * n_hi), take(3)
    gain_peers = exchange(gain_all, sem_gain_sum)
    for copy in gain_peers:
        copy.start()
    for k in range(n_cols):
        back_lat.y_copy(k).start()
    part = width // n_dp

    def dp_cols(d, n):
        return pl.ds(pl.multiple_of(d * part, 128), n * part)

    gain_targets = [(i, lax.rem(z + i, n_hi) * 2 + x, far_dev(i)) for i in others]
    gain_targets += [(n_hi, z * 2 + 1 - x, x_dev)]
    gain_targets += [(n_hi + i, lax.rem(z + i, n_hi) * 2 + 1 - x, far_x_dev(i)) for i in others]
    gain_copies = [
        remote(gain_sum.at[:, dp_cols(d, 1)], gain_recv.at[i], sem_gain + i, dev)
        for i, d, dev in gain_targets
    ]
    pair_step(1, 0)

    @pl.when(late)
    def _():
        patient_rows(lat_all, lat_x, sem_lat_x)
        grad_q.second()

    pair_step(2, 0)
    def finish(k, carry):
        value = raw_lat[:, part_cols(k)].astype(f32) + branch.total(k)
        y_recv[0, :, part_cols(k)] = value.astype(bf16)
        return carry

    def finish_lat(k):
        value = back_lat.total(k) + nn(sgl[...], w_own[:, part_cols(k)])
        value = value * gain_lat[:, cols_at(f, k)]
        value = value - raw_lat[:, part_cols(k)].astype(f32) * coef_cols[:, 1:2]
        value = value + cot_all[f, :, part_cols(k)].astype(f32)
        y_recv[1, :, part_cols(k)] = value.astype(bf16)
        put(y_recv.at[1, :, part_cols(k)], out_grad_lat.at[:, part_cols(k)], 20 + k)

    def put_weight(spread, at, out, i):
        spread.final()
        at[...] = dp_acc[...].T
        put(at, out, i)

    out_copy = local_copy(acc_q, out_out, 6)
    outs.append(out_copy)

    def finish_out():
        grad_o.final()
        acc_q[...] = dp_acc[...].T
        out_copy.start()

    for copy in gain_peers:
        copy.wait()
    gain_sum[...] = gain_all[0] + gain_all[1] + gain_all[2] + gain_all[3]
    for copy in gain_copies:
        copy.start()
    pair_step(3, 0)
    lax.fori_loop(0, n_cols, finish, 0)
    put(y_recv.at[0], out_latents, 9)
    pl.when(late)(finish_out)
    finish_lat(0)
    pair_step(0, 1)
    pair_step(1, 1)
    finish_lat(1)
    pair_step(2, 1)

    pair_step(3, 1)

    @pl.when(early)
    def _():
        patient_rows(cot_all, cot_x, sem_cot_x)
        finish_out()

    for buf, base in ((lat_all, sem_lat), (cot_all, sem_cot)):
        gather_done(buf, base)
    branch.wait_y_sends()
    for p in range(n_rows):
        att_x_copy(p).wait_send()
        sgq_x_copy(p).wait_send()
    w_core().wait_send()
    for i in range(2):
        w_y(y_dev, f_y, i).wait_send()
    for i in others:
        w_z(i).wait_send()
    for i in range(n_hi):
        w_x(i).wait_send()
    for j in range(2):
        kv_core_copy(j).wait_send()
    kv_y_copy().wait_send()
    for i in range(3):
        gkv_copy(f, i, core_dev).wait_send()
    pl.when(early)(lambda: patient_rows(lat_all, lat_x, sem_lat_x))
    pl.when(late)(patient_own_lat)
    finish_lat(2)
    put_weight(grad_q, far_s.at[:, pl.ds(0, heads * head)], out_query, 7)
    finish_lat(3)
    pair_result()
    for i, out in enumerate((out_key, out_value)):
        put(kv_acc.at[pl.ds(i * head, head), pl.ds(feat, feat)], out, 8 + 5 * i)
    mine_all = gain_sum[:, dp_cols(dp, 1)]
    for copy in gain_copies:
        copy.wait()
    for i, _, _ in gain_targets:
        mine_all = mine_all + gain_recv[i]
    index = lax.broadcasted_iota(jnp.int32, mine_all.shape, 0)
    gain_out[0] = jnp.sum(jnp.where(index == f, mine_all, 0.0), axis=0, keepdims=True)
    gain_out[1] = jnp.sum(jnp.where(index == 4 + f, mine_all, 0.0), axis=0, keepdims=True)
    put(gain_out.at[0], out_gain_c, 2)
    put(gain_out.at[1], out_gain_l, 14)
    for copy in outs:
        copy.wait()
    back_lat.wait_y_sends()
    for spread in (grad_o, grad_q):
        spread.wait_sends()
    for buf, held, base in ((lat_all, lat_x, sem_lat_x), (cot_all, cot_x, sem_cot_x)):
        across_x(buf, held, base).wait_send()
        across_core(held, base).wait_send()
        for k in range(n_rows):
            rows_x(buf, held, base, k).wait_send()
            rows_core(held, base, k).wait_send()
    pair_sends_done()


def hand_on(*refs):
    n = (len(refs) - 2) // 3
    ins, outs, held, sem_in, sem_out = refs[:n], refs[n : 2 * n], refs[2 * n : 3 * n], *refs[3 * n :]
    take_in = [pltpu.make_async_copy(ins[i], held[i], sem_in.at[i]) for i in range(n)]
    give_out = [pltpu.make_async_copy(held[i], outs[i], sem_out.at[i]) for i in range(n)]
    for copy in take_in:
        copy.start()
    for i in range(n):
        take_in[i].wait()
        give_out[i].start()
    for copy in give_out:
        copy.wait()


def kernel_local(
    n_dp,
    context,
    latents,
    gain_ctx,
    gain_lat,
    w_query,
    key_matrix,
    value_matrix,
    w_out,
    lengths,
    patch_flags,
    cotangent,
):
    rows, width = context.shape
    model_width = gain_ctx.shape[0]
    units = w_query.shape[1]
    kv = 2 * key_matrix.shape[1]
    heads = units // HEAD_DIM
    n_hi = n_dp // 2
    feat = model_width // n_dp
    any_space = pl.BlockSpec(memory_space=pl.ANY)
    block = jax.ShapeDtypeStruct((rows, width), bf16)
    shaped = jax.ShapeDtypeStruct
    out = pl.pallas_call(
        functools.partial(block_kernel, n_dp),
        out_shape=(
            block,
            block,
            block,
            shaped((feat, units), f32),
            shaped((kv // 2, feat), f32),
            shaped((kv // 2, feat), f32),
            shaped((feat, units), f32),
            shaped((1, width // n_dp), f32),
            shaped((1, width // n_dp), f32),
        ),
        in_specs=[any_space] * 11,
        out_specs=(any_space,) * 9,
        scratch_shapes=[
            pltpu.VMEM((1, model_width), f32),
            pltpu.VMEM((1, model_width), f32),
            pltpu.SMEM(lengths.shape, jnp.int32),
            pltpu.VMEM((1, rows), jnp.int32),
            pltpu.VMEM((2, 1, width // n_dp), f32),
            pltpu.VMEM((4, rows, width), bf16),
            pltpu.VMEM((4, rows, width), bf16),
            pltpu.VMEM((rows, width), bf16),
            pltpu.VMEM((rows, width), bf16),
            pltpu.VMEM((rows, width), bf16),
            pltpu.VMEM((model_width, units), bf16),
            pltpu.VMEM((kv, model_width), bf16),
            pltpu.VMEM((4 * kv, width), bf16),
            pltpu.VMEM((model_width, units), bf16),
            pltpu.VMEM((rows, units), f32),
            pltpu.VMEM((4 * kv, 2 * rows), f32),
            pltpu.VMEM((units, rows), bf16),
            pltpu.VMEM((units, rows), bf16),
            pltpu.VMEM((rows // ROWS, heads * ROWS, HEAD_DIM), bf16),
            pltpu.VMEM((rows // ROWS, HEAD_DIM, heads * ROWS), bf16),
            pltpu.VMEM((rows // ROWS, heads * ROWS, HEAD_DIM), bf16),
            pltpu.VMEM((rows // ROWS, HEAD_DIM, heads * ROWS), bf16),
            pltpu.VMEM((2 * rows, HEAD_DIM), bf16),
            pltpu.VMEM((2 * rows, HEAD_DIM), bf16),
            pltpu.VMEM((heads * ROWS, rows), f32),
            pltpu.VMEM((heads * ROWS, ROWS), f32),
            pltpu.VMEM((heads * ROWS, rows), bf16),
            pltpu.VMEM((heads * ROWS, ROWS), bf16),
            pltpu.VMEM((rows, units), bf16),
            pltpu.VMEM((rows, units), bf16),
            pltpu.VMEM((kv, 2 * rows), bf16),
            pltpu.VMEM((2, kv, rows), bf16),
            pltpu.VMEM((2, kv, rows), bf16),
            pltpu.VMEM((kv, rows), bf16),
            pltpu.VMEM((rows // ROWS, heads * ROWS, rows), bf16),
            pltpu.VMEM((rows // ROWS, heads * ROWS, ROWS), bf16),
            pltpu.VMEM((kv, 2 * rows), f32),
            pltpu.VMEM((4 * kv, 2 * rows), bf16),
            pltpu.VMEM((rows, 4 * kv), bf16),
            pltpu.VMEM((rows, 4 * kv), bf16),
            pltpu.VMEM((4, 8, rows), f32),
            pltpu.VMEM((4, 8, rows), f32),
            pltpu.VMEM((8, rows), f32),
            pltpu.VMEM((8, rows), f32),
            pltpu.VMEM((8, 8, width), f32),
            pltpu.VMEM((8, width), f32),
            pltpu.VMEM((2 * n_hi, 8, width // n_dp), f32),
            pltpu.VMEM((4, 8, width), f32),
            pltpu.VMEM((2, rows, width), bf16),
            pltpu.VMEM((2, 2, rows, width), bf16),
            pltpu.VMEM((2, rows, width), bf16),
            pltpu.VMEM((4, rows, feat), bf16),
            pltpu.VMEM((4, rows, feat), bf16),
            pltpu.VMEM((units, rows), bf16),
            pltpu.VMEM((units, rows), bf16),
            pltpu.VMEM((3, units, feat), bf16),
            pltpu.VMEM((3, units, feat), bf16),
            pltpu.VMEM((3, units, feat), bf16),
            pltpu.VMEM((3, units, feat), bf16),
            pltpu.VMEM((4 * kv, feat), bf16),
            pltpu.VMEM((4 * kv, feat), bf16),
            pltpu.VMEM((4 * kv, feat), bf16),
            pltpu.VMEM((4, kv, feat), bf16),
            pltpu.VMEM((2, kv, feat), bf16),
            pltpu.VMEM((units, feat), f32),
            pltpu.SemaphoreType.DMA((160,)),
            pltpu.SemaphoreType.DMA((160,)),
            pltpu.SemaphoreType.DMA((24,)),
        ],
        compiler_params=pltpu.CompilerParams(
            collective_id=0, has_side_effects=True, vmem_limit_bytes=64 << 20
        ),
        name="block",
    )(
        context,
        latents,
        cotangent,
        gain_ctx.reshape(1, model_width),
        gain_lat.reshape(1, model_width),
        w_query,
        key_matrix.T,
        value_matrix.T,
        w_out,
        lengths,
        patch_flags.reshape(1, rows),
    )
    out = pl.pallas_call(
        hand_on,
        out_shape=tuple(shaped(a.shape, a.dtype) for a in out),
        in_specs=[any_space] * 9,
        out_specs=(any_space,) * 9,
        scratch_shapes=[pltpu.VMEM(a.shape, a.dtype) for a in out]
        + [pltpu.SemaphoreType.DMA((9,)), pltpu.SemaphoreType.DMA((9,))],
        compiler_params=pltpu.CompilerParams(vmem_limit_bytes=64 << 20),
        name="hand_on",
    )(*out)
    latents_out, grad_context, grad_latents, g_query, g_key, g_value, g_out, gain_c, gain_l = out
    return (
        latents_out,
        grad_context,
        grad_latents,
        g_query,
        g_key.T,
        g_value.T,
        g_out,
        gain_c,
        gain_l,
    )


def solution(mesh):
    n_dp = mesh.shape["dp"]
    body = functools.partial(kernel_local, n_dp) if n_dp == 8 else plain_local
    return jax.shard_map(
        body,
        mesh=mesh,
        in_specs=(
            P("dp", "tensor"),
            P("dp", "tensor"),
            P(),
            P(),
            P(None, "tensor"),
            P(None, "tensor"),
            P(None, "tensor"),
            P(None, "tensor"),
            P("dp", None),
            P("dp"),
            P("dp", "tensor"),
        ),
        out_specs=(
            P("dp", "tensor"),
            P("dp", "tensor"),
            P("dp", "tensor"),
            P("dp", "tensor"),
            P("dp", "tensor"),
            P("dp", "tensor"),
            P("dp", "tensor"),
            P("tensor", "dp"),
            P("tensor", "dp"),
        ),
        check_vma=False,
    )
```

```python
import functools

import jax
import jax.numpy as jnp
from jax import lax
from jax.experimental import pallas as pl
from jax.experimental.pallas import tpu as pltpu
from jax.sharding import PartitionSpec as P

HEAD_DIM = 96
LAT = 64


epsilon = 1e-06
masked_value = -1e30
contract_rows = (((0,), (0,)), ((), ()))
contract_cols = (((1,), (1,)), ((), ()))


def row_scales(rows_in):
    values_f = rows_in.astype(jnp.float32)
    return (values_f, lax.rsqrt(jnp.mean(values_f * values_f, axis=1) + epsilon))


def norm_back(grad_norm, local_vals, row_scale, gain_local, row_inner_all, model_width):
    weighted = grad_norm * gain_local
    grad_input = (
        row_scale[:, None] * weighted
        - local_vals * (row_scale**3 * row_inner_all / model_width)[:, None]
    )
    grad_gain = jnp.sum(grad_norm * local_vals * row_scale[:, None], axis=0)
    return (grad_input, grad_gain)


def plain_local(
    context,
    latents,
    gain_ctx,
    gain_lat,
    w_query,
    key_matrix,
    value_matrix,
    w_out,
    lengths,
    patch_flags,
    cotangent,
):
    patch_rows = context.shape[0]
    latent_rows = latents.shape[0]
    local_width = context.shape[1]
    model_width = gain_ctx.shape[0]
    head_size = HEAD_DIM
    kv_local = key_matrix.shape[1] // head_size
    query_local = w_query.shape[1] // head_size
    repeat = query_local // kv_local
    all_count = patch_rows + latent_rows
    score_scale = head_size ** (-0.5)
    column = lax.axis_index("tensor") * local_width
    whole_ctx, whole_lat = (
        lax.all_gather(context, "tensor", axis=1, tiled=True),
        lax.all_gather(latents, "tensor", axis=1, tiled=True),
    )
    ctx_values, ctx_scale = row_scales(whole_ctx)
    lat_values, lat_scale = row_scales(whole_lat)
    ctx_norm = (ctx_values * ctx_scale[:, None] * gain_ctx).astype(jnp.bfloat16)
    lat_norm = (lat_values * lat_scale[:, None] * gain_lat).astype(jnp.bfloat16)
    queries = jnp.dot(lat_norm, w_query, preferred_element_type=jnp.float32).astype(jnp.bfloat16)
    all_rows = jnp.concatenate([ctx_norm, lat_norm], axis=0)
    w_pair = jnp.concatenate([key_matrix, value_matrix], axis=1)
    pair_rows = jnp.dot(all_rows, w_pair, preferred_element_type=jnp.float32).astype(jnp.bfloat16)
    key_head_split = (
        pair_rows[:, : kv_local * head_size]
        .reshape(all_count, kv_local, head_size)
        .transpose(1, 0, 2)
    )
    value_head_split = (
        pair_rows[:, kv_local * head_size :]
        .reshape(all_count, kv_local, head_size)
        .transpose(1, 0, 2)
    )
    query_heads = queries.reshape(latent_rows, query_local, head_size).transpose(1, 0, 2)
    image_ends = jnp.cumsum(lengths[0])
    patch_image = jnp.sum(
        (jnp.arange(patch_rows)[:, None] >= image_ends[None, :]).astype(jnp.int32), axis=1
    )
    latent_image = jnp.arange(latent_rows) // LAT
    allowed = jnp.concatenate(
        [
            (latent_image[:, None] == patch_image[None, :]) & (patch_flags[None, :] == 1),
            latent_image[:, None] == latent_image[None, :],
        ],
        axis=1,
    )
    head_index = jnp.arange(query_local)

    def head_scores(query_head, head_number):
        key_head = key_head_split[head_number // repeat]
        value_head = value_head_split[head_number // repeat]
        raw_scores = (
            lax.dot_general(query_head, key_head, contract_cols, preferred_element_type=jnp.float32)
            * score_scale
        )
        return (jnp.where(allowed, raw_scores, masked_value), key_head, value_head)

    def head_forward(member):
        query_head, head_number = member
        scores, key_head, value_head = head_scores(query_head, head_number)
        row_top = jnp.max(scores, axis=1, keepdims=True)
        exp_scores = jnp.exp(scores - row_top)
        row_total = jnp.sum(exp_scores, axis=1, keepdims=True)
        attention = (exp_scores / row_total).astype(jnp.bfloat16)
        blended = jnp.dot(attention, value_head, preferred_element_type=jnp.float32).astype(
            jnp.bfloat16
        )
        return (blended, row_top[:, 0] + jnp.log(row_total[:, 0]))

    heads_out, log_totals = lax.map(head_forward, (query_heads, head_index))
    attended = heads_out.transpose(1, 0, 2).reshape(latent_rows, query_local * head_size)
    partial_out = lax.dot_general(
        attended, w_out, contract_cols, preferred_element_type=jnp.float32
    )
    branch = lax.psum_scatter(
        partial_out.astype(jnp.bfloat16), "tensor", scatter_dimension=1, tiled=True
    ).astype(jnp.float32)
    latents_out = (latents.astype(jnp.float32) + branch).astype(jnp.bfloat16)
    full_grad = lax.all_gather(cotangent, "tensor", axis=1, tiled=True)
    grad_attended = jnp.dot(full_grad, w_out, preferred_element_type=jnp.float32).astype(
        jnp.bfloat16
    )
    grad_w_out = lax.dot_general(
        full_grad, attended, contract_rows, preferred_element_type=jnp.float32
    )
    grad_heads = grad_attended.reshape(latent_rows, query_local, head_size).transpose(1, 0, 2)

    def head_backward(member):
        query_head, grad_blended, log_total, head_number = member
        scores, key_head, value_head = head_scores(query_head, head_number)
        attention = jnp.exp(scores - log_total[:, None])
        grad_probs = lax.dot_general(
            grad_blended, value_head, contract_cols, preferred_element_type=jnp.float32
        )
        row_inner = jnp.sum(attention * grad_probs, axis=1, keepdims=True)
        grad_scores = (attention * (grad_probs - row_inner)).astype(jnp.bfloat16)
        grad_query = (
            jnp.dot(grad_scores, key_head, preferred_element_type=jnp.float32) * score_scale
        ).astype(jnp.bfloat16)
        grad_key = (
            lax.dot_general(
                grad_scores, query_head, contract_rows, preferred_element_type=jnp.float32
            )
            * score_scale
        )
        grad_value = lax.dot_general(
            attention.astype(jnp.bfloat16),
            grad_blended,
            contract_rows,
            preferred_element_type=jnp.float32,
        )
        return (grad_query, grad_key, grad_value)

    grad_query_heads, grad_key_heads, grad_value_heads = lax.map(
        head_backward, (query_heads, grad_heads, log_totals, head_index)
    )
    grad_keys = grad_key_heads.reshape(kv_local, repeat, all_count, head_size).sum(axis=1)
    grad_values = grad_value_heads.reshape(kv_local, repeat, all_count, head_size).sum(axis=1)
    grad_pair = jnp.concatenate(
        [
            grad_keys.transpose(1, 0, 2).reshape(all_count, kv_local * head_size),
            grad_values.transpose(1, 0, 2).reshape(all_count, kv_local * head_size),
        ],
        axis=1,
    ).astype(jnp.bfloat16)
    grad_q_rows = grad_query_heads.transpose(1, 0, 2).reshape(latent_rows, query_local * head_size)
    grad_w_query = lax.dot_general(
        lat_norm, grad_q_rows, contract_rows, preferred_element_type=jnp.float32
    )
    grad_w_pair = lax.dot_general(
        all_rows, grad_pair, contract_rows, preferred_element_type=jnp.float32
    )
    grad_rows = lax.dot_general(
        grad_pair, w_pair, contract_cols, preferred_element_type=jnp.float32
    )
    lat_terms = grad_rows[patch_rows:] + lax.dot_general(
        grad_q_rows, w_query, contract_cols, preferred_element_type=jnp.float32
    )
    grad_ctx_norm, grad_lat_norm = (
        lax.psum_scatter(
            grad_rows[:patch_rows].astype(jnp.bfloat16), "tensor", scatter_dimension=1, tiled=True
        ).astype(jnp.float32),
        lax.psum_scatter(
            lat_terms.astype(jnp.bfloat16), "tensor", scatter_dimension=1, tiled=True
        ).astype(jnp.float32),
    )
    ctx_local = context.astype(jnp.float32)
    lat_local = latents.astype(jnp.float32)
    gain_ctx_local = lax.dynamic_slice_in_dim(gain_ctx, column, local_width, 0)
    gain_lat_local = lax.dynamic_slice_in_dim(gain_lat, column, local_width, 0)
    ctx_inner = jnp.sum(grad_ctx_norm * gain_ctx_local * ctx_local, axis=1)
    lat_inner = jnp.sum(grad_lat_norm * gain_lat_local * lat_local, axis=1)
    ctx_inner_all, lat_inner_all = lax.psum((ctx_inner, lat_inner), "tensor")
    grad_ctx_in, grad_gain_c = norm_back(
        grad_ctx_norm, ctx_local, ctx_scale, gain_ctx_local, ctx_inner_all, model_width
    )
    grad_lat_in, grad_gain_l = norm_back(
        grad_lat_norm, lat_local, lat_scale, gain_lat_local, lat_inner_all, model_width
    )
    grad_context = grad_ctx_in.astype(jnp.bfloat16)
    grad_latents = (cotangent.astype(jnp.float32) + grad_lat_in).astype(jnp.bfloat16)
    grad_w_key = grad_w_pair[:, : kv_local * head_size]
    grad_w_value = grad_w_pair[:, kv_local * head_size :]
    sum_query, sum_key, sum_value, sum_out, sum_gain_c, sum_gain_l = (
        lax.psum_scatter(grad_w_query, "dp", scatter_dimension=0, tiled=True),
        lax.psum_scatter(grad_w_key, "dp", scatter_dimension=0, tiled=True),
        lax.psum_scatter(grad_w_value, "dp", scatter_dimension=0, tiled=True),
        lax.psum_scatter(grad_w_out, "dp", scatter_dimension=0, tiled=True),
        lax.psum_scatter(grad_gain_c, "dp", scatter_dimension=0, tiled=True),
        lax.psum_scatter(grad_gain_l, "dp", scatter_dimension=0, tiled=True),
    )
    return (
        latents_out,
        grad_context,
        grad_latents,
        sum_query,
        sum_key,
        sum_value,
        sum_out,
        sum_gain_c.reshape(1, -1),
        sum_gain_l.reshape(1, -1),
    )


MESH = pl.DeviceIdType.MESH
f32 = jnp.float32
bf16 = jnp.bfloat16
ROWS = 128
LOG2_E = 1.4426950408889634


def nn(a, b):
    return jnp.dot(a, b, preferred_element_type=f32)


def nt(a, b):
    return lax.dot_general(a, b, contract_cols, preferred_element_type=f32)


def flip(a):
    return a.astype(f32).T.astype(bf16)


def block_kernel(
    n_dp,
    context,
    latents,
    cotangent,
    gain_ctx_in,
    gain_lat_in,
    w_query,
    key_across,
    value_across,
    w_out,
    lengths_in,
    flags_in,
    out_latents,
    out_context,
    out_grad_lat,
    out_query,
    out_key,
    out_value,
    out_out,
    out_gain_c,
    out_gain_l,
    gain_ctx,
    gain_lat,
    lengths,
    flags,
    gain_out,
    lat_all,
    cot_all,
    ctx_own,
    raw_lat,
    raw_ctx,
    wq,
    wkv,
    w_own,
    wo,
    acc_q,
    kv_acc,
    att_t,
    sgq_t,
    q_rows,
    q_cols,
    ga_rows,
    ga_cols,
    k_rows,
    v_rows,
    far_s,
    near_s,
    far_g,
    near_g,
    att,
    sgq,
    kv_t,
    kv_send,
    kv_core,
    kv_y,
    probs_c,
    probs_l,
    gkv,
    sgkv_all,
    sgc,
    sgl,
    sums,
    inners,
    scale_row,
    coef_row,
    gain_part,
    gain_sum,
    gain_recv,
    gain_all,
    core_send,
    core_recv,
    y_recv,
    lat_x,
    cot_x,
    att_xt,
    sgq_xt,
    z_send_o,
    z_send_q,
    z_recv_o,
    z_recv_q,
    x_send_kv,
    x_recv_kv,
    z_recv_kv,
    own_send,
    own_recv,
    dp_acc,
    send_sem,
    recv_sem,
    local_sem,
):
    rows, width = raw_lat.shape
    n_rows = rows // ROWS
    n_hi = n_dp // 2
    feat = 4 * width // n_dp
    head = HEAD_DIM
    heads = acc_q.shape[1] // head
    model_width = 4 * width
    score_scale = head ** (-0.5)

    dp = lax.axis_index("dp")
    f = lax.axis_index("tensor")
    z, x = dp // 2, lax.rem(dp, 2)
    y, c = f // 2, lax.rem(f, 2)
    f_c = y * 2 + (1 - c)
    f_y = (1 - y) * 2 + c
    f_yc = (1 - y) * 2 + (1 - c)
    core_dev, y_dev, yc_dev = (dp, f_c), (dp, f_y), (dp, f_yc)
    x_dev = (z * 2 + 1 - x, f)
    z_1 = z + 1 - 2 * lax.rem(z, 2)
    z_2 = z + 2 - 4 * (z // 2)
    z1_dev, z2_dev = (z_1 * 2 + x, f), (z_2 * 2 + x, f)
    x_mine = pl.ds(pl.multiple_of(x * feat, 128), feat)
    x_other = pl.ds(pl.multiple_of((1 - x) * feat, 128), feat)

    urgent = lax.rem(c + z, 2) == 1
    patient = jnp.logical_not(urgent)

    count = [0]

    def take(n):
        count[0] += n
        return count[0] - n

    def remote(src, dst, sem, dev, sem_to=None):
        return pltpu.make_async_remote_copy(
            src_ref=src,
            dst_ref=dst,
            send_sem=send_sem.at[sem],
            recv_sem=recv_sem.at[sem if sem_to is None else sem_to],
            device_id=dev,
            device_id_type=MESH,
        )

    def local_copy(src, dst, i):
        return pltpu.make_async_copy(src, dst, local_sem.at[i])

    def part_rows(k):
        if isinstance(k, int):
            return pl.ds(k * ROWS, ROWS)
        return pl.ds(pl.multiple_of(k * ROWS, ROWS), ROWS)

    n_cols = 4
    piece = width // n_cols

    def part_cols(k):
        if isinstance(k, int):
            return pl.ds(k * piece, piece)
        return pl.ds(pl.multiple_of(k * piece, 128), piece)

    def cols_at(fb, k):
        return pl.ds(pl.multiple_of(fb * width + k * piece, 128), piece)

    def block_cols(fb):
        if isinstance(fb, int):
            return pl.ds(fb * width, width)
        return pl.ds(pl.multiple_of(fb * width, width), width)

    loads = [
        local_copy(latents, raw_lat, 0),
        local_copy(key_across, wkv.at[pl.ds(0, head)], 4),
        local_copy(value_across, wkv.at[pl.ds(head, head)], 14),
        local_copy(context, raw_ctx, 1),
        local_copy(cotangent, cot_all.at[f], 13),
        local_copy(w_query, wq, 3),
        local_copy(w_out, wo, 5),
    ]
    small = [
        local_copy(gain_lat_in, gain_lat, 2),
        local_copy(gain_ctx_in, gain_ctx, 6),
        local_copy(lengths_in, lengths, 7),
        local_copy(flags_in, flags, 8),
    ]
    for load in small[:1] + loads + small[1:]:
        load.start()

    barrier = pltpu.get_barrier_semaphore()

    def greet(dev):
        pl.semaphore_signal(barrier, inc=1, device_id=dev, device_id_type=MESH)

    others = [i for i in range(1, n_hi)]

    def far_dev(i):
        return (lax.rem(z + i, n_hi) * 2 + x, f)

    def far_x_dev(i):
        return (lax.rem(z + i, n_hi) * 2 + 1 - x, f)

    always = [core_dev, y_dev, yc_dev, x_dev] + [far_dev(i) for i in others]
    always += [far_x_dev(i) for i in others]
    for dev in always:
        greet(dev)
    pl.when(z != f)(lambda: greet((z_2 * 2 + x, z)))

    def weigh(raw, gain, buf):
        gain_row = gain[:, block_cols(f)]
        for k in range(n_rows):
            values = raw[part_rows(k), :].astype(f32)
            buf[part_rows(k), :] = (values * gain_row).astype(bf16)

    small[0].wait()
    loads[0].wait()
    weigh(raw_lat, gain_lat, lat_all.at[f])
    middle = z_2 == f
    pl.semaphore_wait(barrier, len(always) + 3 * middle.astype(jnp.int32))

    sem_lat, sem_cot = (take(2 * n_rows + 1) for _ in range(2))

    def gather_y(buf, base, k):
        return remote(buf.at[f, part_rows(k)], buf.at[f, part_rows(k)], base + k, y_dev)

    def gather_core(buf, base):
        return remote(buf.at[f], buf.at[f], base + n_rows, core_dev)

    def gather_on(buf, base, k):
        return remote(
            buf.at[f_y, part_rows(k)], buf.at[f_y, part_rows(k)], base + n_rows + 1 + k, core_dev
        )

    def pass_on(buf, base, held=None, base_x=None):
        def step(k, carry):
            gather_y(buf, base, k).wait_recv()
            gather_on(buf, base, k).start()
            if held is not None:
                rows_x(buf, held, base_x, k).start()
            return carry

        lax.fori_loop(0, n_rows, step, 0)

    def wait_on(buf, base):
        for k in range(n_rows):
            gather_on(buf, base, k).wait_recv()

    def gather_done(buf, base):
        for k in range(n_rows):
            gather_y(buf, base, k).wait_send()
            gather_on(buf, base, k).wait_send()
        gather_core(buf, base).wait_send()

    def square_sums(raw, index):
        for k in range(n_rows):
            values = raw[part_rows(k), :].astype(f32)
            total = jnp.sum(values * values, axis=1, keepdims=True)
            across = jnp.broadcast_to(total, (ROWS, 128)).T
            sums[f, pl.ds(index, 1), part_rows(k)] = across[0:1, :]

    sem_lat_x, sem_cot_x = take(2 * n_rows + 2), take(2 * n_rows + 2)
    sem_att_x, sem_sgq_x = take(n_rows), take(n_rows)

    def across_x(buf, held, base):
        return remote(buf.at[f, :, x_other], held.at[f], base, x_dev)

    def across_core(held, base):
        return remote(held.at[f], held.at[f], base + 1, core_dev)

    def rows_x(buf, held, base, k):
        return remote(
            buf.at[f_y, part_rows(k), x_other], held.at[f_y, part_rows(k)], base + 2 + k, x_dev
        )

    def rows_core(held, base, k):
        piece = held.at[f_y, part_rows(k)]
        return remote(piece, piece, base + 2 + n_rows + k, core_dev)

    def hold_own(buf, held, base):
        across_x(buf, held, base).wait_recv()
        across_core(held, base).start()

    def hold_rows(buf, held, base):
        def step(k, carry):
            rows_x(buf, held, base, k).wait_recv()
            rows_core(held, base, k).start()
            return carry

        lax.fori_loop(0, n_rows, step, 0)

    def rows_core_done(held, base):
        for k in range(n_rows):
            rows_core(held, base, k).wait_recv()

    kv = 2 * head
    slice_width = width // n_dp
    pair_rows = pl.ds(pl.multiple_of((1 - y) * 2 * kv, 64), 2 * kv)
    sem_w_core, sem_w_y, sem_w_z, sem_w_x = take(1), take(2), take(n_hi), take(n_hi)

    def head_rows_of(t):
        return pl.ds(pl.multiple_of(t * kv, 64), kv)

    def slice_cols(d, at=0):
        return pl.ds(pl.multiple_of(at + d * slice_width, 128), slice_width)

    def w_y(dev, f_to, i, sender=c):
        return remote(
            wkv.at[:, slice_cols(dp, f_to * width)],
            w_own.at[head_rows_of(f), slice_cols(dp)],
            sem_w_y + i,
            dev,
            sem_w_y + sender,
        )

    def w_core():
        return remote(
            wkv.at[:, block_cols(f_c)], w_own.at[head_rows_of(f)], sem_w_core, core_dev
        )

    def w_z(i):
        piece = w_own.at[pair_rows, slice_cols(dp)]
        return remote(piece, piece, sem_w_z + i, far_dev(i))

    def w_x(i):
        piece = w_own.at[pair_rows, slice_cols(lax.rem(z + i, n_hi) * 2 + x)]
        return remote(piece, piece, sem_w_x + lax.rem(z + i, n_hi), x_dev)

    loads[1].wait()
    loads[2].wait()
    w_y(y_dev, f_y, 0).start()
    w_y(yc_dev, f_yc, 1).start()
    w_core().start()
    for k in range(n_rows):
        gather_y(lat_all, sem_lat, k).start()
    gather_core(lat_all, sem_lat).start()
    loads[4].wait()
    gather_core(cot_all, sem_cot).start()
    across_x(cot_all, cot_x, sem_cot_x).start()
    sums[f] = jnp.zeros(sums.shape[1:], f32)
    inners[f] = jnp.zeros(inners.shape[1:], f32)
    loads[3].wait()
    for load in small[1:]:
        load.wait()
    weigh(raw_ctx, gain_ctx, ctx_own)
    for i in range(2):
        w_y(y_dev, f_y, i, i).wait_recv()
    for i in others:
        w_z(i).start()
    w_x(0).start()
    w_own[head_rows_of(f), :] = wkv[:, block_cols(f)]
    square_sums(raw_lat, 1)
    square_sums(raw_ctx, 0)

    peers = [core_dev, y_dev, yc_dev]
    sem_sums, sem_inner = take(3), take(3)

    def exchange(buf, base):
        return [remote(buf.at[f], buf.at[f], base + i, dev) for i, dev in enumerate(peers)]

    sums_out = exchange(sums, sem_sums)
    for copy in sums_out:
        copy.start()

    def project(acc, values, weight, blocks, first):
        def step(i, carry):
            fb = blocks[0] + i * (blocks[1] - blocks[0])
            for m in range(2):
                half = pl.ds(m * (rows // 2), rows // 2)
                product = nn(values[fb, half, :], weight[block_cols(fb), :])
                if first:
                    @pl.when(i == 0)
                    def _():
                        acc[half, :] = product

                    @pl.when(i > 0)
                    def _():
                        acc[half, :] += product
                else:
                    acc[half, :] += product
            return carry

        lax.fori_loop(0, 2, step, 0)

    def project_pair(blocks, first):
        latent_cols = pl.ds(rows, rows)
        for i, fb in enumerate(blocks):
            product = nt(wkv[:, block_cols(fb)], lat_all[fb])
            if first and i == 0:
                kv_acc[0:kv, latent_cols] = product
            else:
                kv_acc[0:kv, latent_cols] += product

    mine, theirs = (f, f_c), (f_y, f_yc)
    loads[5].wait()
    loads[6].wait()
    gather_core(lat_all, sem_lat).wait_recv()
    project(acc_q, lat_all, wq, mine, True)
    project_pair(mine, True)
    for i in others:
        w_z(n_hi - i).wait_recv()
        w_x(i).start()
    w_core().wait_recv()
    pl.when(urgent)(lambda: across_x(lat_all, lat_x, sem_lat_x).start())
    for i in range(n_hi):
        w_x(i).wait_recv()

    sem_kv_core, sem_kv_y = take(2), take(1)

    def kv_core_copy(j):
        return remote(kv_send.at[j], kv_core.at[j], sem_kv_core + j, core_dev)

    def kv_y_copy():
        return remote(kv_core.at[0], kv_y, sem_kv_y, y_dev)

    patches = pl.ds(0, rows)
    for n in range(2):
        half = slice(n * (rows // 2), (n + 1) * (rows // 2))
        kv_acc[:, half] = nt(w_own[...], ctx_own[half, :])
    for j, t in enumerate((f_yc, f_c)):
        kv_send[j] = kv_acc[head_rows_of(t), patches].astype(bf16)
        kv_core_copy(j).start()
    kv_core_copy(0).wait_recv()
    kv_core[0] = (kv_acc[head_rows_of(f_y), patches] + kv_core[0].astype(f32)).astype(bf16)
    kv_y_copy().start()

    def cot_across_y():
        for k in range(n_rows):
            gather_y(cot_all, sem_cot, k).start()

    pl.when(urgent)(cot_across_y)

    pl.when(urgent)(lambda: pass_on(lat_all, sem_lat, lat_x, sem_lat_x))
    pl.when(patient)(lambda: pass_on(lat_all, sem_lat))
    wait_on(lat_all, sem_lat)
    project(acc_q, lat_all, wq, theirs, False)
    project_pair(theirs, False)

    for copy in sums_out:
        copy.wait()
    total = sums[0] + sums[1] + sums[2] + sums[3]
    scale_row[...] = lax.rsqrt(total / model_width + epsilon)

    def split_heads(across, p, by_rows, by_cols, factor):
        for h in range(heads):
            one = across[h * head : (h + 1) * head, :]
            at = pl.ds(h * ROWS, ROWS)
            by_cols[p, :, at] = one.astype(bf16)
            by_rows[p, at, :] = (one * factor).T.astype(bf16)

    def kv_by_rows(first):
        for n in range(first, first + n_rows):
            k_rows[part_rows(n), :] = flip(kv_t[0:head, part_rows(n)])
            v_rows[part_rows(n), :] = flip(kv_t[head:, part_rows(n)])

    for k in range(n_rows):
        across = acc_q[part_rows(k), :].T * scale_row[1:2, part_rows(k)]
        split_heads(across, k, q_rows, q_cols, score_scale * LOG2_E)
    kv_t[:, rows:] = (kv_acc[0:kv, rows:] * scale_row[1:2, :]).astype(bf16)
    kv_by_rows(n_rows)
    kv_core_copy(1).wait_recv()
    kv_y_copy().wait_recv()
    summed = kv_acc[head_rows_of(f), patches] + kv_core[1].astype(f32) + kv_y[...].astype(f32)
    kv_t[:, 0:rows] = (summed * scale_row[0:1, :]).astype(bf16)
    kv_by_rows(0)

    patch = lax.broadcasted_iota(jnp.int32, (1, rows), 1)
    image = jnp.zeros((1, rows), jnp.int32)
    end = jnp.int32(0)
    for i in range(lengths.shape[1]):
        end = end + lengths[0, i]
        image = image + (patch >= end).astype(jnp.int32)
    image = jnp.where(flags[...] == 1, image, -1)
    per_part = ROWS // LAT
    row_image = lax.broadcasted_iota(jnp.int32, (ROWS, 1), 0) // LAT
    col_image = lax.broadcasted_iota(jnp.int32, (1, ROWS), 1) // LAT
    same = row_image == col_image
    keys, vals = pl.ds(0, head), pl.ds(head, head)
    def own_latents(p):
        return pl.ds(pl.multiple_of(rows + p * ROWS, ROWS), ROWS)


    def head_part(h):
        return slice(h * ROWS, (h + 1) * ROWS)

    def att_x_copy(p):
        cols = part_rows(p)
        return remote(att_t.at[:, cols], att_xt.at[:, cols], sem_att_x + p, x_dev)

    def sgq_x_copy(p):
        cols = part_rows(p)
        return remote(sgq_t.at[:, cols], sgq_xt.at[:, cols], sem_sgq_x + p, x_dev)

    def forward_step(p, carry):
        far_s[...] = nn(q_rows[p], kv_t[keys, patches])
        near_s[...] = nn(q_rows[p], kv_t[keys, own_latents(p)])
        allowed = (row_image + p * per_part) == image
        for h in range(heads):
            far = jnp.where(allowed, far_s[head_part(h), :], masked_value)
            near = jnp.where(same, near_s[head_part(h), :], masked_value)
            top = jnp.maximum(
                jnp.max(far, axis=1, keepdims=True), jnp.max(near, axis=1, keepdims=True)
            )
            far, near = jnp.exp2(far - top), jnp.exp2(near - top)
            total = jnp.sum(far, axis=1, keepdims=True) + jnp.sum(near, axis=1, keepdims=True)
            inverse = 1.0 / total
            probs_c[p, head_part(h), :] = (far * inverse).astype(bf16)
            probs_l[p, head_part(h), :] = (near * inverse).astype(bf16)
        blended = nn(probs_c[p], v_rows[patches, :]) + nn(probs_l[p], v_rows[own_latents(p), :])
        for h in range(heads):
            one = blended[head_part(h), :]
            att_t[h * head : (h + 1) * head, part_rows(p)] = one.T.astype(bf16)
        att_x_copy(p).start()
        return carry

    lax.fori_loop(0, n_rows, forward_step, 0)
    def chunk_out(zt):
        return nn(att_t[...], cot_all[zt, :, x_mine]) + nn(att_xt[...], cot_x[zt])

    def chunk_query(zt):
        return nn(sgq_t[...], lat_all[zt, :, x_mine]) + nn(sgq_xt[...], lat_x[zt])

    def chunk_pair(xt):
        cols = pl.ds(pl.multiple_of(xt * feat, 128), feat)
        return nn(sgkv_all[:, patches], ctx_own[:, cols]) + nn(
            sgkv_all[:, pl.ds(rows, rows)], lat_all[f, :, cols]
        )

    class Spread:
        def __init__(self, chunk, send, recv):
            self.chunk, self.send, self.recv, self.sem = chunk, send, recv, take(3)

        def copy(self, j, dev):
            return remote(self.send.at[j], self.recv.at[j], self.sem + j, dev)

        def first(self, j):
            zt = z_1 + j * (z_2 - z)
            self.send[j] = self.chunk(zt).astype(bf16)
            self.copy(j, z1_dev).start()

        def second(self):
            value = self.chunk(z_2)
            self.copy(1, z1_dev).wait_recv()
            self.send[2] = (value + self.recv[1].astype(f32)).astype(bf16)
            self.copy(2, z2_dev).start()

        def final(self):
            dp_acc[...] = self.chunk(z)
            self.copy(0, z1_dev).wait_recv()
            self.copy(2, z2_dev).wait_recv()
            dp_acc[...] += self.recv[0].astype(f32) + self.recv[2].astype(f32)

        def wait_sends(self):
            for j in range(3):
                self.copy(j, z1_dev).wait_send()

    grad_o = Spread(chunk_out, z_send_o, z_recv_o)
    grad_q = Spread(chunk_query, z_send_q, z_recv_q)

    sem_kv_x, sem_kv_z1, sem_kv_z2 = take(8), take(8), take(8)
    sem_kv_own, sem_kv_in = take(8), take(4)
    pair_acc = kv_acc.at[:, pl.ds(0, feat)]
    passes = lax.rem(z + f, 2) == 1

    def piece_of(q):
        t = lax.rem(q // 2 + 2 * (1 - y), 4)
        return t, pl.ds(pl.multiple_of(t * kv + (q % 2) * head, 32), head)

    def half_of(q):
        return pl.ds((q % 2) * head, head)

    def pair_x_copy(q):
        _, at = piece_of(q)
        return remote(x_send_kv.at[at], x_recv_kv.at[at], sem_kv_x + q, x_dev)

    def pair_z_copy(q):
        _, at = piece_of(q)
        return remote(x_recv_kv.at[at], z_recv_kv.at[at], sem_kv_z1 + q, z1_dev)

    def pair_far_copy(q):
        t, at = piece_of(q)
        to = own_recv.at[1, half_of(q)]
        dev = (z_2 * 2 + x, t)
        return remote(x_recv_kv.at[at], to, sem_kv_z2 + q, dev, sem_kv_in + 2 + q % 2)

    def pair_own_copy(q):
        t, _ = piece_of(q)
        to = own_recv.at[0, half_of(q)]
        return remote(own_send.at[q], to, sem_kv_own + q, (dp, t), sem_kv_in + q % 2)

    def pair_first():
        x_send_kv[...] = chunk_pair(1 - x).astype(bf16)
        for q in range(8):
            pair_x_copy(q).start()
        pair_acc[...] = chunk_pair(x)

    def pair_piece(q, i):
        t, at = piece_of(q)
        if i == 0:
            pair_x_copy(q).wait_recv()
            pair_acc[at, :] += x_recv_kv[at, :].astype(f32)

            @pl.when(passes)
            def _():
                x_recv_kv[at, :] = pair_acc[at, :].astype(bf16)
                pair_z_copy(q).start()

            return

        @pl.when(jnp.logical_not(passes))
        def _():
            pair_z_copy(q).wait_recv()
            pair_acc[at, :] += z_recv_kv[at, :].astype(f32)

        @pl.when(middle)
        def _():
            x_recv_kv[at, :] = pair_acc[at, :].astype(bf16)
            pair_far_copy(q).start()

        @pl.when((z == f) & (f != t))
        def _():
            own_send[q] = pair_acc[at, :].astype(bf16)
            pair_own_copy(q).start()

    def pair_step(n, i):
        pair_piece(2 * n, i)
        pair_piece(2 * n + 1, i)

    def pair_result():
        for q in range(2):
            pair_far_copy(q).wait_recv()
        far = own_recv[1].astype(f32)
        at = pl.ds(feat, feat)

        @pl.when(z == f)
        def _():
            kv_acc[0:kv, at] = kv_acc[head_rows_of(f), pl.ds(0, feat)] + far

        @pl.when(z != f)
        def _():
            for q in range(2):
                pair_own_copy(q).wait_recv()
            kv_acc[0:kv, at] = own_recv[0].astype(f32) + far

    def pair_sends_done():
        for q in range(8):
            pair_x_copy(q).wait_send()
            pl.when(passes)(lambda q=q: pair_z_copy(q).wait_send())
            pl.when(middle)(lambda q=q: pair_far_copy(q).wait_send())

        @pl.when(z == f)
        def _():
            for q in range(8):
                pl.when(piece_of(q)[0] != f)(lambda q=q: pair_own_copy(q).wait_send())

    class Collect:
        def __init__(self, part, index, seen=None):
            self.part, self.index, self.sem = part, index, take(3 * n_cols)
            self.seen = seen

        def core_copy(self, j, k):
            return remote(
                core_send.at[j, :, part_cols(k)],
                core_recv.at[self.index, j, :, part_cols(k)],
                self.sem + j * n_cols + k,
                core_dev,
            )

        def y_copy(self, k):
            return remote(
                core_recv.at[self.index, 0, :, part_cols(k)],
                y_recv.at[self.index, :, part_cols(k)],
                self.sem + 2 * n_cols + k,
                y_dev,
            )

        def product(self, fb, k):
            value = self.part(fb, k)
            if self.seen is not None:
                self.seen(fb, k, value)
            return value

        def send_core(self):
            def core_step(n, carry):
                j, k = n // n_cols, lax.rem(n, n_cols)
                fb = jnp.where(j == 0, f_yc, f_c)
                core_send[j, :, part_cols(k)] = self.product(fb, k).astype(bf16)
                self.core_copy(j, k).start()
                return carry

            lax.fori_loop(0, 2 * n_cols, core_step, 0)

        def send_y(self, first, last, start=True):
            def y_step(k, carry):
                value = self.product(f_y, k)
                self.core_copy(0, k).wait_recv()
                value = value + core_recv[self.index, 0, :, part_cols(k)].astype(f32)
                core_recv[self.index, 0, :, part_cols(k)] = value.astype(bf16)
                if start:
                    self.y_copy(k).start()
                return carry

            lax.fori_loop(first, last, y_step, 0)

        def core_sends_done(self):
            for j in range(2):
                for k in range(n_cols):
                    self.core_copy(j, k).wait_send()

        def total(self, k):
            value = self.part(f, k)
            self.core_copy(1, k).wait_recv()
            self.y_copy(k).wait_recv()
            return (
                value
                + core_recv[self.index, 1, :, part_cols(k)].astype(f32)
                + y_recv[self.index, :, part_cols(k)].astype(f32)
            )

        def wait_y_sends(self):
            for k in range(n_cols):
                self.y_copy(k).wait_send()

    def gain_add(index, k, value, weighed):
        products = (value * weighed.astype(f32)).reshape(rows // 8, 8, piece)
        gain_part[index, :, part_cols(k)] += jnp.sum(products, axis=0)

    def part_branch(fb, k):
        return nt(att[...], wo[cols_at(fb, k), :])

    def part_lat(fb, k):
        return nt(sgq[...], wq[cols_at(fb, k), :])

    def seen_lat(fb, k, value):
        gain_add(4 + fb, k, value, lat_all[fb, :, part_cols(k)])

    branch = Collect(part_branch, 0)
    back_lat = Collect(part_lat, 1, seen_lat)
    gain_part[...] = jnp.zeros(gain_part.shape, f32)

    gather_core(cot_all, sem_cot).wait_recv()
    project(acc_q, cot_all, wo, mine, True)
    for k in range(n_rows):
        att[part_rows(k), :] = flip(att_t[:, part_rows(k)])
    pl.when(patient)(cot_across_y)
    branch.send_core()

    hold_own(cot_all, cot_x, sem_cot_x)
    pl.when(urgent)(lambda: hold_own(lat_all, lat_x, sem_lat_x))
    across_core(cot_x, sem_cot_x).wait_recv()
    for p in range(n_rows):
        att_x_copy(p).wait_recv()
    near_j = jnp.where(z // 2 == y, 0, 1)
    grad_o.first(near_j)

    @pl.when(urgent)
    def _():
        pass_on(cot_all, sem_cot, cot_x, sem_cot_x)
        hold_rows(lat_all, lat_x, sem_lat_x)

    pl.when(patient)(lambda: wait_on(cot_all, sem_cot))

    gkv[:, patches] = jnp.zeros((kv, rows), f32)

    def backward_step(p, carry):
        far_s[...] = nn(ga_rows[p], kv_t[vals, patches])
        near_s[...] = nn(ga_rows[p], kv_t[vals, own_latents(p)])
        for h in range(heads):
            far_p = probs_c[p, head_part(h), :].astype(f32)
            near_p = probs_l[p, head_part(h), :].astype(f32)
            far_d, near_d = far_s[head_part(h), :], near_s[head_part(h), :]
            inner = jnp.sum(far_p * far_d, axis=1, keepdims=True) + jnp.sum(
                near_p * near_d, axis=1, keepdims=True
            )
            far_g[head_part(h), :] = (far_p * (far_d - inner)).astype(bf16)
            near_g[head_part(h), :] = (near_p * (near_d - inner)).astype(bf16)
        grad_query = nn(far_g[...], k_rows[patches, :]) + nn(near_g[...], k_rows[own_latents(p), :])
        total = jnp.zeros((1, ROWS), f32)
        for h in range(heads):
            one = grad_query[head_part(h), :].T * score_scale
            query = q_cols[p, :, head_part(h)].astype(f32)
            total = total + jnp.sum(one * query, axis=0, keepdims=True)
            sgq_t[h * head : (h + 1) * head, part_rows(p)] = (
                one * scale_row[1:2, part_rows(p)]
            ).astype(bf16)
        inners[f, 1:2, part_rows(p)] = total
        sgq_x_copy(p).start()
        gkv[keys, patches] += nn(q_cols[p], far_g[...])
        gkv[keys, own_latents(p)] = nn(q_cols[p], near_g[...])
        gkv[vals, patches] += nn(ga_cols[p], probs_c[p])
        gkv[vals, own_latents(p)] = nn(ga_cols[p], probs_l[p])
        return carry

    def cot_step(p, carry):
        @pl.when(patient)
        def _():
            gather_y(cot_all, sem_cot, p).wait_recv()
            gather_on(cot_all, sem_cot, p).start()

        pl.when(urgent)(lambda: gather_on(cot_all, sem_cot, p).wait_recv())
        value = acc_q[part_rows(p), :]
        for fb in (f_y, f_yc):
            value = value + nn(cot_all[fb, part_rows(p), :], wo[block_cols(fb), :])
        split_heads(value.T, p, ga_rows, ga_cols, 1.0)
        return backward_step(p, carry)

    lax.fori_loop(0, n_rows // 2, cot_step, 0)
    pl.when(urgent)(lambda: hold_rows(cot_all, cot_x, sem_cot_x))
    pl.when(patient)(lambda: rows_core_done(cot_x, sem_cot_x))
    grad_o.first(1 - near_j)
    early = z // 2 != y
    branch.send_y(0, 1)
    lax.fori_loop(n_rows // 2, n_rows - 1, cot_step, 0)
    pl.when(early)(grad_o.second)
    cot_step(n_rows - 1, 0)
    gkv[keys, :] = gkv[keys, :] * score_scale
    products = jnp.sum(gkv[...] * kv_t[...].astype(f32), axis=0, keepdims=True)
    inners[f, 0:1, :] = products[:, 0:rows]
    inners[f, 1:2, :] += products[:, rows:]
    inner_out = exchange(inners, sem_inner)
    for copy in inner_out:
        copy.start()
    sgkv_all[head_rows_of(f), 0:rows] = (gkv[:, 0:rows] * scale_row[0:1, :]).astype(bf16)
    sgkv_all[head_rows_of(f), rows:] = (gkv[:, rows:] * scale_row[1:2, :]).astype(bf16)
    sem_gkv = take(3)

    def gkv_copy(t, i, dev):
        piece = sgkv_all.at[head_rows_of(t)]
        return remote(piece, piece, sem_gkv + i, dev)

    gkv_copy(f, 0, y_dev).start()
    gkv_copy(f, 1, core_dev).start()
    for k in range(n_rows):
        sgq[part_rows(k), :] = flip(sgq_t[:, part_rows(k)])

    late = jnp.logical_not(early)

    def patient_rows(buf, held, base):
        pl.when(patient)(lambda: hold_rows(buf, held, base))
        pl.when(urgent)(lambda: rows_core_done(held, base))

    def all_rows_x(buf, held, base):
        for k in range(n_rows):
            rows_x(buf, held, base, k).start()

    pl.when(patient & early)(lambda: across_x(lat_all, lat_x, sem_lat_x).start())

    @pl.when(patient & late)
    def _():
        all_rows_x(cot_all, cot_x, sem_cot_x)
        all_rows_x(lat_all, lat_x, sem_lat_x)

    @pl.when(patient)
    def _():
        across_core(lat_x, sem_lat_x).wait_recv()
        rows_core_done(lat_x, sem_lat_x)

    for p in range(n_rows):
        sgq_x_copy(p).wait_recv()
    grad_q.first(1)
    grad_q.first(0)
    branch.send_y(1, n_cols)
    branch.core_sends_done()
    back_lat.send_core()
    @pl.when(late)
    def _():
        patient_rows(cot_all, cot_x, sem_cot_x)
        grad_o.second()

    gkv_copy(f, 0, y_dev).wait_recv()
    gkv_copy(f_y, 2, core_dev).start()
    gkv_copy(f, 1, core_dev).wait_recv()
    gkv_copy(f_y, 2, core_dev).wait_recv()
    pair_first()

    @pl.when(patient & early)
    def _():
        all_rows_x(cot_all, cot_x, sem_cot_x)
        all_rows_x(lat_all, lat_x, sem_lat_x)

    pl.when(patient & late)(lambda: across_x(lat_all, lat_x, sem_lat_x).start())

    def patient_own_lat():
        pl.when(patient)(lambda: hold_own(lat_all, lat_x, sem_lat_x))
        pl.when(urgent)(lambda: across_core(lat_x, sem_lat_x).wait_recv())

    @pl.when(early)
    def _():
        patient_own_lat()
        grad_q.second()

    back_lat.send_y(0, n_cols, False)
    outs = []

    def put(src, dst, i):
        copy = local_copy(src, dst, i)
        copy.start()
        outs.append(copy)

    for copy in inner_out:
        copy.wait()
    coef_row[...] = (
        scale_row[...]
        * scale_row[...]
        * (inners[0] + inners[1] + inners[2] + inners[3])
        / model_width
    )

    coef_cols = coef_row[...].T
    back_lat.core_sends_done()
    for k in range(n_rows):
        sgc[part_rows(k), :] = flip(sgkv_all[:, part_rows(k)])
        sgl[part_rows(k), :] = flip(sgkv_all[:, part_rows(n_rows + k)])

    def finish_ctx(k, carry):
        value = nn(sgc[...], w_own[:, part_cols(k)])
        gain_add(f, k, value, ctx_own[:, part_cols(k)])
        value = value * gain_ctx[:, cols_at(f, k)]
        value = value - raw_ctx[:, part_cols(k)].astype(f32) * coef_cols[:, 0:1]
        core_send[0, :, part_cols(k)] = value.astype(bf16)
        return carry

    lax.fori_loop(0, n_cols, finish_ctx, 0)
    put(core_send.at[0], out_context, 10)
    pair_step(0, 0)

    def gain_own(k, carry):
        value = part_lat(f, k) + nn(sgl[...], w_own[:, part_cols(k)])
        gain_add(4 + f, k, value, lat_all[f, :, part_cols(k)])
        return carry

    lax.fori_loop(0, n_cols, gain_own, 0)
    for i in range(4):
        gain_all[f, i : i + 1, :] = (
            jnp.sum(gain_part[i], axis=0, keepdims=True) / gain_ctx[:, block_cols(i)]
        )
        gain_all[f, 4 + i : 5 + i, :] = (
            jnp.sum(gain_part[4 + i], axis=0, keepdims=True) / gain_lat[:, block_cols(i)]
        )
    sem_gain, sem_gain_sum = take(2 * n_hi), take(3)
    gain_peers = exchange(gain_all, sem_gain_sum)
    for copy in gain_peers:
        copy.start()
    for k in range(n_cols):
        back_lat.y_copy(k).start()
    part = width // n_dp

    def dp_cols(d, n):
        return pl.ds(pl.multiple_of(d * part, 128), n * part)

    gain_targets = [(i, lax.rem(z + i, n_hi) * 2 + x, far_dev(i)) for i in others]
    gain_targets += [(n_hi, z * 2 + 1 - x, x_dev)]
    gain_targets += [(n_hi + i, lax.rem(z + i, n_hi) * 2 + 1 - x, far_x_dev(i)) for i in others]
    gain_copies = [
        remote(gain_sum.at[:, dp_cols(d, 1)], gain_recv.at[i], sem_gain + i, dev)
        for i, d, dev in gain_targets
    ]
    pair_step(1, 0)

    @pl.when(late)
    def _():
        patient_rows(lat_all, lat_x, sem_lat_x)
        grad_q.second()

    pair_step(2, 0)
    def finish(k, carry):
        value = raw_lat[:, part_cols(k)].astype(f32) + branch.total(k)
        y_recv[0, :, part_cols(k)] = value.astype(bf16)
        return carry

    def finish_lat(k):
        value = back_lat.total(k) + nn(sgl[...], w_own[:, part_cols(k)])
        value = value * gain_lat[:, cols_at(f, k)]
        value = value - raw_lat[:, part_cols(k)].astype(f32) * coef_cols[:, 1:2]
        value = value + cot_all[f, :, part_cols(k)].astype(f32)
        y_recv[1, :, part_cols(k)] = value.astype(bf16)
        put(y_recv.at[1, :, part_cols(k)], out_grad_lat.at[:, part_cols(k)], 20 + k)

    def put_weight(spread, at, out, i):
        spread.final()
        at[...] = dp_acc[...].T
        put(at, out, i)

    out_copy = local_copy(acc_q, out_out, 6)
    outs.append(out_copy)

    def finish_out():
        grad_o.final()
        acc_q[...] = dp_acc[...].T
        out_copy.start()

    for copy in gain_peers:
        copy.wait()
    gain_sum[...] = gain_all[0] + gain_all[1] + gain_all[2] + gain_all[3]
    for copy in gain_copies:
        copy.start()
    pair_step(3, 0)
    lax.fori_loop(0, n_cols, finish, 0)
    put(y_recv.at[0], out_latents, 9)
    pl.when(late)(finish_out)
    finish_lat(0)
    pair_step(0, 1)
    pair_step(1, 1)
    finish_lat(1)
    pair_step(2, 1)

    pair_step(3, 1)

    @pl.when(early)
    def _():
        patient_rows(cot_all, cot_x, sem_cot_x)
        finish_out()

    for buf, base in ((lat_all, sem_lat), (cot_all, sem_cot)):
        gather_done(buf, base)
    branch.wait_y_sends()
    for p in range(n_rows):
        att_x_copy(p).wait_send()
        sgq_x_copy(p).wait_send()
    w_core().wait_send()
    for i in range(2):
        w_y(y_dev, f_y, i).wait_send()
    for i in others:
        w_z(i).wait_send()
    for i in range(n_hi):
        w_x(i).wait_send()
    for j in range(2):
        kv_core_copy(j).wait_send()
    kv_y_copy().wait_send()
    for i in range(3):
        gkv_copy(f, i, core_dev).wait_send()
    pl.when(early)(lambda: patient_rows(lat_all, lat_x, sem_lat_x))
    pl.when(late)(patient_own_lat)
    finish_lat(2)
    put_weight(grad_q, far_s.at[:, pl.ds(0, heads * head)], out_query, 7)
    finish_lat(3)
    pair_result()
    for i, out in enumerate((out_key, out_value)):
        put(kv_acc.at[pl.ds(i * head, head), pl.ds(feat, feat)], out, 8 + 5 * i)
    mine_all = gain_sum[:, dp_cols(dp, 1)]
    for copy in gain_copies:
        copy.wait()
    for i, _, _ in gain_targets:
        mine_all = mine_all + gain_recv[i]
    index = lax.broadcasted_iota(jnp.int32, mine_all.shape, 0)
    gain_out[0] = jnp.sum(jnp.where(index == f, mine_all, 0.0), axis=0, keepdims=True)
    gain_out[1] = jnp.sum(jnp.where(index == 4 + f, mine_all, 0.0), axis=0, keepdims=True)
    put(gain_out.at[0], out_gain_c, 2)
    put(gain_out.at[1], out_gain_l, 14)
    for copy in outs:
        copy.wait()
    back_lat.wait_y_sends()
    for spread in (grad_o, grad_q):
        spread.wait_sends()
    for buf, held, base in ((lat_all, lat_x, sem_lat_x), (cot_all, cot_x, sem_cot_x)):
        across_x(buf, held, base).wait_send()
        across_core(held, base).wait_send()
        for k in range(n_rows):
            rows_x(buf, held, base, k).wait_send()
            rows_core(held, base, k).wait_send()
    pair_sends_done()


def hand_on(*refs):
    n = (len(refs) - 2) // 3
    ins, outs, held, sem_in, sem_out = refs[:n], refs[n : 2 * n], refs[2 * n : 3 * n], *refs[3 * n :]
    take_in = [pltpu.make_async_copy(ins[i], held[i], sem_in.at[i]) for i in range(n)]
    give_out = [pltpu.make_async_copy(held[i], outs[i], sem_out.at[i]) for i in range(n)]
    for copy in take_in:
        copy.start()
    for i in range(n):
        take_in[i].wait()
        give_out[i].start()
    for copy in give_out:
        copy.wait()


def kernel_local(
    n_dp,
    context,
    latents,
    gain_ctx,
    gain_lat,
    w_query,
    key_matrix,
    value_matrix,
    w_out,
    lengths,
    patch_flags,
    cotangent,
):
    rows, width = context.shape
    model_width = gain_ctx.shape[0]
    units = w_query.shape[1]
    kv = 2 * key_matrix.shape[1]
    heads = units // HEAD_DIM
    n_hi = n_dp // 2
    feat = model_width // n_dp
    any_space = pl.BlockSpec(memory_space=pl.ANY)
    block = jax.ShapeDtypeStruct((rows, width), bf16)
    shaped = jax.ShapeDtypeStruct
    out = pl.pallas_call(
        functools.partial(block_kernel, n_dp),
        out_shape=(
            block,
            block,
            block,
            shaped((feat, units), f32),
            shaped((kv // 2, feat), f32),
            shaped((kv // 2, feat), f32),
            shaped((feat, units), f32),
            shaped((1, width // n_dp), f32),
            shaped((1, width // n_dp), f32),
        ),
        in_specs=[any_space] * 11,
        out_specs=(any_space,) * 9,
        scratch_shapes=[
            pltpu.VMEM((1, model_width), f32),
            pltpu.VMEM((1, model_width), f32),
            pltpu.SMEM(lengths.shape, jnp.int32),
            pltpu.VMEM((1, rows), jnp.int32),
            pltpu.VMEM((2, 1, width // n_dp), f32),
            pltpu.VMEM((4, rows, width), bf16),
            pltpu.VMEM((4, rows, width), bf16),
            pltpu.VMEM((rows, width), bf16),
            pltpu.VMEM((rows, width), bf16),
            pltpu.VMEM((rows, width), bf16),
            pltpu.VMEM((model_width, units), bf16),
            pltpu.VMEM((kv, model_width), bf16),
            pltpu.VMEM((4 * kv, width), bf16),
            pltpu.VMEM((model_width, units), bf16),
            pltpu.VMEM((rows, units), f32),
            pltpu.VMEM((4 * kv, 2 * rows), f32),
            pltpu.VMEM((units, rows), bf16),
            pltpu.VMEM((units, rows), bf16),
            pltpu.VMEM((rows // ROWS, heads * ROWS, HEAD_DIM), bf16),
            pltpu.VMEM((rows // ROWS, HEAD_DIM, heads * ROWS), bf16),
            pltpu.VMEM((rows // ROWS, heads * ROWS, HEAD_DIM), bf16),
            pltpu.VMEM((rows // ROWS, HEAD_DIM, heads * ROWS), bf16),
            pltpu.VMEM((2 * rows, HEAD_DIM), bf16),
            pltpu.VMEM((2 * rows, HEAD_DIM), bf16),
            pltpu.VMEM((heads * ROWS, rows), f32),
            pltpu.VMEM((heads * ROWS, ROWS), f32),
            pltpu.VMEM((heads * ROWS, rows), bf16),
            pltpu.VMEM((heads * ROWS, ROWS), bf16),
            pltpu.VMEM((rows, units), bf16),
            pltpu.VMEM((rows, units), bf16),
            pltpu.VMEM((kv, 2 * rows), bf16),
            pltpu.VMEM((2, kv, rows), bf16),
            pltpu.VMEM((2, kv, rows), bf16),
            pltpu.VMEM((kv, rows), bf16),
            pltpu.VMEM((rows // ROWS, heads * ROWS, rows), bf16),
            pltpu.VMEM((rows // ROWS, heads * ROWS, ROWS), bf16),
            pltpu.VMEM((kv, 2 * rows), f32),
            pltpu.VMEM((4 * kv, 2 * rows), bf16),
            pltpu.VMEM((rows, 4 * kv), bf16),
            pltpu.VMEM((rows, 4 * kv), bf16),
            pltpu.VMEM((4, 8, rows), f32),
            pltpu.VMEM((4, 8, rows), f32),
            pltpu.VMEM((8, rows), f32),
            pltpu.VMEM((8, rows), f32),
            pltpu.VMEM((8, 8, width), f32),
            pltpu.VMEM((8, width), f32),
            pltpu.VMEM((2 * n_hi, 8, width // n_dp), f32),
            pltpu.VMEM((4, 8, width), f32),
            pltpu.VMEM((2, rows, width), bf16),
            pltpu.VMEM((2, 2, rows, width), bf16),
            pltpu.VMEM((2, rows, width), bf16),
            pltpu.VMEM((4, rows, feat), bf16),
            pltpu.VMEM((4, rows, feat), bf16),
            pltpu.VMEM((units, rows), bf16),
            pltpu.VMEM((units, rows), bf16),
            pltpu.VMEM((3, units, feat), bf16),
            pltpu.VMEM((3, units, feat), bf16),
            pltpu.VMEM((3, units, feat), bf16),
            pltpu.VMEM((3, units, feat), bf16),
            pltpu.VMEM((4 * kv, feat), bf16),
            pltpu.VMEM((4 * kv, feat), bf16),
            pltpu.VMEM((4 * kv, feat), bf16),
            pltpu.VMEM((8, HEAD_DIM, feat), bf16),
            pltpu.VMEM((2, kv, feat), bf16),
            pltpu.VMEM((units, feat), f32),
            pltpu.SemaphoreType.DMA((160,)),
            pltpu.SemaphoreType.DMA((160,)),
            pltpu.SemaphoreType.DMA((24,)),
        ],
        compiler_params=pltpu.CompilerParams(
            collective_id=0, has_side_effects=True, vmem_limit_bytes=64 << 20
        ),
        name="block",
    )(
        context,
        latents,
        cotangent,
        gain_ctx.reshape(1, model_width),
        gain_lat.reshape(1, model_width),
        w_query,
        key_matrix.T,
        value_matrix.T,
        w_out,
        lengths,
        patch_flags.reshape(1, rows),
    )
    out = pl.pallas_call(
        hand_on,
        out_shape=tuple(shaped(a.shape, a.dtype) for a in out),
        in_specs=[any_space] * 9,
        out_specs=(any_space,) * 9,
        scratch_shapes=[pltpu.VMEM(a.shape, a.dtype) for a in out]
        + [pltpu.SemaphoreType.DMA((9,)), pltpu.SemaphoreType.DMA((9,))],
        compiler_params=pltpu.CompilerParams(vmem_limit_bytes=64 << 20),
        name="hand_on",
    )(*out)
    latents_out, grad_context, grad_latents, g_query, g_key, g_value, g_out, gain_c, gain_l = out
    return (
        latents_out,
        grad_context,
        grad_latents,
        g_query,
        g_key.T,
        g_value.T,
        g_out,
        gain_c,
        gain_l,
    )


def solution(mesh):
    n_dp = mesh.shape["dp"]
    body = functools.partial(kernel_local, n_dp) if n_dp == 8 else plain_local
    return jax.shard_map(
        body,
        mesh=mesh,
        in_specs=(
            P("dp", "tensor"),
            P("dp", "tensor"),
            P(),
            P(),
            P(None, "tensor"),
            P(None, "tensor"),
            P(None, "tensor"),
            P(None, "tensor"),
            P("dp", None),
            P("dp"),
            P("dp", "tensor"),
        ),
        out_specs=(
            P("dp", "tensor"),
            P("dp", "tensor"),
            P("dp", "tensor"),
            P("dp", "tensor"),
            P("dp", "tensor"),
            P("dp", "tensor"),
            P("dp", "tensor"),
            P("tensor", "dp"),
            P("tensor", "dp"),
        ),
        check_vma=False,
    )
```

```python
import functools

import jax
import jax.numpy as jnp
from jax import lax
from jax.experimental import pallas as pl
from jax.experimental.pallas import tpu as pltpu
from jax.sharding import PartitionSpec as P

HEAD_DIM = 96
LAT = 64


epsilon = 1e-06
masked_value = -1e30
contract_rows = (((0,), (0,)), ((), ()))
contract_cols = (((1,), (1,)), ((), ()))


def row_scales(rows_in):
    values_f = rows_in.astype(jnp.float32)
    return (values_f, lax.rsqrt(jnp.mean(values_f * values_f, axis=1) + epsilon))


def norm_back(grad_norm, local_vals, row_scale, gain_local, row_inner_all, model_width):
    weighted = grad_norm * gain_local
    grad_input = (
        row_scale[:, None] * weighted
        - local_vals * (row_scale**3 * row_inner_all / model_width)[:, None]
    )
    grad_gain = jnp.sum(grad_norm * local_vals * row_scale[:, None], axis=0)
    return (grad_input, grad_gain)


def plain_local(
    context,
    latents,
    gain_ctx,
    gain_lat,
    w_query,
    key_matrix,
    value_matrix,
    w_out,
    lengths,
    patch_flags,
    cotangent,
):
    patch_rows = context.shape[0]
    latent_rows = latents.shape[0]
    local_width = context.shape[1]
    model_width = gain_ctx.shape[0]
    head_size = HEAD_DIM
    kv_local = key_matrix.shape[1] // head_size
    query_local = w_query.shape[1] // head_size
    repeat = query_local // kv_local
    all_count = patch_rows + latent_rows
    score_scale = head_size ** (-0.5)
    column = lax.axis_index("tensor") * local_width
    whole_ctx, whole_lat = (
        lax.all_gather(context, "tensor", axis=1, tiled=True),
        lax.all_gather(latents, "tensor", axis=1, tiled=True),
    )
    ctx_values, ctx_scale = row_scales(whole_ctx)
    lat_values, lat_scale = row_scales(whole_lat)
    ctx_norm = (ctx_values * ctx_scale[:, None] * gain_ctx).astype(jnp.bfloat16)
    lat_norm = (lat_values * lat_scale[:, None] * gain_lat).astype(jnp.bfloat16)
    queries = jnp.dot(lat_norm, w_query, preferred_element_type=jnp.float32).astype(jnp.bfloat16)
    all_rows = jnp.concatenate([ctx_norm, lat_norm], axis=0)
    w_pair = jnp.concatenate([key_matrix, value_matrix], axis=1)
    pair_rows = jnp.dot(all_rows, w_pair, preferred_element_type=jnp.float32).astype(jnp.bfloat16)
    key_head_split = (
        pair_rows[:, : kv_local * head_size]
        .reshape(all_count, kv_local, head_size)
        .transpose(1, 0, 2)
    )
    value_head_split = (
        pair_rows[:, kv_local * head_size :]
        .reshape(all_count, kv_local, head_size)
        .transpose(1, 0, 2)
    )
    query_heads = queries.reshape(latent_rows, query_local, head_size).transpose(1, 0, 2)
    image_ends = jnp.cumsum(lengths[0])
    patch_image = jnp.sum(
        (jnp.arange(patch_rows)[:, None] >= image_ends[None, :]).astype(jnp.int32), axis=1
    )
    latent_image = jnp.arange(latent_rows) // LAT
    allowed = jnp.concatenate(
        [
            (latent_image[:, None] == patch_image[None, :]) & (patch_flags[None, :] == 1),
            latent_image[:, None] == latent_image[None, :],
        ],
        axis=1,
    )
    head_index = jnp.arange(query_local)

    def head_scores(query_head, head_number):
        key_head = key_head_split[head_number // repeat]
        value_head = value_head_split[head_number // repeat]
        raw_scores = (
            lax.dot_general(query_head, key_head, contract_cols, preferred_element_type=jnp.float32)
            * score_scale
        )
        return (jnp.where(allowed, raw_scores, masked_value), key_head, value_head)

    def head_forward(member):
        query_head, head_number = member
        scores, key_head, value_head = head_scores(query_head, head_number)
        row_top = jnp.max(scores, axis=1, keepdims=True)
        exp_scores = jnp.exp(scores - row_top)
        row_total = jnp.sum(exp_scores, axis=1, keepdims=True)
        attention = (exp_scores / row_total).astype(jnp.bfloat16)
        blended = jnp.dot(attention, value_head, preferred_element_type=jnp.float32).astype(
            jnp.bfloat16
        )
        return (blended, row_top[:, 0] + jnp.log(row_total[:, 0]))

    heads_out, log_totals = lax.map(head_forward, (query_heads, head_index))
    attended = heads_out.transpose(1, 0, 2).reshape(latent_rows, query_local * head_size)
    partial_out = lax.dot_general(
        attended, w_out, contract_cols, preferred_element_type=jnp.float32
    )
    branch = lax.psum_scatter(
        partial_out.astype(jnp.bfloat16), "tensor", scatter_dimension=1, tiled=True
    ).astype(jnp.float32)
    latents_out = (latents.astype(jnp.float32) + branch).astype(jnp.bfloat16)
    full_grad = lax.all_gather(cotangent, "tensor", axis=1, tiled=True)
    grad_attended = jnp.dot(full_grad, w_out, preferred_element_type=jnp.float32).astype(
        jnp.bfloat16
    )
    grad_w_out = lax.dot_general(
        full_grad, attended, contract_rows, preferred_element_type=jnp.float32
    )
    grad_heads = grad_attended.reshape(latent_rows, query_local, head_size).transpose(1, 0, 2)

    def head_backward(member):
        query_head, grad_blended, log_total, head_number = member
        scores, key_head, value_head = head_scores(query_head, head_number)
        attention = jnp.exp(scores - log_total[:, None])
        grad_probs = lax.dot_general(
            grad_blended, value_head, contract_cols, preferred_element_type=jnp.float32
        )
        row_inner = jnp.sum(attention * grad_probs, axis=1, keepdims=True)
        grad_scores = (attention * (grad_probs - row_inner)).astype(jnp.bfloat16)
        grad_query = (
            jnp.dot(grad_scores, key_head, preferred_element_type=jnp.float32) * score_scale
        ).astype(jnp.bfloat16)
        grad_key = (
            lax.dot_general(
                grad_scores, query_head, contract_rows, preferred_element_type=jnp.float32
            )
            * score_scale
        )
        grad_value = lax.dot_general(
            attention.astype(jnp.bfloat16),
            grad_blended,
            contract_rows,
            preferred_element_type=jnp.float32,
        )
        return (grad_query, grad_key, grad_value)

    grad_query_heads, grad_key_heads, grad_value_heads = lax.map(
        head_backward, (query_heads, grad_heads, log_totals, head_index)
    )
    grad_keys = grad_key_heads.reshape(kv_local, repeat, all_count, head_size).sum(axis=1)
    grad_values = grad_value_heads.reshape(kv_local, repeat, all_count, head_size).sum(axis=1)
    grad_pair = jnp.concatenate(
        [
            grad_keys.transpose(1, 0, 2).reshape(all_count, kv_local * head_size),
            grad_values.transpose(1, 0, 2).reshape(all_count, kv_local * head_size),
        ],
        axis=1,
    ).astype(jnp.bfloat16)
    grad_q_rows = grad_query_heads.transpose(1, 0, 2).reshape(latent_rows, query_local * head_size)
    grad_w_query = lax.dot_general(
        lat_norm, grad_q_rows, contract_rows, preferred_element_type=jnp.float32
    )
    grad_w_pair = lax.dot_general(
        all_rows, grad_pair, contract_rows, preferred_element_type=jnp.float32
    )
    grad_rows = lax.dot_general(
        grad_pair, w_pair, contract_cols, preferred_element_type=jnp.float32
    )
    lat_terms = grad_rows[patch_rows:] + lax.dot_general(
        grad_q_rows, w_query, contract_cols, preferred_element_type=jnp.float32
    )
    grad_ctx_norm, grad_lat_norm = (
        lax.psum_scatter(
            grad_rows[:patch_rows].astype(jnp.bfloat16), "tensor", scatter_dimension=1, tiled=True
        ).astype(jnp.float32),
        lax.psum_scatter(
            lat_terms.astype(jnp.bfloat16), "tensor", scatter_dimension=1, tiled=True
        ).astype(jnp.float32),
    )
    ctx_local = context.astype(jnp.float32)
    lat_local = latents.astype(jnp.float32)
    gain_ctx_local = lax.dynamic_slice_in_dim(gain_ctx, column, local_width, 0)
    gain_lat_local = lax.dynamic_slice_in_dim(gain_lat, column, local_width, 0)
    ctx_inner = jnp.sum(grad_ctx_norm * gain_ctx_local * ctx_local, axis=1)
    lat_inner = jnp.sum(grad_lat_norm * gain_lat_local * lat_local, axis=1)
    ctx_inner_all, lat_inner_all = lax.psum((ctx_inner, lat_inner), "tensor")
    grad_ctx_in, grad_gain_c = norm_back(
        grad_ctx_norm, ctx_local, ctx_scale, gain_ctx_local, ctx_inner_all, model_width
    )
    grad_lat_in, grad_gain_l = norm_back(
        grad_lat_norm, lat_local, lat_scale, gain_lat_local, lat_inner_all, model_width
    )
    grad_context = grad_ctx_in.astype(jnp.bfloat16)
    grad_latents = (cotangent.astype(jnp.float32) + grad_lat_in).astype(jnp.bfloat16)
    grad_w_key = grad_w_pair[:, : kv_local * head_size]
    grad_w_value = grad_w_pair[:, kv_local * head_size :]
    sum_query, sum_key, sum_value, sum_out, sum_gain_c, sum_gain_l = (
        lax.psum_scatter(grad_w_query, "dp", scatter_dimension=0, tiled=True),
        lax.psum_scatter(grad_w_key, "dp", scatter_dimension=0, tiled=True),
        lax.psum_scatter(grad_w_value, "dp", scatter_dimension=0, tiled=True),
        lax.psum_scatter(grad_w_out, "dp", scatter_dimension=0, tiled=True),
        lax.psum_scatter(grad_gain_c, "dp", scatter_dimension=0, tiled=True),
        lax.psum_scatter(grad_gain_l, "dp", scatter_dimension=0, tiled=True),
    )
    return (
        latents_out,
        grad_context,
        grad_latents,
        sum_query,
        sum_key,
        sum_value,
        sum_out,
        sum_gain_c.reshape(1, -1),
        sum_gain_l.reshape(1, -1),
    )


MESH = pl.DeviceIdType.MESH
f32 = jnp.float32
bf16 = jnp.bfloat16
ROWS = 128
LOG2_E = 1.4426950408889634


def nn(a, b):
    return jnp.dot(a, b, preferred_element_type=f32)


def nt(a, b):
    return lax.dot_general(a, b, contract_cols, preferred_element_type=f32)


def flip(a):
    return a.astype(f32).T.astype(bf16)


def block_kernel(
    n_dp,
    context,
    latents,
    cotangent,
    gain_ctx_in,
    gain_lat_in,
    w_query,
    key_across,
    value_across,
    w_out,
    lengths_in,
    flags_in,
    out_latents,
    out_context,
    out_grad_lat,
    out_query,
    out_key,
    out_value,
    out_out,
    out_gain_c,
    out_gain_l,
    gain_ctx,
    gain_lat,
    lengths,
    flags,
    gain_out,
    lat_all,
    cot_all,
    ctx_own,
    raw_lat,
    raw_ctx,
    wq,
    wkv,
    w_own,
    wo,
    acc_q,
    kv_acc,
    att_t,
    sgq_t,
    q_rows,
    q_cols,
    ga_rows,
    ga_cols,
    k_rows,
    v_rows,
    far_s,
    near_s,
    far_g,
    near_g,
    att,
    sgq,
    kv_t,
    kv_send,
    kv_core,
    kv_y,
    probs_c,
    probs_l,
    gkv,
    sgkv_all,
    sgc,
    sgl,
    sums,
    inners,
    scale_row,
    coef_row,
    gain_part,
    gain_sum,
    gain_recv,
    gain_all,
    core_send,
    core_recv,
    y_recv,
    lat_x,
    cot_x,
    att_xt,
    sgq_xt,
    z_send_o,
    z_send_q,
    z_recv_o,
    z_recv_q,
    x_send_kv,
    x_recv_kv,
    z_recv_kv,
    own_send,
    own_recv,
    dp_acc,
    send_sem,
    recv_sem,
    local_sem,
):
    rows, width = raw_lat.shape
    n_rows = rows // ROWS
    n_hi = n_dp // 2
    feat = 4 * width // n_dp
    head = HEAD_DIM
    heads = acc_q.shape[1] // head
    model_width = 4 * width
    score_scale = head ** (-0.5)

    dp = lax.axis_index("dp")
    f = lax.axis_index("tensor")
    z, x = dp // 2, lax.rem(dp, 2)
    y, c = f // 2, lax.rem(f, 2)
    f_c = y * 2 + (1 - c)
    f_y = (1 - y) * 2 + c
    f_yc = (1 - y) * 2 + (1 - c)
    core_dev, y_dev, yc_dev = (dp, f_c), (dp, f_y), (dp, f_yc)
    x_dev = (z * 2 + 1 - x, f)
    z_1 = z + 1 - 2 * lax.rem(z, 2)
    z_2 = z + 2 - 4 * (z // 2)
    z1_dev, z2_dev = (z_1 * 2 + x, f), (z_2 * 2 + x, f)
    x_mine = pl.ds(pl.multiple_of(x * feat, 128), feat)
    x_other = pl.ds(pl.multiple_of((1 - x) * feat, 128), feat)

    urgent = lax.rem(c + z, 2) == 1
    patient = jnp.logical_not(urgent)

    count = [0]

    def take(n):
        count[0] += n
        return count[0] - n

    def remote(src, dst, sem, dev, sem_to=None):
        return pltpu.make_async_remote_copy(
            src_ref=src,
            dst_ref=dst,
            send_sem=send_sem.at[sem],
            recv_sem=recv_sem.at[sem if sem_to is None else sem_to],
            device_id=dev,
            device_id_type=MESH,
        )

    def local_copy(src, dst, i):
        return pltpu.make_async_copy(src, dst, local_sem.at[i])

    def part_rows(k):
        if isinstance(k, int):
            return pl.ds(k * ROWS, ROWS)
        return pl.ds(pl.multiple_of(k * ROWS, ROWS), ROWS)

    n_cols = 4
    piece = width // n_cols

    def part_cols(k):
        if isinstance(k, int):
            return pl.ds(k * piece, piece)
        return pl.ds(pl.multiple_of(k * piece, 128), piece)

    def cols_at(fb, k):
        return pl.ds(pl.multiple_of(fb * width + k * piece, 128), piece)

    def block_cols(fb):
        if isinstance(fb, int):
            return pl.ds(fb * width, width)
        return pl.ds(pl.multiple_of(fb * width, width), width)

    loads = [
        local_copy(latents, raw_lat, 0),
        local_copy(key_across, wkv.at[pl.ds(0, head)], 4),
        local_copy(value_across, wkv.at[pl.ds(head, head)], 14),
        local_copy(context, raw_ctx, 1),
        local_copy(cotangent, cot_all.at[f], 13),
        local_copy(w_query, wq, 3),
        local_copy(w_out, wo, 5),
    ]
    small = [
        local_copy(gain_lat_in, gain_lat, 2),
        local_copy(gain_ctx_in, gain_ctx, 6),
        local_copy(lengths_in, lengths, 7),
        local_copy(flags_in, flags, 8),
    ]
    for load in small[:1] + loads + small[1:]:
        load.start()

    barrier = pltpu.get_barrier_semaphore()

    def greet(dev):
        pl.semaphore_signal(barrier, inc=1, device_id=dev, device_id_type=MESH)

    others = [i for i in range(1, n_hi)]

    def far_dev(i):
        return (lax.rem(z + i, n_hi) * 2 + x, f)

    def far_x_dev(i):
        return (lax.rem(z + i, n_hi) * 2 + 1 - x, f)

    always = [core_dev, y_dev, yc_dev, x_dev] + [far_dev(i) for i in others]
    always += [far_x_dev(i) for i in others]
    for dev in always:
        greet(dev)
    pl.when(z != f)(lambda: greet((z_2 * 2 + x, z)))

    def weigh(raw, gain, buf):
        gain_row = gain[:, block_cols(f)]
        for k in range(n_rows):
            values = raw[part_rows(k), :].astype(f32)
            buf[part_rows(k), :] = (values * gain_row).astype(bf16)

    small[0].wait()
    loads[0].wait()
    weigh(raw_lat, gain_lat, lat_all.at[f])
    middle = z_2 == f
    pl.semaphore_wait(barrier, len(always) + 3 * middle.astype(jnp.int32))

    sem_lat, sem_cot = (take(2 * n_rows + 1) for _ in range(2))

    def gather_y(buf, base, k):
        return remote(buf.at[f, part_rows(k)], buf.at[f, part_rows(k)], base + k, y_dev)

    def gather_core(buf, base):
        return remote(buf.at[f], buf.at[f], base + n_rows, core_dev)

    def gather_on(buf, base, k):
        return remote(
            buf.at[f_y, part_rows(k)], buf.at[f_y, part_rows(k)], base + n_rows + 1 + k, core_dev
        )

    def pass_on(buf, base, held=None, base_x=None):
        def step(k, carry):
            gather_y(buf, base, k).wait_recv()
            gather_on(buf, base, k).start()
            if held is not None:
                rows_x(buf, held, base_x, k).start()
            return carry

        lax.fori_loop(0, n_rows, step, 0)

    def wait_on(buf, base):
        for k in range(n_rows):
            gather_on(buf, base, k).wait_recv()

    def gather_done(buf, base):
        for k in range(n_rows):
            gather_y(buf, base, k).wait_send()
            gather_on(buf, base, k).wait_send()
        gather_core(buf, base).wait_send()

    def square_sums(raw, index):
        for k in range(n_rows):
            values = raw[part_rows(k), :].astype(f32)
            total = jnp.sum(values * values, axis=1, keepdims=True)
            across = jnp.broadcast_to(total, (ROWS, 128)).T
            sums[f, pl.ds(index, 1), part_rows(k)] = across[0:1, :]

    sem_lat_x, sem_cot_x = take(2 * n_rows + 2), take(2 * n_rows + 2)
    sem_att_x, sem_sgq_x = take(n_rows), take(n_rows)

    def across_x(buf, held, base):
        return remote(buf.at[f, :, x_other], held.at[f], base, x_dev)

    def across_core(held, base):
        return remote(held.at[f], held.at[f], base + 1, core_dev)

    def rows_x(buf, held, base, k):
        return remote(
            buf.at[f_y, part_rows(k), x_other], held.at[f_y, part_rows(k)], base + 2 + k, x_dev
        )

    def rows_core(held, base, k):
        piece = held.at[f_y, part_rows(k)]
        return remote(piece, piece, base + 2 + n_rows + k, core_dev)

    def hold_own(buf, held, base):
        across_x(buf, held, base).wait_recv()
        across_core(held, base).start()

    def hold_rows(buf, held, base):
        def step(k, carry):
            rows_x(buf, held, base, k).wait_recv()
            rows_core(held, base, k).start()
            return carry

        lax.fori_loop(0, n_rows, step, 0)

    def rows_core_done(held, base):
        for k in range(n_rows):
            rows_core(held, base, k).wait_recv()

    kv = 2 * head
    slice_width = width // n_dp
    pair_rows = pl.ds(pl.multiple_of((1 - y) * 2 * kv, 64), 2 * kv)
    sem_w_core, sem_w_y, sem_w_z, sem_w_x = take(1), take(2), take(n_hi), take(n_hi)

    def head_rows_of(t):
        return pl.ds(pl.multiple_of(t * kv, 64), kv)

    def slice_cols(d, at=0):
        return pl.ds(pl.multiple_of(at + d * slice_width, 128), slice_width)

    def w_y(dev, f_to, i, sender=c):
        return remote(
            wkv.at[:, slice_cols(dp, f_to * width)],
            w_own.at[head_rows_of(f), slice_cols(dp)],
            sem_w_y + i,
            dev,
            sem_w_y + sender,
        )

    def w_core():
        return remote(
            wkv.at[:, block_cols(f_c)], w_own.at[head_rows_of(f)], sem_w_core, core_dev
        )

    def w_z(i):
        piece = w_own.at[pair_rows, slice_cols(dp)]
        return remote(piece, piece, sem_w_z + i, far_dev(i))

    def w_x(i):
        piece = w_own.at[pair_rows, slice_cols(lax.rem(z + i, n_hi) * 2 + x)]
        return remote(piece, piece, sem_w_x + lax.rem(z + i, n_hi), x_dev)

    loads[1].wait()
    loads[2].wait()
    w_y(y_dev, f_y, 0).start()
    w_y(yc_dev, f_yc, 1).start()
    w_core().start()
    for k in range(n_rows):
        gather_y(lat_all, sem_lat, k).start()
    gather_core(lat_all, sem_lat).start()
    loads[4].wait()
    gather_core(cot_all, sem_cot).start()
    across_x(cot_all, cot_x, sem_cot_x).start()
    sums[f] = jnp.zeros(sums.shape[1:], f32)
    inners[f] = jnp.zeros(inners.shape[1:], f32)
    loads[3].wait()
    for load in small[1:]:
        load.wait()
    weigh(raw_ctx, gain_ctx, ctx_own)
    for i in range(2):
        w_y(y_dev, f_y, i, i).wait_recv()
    for i in others:
        w_z(i).start()
    w_x(0).start()
    w_own[head_rows_of(f), :] = wkv[:, block_cols(f)]
    square_sums(raw_lat, 1)
    square_sums(raw_ctx, 0)

    peers = [core_dev, y_dev, yc_dev]
    sem_sums, sem_inner = take(3), take(3)

    def exchange(buf, base):
        return [remote(buf.at[f], buf.at[f], base + i, dev) for i, dev in enumerate(peers)]

    sums_out = exchange(sums, sem_sums)
    for copy in sums_out:
        copy.start()

    def project(acc, values, weight, blocks, first):
        def step(i, carry):
            fb = blocks[0] + i * (blocks[1] - blocks[0])
            for m in range(2):
                half = pl.ds(m * (rows // 2), rows // 2)
                product = nn(values[fb, half, :], weight[block_cols(fb), :])
                if first:
                    @pl.when(i == 0)
                    def _():
                        acc[half, :] = product

                    @pl.when(i > 0)
                    def _():
                        acc[half, :] += product
                else:
                    acc[half, :] += product
            return carry

        lax.fori_loop(0, 2, step, 0)

    def project_pair(blocks, first):
        latent_cols = pl.ds(rows, rows)
        for i, fb in enumerate(blocks):
            product = nt(wkv[:, block_cols(fb)], lat_all[fb])
            if first and i == 0:
                kv_acc[0:kv, latent_cols] = product
            else:
                kv_acc[0:kv, latent_cols] += product

    mine, theirs = (f, f_c), (f_y, f_yc)
    loads[5].wait()
    loads[6].wait()
    gather_core(lat_all, sem_lat).wait_recv()
    project(acc_q, lat_all, wq, mine, True)
    project_pair(mine, True)
    for i in others:
        w_z(n_hi - i).wait_recv()
        w_x(i).start()
    w_core().wait_recv()
    pl.when(urgent)(lambda: across_x(lat_all, lat_x, sem_lat_x).start())
    for i in range(n_hi):
        w_x(i).wait_recv()

    sem_kv_core, sem_kv_y = take(2), take(1)

    def kv_core_copy(j):
        return remote(kv_send.at[j], kv_core.at[j], sem_kv_core + j, core_dev)

    def kv_y_copy():
        return remote(kv_core.at[0], kv_y, sem_kv_y, y_dev)

    patches = pl.ds(0, rows)
    for n in range(2):
        half = slice(n * (rows // 2), (n + 1) * (rows // 2))
        kv_acc[:, half] = nt(w_own[...], ctx_own[half, :])
    for j, t in enumerate((f_yc, f_c)):
        kv_send[j] = kv_acc[head_rows_of(t), patches].astype(bf16)
        kv_core_copy(j).start()
    kv_core_copy(0).wait_recv()
    kv_core[0] = (kv_acc[head_rows_of(f_y), patches] + kv_core[0].astype(f32)).astype(bf16)
    kv_y_copy().start()

    def cot_across_y():
        for k in range(n_rows):
            gather_y(cot_all, sem_cot, k).start()

    pl.when(urgent)(cot_across_y)

    pl.when(urgent)(lambda: pass_on(lat_all, sem_lat, lat_x, sem_lat_x))
    pl.when(patient)(lambda: pass_on(lat_all, sem_lat))
    wait_on(lat_all, sem_lat)
    project(acc_q, lat_all, wq, theirs, False)
    project_pair(theirs, False)

    for copy in sums_out:
        copy.wait()
    total = sums[0] + sums[1] + sums[2] + sums[3]
    scale_row[...] = lax.rsqrt(total / model_width + epsilon)

    def split_heads(across, p, by_rows, by_cols, factor):
        for h in range(heads):
            one = across[h * head : (h + 1) * head, :]
            at = pl.ds(h * ROWS, ROWS)
            by_cols[p, :, at] = one.astype(bf16)
            by_rows[p, at, :] = (one * factor).T.astype(bf16)

    def kv_by_rows(first):
        for n in range(first, first + n_rows):
            k_rows[part_rows(n), :] = flip(kv_t[0:head, part_rows(n)])
            v_rows[part_rows(n), :] = flip(kv_t[head:, part_rows(n)])

    for k in range(n_rows):
        across = acc_q[part_rows(k), :].T * scale_row[1:2, part_rows(k)]
        split_heads(across, k, q_rows, q_cols, score_scale * LOG2_E)
    kv_t[:, rows:] = (kv_acc[0:kv, rows:] * scale_row[1:2, :]).astype(bf16)
    kv_by_rows(n_rows)
    kv_core_copy(1).wait_recv()
    kv_y_copy().wait_recv()
    summed = kv_acc[head_rows_of(f), patches] + kv_core[1].astype(f32) + kv_y[...].astype(f32)
    kv_t[:, 0:rows] = (summed * scale_row[0:1, :]).astype(bf16)
    kv_by_rows(0)

    patch = lax.broadcasted_iota(jnp.int32, (1, rows), 1)
    image = jnp.zeros((1, rows), jnp.int32)
    end = jnp.int32(0)
    for i in range(lengths.shape[1]):
        end = end + lengths[0, i]
        image = image + (patch >= end).astype(jnp.int32)
    image = jnp.where(flags[...] == 1, image, -1)
    per_part = ROWS // LAT
    row_image = lax.broadcasted_iota(jnp.int32, (ROWS, 1), 0) // LAT
    col_image = lax.broadcasted_iota(jnp.int32, (1, ROWS), 1) // LAT
    same = row_image == col_image
    keys, vals = pl.ds(0, head), pl.ds(head, head)
    def own_latents(p):
        return pl.ds(pl.multiple_of(rows + p * ROWS, ROWS), ROWS)


    def head_part(h):
        return slice(h * ROWS, (h + 1) * ROWS)

    def att_x_copy(p):
        cols = part_rows(p)
        return remote(att_t.at[:, cols], att_xt.at[:, cols], sem_att_x + p, x_dev)

    def sgq_x_copy(p):
        cols = part_rows(p)
        return remote(sgq_t.at[:, cols], sgq_xt.at[:, cols], sem_sgq_x + p, x_dev)

    def forward_step(p, carry):
        far_s[...] = nn(q_rows[p], kv_t[keys, patches])
        near_s[...] = nn(q_rows[p], kv_t[keys, own_latents(p)])
        allowed = (row_image + p * per_part) == image
        for h in range(heads):
            far = jnp.where(allowed, far_s[head_part(h), :], masked_value)
            near = jnp.where(same, near_s[head_part(h), :], masked_value)
            top = jnp.maximum(
                jnp.max(far, axis=1, keepdims=True), jnp.max(near, axis=1, keepdims=True)
            )
            far, near = jnp.exp2(far - top), jnp.exp2(near - top)
            total = jnp.sum(far, axis=1, keepdims=True) + jnp.sum(near, axis=1, keepdims=True)
            inverse = 1.0 / total
            probs_c[p, head_part(h), :] = (far * inverse).astype(bf16)
            probs_l[p, head_part(h), :] = (near * inverse).astype(bf16)
        blended = nn(probs_c[p], v_rows[patches, :]) + nn(probs_l[p], v_rows[own_latents(p), :])
        for h in range(heads):
            one = blended[head_part(h), :]
            att_t[h * head : (h + 1) * head, part_rows(p)] = one.T.astype(bf16)
        att_x_copy(p).start()
        return carry

    lax.fori_loop(0, n_rows, forward_step, 0)
    def chunk_out(zt):
        return nn(att_t[...], cot_all[zt, :, x_mine]) + nn(att_xt[...], cot_x[zt])

    def chunk_query(zt):
        return nn(sgq_t[...], lat_all[zt, :, x_mine]) + nn(sgq_xt[...], lat_x[zt])

    def chunk_pair(xt):
        cols = pl.ds(pl.multiple_of(xt * feat, 128), feat)
        return nn(sgkv_all[:, patches], ctx_own[:, cols]) + nn(
            sgkv_all[:, pl.ds(rows, rows)], lat_all[f, :, cols]
        )

    class Spread:
        def __init__(self, chunk, send, recv):
            self.chunk, self.send, self.recv, self.sem = chunk, send, recv, take(3)

        def copy(self, j, dev):
            return remote(self.send.at[j], self.recv.at[j], self.sem + j, dev)

        def first(self, j):
            zt = z_1 + j * (z_2 - z)
            self.send[j] = self.chunk(zt).astype(bf16)
            self.copy(j, z1_dev).start()

        def second(self):
            value = self.chunk(z_2)
            self.copy(1, z1_dev).wait_recv()
            self.send[2] = (value + self.recv[1].astype(f32)).astype(bf16)
            self.copy(2, z2_dev).start()

        def final(self):
            dp_acc[...] = self.chunk(z)
            self.copy(0, z1_dev).wait_recv()
            self.copy(2, z2_dev).wait_recv()
            dp_acc[...] += self.recv[0].astype(f32) + self.recv[2].astype(f32)

        def wait_sends(self):
            for j in range(3):
                self.copy(j, z1_dev).wait_send()

    grad_o = Spread(chunk_out, z_send_o, z_recv_o)
    grad_q = Spread(chunk_query, z_send_q, z_recv_q)

    sem_kv_x, sem_kv_z1, sem_kv_z2 = take(8), take(8), take(8)
    sem_kv_own, sem_kv_in = take(8), take(4)
    pair_acc = kv_acc.at[:, pl.ds(0, feat)]
    passes = lax.rem(z + f, 2) == 1

    def piece_of(q):
        t = lax.rem(q // 2 + 2 * (1 - y), 4)
        return t, pl.ds(pl.multiple_of(t * kv + (q % 2) * head, 32), head)

    def half_of(q):
        return pl.ds((q % 2) * head, head)

    def pair_x_copy(q):
        _, at = piece_of(q)
        return remote(x_send_kv.at[at], x_recv_kv.at[at], sem_kv_x + q, x_dev)

    def pair_z_copy(q):
        _, at = piece_of(q)
        return remote(x_recv_kv.at[at], z_recv_kv.at[at], sem_kv_z1 + q, z1_dev)

    def pair_far_copy(q):
        t, at = piece_of(q)
        to = own_recv.at[1, half_of(q)]
        dev = (z_2 * 2 + x, t)
        return remote(x_recv_kv.at[at], to, sem_kv_z2 + q, dev, sem_kv_in + 2 + q % 2)

    def pair_own_copy(q):
        t, _ = piece_of(q)
        to = own_recv.at[0, half_of(q)]
        return remote(own_send.at[q], to, sem_kv_own + q, (dp, t), sem_kv_in + q % 2)

    def pair_first():
        x_send_kv[...] = chunk_pair(1 - x).astype(bf16)
        for q in range(8):
            pair_x_copy(q).start()
        pair_acc[...] = chunk_pair(x)

    def pair_piece(q, i):
        t, at = piece_of(q)
        if i == 0:
            pair_x_copy(q).wait_recv()
            pair_acc[at, :] += x_recv_kv[at, :].astype(f32)

            @pl.when(passes)
            def _():
                x_recv_kv[at, :] = pair_acc[at, :].astype(bf16)
                pair_z_copy(q).start()

            return

        @pl.when(jnp.logical_not(passes))
        def _():
            pair_z_copy(q).wait_recv()
            pair_acc[at, :] += z_recv_kv[at, :].astype(f32)

        @pl.when(middle)
        def _():
            x_recv_kv[at, :] = pair_acc[at, :].astype(bf16)
            pair_far_copy(q).start()

        @pl.when((z == f) & (f != t))
        def _():
            own_send[q] = pair_acc[at, :].astype(bf16)
            pair_own_copy(q).start()

    def pair_step(n, i):
        pair_piece(2 * n, i)
        pair_piece(2 * n + 1, i)

    def pair_result():
        for q in range(2):
            pair_far_copy(q).wait_recv()
        far = own_recv[1].astype(f32)
        at = pl.ds(feat, feat)

        @pl.when(z == f)
        def _():
            kv_acc[0:kv, at] = kv_acc[head_rows_of(f), pl.ds(0, feat)] + far

        @pl.when(z != f)
        def _():
            for q in range(2):
                pair_own_copy(q).wait_recv()
            kv_acc[0:kv, at] = own_recv[0].astype(f32) + far

    def pair_sends_done():
        for q in range(8):
            pair_x_copy(q).wait_send()
            pl.when(passes)(lambda q=q: pair_z_copy(q).wait_send())
            pl.when(middle)(lambda q=q: pair_far_copy(q).wait_send())

        @pl.when(z == f)
        def _():
            for q in range(8):
                pl.when(piece_of(q)[0] != f)(lambda q=q: pair_own_copy(q).wait_send())

    class Collect:
        def __init__(self, part, index, seen=None):
            self.part, self.index, self.sem = part, index, take(3 * n_cols)
            self.seen = seen

        def core_copy(self, j, k):
            return remote(
                core_send.at[j, :, part_cols(k)],
                core_recv.at[self.index, j, :, part_cols(k)],
                self.sem + j * n_cols + k,
                core_dev,
            )

        def y_copy(self, k):
            return remote(
                core_recv.at[self.index, 0, :, part_cols(k)],
                y_recv.at[self.index, :, part_cols(k)],
                self.sem + 2 * n_cols + k,
                y_dev,
            )

        def product(self, fb, k):
            value = self.part(fb, k)
            if self.seen is not None:
                self.seen(fb, k, value)
            return value

        def send_core(self):
            def core_step(n, carry):
                j, k = n // n_cols, lax.rem(n, n_cols)
                fb = jnp.where(j == 0, f_yc, f_c)
                core_send[j, :, part_cols(k)] = self.product(fb, k).astype(bf16)
                self.core_copy(j, k).start()
                return carry

            lax.fori_loop(0, 2 * n_cols, core_step, 0)

        def send_y(self, first, last, start=True):
            def y_step(k, carry):
                value = self.product(f_y, k)
                self.core_copy(0, k).wait_recv()
                value = value + core_recv[self.index, 0, :, part_cols(k)].astype(f32)
                core_recv[self.index, 0, :, part_cols(k)] = value.astype(bf16)
                if start:
                    self.y_copy(k).start()
                return carry

            lax.fori_loop(first, last, y_step, 0)

        def core_sends_done(self):
            for j in range(2):
                for k in range(n_cols):
                    self.core_copy(j, k).wait_send()

        def total(self, k):
            value = self.part(f, k)
            self.core_copy(1, k).wait_recv()
            self.y_copy(k).wait_recv()
            return (
                value
                + core_recv[self.index, 1, :, part_cols(k)].astype(f32)
                + y_recv[self.index, :, part_cols(k)].astype(f32)
            )

        def wait_y_sends(self):
            for k in range(n_cols):
                self.y_copy(k).wait_send()

    def gain_add(index, k, value, weighed):
        products = (value * weighed.astype(f32)).reshape(rows // 8, 8, piece)
        gain_part[index, :, part_cols(k)] += jnp.sum(products, axis=0)

    def part_branch(fb, k):
        return nt(att[...], wo[cols_at(fb, k), :])

    def part_lat(fb, k):
        return nt(sgq[...], wq[cols_at(fb, k), :])

    def seen_lat(fb, k, value):
        gain_add(4 + fb, k, value, lat_all[fb, :, part_cols(k)])

    branch = Collect(part_branch, 0)
    back_lat = Collect(part_lat, 1, seen_lat)
    gain_part[...] = jnp.zeros(gain_part.shape, f32)

    gather_core(cot_all, sem_cot).wait_recv()
    project(acc_q, cot_all, wo, mine, True)
    for k in range(n_rows):
        att[part_rows(k), :] = flip(att_t[:, part_rows(k)])
    pl.when(patient)(cot_across_y)
    branch.send_core()

    hold_own(cot_all, cot_x, sem_cot_x)
    pl.when(urgent)(lambda: hold_own(lat_all, lat_x, sem_lat_x))
    across_core(cot_x, sem_cot_x).wait_recv()
    for p in range(n_rows):
        att_x_copy(p).wait_recv()
    near_j = jnp.where(z // 2 == y, 0, 1)
    grad_o.first(near_j)

    @pl.when(urgent)
    def _():
        pass_on(cot_all, sem_cot, cot_x, sem_cot_x)
        hold_rows(lat_all, lat_x, sem_lat_x)

    pl.when(patient)(lambda: wait_on(cot_all, sem_cot))

    gkv[:, patches] = jnp.zeros((kv, rows), f32)

    def backward_step(p, carry):
        far_s[...] = nn(ga_rows[p], kv_t[vals, patches])
        near_s[...] = nn(ga_rows[p], kv_t[vals, own_latents(p)])
        for h in range(heads):
            far_p = probs_c[p, head_part(h), :].astype(f32)
            near_p = probs_l[p, head_part(h), :].astype(f32)
            far_d, near_d = far_s[head_part(h), :], near_s[head_part(h), :]
            inner = jnp.sum(far_p * far_d, axis=1, keepdims=True) + jnp.sum(
                near_p * near_d, axis=1, keepdims=True
            )
            far_g[head_part(h), :] = (far_p * (far_d - inner)).astype(bf16)
            near_g[head_part(h), :] = (near_p * (near_d - inner)).astype(bf16)
        grad_query = nn(far_g[...], k_rows[patches, :]) + nn(near_g[...], k_rows[own_latents(p), :])
        total = jnp.zeros((1, ROWS), f32)
        for h in range(heads):
            one = grad_query[head_part(h), :].T * score_scale
            query = q_cols[p, :, head_part(h)].astype(f32)
            total = total + jnp.sum(one * query, axis=0, keepdims=True)
            sgq_t[h * head : (h + 1) * head, part_rows(p)] = (
                one * scale_row[1:2, part_rows(p)]
            ).astype(bf16)
        inners[f, 1:2, part_rows(p)] = total
        sgq_x_copy(p).start()
        gkv[keys, patches] += nn(q_cols[p], far_g[...])
        gkv[keys, own_latents(p)] = nn(q_cols[p], near_g[...])
        gkv[vals, patches] += nn(ga_cols[p], probs_c[p])
        gkv[vals, own_latents(p)] = nn(ga_cols[p], probs_l[p])
        return carry

    def cot_step(p, carry):
        @pl.when(patient)
        def _():
            gather_y(cot_all, sem_cot, p).wait_recv()
            gather_on(cot_all, sem_cot, p).start()

        pl.when(urgent)(lambda: gather_on(cot_all, sem_cot, p).wait_recv())
        value = acc_q[part_rows(p), :]
        for fb in (f_y, f_yc):
            value = value + nn(cot_all[fb, part_rows(p), :], wo[block_cols(fb), :])
        split_heads(value.T, p, ga_rows, ga_cols, 1.0)
        return backward_step(p, carry)

    lax.fori_loop(0, n_rows // 2, cot_step, 0)
    pl.when(urgent)(lambda: hold_rows(cot_all, cot_x, sem_cot_x))
    pl.when(patient)(lambda: rows_core_done(cot_x, sem_cot_x))
    grad_o.first(1 - near_j)
    early = z // 2 != y
    pl.when(early)(grad_o.second)
    branch.send_y(0, 1)
    lax.fori_loop(n_rows // 2, n_rows, cot_step, 0)
    gkv[keys, :] = gkv[keys, :] * score_scale
    products = jnp.sum(gkv[...] * kv_t[...].astype(f32), axis=0, keepdims=True)
    inners[f, 0:1, :] = products[:, 0:rows]
    inners[f, 1:2, :] += products[:, rows:]
    inner_out = exchange(inners, sem_inner)
    for copy in inner_out:
        copy.start()
    sgkv_all[head_rows_of(f), 0:rows] = (gkv[:, 0:rows] * scale_row[0:1, :]).astype(bf16)
    sgkv_all[head_rows_of(f), rows:] = (gkv[:, rows:] * scale_row[1:2, :]).astype(bf16)
    sem_gkv = take(3)

    def gkv_copy(t, i, dev):
        piece = sgkv_all.at[head_rows_of(t)]
        return remote(piece, piece, sem_gkv + i, dev)

    gkv_copy(f, 0, y_dev).start()
    gkv_copy(f, 1, core_dev).start()
    for k in range(n_rows):
        sgq[part_rows(k), :] = flip(sgq_t[:, part_rows(k)])

    late = jnp.logical_not(early)

    def all_rows_x(buf, held, base):
        for k in range(n_rows):
            rows_x(buf, held, base, k).start()

    pl.when(patient & early)(lambda: across_x(lat_all, lat_x, sem_lat_x).start())

    @pl.when(patient & late)
    def _():
        all_rows_x(cot_all, cot_x, sem_cot_x)
        all_rows_x(lat_all, lat_x, sem_lat_x)

    @pl.when(patient)
    def _():
        across_core(lat_x, sem_lat_x).wait_recv()
        rows_core_done(lat_x, sem_lat_x)

    for p in range(n_rows):
        sgq_x_copy(p).wait_recv()
    grad_q.first(1)
    grad_q.first(0)
    branch.send_y(1, n_cols)
    branch.core_sends_done()
    back_lat.send_core()
    gkv_copy(f, 0, y_dev).wait_recv()
    gkv_copy(f_y, 2, core_dev).start()
    gkv_copy(f, 1, core_dev).wait_recv()
    gkv_copy(f_y, 2, core_dev).wait_recv()
    pair_first()

    @pl.when(patient & early)
    def _():
        all_rows_x(cot_all, cot_x, sem_cot_x)
        all_rows_x(lat_all, lat_x, sem_lat_x)

    pl.when(patient & late)(lambda: across_x(lat_all, lat_x, sem_lat_x).start())

    def patient_own_lat():
        pl.when(patient)(lambda: hold_own(lat_all, lat_x, sem_lat_x))
        pl.when(urgent)(lambda: across_core(lat_x, sem_lat_x).wait_recv())

    def patient_rows(buf, held, base):
        pl.when(patient)(lambda: hold_rows(buf, held, base))
        pl.when(urgent)(lambda: rows_core_done(held, base))

    @pl.when(early)
    def _():
        patient_own_lat()
        grad_q.second()

    @pl.when(late)
    def _():
        patient_rows(cot_all, cot_x, sem_cot_x)
        grad_o.second()

    back_lat.send_y(0, n_cols, False)
    outs = []

    def put(src, dst, i):
        copy = local_copy(src, dst, i)
        copy.start()
        outs.append(copy)

    for copy in inner_out:
        copy.wait()
    coef_row[...] = (
        scale_row[...]
        * scale_row[...]
        * (inners[0] + inners[1] + inners[2] + inners[3])
        / model_width
    )

    coef_cols = coef_row[...].T
    back_lat.core_sends_done()
    for k in range(n_rows):
        sgc[part_rows(k), :] = flip(sgkv_all[:, part_rows(k)])
        sgl[part_rows(k), :] = flip(sgkv_all[:, part_rows(n_rows + k)])

    def finish_ctx(k, carry):
        value = nn(sgc[...], w_own[:, part_cols(k)])
        gain_add(f, k, value, ctx_own[:, part_cols(k)])
        value = value * gain_ctx[:, cols_at(f, k)]
        value = value - raw_ctx[:, part_cols(k)].astype(f32) * coef_cols[:, 0:1]
        core_send[0, :, part_cols(k)] = value.astype(bf16)
        return carry

    lax.fori_loop(0, n_cols, finish_ctx, 0)
    put(core_send.at[0], out_context, 10)
    pair_step(0, 0)

    def gain_own(k, carry):
        value = part_lat(f, k) + nn(sgl[...], w_own[:, part_cols(k)])
        gain_add(4 + f, k, value, lat_all[f, :, part_cols(k)])
        return carry

    lax.fori_loop(0, n_cols, gain_own, 0)
    for i in range(4):
        gain_all[f, i : i + 1, :] = (
            jnp.sum(gain_part[i], axis=0, keepdims=True) / gain_ctx[:, block_cols(i)]
        )
        gain_all[f, 4 + i : 5 + i, :] = (
            jnp.sum(gain_part[4 + i], axis=0, keepdims=True) / gain_lat[:, block_cols(i)]
        )
    sem_gain, sem_gain_sum = take(2 * n_hi), take(3)
    gain_peers = exchange(gain_all, sem_gain_sum)
    for copy in gain_peers:
        copy.start()
    for k in range(n_cols):
        back_lat.y_copy(k).start()
    part = width // n_dp

    def dp_cols(d, n):
        return pl.ds(pl.multiple_of(d * part, 128), n * part)

    gain_targets = [(i, lax.rem(z + i, n_hi) * 2 + x, far_dev(i)) for i in others]
    gain_targets += [(n_hi, z * 2 + 1 - x, x_dev)]
    gain_targets += [(n_hi + i, lax.rem(z + i, n_hi) * 2 + 1 - x, far_x_dev(i)) for i in others]
    gain_copies = [
        remote(gain_sum.at[:, dp_cols(d, 1)], gain_recv.at[i], sem_gain + i, dev)
        for i, d, dev in gain_targets
    ]
    pair_step(1, 0)

    @pl.when(late)
    def _():
        patient_rows(lat_all, lat_x, sem_lat_x)
        grad_q.second()

    pair_step(2, 0)
    def finish(k, carry):
        value = raw_lat[:, part_cols(k)].astype(f32) + branch.total(k)
        y_recv[0, :, part_cols(k)] = value.astype(bf16)
        return carry

    def finish_lat(k):
        value = back_lat.total(k) + nn(sgl[...], w_own[:, part_cols(k)])
        value = value * gain_lat[:, cols_at(f, k)]
        value = value - raw_lat[:, part_cols(k)].astype(f32) * coef_cols[:, 1:2]
        value = value + cot_all[f, :, part_cols(k)].astype(f32)
        y_recv[1, :, part_cols(k)] = value.astype(bf16)
        put(y_recv.at[1, :, part_cols(k)], out_grad_lat.at[:, part_cols(k)], 20 + k)

    def put_weight(spread, at, out, i):
        spread.final()
        at[...] = dp_acc[...].T
        put(at, out, i)

    out_copy = local_copy(acc_q, out_out, 6)
    outs.append(out_copy)

    def finish_out():
        grad_o.final()
        acc_q[...] = dp_acc[...].T
        out_copy.start()

    for copy in gain_peers:
        copy.wait()
    gain_sum[...] = gain_all[0] + gain_all[1] + gain_all[2] + gain_all[3]
    for copy in gain_copies:
        copy.start()
    pair_step(3, 0)
    lax.fori_loop(0, n_cols, finish, 0)
    put(y_recv.at[0], out_latents, 9)
    pl.when(late)(finish_out)
    finish_lat(0)
    pair_step(0, 1)
    pair_step(1, 1)
    finish_lat(1)
    pair_step(2, 1)

    pair_step(3, 1)

    @pl.when(early)
    def _():
        patient_rows(cot_all, cot_x, sem_cot_x)
        finish_out()

    for buf, base in ((lat_all, sem_lat), (cot_all, sem_cot)):
        gather_done(buf, base)
    branch.wait_y_sends()
    for p in range(n_rows):
        att_x_copy(p).wait_send()
        sgq_x_copy(p).wait_send()
    w_core().wait_send()
    for i in range(2):
        w_y(y_dev, f_y, i).wait_send()
    for i in others:
        w_z(i).wait_send()
    for i in range(n_hi):
        w_x(i).wait_send()
    for j in range(2):
        kv_core_copy(j).wait_send()
    kv_y_copy().wait_send()
    for i in range(3):
        gkv_copy(f, i, core_dev).wait_send()
    pl.when(early)(lambda: patient_rows(lat_all, lat_x, sem_lat_x))
    pl.when(late)(patient_own_lat)
    finish_lat(2)
    put_weight(grad_q, far_s.at[:, pl.ds(0, heads * head)], out_query, 7)
    finish_lat(3)
    pair_result()
    for i, out in enumerate((out_key, out_value)):
        put(kv_acc.at[pl.ds(i * head, head), pl.ds(feat, feat)], out, 8 + 5 * i)
    mine_all = gain_sum[:, dp_cols(dp, 1)]
    for copy in gain_copies:
        copy.wait()
    for i, _, _ in gain_targets:
        mine_all = mine_all + gain_recv[i]
    index = lax.broadcasted_iota(jnp.int32, mine_all.shape, 0)
    gain_out[0] = jnp.sum(jnp.where(index == f, mine_all, 0.0), axis=0, keepdims=True)
    gain_out[1] = jnp.sum(jnp.where(index == 4 + f, mine_all, 0.0), axis=0, keepdims=True)
    put(gain_out.at[0], out_gain_c, 2)
    put(gain_out.at[1], out_gain_l, 14)
    for copy in outs:
        copy.wait()
    back_lat.wait_y_sends()
    for spread in (grad_o, grad_q):
        spread.wait_sends()
    for buf, held, base in ((lat_all, lat_x, sem_lat_x), (cot_all, cot_x, sem_cot_x)):
        across_x(buf, held, base).wait_send()
        across_core(held, base).wait_send()
        for k in range(n_rows):
            rows_x(buf, held, base, k).wait_send()
            rows_core(held, base, k).wait_send()
    pair_sends_done()


def hand_on(*refs):
    n = (len(refs) - 2) // 3
    ins, outs, held, sem_in, sem_out = refs[:n], refs[n : 2 * n], refs[2 * n : 3 * n], *refs[3 * n :]
    take_in = [pltpu.make_async_copy(ins[i], held[i], sem_in.at[i]) for i in range(n)]
    give_out = [pltpu.make_async_copy(held[i], outs[i], sem_out.at[i]) for i in range(n)]
    for copy in take_in:
        copy.start()
    for i in range(n):
        take_in[i].wait()
        give_out[i].start()
    for copy in give_out:
        copy.wait()


def kernel_local(
    n_dp,
    context,
    latents,
    gain_ctx,
    gain_lat,
    w_query,
    key_matrix,
    value_matrix,
    w_out,
    lengths,
    patch_flags,
    cotangent,
):
    rows, width = context.shape
    model_width = gain_ctx.shape[0]
    units = w_query.shape[1]
    kv = 2 * key_matrix.shape[1]
    heads = units // HEAD_DIM
    n_hi = n_dp // 2
    feat = model_width // n_dp
    any_space = pl.BlockSpec(memory_space=pl.ANY)
    block = jax.ShapeDtypeStruct((rows, width), bf16)
    shaped = jax.ShapeDtypeStruct
    out = pl.pallas_call(
        functools.partial(block_kernel, n_dp),
        out_shape=(
            block,
            block,
            block,
            shaped((feat, units), f32),
            shaped((kv // 2, feat), f32),
            shaped((kv // 2, feat), f32),
            shaped((feat, units), f32),
            shaped((1, width // n_dp), f32),
            shaped((1, width // n_dp), f32),
        ),
        in_specs=[any_space] * 11,
        out_specs=(any_space,) * 9,
        scratch_shapes=[
            pltpu.VMEM((1, model_width), f32),
            pltpu.VMEM((1, model_width), f32),
            pltpu.SMEM(lengths.shape, jnp.int32),
            pltpu.VMEM((1, rows), jnp.int32),
            pltpu.VMEM((2, 1, width // n_dp), f32),
            pltpu.VMEM((4, rows, width), bf16),
            pltpu.VMEM((4, rows, width), bf16),
            pltpu.VMEM((rows, width), bf16),
            pltpu.VMEM((rows, width), bf16),
            pltpu.VMEM((rows, width), bf16),
            pltpu.VMEM((model_width, units), bf16),
            pltpu.VMEM((kv, model_width), bf16),
            pltpu.VMEM((4 * kv, width), bf16),
            pltpu.VMEM((model_width, units), bf16),
            pltpu.VMEM((rows, units), f32),
            pltpu.VMEM((4 * kv, 2 * rows), f32),
            pltpu.VMEM((units, rows), bf16),
            pltpu.VMEM((units, rows), bf16),
            pltpu.VMEM((rows // ROWS, heads * ROWS, HEAD_DIM), bf16),
            pltpu.VMEM((rows // ROWS, HEAD_DIM, heads * ROWS), bf16),
            pltpu.VMEM((rows // ROWS, heads * ROWS, HEAD_DIM), bf16),
            pltpu.VMEM((rows // ROWS, HEAD_DIM, heads * ROWS), bf16),
            pltpu.VMEM((2 * rows, HEAD_DIM), bf16),
            pltpu.VMEM((2 * rows, HEAD_DIM), bf16),
            pltpu.VMEM((heads * ROWS, rows), f32),
            pltpu.VMEM((heads * ROWS, ROWS), f32),
            pltpu.VMEM((heads * ROWS, rows), bf16),
            pltpu.VMEM((heads * ROWS, ROWS), bf16),
            pltpu.VMEM((rows, units), bf16),
            pltpu.VMEM((rows, units), bf16),
            pltpu.VMEM((kv, 2 * rows), bf16),
            pltpu.VMEM((2, kv, rows), bf16),
            pltpu.VMEM((2, kv, rows), bf16),
            pltpu.VMEM((kv, rows), bf16),
            pltpu.VMEM((rows // ROWS, heads * ROWS, rows), bf16),
            pltpu.VMEM((rows // ROWS, heads * ROWS, ROWS), bf16),
            pltpu.VMEM((kv, 2 * rows), f32),
            pltpu.VMEM((4 * kv, 2 * rows), bf16),
            pltpu.VMEM((rows, 4 * kv), bf16),
            pltpu.VMEM((rows, 4 * kv), bf16),
            pltpu.VMEM((4, 8, rows), f32),
            pltpu.VMEM((4, 8, rows), f32),
            pltpu.VMEM((8, rows), f32),
            pltpu.VMEM((8, rows), f32),
            pltpu.VMEM((8, 8, width), f32),
            pltpu.VMEM((8, width), f32),
            pltpu.VMEM((2 * n_hi, 8, width // n_dp), f32),
            pltpu.VMEM((4, 8, width), f32),
            pltpu.VMEM((2, rows, width), bf16),
            pltpu.VMEM((2, 2, rows, width), bf16),
            pltpu.VMEM((2, rows, width), bf16),
            pltpu.VMEM((4, rows, feat), bf16),
            pltpu.VMEM((4, rows, feat), bf16),
            pltpu.VMEM((units, rows), bf16),
            pltpu.VMEM((units, rows), bf16),
            pltpu.VMEM((3, units, feat), bf16),
            pltpu.VMEM((3, units, feat), bf16),
            pltpu.VMEM((3, units, feat), bf16),
            pltpu.VMEM((3, units, feat), bf16),
            pltpu.VMEM((4 * kv, feat), bf16),
            pltpu.VMEM((4 * kv, feat), bf16),
            pltpu.VMEM((4 * kv, feat), bf16),
            pltpu.VMEM((8, HEAD_DIM, feat), bf16),
            pltpu.VMEM((2, kv, feat), bf16),
            pltpu.VMEM((units, feat), f32),
            pltpu.SemaphoreType.DMA((160,)),
            pltpu.SemaphoreType.DMA((160,)),
            pltpu.SemaphoreType.DMA((24,)),
        ],
        compiler_params=pltpu.CompilerParams(
            collective_id=0, has_side_effects=True, vmem_limit_bytes=64 << 20
        ),
        name="block",
    )(
        context,
        latents,
        cotangent,
        gain_ctx.reshape(1, model_width),
        gain_lat.reshape(1, model_width),
        w_query,
        key_matrix.T,
        value_matrix.T,
        w_out,
        lengths,
        patch_flags.reshape(1, rows),
    )
    out = pl.pallas_call(
        hand_on,
        out_shape=tuple(shaped(a.shape, a.dtype) for a in out),
        in_specs=[any_space] * 9,
        out_specs=(any_space,) * 9,
        scratch_shapes=[pltpu.VMEM(a.shape, a.dtype) for a in out]
        + [pltpu.SemaphoreType.DMA((9,)), pltpu.SemaphoreType.DMA((9,))],
        compiler_params=pltpu.CompilerParams(vmem_limit_bytes=64 << 20),
        name="hand_on",
    )(*out)
    latents_out, grad_context, grad_latents, g_query, g_key, g_value, g_out, gain_c, gain_l = out
    return (
        latents_out,
        grad_context,
        grad_latents,
        g_query,
        g_key.T,
        g_value.T,
        g_out,
        gain_c,
        gain_l,
    )


def solution(mesh):
    n_dp = mesh.shape["dp"]
    body = functools.partial(kernel_local, n_dp) if n_dp == 8 else plain_local
    return jax.shard_map(
        body,
        mesh=mesh,
        in_specs=(
            P("dp", "tensor"),
            P("dp", "tensor"),
            P(),
            P(),
            P(None, "tensor"),
            P(None, "tensor"),
            P(None, "tensor"),
            P(None, "tensor"),
            P("dp", None),
            P("dp"),
            P("dp", "tensor"),
        ),
        out_specs=(
            P("dp", "tensor"),
            P("dp", "tensor"),
            P("dp", "tensor"),
            P("dp", "tensor"),
            P("dp", "tensor"),
            P("dp", "tensor"),
            P("dp", "tensor"),
            P("tensor", "dp"),
            P("tensor", "dp"),
        ),
        check_vma=False,
    )
```
